32 devices in a mesh: dp: 16 (over z, x, core), tensor: 2 (over y).
Axes of the slice: x: 2, y: 2, z: 4, core: 2. Of those that a mesh axis runs over, the one named last changes fastest.
Arguments:
- layer_input: bfloat16 [8192, 1024], P(('dp', 'tensor')), may hold values from -6 to 6
- input_gain: bfloat16 [1024], replicated, may hold values from 0.5 to 1.5
- middle_gain: bfloat16 [1024], replicated, may hold values from 0.5 to 1.5
- mamba_gate: bfloat16 [1024, 1536], P(None, 'tensor'), may hold values from -0.1875 to 0.1875
- mamba_input: bfloat16 [1024, 1536], P(None, 'tensor'), may hold values from -0.1875 to 0.1875
- step_weight: bfloat16 [1024, 24], P(None, 'tensor'), may hold values from -0.1875 to 0.1875
- state_weight: bfloat16 [1024, 256], replicated, may hold values from -0.046875 to 0.046875
- input_kernel: bfloat16 [4, 1536], P(None, 'tensor'), may hold values from -3 to 3
- input_shift: bfloat16 [1536], P('tensor'), may hold values from -3 to 3
- state_kernel: bfloat16 [4, 256], replicated, may hold values from -3 to 3
- state_shift: bfloat16 [256], replicated, may hold values from -2 to 2
- step_bias: bfloat16 [24], P('tensor'), may hold values from -5 to 0
- decay_log: bfloat16 [24], P('tensor'), may hold values from -1 to 2
- skip_gain: bfloat16 [24], P('tensor'), may hold values from 0.5 to 1.5
- mamba_output: bfloat16 [1536, 1024], P('tensor'), may hold values from -0.15625 to 0.15625
- query_weight: bfloat16 [1024, 512], P(None, 'tensor'), may hold values from -0.1875 to 0.1875
- keyvalue_weight: bfloat16 [1024, 256], replicated, may hold values from -0.1875 to 0.1875
- context_weight: bfloat16 [512, 1024], P('tensor'), may hold values from -0.75 to 0.75
- gate_weight: bfloat16 [1024, 2048], P(None, 'tensor'), may hold values from -0.1875 to 0.1875
- up_weight: bfloat16 [1024, 2048], P(None, 'tensor'), may hold values from -0.1875 to 0.1875
- down_weight: bfloat16 [2048, 1024], P('tensor'), may hold values from -0.125 to 0.125
- cotangent: bfloat16 [8192, 1024], P(('dp', 'tensor')), may hold values from -6 to 6
Outputs:
- layer_output: bfloat16 [8192, 1024], P(('dp', 'tensor'))
- input_grad: float32 [8192, 1024], P(('dp', 'tensor'))
- grad_input_gain: float32 [1024], replicated
- grad_middle_gain: float32 [1024], replicated
- grad_mamba_gate: float32 [1024, 1536], P(None, 'tensor')
- grad_mamba_input: float32 [1024, 1536], P(None, 'tensor')
- grad_step_weight: float32 [1024, 24], P(None, 'tensor')
- grad_state_weight: float32 [1024, 256], replicated
- grad_input_kernel: float32 [4, 1536], P(None, 'tensor')
- grad_input_shift: float32 [1536], P('tensor')
- grad_state_kernel: float32 [4, 256], replicated
- grad_state_shift: float32 [256], replicated
- grad_step_bias: float32 [24], P('tensor')
- grad_decay_log: float32 [24], P('tensor')
- grad_skip_gain: float32 [24], P('tensor')
- grad_mamba_output: float32 [1536, 1024], P('tensor')
- grad_query_weight: float32 [1024, 512], P(None, 'tensor')
- grad_keyvalue_weight: float32 [1024, 256], replicated
- grad_context_weight: float32 [512, 1024], P('tensor')
- grad_gate_weight: float32 [1024, 2048], P(None, 'tensor')
- grad_up_weight: float32 [1024, 2048], P(None, 'tensor')
- grad_down_weight: float32 [2048, 1024], P('tensor')
The draws below stay inside these ranges and needn't reach their ends.
All inputs are finite; a program needn't handle non-finite values.
Results may differ from the reference program's by a relative error of at most 0.03.
Values may be sent and summed in bfloat16 or wider, within the bound.
No kernel may reach another device: no remote copies, remote signals or barrier semaphores. Data moves between devices by JAX's collectives and lax.ppermute only.
A program may use at most 192 MiB of HBM per device.

```python
from functools import partial
import jax
import jax.numpy as jnp
from jax import lax

D = 1024
NH = 24
HD = 64
NS = 128
HQ = 8
KVH = 2
FF = 2048
KW = 4
SPAN = 128
DSSM = 1536
GROUP = 512
LENGTH = 512
TOKENS = 8192
N_TENSOR = 2


def shard_levels(key, extent, cuts, smallest, high):
    def one(dim, parts):
        heights = jax.random.uniform(jax.random.fold_in(jax.random.fold_in(key, 6), dim), (parts,), jnp.float32, smallest / len(cuts), high / len(cuts))
        return jnp.repeat(jnp.exp(heights), extent[dim] // parts).reshape((-1,) + (1,) * (len(extent) - dim - 1))

    factor_of = one(*cuts[0])
    for cut in cuts[1:]:
        factor_of = factor_of * one(*cut)
    return factor_of


def centred(own_key, dims, deviation, most, cuts=(), held_as=jnp.bfloat16):
    level = shard_levels(own_key, dims, cuts, -0.22, 0.18) if cuts else 1.0
    result = jax.random.normal(own_key, dims, jnp.float32) * deviation * level
    return jnp.minimum(jnp.maximum(result, -most), most).astype(held_as)


def setup_inputs(seed: int = 0) -> dict:
    streams_of = jax.random.split(jax.random.key(seed), 23)
    layer_input = centred(streams_of[0], (TOKENS, D), 1.0, 6.0, ((0, 32),))
    input_gain = jnp.clip(1.0 + 0.1 * jax.random.normal(streams_of[1], (D,), jnp.float32), 0.5, 1.5).astype(jnp.bfloat16)
    middle_gain = jnp.clip(1.0 + 0.1 * jax.random.normal(streams_of[2], (D,), jnp.float32), 0.5, 1.5).astype(jnp.bfloat16)
    mamba_gate = centred(streams_of[3], (D, DSSM), D ** -0.5, 0.1875, ((1, 2),))
    mamba_input = centred(streams_of[4], (D, DSSM), D ** -0.5, 0.1875, ((1, 2),))
    step_weight = centred(streams_of[5], (D, NH), D ** -0.5, 0.1875, ((1, 2),))
    state_weight = centred(streams_of[6], (D, 2 * NS), (16 * D) ** -0.5, 0.046875)
    input_kernel = centred(streams_of[7], (KW, DSSM), KW ** -0.5, 3.0, ((1, 2),))
    input_shift = centred(streams_of[8], (DSSM,), 0.5, 3.0, ((0, 2),))
    state_kernel = centred(streams_of[9], (KW, 2 * NS), KW ** -0.5, 3.0)
    state_shift = centred(streams_of[10], (2 * NS,), 0.3, 2.0)
    step_bias = jnp.clip(-5.0 + 5.0 * jax.random.uniform(streams_of[11], (NH,), jnp.float32) ** shard_levels(streams_of[11], (NH,), ((0, 2),), -0.2, 0.2), -5.0, 0.0).astype(jnp.bfloat16)
    decay_log = jnp.clip(-1.0 + 3.0 * jax.random.uniform(streams_of[12], (NH,), jnp.float32) ** shard_levels(streams_of[12], (NH,), ((0, 2),), -0.2, 0.2), -1.0, 2.0).astype(jnp.bfloat16)
    skip_gain = jnp.clip(0.5 + 1.0 * jax.random.uniform(streams_of[13], (NH,), jnp.float32) ** shard_levels(streams_of[13], (NH,), ((0, 2),), -0.2, 0.2), 0.5, 1.5).astype(jnp.bfloat16)
    mamba_output = centred(streams_of[14], (DSSM, D), DSSM ** -0.5, 0.15625, ((0, 2),))
    query_weight = centred(streams_of[15], (D, HQ * HD), D ** -0.5, 0.1875, ((1, 2),))
    keyvalue_weight = centred(streams_of[16], (D, 2 * KVH * HD), D ** -0.5, 0.1875)
    context_weight = centred(streams_of[17], (HQ * HD, D), (HQ * HD // 8) ** -0.5, 0.75, ((0, 2),))
    gate_weight = centred(streams_of[18], (D, FF), D ** -0.5, 0.1875, ((1, 2),))
    up_weight = centred(streams_of[19], (D, FF), D ** -0.5, 0.1875, ((1, 2),))
    down_weight = centred(streams_of[20], (FF, D), FF ** -0.5, 0.125, ((0, 2),))
    cotangent = centred(streams_of[21], (TOKENS, D), 1.0, 6.0, ((0, 32),))
    return dict(layer_input=layer_input, input_gain=input_gain, middle_gain=middle_gain, mamba_gate=mamba_gate, mamba_input=mamba_input, step_weight=step_weight, state_weight=state_weight, input_kernel=input_kernel, input_shift=input_shift, state_kernel=state_kernel, state_shift=state_shift, step_bias=step_bias, decay_log=decay_log, skip_gain=skip_gain, mamba_output=mamba_output, query_weight=query_weight, keyvalue_weight=keyvalue_weight, context_weight=context_weight, gate_weight=gate_weight, up_weight=up_weight, down_weight=down_weight, cotangent=cotangent)


EPSILON = 1e-05
ROPE_BASE = 10000.0
PRECISE = lax.Precision.HIGHEST

@jax.custom_vjp
def low(v):
    return lax.optimization_barrier(v.astype(jnp.bfloat16)).astype(jnp.float32)

@jax.custom_vjp
def low_back(v):
    return v

def low_keep(v):
    return (low(v), None)

def low_pass(kept, grad):
    return (grad,)

def back_keep(v):
    return (v, None)

def back_low(kept, grad):
    return (low(grad),)
low.defvjp(low_keep, low_pass)
low_back.defvjp(back_keep, back_low)

def matmul(left, right):
    return jnp.dot(left, right, precision=PRECISE, preferred_element_type=jnp.float32)

def rms_hat(rows):
    return rows * lax.rsqrt(lax.optimization_barrier(jnp.mean(rows * rows, axis=-1, keepdims=True)) + EPSILON)

def ssd_block(rates, carry, block):
    inputs, steps, entry, readout = block
    logdec = steps * rates[None, :]
    cumul = jnp.cumsum(logdec, axis=0)
    count = cumul.shape[0]
    lower = jnp.arange(count)[:, None] >= jnp.arange(count)[None, :]
    spread = cumul[:, None, :] - cumul[None, :, :]
    decay = jnp.exp(jnp.where(lower[:, :, None], spread, -jnp.inf))
    intersection = jnp.dot(readout, entry.T, precision=PRECISE)
    scaled = inputs * steps[:, :, None]
    within = jnp.einsum('ijh,jhp->ihp', decay * intersection[:, :, None], scaled, precision=PRECISE)
    carried = jnp.einsum('in,hpn->ihp', readout, carry, precision=PRECISE) * jnp.exp(cumul)[:, :, None]
    tail = jnp.exp(cumul[-1][None, :] - cumul)
    update = jnp.einsum('jhp,jn->hpn', scaled * tail[:, :, None], entry, precision=PRECISE)
    carry = carry * jnp.exp(cumul[-1])[:, None, None] + update
    return (carry, within + carried)

def ssd_sequence(inputs, steps, entry, readout, rates):
    length = inputs.shape[0]
    blocks = length // SPAN
    heads = inputs.shape[1]
    size = inputs.shape[2]
    states = entry.shape[1]
    stacked = (inputs.reshape(blocks, SPAN, heads, size), steps.reshape(blocks, SPAN, heads), entry.reshape(blocks, SPAN, states), readout.reshape(blocks, SPAN, states))
    start = jnp.zeros((heads, size, states), jnp.float32)
    final, outputs = lax.scan(jax.checkpoint(partial(ssd_block, rates)), start, stacked)
    return outputs.reshape(length, heads, size)

def ssm_branch(ssm_gate, ssm_input, step_raw, state_raw, input_kernel, input_shift, state_kernel, state_shift, step_bias, decay_log, skip_gain, length):
    total_rows = ssm_input.shape[0]
    seqs = total_rows // length
    heads = step_raw.shape[1]
    channels = ssm_input.shape[1]
    head_size = channels // heads
    states = state_raw.shape[1] // 2
    joined = jnp.concatenate([ssm_input, state_raw], axis=1)
    kernel = jnp.concatenate([input_kernel, state_kernel], axis=1)
    shifts = jnp.concatenate([input_shift, state_shift], axis=0)
    taps = kernel.shape[0]
    seqwise = joined.reshape(seqs, length, joined.shape[1])
    padded = jnp.pad(seqwise, ((0, 0), (taps - 1, 0), (0, 0)))
    filtered = jnp.broadcast_to(shifts, seqwise.shape)
    for index in range(taps):
        filtered = filtered + kernel[index] * padded[:, index:index + length]
    active = jax.nn.silu(filtered)
    inputs = active[:, :, :channels].reshape(seqs, length, heads, head_size)
    entry = active[:, :, channels:channels + states]
    readout = active[:, :, channels + states:]
    steps = jax.nn.softplus(step_raw.reshape(seqs, length, heads) + step_bias)
    rates = -jnp.exp(decay_log)
    outputs = lax.map(lambda group: ssd_sequence(group[0], group[1], group[2], group[3], rates), (inputs, steps, entry, readout))
    outputs = outputs + skip_gain[:, None] * inputs
    return outputs.reshape(total_rows, channels) * jax.nn.silu(ssm_gate)

def rope_tables(length, head_size):
    half = head_size // 2
    freqs = ROPE_BASE ** (-jnp.arange(half, dtype=jnp.float32) * 2.0 / head_size)
    angles = jnp.arange(length, dtype=jnp.float32)[:, None] * freqs[None, :]
    return (jnp.cos(angles), jnp.sin(angles))

def rotate(vecs, cosine, sine):
    half = vecs.shape[-1] // 2
    first = vecs[..., :half]
    second = vecs[..., half:]
    cosine = cosine[:, None, :]
    sine = sine[:, None, :]
    return jnp.concatenate([first * cosine - second * sine, second * cosine + first * sine], axis=-1)

def attend(query_raw, key_raw, value_raw):
    length = query_raw.shape[0]
    heads = query_raw.shape[1] // HD
    cosine, sine = rope_tables(length, HD)
    query = low(rotate(query_raw.reshape(length, heads, HD), cosine, sine))
    key = low(rotate(key_raw.reshape(length, 1, HD), cosine, sine))[:, 0]
    value = low(value_raw)
    scores = low_back(jnp.einsum('ihd,jd->hij', query, key, precision=PRECISE) * HD ** (-0.5))
    causal = jnp.arange(length)[:, None] >= jnp.arange(length)[None, :]
    scores = jnp.where(causal[None], scores, -jnp.inf)
    probs = low(jax.nn.softmax(scores, axis=-1))
    context = jnp.einsum('hij,jd->ihd', probs, value, precision=PRECISE)
    return context.reshape(length, heads * HD)

def group_forward(rows, params):
    input_gain, middle_gain, mamba_gate, mamba_input, step_weight, state_weight, input_kernel, input_shift, state_kernel, state_shift, step_bias, decay_log, skip_gain, mamba_output, query_weight, keyvalue_weight, context_weight, gate_weight, up_weight, down_weight = params
    shards = N_TENSOR
    length = LENGTH
    seqs = GROUP // LENGTH
    ssm_cols = DSSM // shards
    head_cols = NH // shards
    query_heads = HQ // shards
    query_cols = query_heads * HD
    hidden_cols = FF // shards
    normed = low(rms_hat(rows) * input_gain)
    mixed = jnp.zeros_like(rows)
    for shard in range(shards):
        local = low_back(normed)
        lo_c = shard * ssm_cols
        lo_h = shard * head_cols
        lo_q = shard * query_cols
        gated = ssm_branch(low_back(matmul(local, mamba_gate[:, lo_c:lo_c + ssm_cols])), low_back(matmul(local, mamba_input[:, lo_c:lo_c + ssm_cols])), low_back(matmul(local, step_weight[:, lo_h:lo_h + head_cols])), low_back(matmul(local, state_weight)), input_kernel[:, lo_c:lo_c + ssm_cols], input_shift[lo_c:lo_c + ssm_cols], state_kernel, state_shift, step_bias[lo_h:lo_h + head_cols], decay_log[lo_h:lo_h + head_cols], skip_gain[lo_h:lo_h + head_cols], length)
        kv_head = shard * query_heads // (HQ // KVH)
        query_raw = low_back(matmul(local, query_weight[:, lo_q:lo_q + query_cols]))
        key_raw = low_back(matmul(local, keyvalue_weight[:, kv_head * HD:(kv_head + 1) * HD]))
        value_raw = low_back(matmul(local, keyvalue_weight[:, (KVH + kv_head) * HD:(KVH + kv_head + 1) * HD]))
        context = lax.map(jax.checkpoint(lambda seq: attend(seq[0], seq[1], seq[2])), (query_raw.reshape(seqs, length, query_cols), key_raw.reshape(seqs, length, HD), value_raw.reshape(seqs, length, HD)))
        context = low(low_back(context.reshape(GROUP, query_cols)))
        term = matmul(low(gated), mamba_output[lo_c:lo_c + ssm_cols]) + matmul(context, context_weight[lo_q:lo_q + query_cols])
        mixed = mixed + low(term)
    resid = rows + low_back(mixed)
    normed2 = low(rms_hat(resid) * middle_gain)
    summed = jnp.zeros_like(rows)
    for shard in range(shards):
        local = low_back(normed2)
        lo_f = shard * hidden_cols
        gate = low_back(matmul(local, gate_weight[:, lo_f:lo_f + hidden_cols]))
        upper = low_back(matmul(local, up_weight[:, lo_f:lo_f + hidden_cols]))
        hidden = low(jax.nn.silu(gate) * upper)
        summed = summed + low(matmul(hidden, down_weight[lo_f:lo_f + hidden_cols]))
    return resid + low_back(summed)

def reference(layer_input, input_gain, middle_gain, mamba_gate, mamba_input, step_weight, state_weight, input_kernel, input_shift, state_kernel, state_shift, step_bias, decay_log, skip_gain, mamba_output, query_weight, keyvalue_weight, context_weight, gate_weight, up_weight, down_weight, cotangent):
    params = tuple((item.astype(jnp.float32) for item in (input_gain, middle_gain, mamba_gate, mamba_input, step_weight, state_weight, input_kernel, input_shift, state_kernel, state_shift, step_bias, decay_log, skip_gain, mamba_output, query_weight, keyvalue_weight, context_weight, gate_weight, up_weight, down_weight)))
    groups = TOKENS // GROUP
    inputs = layer_input.astype(jnp.float32).reshape(groups, GROUP, D)
    cotans = cotangent.astype(jnp.float32).reshape(groups, GROUP, D)
    zeros = jax.tree.map(jnp.zeros_like, params)

    def advance(totals, pair):
        rows, cotan = pair
        output, pullback = jax.vjp(group_forward, rows, params)
        row_grad, param_grads = pullback(cotan)
        totals = jax.tree.map(jnp.add, totals, param_grads)
        return (totals, (output, row_grad))
    totals, (outputs, row_grads) = lax.scan(advance, zeros, (inputs, cotans))
    return (outputs.reshape(TOKENS, D).astype(jnp.bfloat16), row_grads.reshape(TOKENS, D), totals[0], totals[1], totals[2], totals[3], totals[4], totals[5], totals[6], totals[7], totals[8], totals[9], totals[10], totals[11], totals[12], totals[13], totals[14], totals[15], totals[16], totals[17], totals[18], totals[19])
```

```python
from functools import partial

import jax
import jax.numpy as jnp
from jax import lax
from jax.sharding import PartitionSpec as P

HD = 64
HQ = 8
KVH = 2
SPAN = 128
SEQ_LEN = 1024


EPSILON = 1e-05
ROPE_BASE = 10000.0
PRECISE = lax.Precision.HIGHEST


def ssd_block(rates, carry, block):
    inputs, steps, entry, readout = block
    logdec = steps * rates[None, :]
    cumul = jnp.cumsum(logdec, axis=0)
    count = cumul.shape[0]
    lower = jnp.arange(count)[:, None] >= jnp.arange(count)[None, :]
    spread = cumul[:, None, :] - cumul[None, :, :]
    decay = jnp.exp(jnp.where(lower[:, :, None], spread, -jnp.inf))
    intersection = jnp.dot(readout, entry.T, precision=PRECISE)
    scaled = inputs * steps[:, :, None]
    within = jnp.einsum("ijh,jhp->ihp", decay * intersection[:, :, None], scaled, precision=PRECISE)
    carried = (
        jnp.einsum("in,hpn->ihp", readout, carry, precision=PRECISE) * jnp.exp(cumul)[:, :, None]
    )
    tail = jnp.exp(cumul[-1][None, :] - cumul)
    update = jnp.einsum("jhp,jn->hpn", scaled * tail[:, :, None], entry, precision=PRECISE)
    carry = carry * jnp.exp(cumul[-1])[:, None, None] + update
    return (carry, within + carried)


def ssd_sequence(inputs, steps, entry, readout, rates):
    length = inputs.shape[0]
    blocks = length // SPAN
    heads = inputs.shape[1]
    size = inputs.shape[2]
    states = entry.shape[1]
    stacked = (
        inputs.reshape(blocks, SPAN, heads, size),
        steps.reshape(blocks, SPAN, heads),
        entry.reshape(blocks, SPAN, states),
        readout.reshape(blocks, SPAN, states),
    )
    start = jnp.zeros((heads, size, states), jnp.float32)
    final, outputs = lax.scan(jax.checkpoint(partial(ssd_block, rates)), start, stacked)
    return outputs.reshape(length, heads, size)


def ssm_branch(
    ssm_gate,
    ssm_input,
    step_raw,
    state_raw,
    input_kernel,
    input_shift,
    state_kernel,
    state_shift,
    step_bias,
    decay_log,
    skip_gain,
    length,
):
    total_rows = ssm_input.shape[0]
    seqs = total_rows // length
    heads = step_raw.shape[1]
    channels = ssm_input.shape[1]
    head_size = channels // heads
    states = state_raw.shape[1] // 2
    joined = jnp.concatenate([ssm_input, state_raw], axis=1)
    kernel = jnp.concatenate([input_kernel, state_kernel], axis=1)
    shifts = jnp.concatenate([input_shift, state_shift], axis=0)
    taps = kernel.shape[0]
    seqwise = joined.reshape(seqs, length, joined.shape[1])
    padded = jnp.pad(seqwise, ((0, 0), (taps - 1, 0), (0, 0)))
    filtered = jnp.broadcast_to(shifts, seqwise.shape)
    for index in range(taps):
        filtered = filtered + kernel[index] * padded[:, index : index + length]
    active = jax.nn.silu(filtered)
    inputs = active[:, :, :channels].reshape(seqs, length, heads, head_size)
    entry = active[:, :, channels : channels + states]
    readout = active[:, :, channels + states :]
    steps = jax.nn.softplus(step_raw.reshape(seqs, length, heads) + step_bias)
    rates = -jnp.exp(decay_log)
    outputs = lax.map(
        lambda group: ssd_sequence(group[0], group[1], group[2], group[3], rates),
        (inputs, steps, entry, readout),
    )
    outputs = outputs + skip_gain[:, None] * inputs
    return outputs.reshape(total_rows, channels) * jax.nn.silu(ssm_gate)


def rope_tables(length, head_size):
    half = head_size // 2
    freqs = ROPE_BASE ** (-jnp.arange(half, dtype=jnp.float32) * 2.0 / head_size)
    angles = jnp.arange(length, dtype=jnp.float32)[:, None] * freqs[None, :]
    return (jnp.cos(angles), jnp.sin(angles))


def rotate(vecs, cosine, sine):
    half = vecs.shape[-1] // 2
    first = vecs[..., :half]
    second = vecs[..., half:]
    cosine = cosine[:, None, :]
    sine = sine[:, None, :]
    return jnp.concatenate(
        [first * cosine - second * sine, second * cosine + first * sine], axis=-1
    )


def unrotate(vecs, cosine, sine):
    half = vecs.shape[-1] // 2
    first = vecs[..., :half]
    second = vecs[..., half:]
    cosine = cosine[:, None, :]
    sine = sine[:, None, :]
    return jnp.concatenate(
        [first * cosine + second * sine, second * cosine - first * sine], axis=-1
    )


def forward_dot(left, right):
    return jnp.dot(left, right, preferred_element_type=jnp.float32)


def inner_rows(left, right):
    return lax.dot_general(
        left, right, (((0,), (0,)), ((), ())), preferred_element_type=jnp.float32
    )


def against(left, right):
    return lax.dot_general(
        left, right, (((1,), (1,)), ((), ())), preferred_element_type=jnp.float32
    )


def norm_back(upstream, gain, normal, factor):
    scaled = upstream * gain
    return factor * (scaled - normal * jnp.mean(scaled * normal, axis=-1, keepdims=True))


def bit_pairs(size, bit):
    return [(index, index ^ (1 << bit)) for index in range(size)]


def split_half(part, bit, size):
    side = (lax.axis_index("dp") >> bit) & 1
    halves = part.reshape(2, part.shape[0] // 2, part.shape[1])
    keep = lax.dynamic_index_in_dim(halves, side, 0, False)
    give = lax.dynamic_index_in_dim(halves, 1 - side, 0, False)
    got = lax.ppermute(give, "dp", bit_pairs(size, bit))
    return (keep.astype(jnp.float32) + got.astype(jnp.float32)).astype(jnp.bfloat16)


def join_half(part, bit, size):
    side = (lax.axis_index("dp") >> bit) & 1
    got = lax.ppermute(part, "dp", bit_pairs(size, bit))
    return jnp.where(
        side == 0, jnp.concatenate([part, got], axis=0), jnp.concatenate([got, part], axis=0)
    )


def bit_order(size, swapped):
    order = list(range(size.bit_length() - 1))
    if swapped and len(order) > 2:
        order[1], order[2] = order[2], order[1]
    return order


def sum_dp(part, size, swapped, middle=None):
    if size & (size - 1) or part.shape[0] % size:
        part = lax.psum(part, "dp")
        return part if middle is None else middle(part)
    order = bit_order(size, swapped)
    for bit in order:
        part = split_half(part, bit, size)
    if middle is not None:
        part = middle(part)
    for bit in reversed(order):
        part = join_half(part, bit, size)
    return part


def other(part):
    return lax.ppermute(part, "tensor", [(0, 1), (1, 0)])


def all_rows(part, shards):
    if shards != 2:
        return lax.all_gather(part, "tensor", axis=0, tiled=True)
    got = other(part)
    return jnp.where(
        lax.axis_index("tensor") == 0,
        jnp.concatenate([part, got], axis=0),
        jnp.concatenate([got, part], axis=0),
    )


def sum_all(part, shards):
    if shards != 2:
        return lax.psum(part, "tensor").astype(jnp.float32)
    return part.astype(jnp.float32) + other(part).astype(jnp.float32)


def sum_own(part, shards):
    if shards != 2:
        return lax.psum_scatter(part, "tensor", scatter_dimension=0, tiled=True).astype(jnp.float32)
    me = lax.axis_index("tensor")
    halves = part.reshape(2, part.shape[0] // 2, part.shape[1])
    keep = lax.dynamic_index_in_dim(halves, me, 0, False)
    got = other(lax.dynamic_index_in_dim(halves, 1 - me, 0, False))
    return keep.astype(jnp.float32) + got.astype(jnp.float32)


def own_rows(part, rows):
    return lax.dynamic_slice_in_dim(part, lax.axis_index("tensor") * rows, rows, 0)


def column_pack(vectors, rows):
    flat = jnp.concatenate([item.reshape(-1) for item in vectors])
    width = -(-flat.shape[0] // rows)
    return jnp.pad(flat, (0, width * rows - flat.shape[0])).reshape(width, rows).T


def column_unpack(packed, shapes):
    flat = packed.T.reshape(-1)
    out, start = [], 0
    for shape in shapes:
        count = 1
        for size in shape:
            count *= size
        out.append(flat[start : start + count].reshape(shape))
        start += count
    return out


def body(
    dp_size,
    shards,
    layer_input,
    input_gain,
    middle_gain,
    mamba_gate,
    mamba_input,
    step_weight,
    state_weight,
    input_kernel,
    input_shift,
    state_kernel,
    state_shift,
    step_bias,
    decay_log,
    skip_gain,
    mamba_output,
    query_weight,
    keyvalue_weight,
    context_weight,
    gate_weight,
    up_weight,
    down_weight,
    cotangent,
):
    own = layer_input.shape[0]
    rows_low = all_rows(layer_input, shards)
    cotan_low = all_rows(cotangent, shards)
    rows = rows_low.astype(jnp.float32)
    gain_first = input_gain.astype(jnp.float32)
    gain_second = middle_gain.astype(jnp.float32)
    factor_first = lax.rsqrt(jnp.mean(rows * rows, axis=-1, keepdims=True) + EPSILON)
    normal_first = rows * factor_first
    whole = (normal_first * gain_first).astype(jnp.bfloat16)
    group = whole.shape[0]
    length = min(SEQ_LEN, group)
    seqs = group // length
    heads_here = query_weight.shape[1] // HD
    kv_head = lax.axis_index("tensor") * heads_here // (HQ // KVH)
    key_cols = lax.dynamic_slice_in_dim(keyvalue_weight, kv_head * HD, HD, 1)
    value_cols = lax.dynamic_slice_in_dim(keyvalue_weight, (KVH + kv_head) * HD, HD, 1)
    pair_weight = jnp.concatenate([key_cols, value_cols], axis=1)
    gate_raw = forward_dot(whole, mamba_gate)
    input_raw = forward_dot(whole, mamba_input)
    step_raw = forward_dot(whole, step_weight)
    state_raw = forward_dot(whole, state_weight)
    query_raw = forward_dot(whole, query_weight)
    pair_raw = forward_dot(whole, pair_weight)
    small = (
        input_kernel.astype(jnp.float32),
        input_shift.astype(jnp.float32),
        state_kernel.astype(jnp.float32),
        state_shift.astype(jnp.float32),
        step_bias.astype(jnp.float32),
        decay_log.astype(jnp.float32),
        skip_gain.astype(jnp.float32),
    )
    gated, mamba_pull = jax.vjp(
        partial(ssm_branch, length=length),
        gate_raw,
        input_raw,
        step_raw,
        state_raw,
        small[0],
        small[1],
        small[2],
        small[3],
        small[4],
        small[5],
        small[6],
    )
    gated_low = gated.astype(jnp.bfloat16)
    cosine, sine = rope_tables(length, HD)
    scale = HD ** (-0.5)
    causal = jnp.arange(length)[:, None] >= jnp.arange(length)[None, :]

    def attend_forward(seq):
        query_seq, pair_seq = seq
        query = rotate(query_seq.reshape(length, heads_here, HD), cosine, sine).astype(jnp.bfloat16)
        key = rotate(pair_seq[:, None, :HD], cosine, sine)[:, 0].astype(jnp.bfloat16)
        value = pair_seq[:, HD:].astype(jnp.bfloat16)
        scores = jnp.einsum("ihd,jd->hij", query, key, preferred_element_type=jnp.float32) * scale
        scores = jnp.where(causal[None], scores, -jnp.inf)
        peak = jnp.max(scores, axis=-1, keepdims=True)
        total = jnp.log(jnp.sum(jnp.exp(scores - peak), axis=-1, keepdims=True)) + peak
        probs = jnp.exp(scores - total).astype(jnp.bfloat16)
        context = jnp.einsum("hij,jd->ihd", probs, value, preferred_element_type=jnp.float32)
        return (
            context.reshape(length, heads_here * HD).astype(jnp.bfloat16),
            total,
            query,
            key,
            value,
        )

    context_seq, totals, queries, keys, values = lax.map(
        attend_forward,
        (query_raw.reshape(seqs, length, heads_here * HD), pair_raw.reshape(seqs, length, 2 * HD)),
    )
    context_rows = context_seq.reshape(group, heads_here * HD)
    mixed_part = forward_dot(gated_low, mamba_output) + forward_dot(context_rows, context_weight)
    resid = rows + sum_all(mixed_part.astype(jnp.bfloat16), shards)
    factor_second = lax.rsqrt(jnp.mean(resid * resid, axis=-1, keepdims=True) + EPSILON)
    normal_second = resid * factor_second
    whole_mid = (normal_second * gain_second).astype(jnp.bfloat16)
    gate = forward_dot(whole_mid, gate_weight)
    upper = forward_dot(whole_mid, up_weight)
    sigmoid_gate = jax.nn.sigmoid(gate)
    silu_gate = gate * sigmoid_gate
    hidden = (silu_gate * upper).astype(jnp.bfloat16)
    grad_hidden = against(cotan_low, down_weight)
    slope = sigmoid_gate * (1.0 + gate * (1.0 - sigmoid_gate))
    grad_gate_low = (grad_hidden * upper * slope).astype(jnp.bfloat16)
    grad_upper_low = (grad_hidden * silu_gate).astype(jnp.bfloat16)
    back_part = (against(grad_gate_low, gate_weight) + against(grad_upper_low, up_weight)).astype(
        jnp.bfloat16
    )
    back_mid = sum_all(back_part, shards)
    feed = sum_own(forward_dot(hidden, down_weight).astype(jnp.bfloat16), shards)
    layer_output = (own_rows(resid, own) + feed).astype(jnp.bfloat16)
    grad_down = inner_rows(hidden, cotan_low).astype(jnp.bfloat16)
    grad_gate = inner_rows(whole_mid, grad_gate_low).astype(jnp.bfloat16)
    grad_up = inner_rows(whole_mid, grad_upper_low).astype(jnp.bfloat16)
    grad_gate = sum_dp(grad_gate, dp_size, False)
    grad_up = sum_dp(grad_up, dp_size, True)
    grad_down = sum_dp(grad_down, dp_size, False)
    grad_middle = jnp.sum(back_part.astype(jnp.float32) * normal_second, axis=0)
    grad_resid = cotan_low.astype(jnp.float32) + norm_back(
        back_mid, gain_second, normal_second, factor_second
    )
    mixer_all = grad_resid.astype(jnp.bfloat16)
    grad_mixer_out = inner_rows(
        jnp.concatenate([gated_low, context_rows], axis=1), mixer_all
    ).astype(jnp.bfloat16)
    grad_mixer_out = sum_dp(grad_mixer_out, dp_size, True)
    ssm_rows = gated_low.shape[1]
    grad_mamba_out = grad_mixer_out[:ssm_rows]
    grad_context_w = grad_mixer_out[ssm_rows:]
    grad_gated = against(mixer_all, mamba_output)
    pulled = mamba_pull(grad_gated)
    grad_gate_raw = pulled[0].astype(jnp.bfloat16)
    grad_input_raw = pulled[1].astype(jnp.bfloat16)
    grad_step_raw = pulled[2].astype(jnp.bfloat16)
    grad_state_raw = pulled[3].astype(jnp.bfloat16)
    grad_context = against(mixer_all, context_weight).astype(jnp.bfloat16)

    def attend_backward(seq):
        grad_seq, query, key, value, total = seq
        grad_seq = grad_seq.reshape(length, heads_here, HD)
        scores = jnp.einsum("ihd,jd->hij", query, key, preferred_element_type=jnp.float32) * scale
        scores = jnp.where(causal[None], scores, -jnp.inf)
        probs = jnp.exp(scores - total)
        grad_value = jnp.einsum(
            "hij,ihd->jd", probs.astype(jnp.bfloat16), grad_seq, preferred_element_type=jnp.float32
        )
        grad_probs = jnp.einsum("ihd,jd->hij", grad_seq, value, preferred_element_type=jnp.float32)
        grad_scores = (
            probs * (grad_probs - jnp.sum(probs * grad_probs, axis=-1, keepdims=True))
        ).astype(jnp.bfloat16)
        grad_query = (
            jnp.einsum("hij,jd->ihd", grad_scores, key, preferred_element_type=jnp.float32) * scale
        )
        grad_key = (
            jnp.einsum("hij,ihd->jd", grad_scores, query, preferred_element_type=jnp.float32)
            * scale
        )
        grad_query = (
            unrotate(grad_query, cosine, sine).reshape(length, heads_here * HD).astype(jnp.bfloat16)
        )
        grad_key = unrotate(grad_key[:, None, :], cosine, sine)[:, 0]
        return (grad_query, jnp.concatenate([grad_key, grad_value], axis=1).astype(jnp.bfloat16))

    grad_query_seq, grad_pair_seq = lax.map(
        attend_backward,
        (grad_context.reshape(seqs, length, heads_here * HD), queries, keys, values, totals),
    )
    grad_query_raw = grad_query_seq.reshape(group, heads_here * HD)
    grad_pair_raw = grad_pair_seq.reshape(group, 2 * HD)
    total = against(grad_gate_raw, mamba_gate)
    total = total + against(grad_input_raw, mamba_input)
    total = total + against(grad_step_raw, step_weight)
    total = total + against(grad_state_raw, state_weight)
    total = total + against(grad_query_raw, query_weight)
    total = total + against(grad_pair_raw, pair_weight)
    total_low = total.astype(jnp.bfloat16)
    grad_first = jnp.sum(total_low.astype(jnp.float32) * normal_first, axis=0)
    width = whole.shape[1]
    gate_cols = grad_gate_raw.shape[1]
    query_cols = grad_query_raw.shape[1]
    input_cols = grad_input_raw.shape[1]
    state_cols = grad_state_raw.shape[1]
    step_cols = grad_step_raw.shape[1]
    pair_cols = grad_pair_raw.shape[1]

    own_vectors = (pulled[4], pulled[5], pulled[8], pulled[9], pulled[10])
    shared_vectors = (grad_first, grad_middle, pulled[6], pulled[7])
    own_pack = column_pack(own_vectors, width).astype(jnp.bfloat16)
    shared_pack = column_pack(shared_vectors, width).astype(jnp.bfloat16)
    own_width = own_pack.shape[1]
    shared_width = shared_pack.shape[1]

    early = inner_rows(whole, jnp.concatenate([grad_gate_raw, grad_query_raw], axis=1))
    early = sum_dp(early.astype(jnp.bfloat16), dp_size, False)

    split_pairs = shards == KVH
    late = inner_rows(
        whole,
        jnp.concatenate([grad_input_raw, grad_state_raw, grad_pair_raw, grad_step_raw], axis=1),
    ).astype(jnp.bfloat16)
    marks = (input_cols, input_cols + state_cols, input_cols + state_cols + pair_cols)
    late_pair = late[:, marks[1] : marks[2]]
    if not split_pairs:
        spread = jnp.zeros((width, 2 * KVH * HD), jnp.bfloat16)
        spread = lax.dynamic_update_slice_in_dim(spread, late_pair[:, :HD], kv_head * HD, 1)
        late_pair = lax.dynamic_update_slice_in_dim(
            spread, late_pair[:, HD:], (KVH + kv_head) * HD, 1
        )
    tail = jnp.concatenate(
        [late[:, input_cols : marks[1]], late_pair, shared_pack, late[:, marks[2] :], own_pack],
        axis=1,
    )
    sent = state_cols + late_pair.shape[1] + shared_width

    def over_tensor(part):
        shared, rest = part[:, :sent], part[:, sent:]
        if not split_pairs:
            return jnp.concatenate([lax.psum(shared, "tensor"), rest], axis=1)
        got = other(shared)
        first = lax.axis_index("tensor") == 0
        low = jnp.where(first, shared, got)[:, state_cols : state_cols + pair_cols]
        high = jnp.where(first, got, shared)[:, state_cols : state_cols + pair_cols]
        both = (shared.astype(jnp.float32) + got.astype(jnp.float32)).astype(jnp.bfloat16)
        return jnp.concatenate(
            [
                both[:, :state_cols],
                low[:, :HD],
                high[:, :HD],
                low[:, HD:],
                high[:, HD:],
                both[:, state_cols + pair_cols :],
                rest,
            ],
            axis=1,
        )

    tail = sum_dp(tail, dp_size, True, over_tensor)
    grad_mamba_input = sum_dp(late[:, :input_cols], dp_size, False)
    back_in = sum_own(total_low, shards)
    normal_own = own_rows(normal_first, own)
    factor_own = own_rows(factor_first, own)
    input_grad = own_rows(grad_resid, own) + norm_back(back_in, gain_first, normal_own, factor_own)
    after = state_cols + keyvalue_weight.shape[1]
    grad_first, grad_middle, grad_st_kernel, grad_st_shift = column_unpack(
        tail[:, after : after + shared_width], [item.shape for item in shared_vectors]
    )
    after = after + shared_width
    grad_step = tail[:, after : after + step_cols]
    grad_in_kernel, grad_in_shift, grad_bias, grad_decay, grad_skip = column_unpack(
        tail[:, after + step_cols :], [item.shape for item in own_vectors]
    )
    results = (
        grad_first,
        grad_middle,
        early[:, :gate_cols],
        grad_mamba_input,
        grad_step,
        tail[:, :state_cols],
        grad_in_kernel,
        grad_in_shift,
        grad_st_kernel,
        grad_st_shift,
        grad_bias,
        grad_decay,
        grad_skip,
        grad_mamba_out,
        early[:, gate_cols:],
        tail[:, state_cols : state_cols + keyvalue_weight.shape[1]],
        grad_context_w,
        grad_gate,
        grad_up,
        grad_down,
    )
    return (layer_output, input_grad) + tuple(item.astype(jnp.float32) for item in results)


def solution(mesh):
    in_specs = (
        P(("dp", "tensor"), None),
        P(),
        P(),
        P(None, "tensor"),
        P(None, "tensor"),
        P(None, "tensor"),
        P(),
        P(None, "tensor"),
        P("tensor"),
        P(),
        P(),
        P("tensor"),
        P("tensor"),
        P("tensor"),
        P("tensor", None),
        P(None, "tensor"),
        P(),
        P("tensor", None),
        P(None, "tensor"),
        P(None, "tensor"),
        P("tensor", None),
        P(("dp", "tensor"), None),
    )
    out_specs = (
        P(("dp", "tensor"), None),
        P(("dp", "tensor"), None),
        P(),
        P(),
        P(None, "tensor"),
        P(None, "tensor"),
        P(None, "tensor"),
        P(),
        P(None, "tensor"),
        P("tensor"),
        P(),
        P(),
        P("tensor"),
        P("tensor"),
        P("tensor"),
        P("tensor", None),
        P(None, "tensor"),
        P(),
        P("tensor", None),
        P(None, "tensor"),
        P(None, "tensor"),
        P("tensor", None),
    )
    run = partial(body, mesh.shape["dp"], mesh.shape["tensor"])
    return jax.shard_map(run, mesh=mesh, in_specs=in_specs, out_specs=out_specs, check_vma=False)
```

```python
from functools import partial

import jax
import jax.numpy as jnp
import numpy as np
from jax import lax
from jax.experimental import pallas as pl
from jax.experimental.pallas import tpu as pltpu
from jax.sharding import PartitionSpec as P

HD = 64
HQ = 8
KVH = 2
SPAN = 128
SEQ_LEN = 1024


EPSILON = 1e-05
ROPE_BASE = 10000.0
PRECISE = lax.Precision.HIGHEST


def forward_dot(left, right):
    return jnp.dot(left, right, preferred_element_type=jnp.float32)


def inner_rows(left, right):
    return lax.dot_general(
        left, right, (((0,), (0,)), ((), ())), preferred_element_type=jnp.float32
    )


def against(left, right):
    return lax.dot_general(
        left, right, (((1,), (1,)), ((), ())), preferred_element_type=jnp.float32
    )


def norm_back(upstream, gain, normal, factor):
    scaled = upstream * gain
    return factor * (scaled - normal * jnp.mean(scaled * normal, axis=-1, keepdims=True))


LANES = 128
VMEM_LIMIT = 44 * 1024 * 1024


def exact_dot(left, right):
    return jnp.dot(left, right, precision=PRECISE, preferred_element_type=jnp.float32)


def low_dot(left, right):
    return jnp.dot(
        left.astype(jnp.bfloat16), right.astype(jnp.bfloat16), preferred_element_type=jnp.float32
    )


def low_against(left, right):
    return lax.dot_general(
        left.astype(jnp.bfloat16),
        right.astype(jnp.bfloat16),
        (((1,), (1,)), ((), ())),
        preferred_element_type=jnp.float32,
    )


def low_inner(left, right):
    return lax.dot_general(
        left.astype(jnp.bfloat16),
        right.astype(jnp.bfloat16),
        (((0,), (0,)), ((), ())),
        preferred_element_type=jnp.float32,
    )


def row_index(shape):
    return lax.broadcasted_iota(jnp.int32, shape, 0)


def lane_index(shape):
    return lax.broadcasted_iota(jnp.int32, shape, 1)


def later(part, count):
    if count == 0:
        return part
    return jnp.where(row_index(part.shape) >= count, pltpu.roll(part, count, 0), 0.0)


def sooner(part, count):
    if count == 0:
        return part
    rows = part.shape[0]
    return jnp.where(row_index(part.shape) < rows - count, pltpu.roll(part, rows - count, 0), 0.0)


def slabs(width):
    return [(start, min(LANES, width - start)) for start in range(0, width, LANES)]


def soft_plus(value):
    return jnp.maximum(value, 0.0) + jnp.log1p(jnp.exp(-jnp.abs(value)))


def stacked_heads(part, heads):
    if heads == 1:
        return part
    lane = lane_index(part.shape)
    return jnp.concatenate(
        [jnp.where((lane >= head * HD) & (lane < head * HD + HD), part, 0.0) for head in range(heads)],
        axis=0,
    )


def convolve(raw, kernel_ref, shift_ref, cols):
    taps = kernel_ref.shape[0]
    out = shift_ref[:, cols] + kernel_ref[taps - 1 : taps, cols] * raw
    for tap in range(taps - 1):
        out = out + kernel_ref[tap : tap + 1, cols] * later(raw, taps - 1 - tap)
    return out


def chunk_steps(step_ref, bias_ref, rate_ref, expand_ref, rows):
    raw = step_ref[rows, :] + bias_ref[...]
    steps = soft_plus(raw)
    logdec = steps * rate_ref[...]
    square = (SPAN, SPAN)
    lower = (row_index(square) >= lane_index(square)).astype(jnp.float32)
    cumul = exact_dot(lower, logdec)
    grown = jnp.exp(cumul)
    tail = jnp.exp(cumul[SPAN - 1 : SPAN, :] - cumul)
    wide = exact_dot(jnp.concatenate([steps, grown, tail], axis=0), expand_ref[...])
    return raw, steps, cumul, wide[:SPAN], wide[SPAN : 2 * SPAN], wide[2 * SPAN :]


def ssd_forward_kernel(
    input_ref,
    state_ref,
    gate_ref,
    step_ref,
    input_kernel_ref,
    input_shift_ref,
    state_kernel_ref,
    state_shift_ref,
    bias_ref,
    rate_ref,
    skip_ref,
    expand_ref,
    gated_ref,
    out_ref,
    carry_ref,
    act_ref,
    both_ref,
    held_ref,
):
    channels = input_ref.shape[1]
    states = state_ref.shape[1] // 2
    for start, width in slabs(channels):
        cols = pl.ds(start, width)
        pre = convolve(input_ref[:, cols], input_kernel_ref, input_shift_ref, cols)
        act_ref[:, cols] = pre * jax.nn.sigmoid(pre)
    for start, width in slabs(2 * states):
        cols = pl.ds(start, width)
        pre = convolve(state_ref[:, cols], state_kernel_ref, state_shift_ref, cols)
        both_ref[:, cols] = pre * jax.nn.sigmoid(pre)
    held_ref[...] = jnp.zeros_like(held_ref)

    def chunk(index, unused):
        rows = pl.ds(pl.multiple_of(index * SPAN, SPAN), SPAN)
        raw, steps, cumul, step_wide, grown_wide, tail_wide = chunk_steps(
            step_ref, bias_ref, rate_ref, expand_ref, rows
        )
        cumul_turned = cumul.T
        entry = both_ref[rows, pl.ds(0, states)].astype(jnp.bfloat16)
        readout = both_ref[rows, pl.ds(states, states)].astype(jnp.bfloat16)
        cross = low_against(readout, entry)
        square = (SPAN, SPAN)
        lower = row_index(square) >= lane_index(square)
        for start, width in slabs(channels):
            cols = pl.ds(start, width)
            span = slice(start, start + width)
            heads = width // HD
            values = act_ref[rows, cols]
            scaled = values * step_wide[:, span]
            held = held_ref[:, cols]
            carry_ref[index, :, cols] = held
            weights = []
            for head in range(start // HD, start // HD + heads):
                spread = cumul[:, head : head + 1] - cumul_turned[head : head + 1, :]
                decay = jnp.exp(jnp.where(lower, spread, -jnp.inf))
                weights.append((decay * cross).astype(jnp.bfloat16))
            weights = jnp.concatenate(weights, axis=1) if heads > 1 else weights[0]
            result = low_dot(weights, stacked_heads(scaled, heads))
            result = result + low_dot(readout, held) * grown_wide[:, span]
            held_ref[:, cols] = held * grown_wide[SPAN - 1 : SPAN, span] + low_inner(
                entry, scaled * tail_wide[:, span]
            )
            result = result + skip_ref[:, cols] * values
            out_ref[rows, cols] = result
            gate = gate_ref[rows, cols]
            gated_ref[rows, cols] = (result * (gate * jax.nn.sigmoid(gate))).astype(jnp.bfloat16)
        return unused

    lax.fori_loop(0, input_ref.shape[0] // SPAN, chunk, 0)


def ssd_backward_kernel(
    input_ref,
    state_ref,
    gate_ref,
    step_ref,
    grad_ref,
    carry_ref,
    input_kernel_ref,
    input_shift_ref,
    state_kernel_ref,
    state_shift_ref,
    bias_ref,
    rate_ref,
    skip_ref,
    expand_ref,
    collect_ref,
    grad_input_ref,
    grad_state_ref,
    grad_step_ref,
    grad_input_conv_ref,
    grad_state_conv_ref,
    grad_head_ref,
    act_ref,
    slope_ref,
    both_ref,
    both_slope_ref,
    held_ref,
    wide_ref,
    turned_ref,
    column_ref,
    skip_sum_ref,
    scale_sum_ref,
):
    channels = input_ref.shape[1]
    states = state_ref.shape[1] // 2
    taps = input_kernel_ref.shape[0]
    for start, width in slabs(channels):
        cols = pl.ds(start, width)
        pre = convolve(input_ref[:, cols], input_kernel_ref, input_shift_ref, cols)
        sigma = jax.nn.sigmoid(pre)
        act_ref[:, cols] = pre * sigma
        slope_ref[:, cols] = sigma * (1.0 + pre * (1.0 - sigma))
    for start, width in slabs(2 * states):
        cols = pl.ds(start, width)
        pre = convolve(state_ref[:, cols], state_kernel_ref, state_shift_ref, cols)
        sigma = jax.nn.sigmoid(pre)
        both_ref[:, cols] = pre * sigma
        both_slope_ref[:, cols] = sigma * (1.0 + pre * (1.0 - sigma))
    held_ref[...] = jnp.zeros_like(held_ref)
    turned_ref[...] = jnp.zeros_like(turned_ref)
    column_ref[...] = jnp.zeros_like(column_ref)
    grad_head_ref[...] = jnp.zeros_like(grad_head_ref)
    skip_sum_ref[...] = jnp.zeros_like(skip_sum_ref)
    chunks = input_ref.shape[0] // SPAN

    def chunk(count, unused):
        index = chunks - 1 - count
        rows = pl.ds(pl.multiple_of(index * SPAN, SPAN), SPAN)
        raw, steps, cumul, step_wide, grown_wide, tail_wide = chunk_steps(
            step_ref, bias_ref, rate_ref, expand_ref, rows
        )
        cumul_turned = cumul.T
        entry = both_ref[rows, pl.ds(0, states)].astype(jnp.bfloat16)
        readout = both_ref[rows, pl.ds(states, states)].astype(jnp.bfloat16)
        cross = low_against(entry, readout)
        square = (SPAN, SPAN)
        upper = row_index(square) <= lane_index(square)
        grad_cross = jnp.zeros(square, jnp.float32)
        grad_entry = jnp.zeros((SPAN, states), jnp.float32)
        grad_readout = jnp.zeros((SPAN, states), jnp.float32)
        for start, width in slabs(channels):
            cols = pl.ds(start, width)
            span = slice(start, start + width)
            heads = width // HD
            values = act_ref[rows, cols]
            scaled = values * step_wide[:, span]
            gate = gate_ref[rows, cols]
            upstream = grad_ref[rows, cols] * (gate * jax.nn.sigmoid(gate))
            held = held_ref[:, cols]
            before = carry_ref[index, :, cols]
            stacked_up = stacked_heads(upstream, heads).astype(jnp.bfloat16)
            products = low_against(scaled, stacked_up)
            weights = []
            for place in range(heads):
                head = start // HD + place
                spread = cumul_turned[head : head + 1, :] - cumul[:, head : head + 1]
                decay = jnp.exp(jnp.where(upper, spread, -jnp.inf))
                product = products[:, place * SPAN : (place + 1) * SPAN] * decay
                grad_cross = grad_cross + product
                flow = product * cross
                turned_ref[head : head + 1, :] = jnp.sum(flow, axis=0, keepdims=True)
                column_ref[:, head : head + 1] = jnp.sum(flow, axis=1, keepdims=True)
                weights.append((decay * cross).astype(jnp.bfloat16))
            weights = jnp.concatenate(weights, axis=1) if heads > 1 else weights[0]
            grown_up = upstream * grown_wide[:, span]
            tailed = scaled * tail_wide[:, span]
            from_held = low_dot(entry, held)
            grad_scaled = low_dot(weights, stacked_up) + tail_wide[:, span] * from_held
            wide_ref[0, :, cols] = grown_up * low_dot(readout, before)
            wide_ref[1, :, cols] = tailed * from_held
            wide_ref[2, :, cols] = values * grad_scaled
            grad_readout = grad_readout + low_against(grown_up, before)
            grad_entry = grad_entry + low_against(tailed, held)
            last = grown_wide[SPAN - 1 : SPAN, span]
            scale_sum_ref[:, cols] = jnp.sum(held * before, axis=0, keepdims=True) * last
            skip_sum_ref[:, cols] += jnp.sum(upstream * values, axis=0, keepdims=True)
            held_ref[:, cols] = held * last + low_inner(readout, grown_up)
            act_ref[rows, cols] = step_wide[:, span] * grad_scaled + skip_ref[:, cols] * upstream
        sums = exact_dot(
            jnp.concatenate([wide_ref[0], wide_ref[1], wide_ref[2]], axis=0), collect_ref[...]
        )
        scale_sum = exact_dot(jnp.broadcast_to(scale_sum_ref[...], (8, channels)), collect_ref[...])
        flows = turned_ref[...].T - column_ref[...] + sums[:SPAN]
        onward = (row_index(square) <= lane_index(square)).astype(jnp.float32)
        strict = (row_index(square) > lane_index(square)).astype(jnp.float32)
        grad_log = (
            exact_dot(onward, flows)
            + exact_dot(strict, sums[SPAN : 2 * SPAN])
            + scale_sum[:1]
        )
        grad_steps = grad_log * rate_ref[...] + sums[2 * SPAN :]
        grad_raw = grad_steps * jax.nn.sigmoid(raw)
        grad_step_ref[rows, :] = grad_raw.astype(jnp.bfloat16)
        grad_head_ref[0, 0:1, :] += jnp.sum(grad_raw, axis=0, keepdims=True)
        grad_head_ref[0, 1:2, :] += (
            jnp.sum(grad_log * steps, axis=0, keepdims=True) * rate_ref[...]
        )
        both_ref[rows, pl.ds(0, states)] = grad_entry + low_dot(grad_cross, readout)
        both_ref[rows, pl.ds(states, states)] = grad_readout + low_inner(grad_cross, entry)
        return unused

    lax.fori_loop(0, chunks, chunk, 0)
    grad_head_ref[0, 2:3, :] = exact_dot(
        jnp.broadcast_to(skip_sum_ref[...], (8, channels)), collect_ref[...]
    )[:1]

    def convolve_back(raw_ref, grads_ref, slopes_ref, kernel_ref, out_ref, sums_ref, width_all):
        for start, width in slabs(width_all):
            cols = pl.ds(start, width)
            grad = grads_ref[:, cols] * slopes_ref[:, cols]
            raw = raw_ref[:, cols]
            total = kernel_ref[taps - 1 : taps, cols] * grad
            sums_ref[0, taps - 1 : taps, cols] = jnp.sum(grad * raw, axis=0, keepdims=True)
            for tap in range(taps - 1):
                shifted = sooner(grad, taps - 1 - tap)
                total = total + kernel_ref[tap : tap + 1, cols] * shifted
                sums_ref[0, tap : tap + 1, cols] = jnp.sum(shifted * raw, axis=0, keepdims=True)
            sums_ref[0, taps : taps + 1, cols] = jnp.sum(grad, axis=0, keepdims=True)
            out_ref[:, cols] = total.astype(jnp.bfloat16)

    convolve_back(
        input_ref,
        act_ref,
        slope_ref,
        input_kernel_ref,
        grad_input_ref,
        grad_input_conv_ref,
        channels,
    )
    convolve_back(
        state_ref,
        both_ref,
        both_slope_ref,
        state_kernel_ref,
        grad_state_ref,
        grad_state_conv_ref,
        2 * states,
    )


def by_sequence(length, width):
    return pl.BlockSpec((length, width), lambda seq: (seq, 0))


def fixed(*shape):
    return pl.BlockSpec(shape, lambda seq: (0,) * len(shape))


def head_spread(heads):
    marks = np.zeros((LANES, heads * HD), np.float32)
    for head in range(heads):
        marks[head, head * HD : (head + 1) * HD] = 1.0
    return marks


def pad_lanes(part):
    return jnp.pad(part, ((0, 0), (0, LANES - part.shape[1])))


def ssd_small(input_kernel, input_shift, state_kernel, state_shift, step_bias, decay_log, skip_gain):
    rates = -jnp.exp(decay_log)
    return (
        input_kernel,
        input_shift[None, :],
        state_kernel,
        state_shift[None, :],
        pad_lanes(step_bias[None, :]),
        pad_lanes(rates[None, :]),
        jnp.repeat(skip_gain, HD)[None, :],
    )


def ssd_forward(inputs, states_raw, gate, step, small, heads, length):
    group, channels = inputs.shape
    seqs = group // length
    both = states_raw.shape[1]
    states = both // 2
    chunks = length // SPAN
    taps = small[0].shape[0]
    return pl.pallas_call(
        ssd_forward_kernel,
        grid=(seqs,),
        in_specs=[
            by_sequence(length, channels),
            by_sequence(length, both),
            by_sequence(length, channels),
            by_sequence(length, LANES),
            fixed(taps, channels),
            fixed(1, channels),
            fixed(taps, both),
            fixed(1, both),
            fixed(1, LANES),
            fixed(1, LANES),
            fixed(1, channels),
            fixed(LANES, channels),
        ],
        out_specs=[
            by_sequence(length, channels),
            by_sequence(length, channels),
            pl.BlockSpec((chunks, states, channels), lambda seq: (seq, 0, 0)),
        ],
        out_shape=[
            jax.ShapeDtypeStruct((group, channels), jnp.bfloat16),
            jax.ShapeDtypeStruct((group, channels), jnp.float32),
            jax.ShapeDtypeStruct((seqs * chunks, states, channels), jnp.float32),
        ],
        scratch_shapes=[
            pltpu.VMEM((length, channels), jnp.float32),
            pltpu.VMEM((length, both), jnp.float32),
            pltpu.VMEM((states, channels), jnp.float32),
        ],
        compiler_params=pltpu.CompilerParams(vmem_limit_bytes=VMEM_LIMIT),
        cost_estimate=pl.CostEstimate(
            flops=8 * group * channels * SPAN,
            bytes_accessed=20 * group * channels,
            transcendentals=group * heads * SPAN,
        ),
        name="ssd_forward",
    )(inputs, states_raw, gate, step, *small, jnp.asarray(head_spread(heads)))


def ssd_backward(inputs, states_raw, gate, step, grad, carry, small, heads, length):
    group, channels = inputs.shape
    seqs = group // length
    both = states_raw.shape[1]
    states = both // 2
    chunks = length // SPAN
    taps = small[0].shape[0]
    return pl.pallas_call(
        ssd_backward_kernel,
        grid=(seqs,),
        in_specs=[
            by_sequence(length, channels),
            by_sequence(length, both),
            by_sequence(length, channels),
            by_sequence(length, LANES),
            by_sequence(length, channels),
            pl.BlockSpec((chunks, states, channels), lambda seq: (seq, 0, 0)),
            fixed(taps, channels),
            fixed(1, channels),
            fixed(taps, both),
            fixed(1, both),
            fixed(1, LANES),
            fixed(1, LANES),
            fixed(1, channels),
            fixed(LANES, channels),
            fixed(channels, LANES),
        ],
        out_specs=[
            by_sequence(length, channels),
            by_sequence(length, both),
            by_sequence(length, LANES),
            pl.BlockSpec((1, 8, channels), lambda seq: (seq, 0, 0)),
            pl.BlockSpec((1, 8, both), lambda seq: (seq, 0, 0)),
            pl.BlockSpec((1, 8, LANES), lambda seq: (seq, 0, 0)),
        ],
        out_shape=[
            jax.ShapeDtypeStruct((group, channels), jnp.bfloat16),
            jax.ShapeDtypeStruct((group, both), jnp.bfloat16),
            jax.ShapeDtypeStruct((group, LANES), jnp.bfloat16),
            jax.ShapeDtypeStruct((seqs, 8, channels), jnp.float32),
            jax.ShapeDtypeStruct((seqs, 8, both), jnp.float32),
            jax.ShapeDtypeStruct((seqs, 8, LANES), jnp.float32),
        ],
        scratch_shapes=[
            pltpu.VMEM((length, channels), jnp.float32),
            pltpu.VMEM((length, channels), jnp.float32),
            pltpu.VMEM((length, both), jnp.float32),
            pltpu.VMEM((length, both), jnp.float32),
            pltpu.VMEM((states, channels), jnp.float32),
            pltpu.VMEM((3, SPAN, channels), jnp.float32),
            pltpu.VMEM((LANES, SPAN), jnp.float32),
            pltpu.VMEM((SPAN, LANES), jnp.float32),
            pltpu.VMEM((1, channels), jnp.float32),
            pltpu.VMEM((1, channels), jnp.float32),
        ],
        compiler_params=pltpu.CompilerParams(vmem_limit_bytes=VMEM_LIMIT),
        cost_estimate=pl.CostEstimate(
            flops=20 * group * channels * SPAN,
            bytes_accessed=20 * group * channels,
            transcendentals=group * heads * SPAN,
        ),
        name="ssd_backward",
    )(
        inputs,
        states_raw,
        gate,
        step,
        grad,
        carry,
        *small,
        jnp.asarray(head_spread(heads)),
        jnp.asarray(head_spread(heads).T.copy()),
    )


def rope_wide(length):
    half = HD // 2
    freqs = np.float32(ROPE_BASE) ** (-np.arange(half, dtype=np.float32) * np.float32(2.0 / HD))
    angles = np.arange(length, dtype=np.float32)[:, None] * freqs[None, :].astype(np.float32)
    cosine, sine = np.cos(angles), np.sin(angles)
    count = LANES // HD
    return (
        np.concatenate([cosine, cosine] * count, axis=1).astype(np.float32),
        np.concatenate([-sine, sine] * count, axis=1).astype(np.float32),
    )


def turn(part, cosine, sine):
    half = HD // 2
    first = lane_index(part.shape) % HD < half
    swapped = jnp.where(first, pltpu.roll(part, LANES - half, 1), pltpu.roll(part, half, 1))
    return part * cosine + swapped * sine


def attend_forward_kernel(
    query_ref, pair_ref, cosine_ref, sine_ref, context_ref, query_out_ref, pair_out_ref, total_ref
):
    length = query_ref.shape[0]
    cosine, sine = cosine_ref[...], sine_ref[...]
    pair = pair_ref[...]
    left = lane_index(pair.shape) < HD
    pair = jnp.where(left, turn(pair, cosine, sine), pair)
    pair_out_ref[...] = pair.astype(jnp.bfloat16)
    moved = pltpu.roll(pair, HD, 1)
    keys = jnp.where(left, pair, moved).astype(jnp.bfloat16)
    values = jnp.where(left, moved, pair).astype(jnp.bfloat16)
    scale = HD ** (-0.5)
    for slab in range(query_ref.shape[1] // LANES):
        cols = pl.ds(slab * LANES, LANES)
        query_out_ref[:, cols] = turn(query_ref[:, cols], cosine, sine).astype(jnp.bfloat16)
        for tile in range(length // SPAN):
            rows = slice(tile * SPAN, (tile + 1) * SPAN)
            count = (tile + 1) * SPAN
            query = query_out_ref[rows, cols]
            lane = lane_index(query.shape)
            square = (SPAN, count)
            causal = row_index(square) + tile * SPAN >= lane_index(square)
            results = []
            for place in range(LANES // HD):
                mine = (lane >= place * HD) & (lane < place * HD + HD)
                scores = low_against(jnp.where(mine, query, 0), keys[:count]) * scale
                scores = jnp.where(causal, scores, -jnp.inf)
                peak = jnp.max(scores, axis=-1, keepdims=True)
                grown = jnp.exp(scores - peak)
                total = jnp.sum(grown, axis=-1, keepdims=True)
                probs = grown * (1.0 / total)
                results.append(low_dot(probs, values[:count]))
                head = slab * (LANES // HD) + place
                total_ref[rows, head : head + 1] = jnp.log(total) + peak
            context_ref[rows, cols] = jnp.where(lane < HD, results[0], results[1]).astype(
                jnp.bfloat16
            )


def attend_backward_kernel(
    query_ref,
    pair_ref,
    total_ref,
    grad_ref,
    cosine_ref,
    sine_ref,
    grad_query_ref,
    grad_pair_ref,
    key_sum_ref,
    value_sum_ref,
):
    length = query_ref.shape[0]
    cosine, sine = cosine_ref[...], -sine_ref[...]
    pair = pair_ref[...].astype(jnp.float32)
    left = lane_index(pair.shape) < HD
    moved = pltpu.roll(pair, HD, 1)
    keys = jnp.where(left, pair, moved).astype(jnp.bfloat16)
    values = jnp.where(left, moved, pair).astype(jnp.bfloat16)
    scale = HD ** (-0.5)
    key_sum_ref[...] = jnp.zeros_like(key_sum_ref)
    value_sum_ref[...] = jnp.zeros_like(value_sum_ref)
    for slab in range(query_ref.shape[1] // LANES):
        cols = pl.ds(slab * LANES, LANES)
        for tile in range(length // SPAN):
            rows = slice(tile * SPAN, (tile + 1) * SPAN)
            count = (tile + 1) * SPAN
            query = query_ref[rows, cols]
            upstream = grad_ref[rows, cols]
            lane = lane_index(query.shape)
            square = (SPAN, count)
            causal = row_index(square) + tile * SPAN >= lane_index(square)
            results = []
            for place in range(LANES // HD):
                mine = (lane >= place * HD) & (lane < place * HD + HD)
                head = slab * (LANES // HD) + place
                own_query = jnp.where(mine, query, 0)
                own_up = jnp.where(mine, upstream, 0)
                scores = low_against(own_query, keys[:count]) * scale
                scores = jnp.where(causal, scores, -jnp.inf)
                probs = jnp.exp(scores - total_ref[rows, head : head + 1])
                grad_probs = low_against(own_up, values[:count])
                mean = jnp.sum(probs * grad_probs, axis=-1, keepdims=True)
                grad_scores = (probs * (grad_probs - mean)).astype(jnp.bfloat16)
                results.append(low_dot(grad_scores, keys[:count]))
                key_sum_ref[0:count, :] += low_inner(grad_scores, own_query)
                value_sum_ref[0:count, :] += low_inner(probs, own_up)
            grad_query = jnp.where(lane < HD, results[0], results[1]) * scale
            grad_query_ref[rows, cols] = turn(
                grad_query, cosine[rows, :], sine[rows, :]
            ).astype(jnp.bfloat16)
    grad_key = key_sum_ref[...]
    grad_key = turn((grad_key + pltpu.roll(grad_key, HD, 1)) * scale, cosine, sine)
    grad_value = value_sum_ref[...]
    grad_value = grad_value + pltpu.roll(grad_value, HD, 1)
    grad_pair_ref[...] = jnp.where(left, grad_key, grad_value).astype(jnp.bfloat16)


def attend_forward(query, pair, length):
    group, width = query.shape
    heads = width // HD
    cosine, sine = rope_wide(length)
    return pl.pallas_call(
        attend_forward_kernel,
        grid=(group // length,),
        in_specs=[
            by_sequence(length, width),
            by_sequence(length, LANES),
            fixed(length, LANES),
            fixed(length, LANES),
        ],
        out_specs=[
            by_sequence(length, width),
            by_sequence(length, width),
            by_sequence(length, LANES),
            by_sequence(length, LANES),
        ],
        out_shape=[
            jax.ShapeDtypeStruct((group, width), jnp.bfloat16),
            jax.ShapeDtypeStruct((group, width), jnp.bfloat16),
            jax.ShapeDtypeStruct((group, LANES), jnp.bfloat16),
            jax.ShapeDtypeStruct((group, LANES), jnp.float32),
        ],
        compiler_params=pltpu.CompilerParams(vmem_limit_bytes=VMEM_LIMIT),
        cost_estimate=pl.CostEstimate(
            flops=4 * group * width * length,
            bytes_accessed=12 * group * width,
            transcendentals=group * heads * length // 2,
        ),
        name="attend_forward",
    )(query, pair, jnp.asarray(cosine), jnp.asarray(sine))


def attend_backward(query, pair, total, grad, length):
    group, width = query.shape
    heads = width // HD
    cosine, sine = rope_wide(length)
    return pl.pallas_call(
        attend_backward_kernel,
        grid=(group // length,),
        in_specs=[
            by_sequence(length, width),
            by_sequence(length, LANES),
            by_sequence(length, LANES),
            by_sequence(length, width),
            fixed(length, LANES),
            fixed(length, LANES),
        ],
        out_specs=[by_sequence(length, width), by_sequence(length, LANES)],
        out_shape=[
            jax.ShapeDtypeStruct((group, width), jnp.bfloat16),
            jax.ShapeDtypeStruct((group, LANES), jnp.bfloat16),
        ],
        scratch_shapes=[
            pltpu.VMEM((length, LANES), jnp.float32),
            pltpu.VMEM((length, LANES), jnp.float32),
        ],
        compiler_params=pltpu.CompilerParams(vmem_limit_bytes=VMEM_LIMIT),
        cost_estimate=pl.CostEstimate(
            flops=10 * group * width * length,
            bytes_accessed=12 * group * width,
            transcendentals=group * heads * length // 2,
        ),
        name="attend_backward",
    )(query, pair, total, grad, jnp.asarray(cosine), jnp.asarray(sine))


def bit_pairs(size, bit):
    return [(index, index ^ (1 << bit)) for index in range(size)]


def split_half(part, bit, size):
    side = (lax.axis_index("dp") >> bit) & 1
    halves = part.reshape(2, part.shape[0] // 2, part.shape[1])
    keep = lax.dynamic_index_in_dim(halves, side, 0, False)
    give = lax.dynamic_index_in_dim(halves, 1 - side, 0, False)
    got = lax.ppermute(give, "dp", bit_pairs(size, bit))
    return (keep.astype(jnp.float32) + got.astype(jnp.float32)).astype(jnp.bfloat16)


def join_half(part, bit, size):
    side = (lax.axis_index("dp") >> bit) & 1
    got = lax.ppermute(part, "dp", bit_pairs(size, bit))
    return jnp.where(
        side == 0, jnp.concatenate([part, got], axis=0), jnp.concatenate([got, part], axis=0)
    )


def bit_order(size, swapped):
    order = list(range(size.bit_length() - 1))
    if swapped and len(order) > 2:
        order[1], order[2] = order[2], order[1]
    return order


def sum_dp(part, size, swapped, middle=None):
    if size & (size - 1) or part.shape[0] % size:
        part = lax.psum(part, "dp")
        return part if middle is None else middle(part)
    order = bit_order(size, swapped)
    for bit in order:
        part = split_half(part, bit, size)
    if middle is not None:
        part = middle(part)
    for bit in reversed(order):
        part = join_half(part, bit, size)
    return part


def other(part):
    return lax.ppermute(part, "tensor", [(0, 1), (1, 0)])


def all_rows(part, shards):
    if shards != 2:
        return lax.all_gather(part, "tensor", axis=0, tiled=True)
    got = other(part)
    return jnp.where(
        lax.axis_index("tensor") == 0,
        jnp.concatenate([part, got], axis=0),
        jnp.concatenate([got, part], axis=0),
    )


def sum_all(part, shards):
    if shards != 2:
        return lax.psum(part, "tensor").astype(jnp.float32)
    return part.astype(jnp.float32) + other(part).astype(jnp.float32)


def sum_own(part, shards):
    if shards != 2:
        return lax.psum_scatter(part, "tensor", scatter_dimension=0, tiled=True).astype(jnp.float32)
    me = lax.axis_index("tensor")
    halves = part.reshape(2, part.shape[0] // 2, part.shape[1])
    keep = lax.dynamic_index_in_dim(halves, me, 0, False)
    got = other(lax.dynamic_index_in_dim(halves, 1 - me, 0, False))
    return keep.astype(jnp.float32) + got.astype(jnp.float32)


def own_rows(part, rows):
    return lax.dynamic_slice_in_dim(part, lax.axis_index("tensor") * rows, rows, 0)


def column_pack(vectors, rows):
    flat = jnp.concatenate([item.reshape(-1) for item in vectors])
    width = -(-flat.shape[0] // rows)
    return jnp.pad(flat, (0, width * rows - flat.shape[0])).reshape(width, rows).T


def column_unpack(packed, shapes):
    flat = packed.T.reshape(-1)
    out, start = [], 0
    for shape in shapes:
        count = 1
        for size in shape:
            count *= size
        out.append(flat[start : start + count].reshape(shape))
        start += count
    return out


def body(
    dp_size,
    shards,
    layer_input,
    input_gain,
    middle_gain,
    mamba_gate,
    mamba_input,
    step_weight,
    state_weight,
    input_kernel,
    input_shift,
    state_kernel,
    state_shift,
    step_bias,
    decay_log,
    skip_gain,
    mamba_output,
    query_weight,
    keyvalue_weight,
    context_weight,
    gate_weight,
    up_weight,
    down_weight,
    cotangent,
):
    own = layer_input.shape[0]
    rows_low = all_rows(layer_input, shards)
    cotan_low = all_rows(cotangent, shards)
    rows = rows_low.astype(jnp.float32)
    gain_first = input_gain.astype(jnp.float32)
    gain_second = middle_gain.astype(jnp.float32)
    factor_first = lax.rsqrt(jnp.mean(rows * rows, axis=-1, keepdims=True) + EPSILON)
    normal_first = rows * factor_first
    whole = (normal_first * gain_first).astype(jnp.bfloat16)
    group = whole.shape[0]
    length = min(SEQ_LEN, group)
    seqs = group // length
    heads_here = query_weight.shape[1] // HD
    kv_head = lax.axis_index("tensor") * heads_here // (HQ // KVH)
    key_cols = lax.dynamic_slice_in_dim(keyvalue_weight, kv_head * HD, HD, 1)
    value_cols = lax.dynamic_slice_in_dim(keyvalue_weight, (KVH + kv_head) * HD, HD, 1)
    pair_weight = jnp.concatenate([key_cols, value_cols], axis=1)
    query_cols = query_weight.shape[1]
    query_pad = -query_cols % LANES
    query_wide = jnp.pad(query_weight, ((0, 0), (0, query_pad)))
    step_wide = pad_lanes(step_weight)
    heads = step_weight.shape[1]
    input_raw = forward_dot(whole, mamba_input)
    state_raw = forward_dot(whole, state_weight)
    step_raw = forward_dot(whole, step_wide)
    gate_raw = forward_dot(whole, mamba_gate)
    query_raw = forward_dot(whole, query_wide)
    pair_raw = forward_dot(whole, pair_weight)
    small = ssd_small(
        input_kernel.astype(jnp.float32),
        input_shift.astype(jnp.float32),
        state_kernel.astype(jnp.float32),
        state_shift.astype(jnp.float32),
        step_bias.astype(jnp.float32),
        decay_log.astype(jnp.float32),
        skip_gain.astype(jnp.float32),
    )
    gated_low, ssm_out, carries = ssd_forward(
        input_raw, state_raw, gate_raw, step_raw, small, heads, length
    )
    context_wide, queries, pairs, totals = attend_forward(query_raw, pair_raw, length)
    context_rows = context_wide[:, :query_cols]
    mixed_part = forward_dot(gated_low, mamba_output) + forward_dot(context_rows, context_weight)
    resid = rows + sum_all(mixed_part.astype(jnp.bfloat16), shards)
    factor_second = lax.rsqrt(jnp.mean(resid * resid, axis=-1, keepdims=True) + EPSILON)
    normal_second = resid * factor_second
    whole_mid = (normal_second * gain_second).astype(jnp.bfloat16)
    gate = forward_dot(whole_mid, gate_weight)
    upper = forward_dot(whole_mid, up_weight)
    sigmoid_gate = jax.nn.sigmoid(gate)
    silu_gate = gate * sigmoid_gate
    hidden = (silu_gate * upper).astype(jnp.bfloat16)
    grad_hidden = against(cotan_low, down_weight)
    slope = sigmoid_gate * (1.0 + gate * (1.0 - sigmoid_gate))
    grad_gate_low = (grad_hidden * upper * slope).astype(jnp.bfloat16)
    grad_upper_low = (grad_hidden * silu_gate).astype(jnp.bfloat16)
    back_part = (against(grad_gate_low, gate_weight) + against(grad_upper_low, up_weight)).astype(
        jnp.bfloat16
    )
    back_mid = sum_all(back_part, shards)
    feed = sum_own(forward_dot(hidden, down_weight).astype(jnp.bfloat16), shards)
    layer_output = (own_rows(resid, own) + feed).astype(jnp.bfloat16)
    grad_down = inner_rows(hidden, cotan_low).astype(jnp.bfloat16)
    grad_gate = inner_rows(whole_mid, grad_gate_low).astype(jnp.bfloat16)
    grad_up = inner_rows(whole_mid, grad_upper_low).astype(jnp.bfloat16)
    grad_gate = sum_dp(grad_gate, dp_size, False)
    grad_up = sum_dp(grad_up, dp_size, True)
    grad_down = sum_dp(grad_down, dp_size, False)
    grad_middle = jnp.sum(back_part.astype(jnp.float32) * normal_second, axis=0)
    grad_resid = cotan_low.astype(jnp.float32) + norm_back(
        back_mid, gain_second, normal_second, factor_second
    )
    mixer_all = grad_resid.astype(jnp.bfloat16)
    grad_mixer_out = inner_rows(
        jnp.concatenate([gated_low, context_rows], axis=1), mixer_all
    ).astype(jnp.bfloat16)
    grad_mixer_out = sum_dp(grad_mixer_out, dp_size, True)
    ssm_rows = gated_low.shape[1]
    grad_mamba_out = grad_mixer_out[:ssm_rows]
    grad_context_w = grad_mixer_out[ssm_rows:]
    grad_gated = against(mixer_all, mamba_output)
    sigmoid_raw = jax.nn.sigmoid(gate_raw)
    grad_gate_raw = (
        grad_gated * ssm_out * (sigmoid_raw * (1.0 + gate_raw * (1.0 - sigmoid_raw)))
    ).astype(jnp.bfloat16)
    grad_context = against(mixer_all, context_weight).astype(jnp.bfloat16)
    grad_query_raw, grad_pair_raw = attend_backward(
        queries, pairs, totals, jnp.pad(grad_context, ((0, 0), (0, query_pad))), length
    )
    grad_query_raw = grad_query_raw[:, :query_cols]
    early_cols = jnp.concatenate([grad_gate_raw, grad_query_raw], axis=1)
    early = inner_rows(whole, early_cols)
    early = sum_dp(early.astype(jnp.bfloat16), dp_size, False)
    grad_input_raw, grad_state_raw, grad_step_raw, input_sums, state_sums, head_sums = ssd_backward(
        input_raw, state_raw, gate_raw, step_raw, grad_gated, carries, small, heads, length
    )
    input_sums = jnp.sum(input_sums, axis=0)
    state_sums = jnp.sum(state_sums, axis=0)
    head_sums = jnp.sum(head_sums, axis=0)[:, :heads]
    taps = input_kernel.shape[0]
    late_cols = jnp.concatenate(
        [grad_input_raw, grad_state_raw, grad_pair_raw, grad_step_raw], axis=1
    )
    total = against(early_cols, jnp.concatenate([mamba_gate, query_weight], axis=1))
    total = total + against(
        late_cols, jnp.concatenate([mamba_input, state_weight, pair_weight, step_wide], axis=1)
    )
    total_low = total.astype(jnp.bfloat16)
    grad_first = jnp.sum(total_low.astype(jnp.float32) * normal_first, axis=0)
    width = whole.shape[1]
    gate_cols = grad_gate_raw.shape[1]
    input_cols = grad_input_raw.shape[1]
    state_cols = grad_state_raw.shape[1]
    step_cols = heads
    pair_cols = grad_pair_raw.shape[1]

    own_vectors = (input_sums[:taps], input_sums[taps], head_sums[0], head_sums[1], head_sums[2])
    shared_vectors = (grad_first, grad_middle, state_sums[:taps], state_sums[taps])
    own_pack = column_pack(own_vectors, width).astype(jnp.bfloat16)
    shared_pack = column_pack(shared_vectors, width).astype(jnp.bfloat16)
    own_width = own_pack.shape[1]
    shared_width = shared_pack.shape[1]

    split_pairs = shards == KVH
    late = inner_rows(whole, late_cols).astype(jnp.bfloat16)
    marks = (input_cols, input_cols + state_cols, input_cols + state_cols + pair_cols)
    late_pair = late[:, marks[1] : marks[2]]
    if not split_pairs:
        spread = jnp.zeros((width, 2 * KVH * HD), jnp.bfloat16)
        spread = lax.dynamic_update_slice_in_dim(spread, late_pair[:, :HD], kv_head * HD, 1)
        late_pair = lax.dynamic_update_slice_in_dim(
            spread, late_pair[:, HD:], (KVH + kv_head) * HD, 1
        )
    tail = jnp.concatenate(
        [late[:, input_cols : marks[1]], late_pair, shared_pack, late[:, marks[2] : marks[2] + step_cols], own_pack],
        axis=1,
    )
    sent = state_cols + late_pair.shape[1] + shared_width

    def over_tensor(part):
        shared, rest = part[:, :sent], part[:, sent:]
        if not split_pairs:
            return jnp.concatenate([lax.psum(shared, "tensor"), rest], axis=1)
        got = other(shared)
        first = lax.axis_index("tensor") == 0
        low = jnp.where(first, shared, got)[:, state_cols : state_cols + pair_cols]
        high = jnp.where(first, got, shared)[:, state_cols : state_cols + pair_cols]
        both = (shared.astype(jnp.float32) + got.astype(jnp.float32)).astype(jnp.bfloat16)
        return jnp.concatenate(
            [
                both[:, :state_cols],
                low[:, :HD],
                high[:, :HD],
                low[:, HD:],
                high[:, HD:],
                both[:, state_cols + pair_cols :],
                rest,
            ],
            axis=1,
        )

    tail = sum_dp(tail, dp_size, True, over_tensor)
    grad_mamba_input = sum_dp(late[:, :input_cols], dp_size, False)
    back_in = sum_own(total_low, shards)
    normal_own = own_rows(normal_first, own)
    factor_own = own_rows(factor_first, own)
    input_grad = own_rows(grad_resid, own) + norm_back(back_in, gain_first, normal_own, factor_own)
    after = state_cols + keyvalue_weight.shape[1]
    grad_first, grad_middle, grad_st_kernel, grad_st_shift = column_unpack(
        tail[:, after : after + shared_width], [item.shape for item in shared_vectors]
    )
    after = after + shared_width
    grad_step = tail[:, after : after + step_cols]
    grad_in_kernel, grad_in_shift, grad_bias, grad_decay, grad_skip = column_unpack(
        tail[:, after + step_cols :], [item.shape for item in own_vectors]
    )
    results = (
        grad_first,
        grad_middle,
        early[:, :gate_cols],
        grad_mamba_input,
        grad_step,
        tail[:, :state_cols],
        grad_in_kernel,
        grad_in_shift,
        grad_st_kernel,
        grad_st_shift,
        grad_bias,
        grad_decay,
        grad_skip,
        grad_mamba_out,
        early[:, gate_cols:],
        tail[:, state_cols : state_cols + keyvalue_weight.shape[1]],
        grad_context_w,
        grad_gate,
        grad_up,
        grad_down,
    )
    return (layer_output, input_grad) + tuple(item.astype(jnp.float32) for item in results)


def solution(mesh):
    in_specs = (
        P(("dp", "tensor"), None),
        P(),
        P(),
        P(None, "tensor"),
        P(None, "tensor"),
        P(None, "tensor"),
        P(),
        P(None, "tensor"),
        P("tensor"),
        P(),
        P(),
        P("tensor"),
        P("tensor"),
        P("tensor"),
        P("tensor", None),
        P(None, "tensor"),
        P(),
        P("tensor", None),
        P(None, "tensor"),
        P(None, "tensor"),
        P("tensor", None),
        P(("dp", "tensor"), None),
    )
    out_specs = (
        P(("dp", "tensor"), None),
        P(("dp", "tensor"), None),
        P(),
        P(),
        P(None, "tensor"),
        P(None, "tensor"),
        P(None, "tensor"),
        P(),
        P(None, "tensor"),
        P("tensor"),
        P(),
        P(),
        P("tensor"),
        P("tensor"),
        P("tensor"),
        P("tensor", None),
        P(None, "tensor"),
        P(),
        P("tensor", None),
        P(None, "tensor"),
        P(None, "tensor"),
        P("tensor", None),
    )
    run = partial(body, mesh.shape["dp"], mesh.shape["tensor"])
    return jax.shard_map(run, mesh=mesh, in_specs=in_specs, out_specs=out_specs, check_vma=False)
```

```python
from functools import partial

import jax
import jax.numpy as jnp
import numpy as np
from jax import lax
from jax.experimental import pallas as pl
from jax.experimental.pallas import tpu as pltpu
from jax.sharding import PartitionSpec as P

HD = 64
HQ = 8
KVH = 2
SPAN = 128
SEQ_LEN = 1024


EPSILON = 1e-05
ROPE_BASE = 10000.0
PRECISE = lax.Precision.HIGHEST


def forward_dot(left, right):
    return jnp.dot(left, right, preferred_element_type=jnp.float32)


def inner_rows(left, right):
    return lax.dot_general(
        left, right, (((0,), (0,)), ((), ())), preferred_element_type=jnp.float32
    )


def against(left, right):
    return lax.dot_general(
        left, right, (((1,), (1,)), ((), ())), preferred_element_type=jnp.float32
    )


def norm_back(upstream, gain, normal, factor):
    scaled = upstream * gain
    return factor * (scaled - normal * jnp.mean(scaled * normal, axis=-1, keepdims=True))


LANES = 128
VMEM_LIMIT = 44 * 1024 * 1024


def exact_dot(left, right):
    return jnp.dot(left, right, precision=PRECISE, preferred_element_type=jnp.float32)


def low_dot(left, right):
    return jnp.dot(
        left.astype(jnp.bfloat16), right.astype(jnp.bfloat16), preferred_element_type=jnp.float32
    )


def low_against(left, right):
    return lax.dot_general(
        left.astype(jnp.bfloat16),
        right.astype(jnp.bfloat16),
        (((1,), (1,)), ((), ())),
        preferred_element_type=jnp.float32,
    )


def low_inner(left, right):
    return lax.dot_general(
        left.astype(jnp.bfloat16),
        right.astype(jnp.bfloat16),
        (((0,), (0,)), ((), ())),
        preferred_element_type=jnp.float32,
    )


def row_index(shape):
    return lax.broadcasted_iota(jnp.int32, shape, 0)


def lane_index(shape):
    return lax.broadcasted_iota(jnp.int32, shape, 1)


def later(part, count):
    if count == 0:
        return part
    return jnp.where(row_index(part.shape) >= count, pltpu.roll(part, count, 0), 0.0)


def sooner(part, count):
    if count == 0:
        return part
    rows = part.shape[0]
    return jnp.where(row_index(part.shape) < rows - count, pltpu.roll(part, rows - count, 0), 0.0)


def slabs(width):
    return [(start, min(LANES, width - start)) for start in range(0, width, LANES)]


def soft_plus(value):
    return jnp.maximum(value, 0.0) + jnp.log1p(jnp.exp(-jnp.abs(value)))


def stacked_heads(part, heads):
    if heads == 1:
        return part
    lane = lane_index(part.shape)
    return jnp.concatenate(
        [jnp.where((lane >= head * HD) & (lane < head * HD + HD), part, 0.0) for head in range(heads)],
        axis=0,
    )


def convolve(raw, kernel_ref, shift_ref, cols):
    taps = kernel_ref.shape[0]
    out = shift_ref[:, cols] + kernel_ref[taps - 1 : taps, cols] * raw
    for tap in range(taps - 1):
        out = out + kernel_ref[tap : tap + 1, cols] * later(raw, taps - 1 - tap)
    return out


def chunk_steps(step_ref, bias_ref, rate_ref, expand_ref, rows):
    raw = step_ref[rows, :] + bias_ref[...]
    steps = soft_plus(raw)
    logdec = steps * rate_ref[...]
    square = (SPAN, SPAN)
    lower = (row_index(square) >= lane_index(square)).astype(jnp.float32)
    cumul = exact_dot(lower, logdec)
    grown = jnp.exp(cumul)
    tail = jnp.exp(cumul[SPAN - 1 : SPAN, :] - cumul)
    wide = exact_dot(jnp.concatenate([steps, grown, tail], axis=0), expand_ref[...])
    return raw, steps, cumul, wide[:SPAN], wide[SPAN : 2 * SPAN], wide[2 * SPAN :]


def ssd_forward_kernel(
    input_ref,
    state_ref,
    gate_ref,
    step_ref,
    input_kernel_ref,
    input_shift_ref,
    state_kernel_ref,
    state_shift_ref,
    bias_ref,
    rate_ref,
    skip_ref,
    expand_ref,
    gated_ref,
    out_ref,
    carry_ref,
    act_ref,
    both_ref,
    held_ref,
):
    channels = input_ref.shape[1]
    states = state_ref.shape[1] // 2
    for start, width in slabs(channels):
        cols = pl.ds(start, width)
        pre = convolve(input_ref[:, cols], input_kernel_ref, input_shift_ref, cols)
        act_ref[:, cols] = pre * jax.nn.sigmoid(pre)
    for start, width in slabs(2 * states):
        cols = pl.ds(start, width)
        pre = convolve(state_ref[:, cols], state_kernel_ref, state_shift_ref, cols)
        both_ref[:, cols] = pre * jax.nn.sigmoid(pre)
    held_ref[...] = jnp.zeros_like(held_ref)

    def chunk(index, unused):
        rows = pl.ds(pl.multiple_of(index * SPAN, SPAN), SPAN)
        raw, steps, cumul, step_wide, grown_wide, tail_wide = chunk_steps(
            step_ref, bias_ref, rate_ref, expand_ref, rows
        )
        cumul_turned = cumul.T
        entry = both_ref[rows, pl.ds(0, states)].astype(jnp.bfloat16)
        readout = both_ref[rows, pl.ds(states, states)].astype(jnp.bfloat16)
        cross = low_against(readout, entry)
        square = (SPAN, SPAN)
        lower = row_index(square) >= lane_index(square)
        for start, width in slabs(channels):
            cols = pl.ds(start, width)
            span = slice(start, start + width)
            heads = width // HD
            values = act_ref[rows, cols]
            scaled = values * step_wide[:, span]
            held = held_ref[:, cols]
            carry_ref[index, :, cols] = held
            weights = []
            for head in range(start // HD, start // HD + heads):
                spread = cumul[:, head : head + 1] - cumul_turned[head : head + 1, :]
                decay = jnp.exp(jnp.where(lower, spread, -jnp.inf))
                weights.append((decay * cross).astype(jnp.bfloat16))
            weights = jnp.concatenate(weights, axis=1) if heads > 1 else weights[0]
            result = low_dot(weights, stacked_heads(scaled, heads))
            result = result + low_dot(readout, held) * grown_wide[:, span]
            held_ref[:, cols] = held * grown_wide[SPAN - 1 : SPAN, span] + low_inner(
                entry, scaled * tail_wide[:, span]
            )
            result = result + skip_ref[:, cols] * values
            out_ref[rows, cols] = result
            gate = gate_ref[rows, cols]
            gated_ref[rows, cols] = (result * (gate * jax.nn.sigmoid(gate))).astype(jnp.bfloat16)
        return unused

    lax.fori_loop(0, input_ref.shape[0] // SPAN, chunk, 0)


def ssd_backward_kernel(
    input_ref,
    state_ref,
    gate_ref,
    step_ref,
    grad_ref,
    carry_ref,
    input_kernel_ref,
    input_shift_ref,
    state_kernel_ref,
    state_shift_ref,
    bias_ref,
    rate_ref,
    skip_ref,
    expand_ref,
    collect_ref,
    grad_input_ref,
    grad_state_ref,
    grad_step_ref,
    grad_input_conv_ref,
    grad_state_conv_ref,
    grad_head_ref,
    act_ref,
    slope_ref,
    both_ref,
    both_slope_ref,
    held_ref,
    wide_ref,
    turned_ref,
    column_ref,
    skip_sum_ref,
    scale_sum_ref,
):
    channels = input_ref.shape[1]
    states = state_ref.shape[1] // 2
    taps = input_kernel_ref.shape[0]
    for start, width in slabs(channels):
        cols = pl.ds(start, width)
        pre = convolve(input_ref[:, cols], input_kernel_ref, input_shift_ref, cols)
        sigma = jax.nn.sigmoid(pre)
        act_ref[:, cols] = pre * sigma
        slope_ref[:, cols] = sigma * (1.0 + pre * (1.0 - sigma))
    for start, width in slabs(2 * states):
        cols = pl.ds(start, width)
        pre = convolve(state_ref[:, cols], state_kernel_ref, state_shift_ref, cols)
        sigma = jax.nn.sigmoid(pre)
        both_ref[:, cols] = pre * sigma
        both_slope_ref[:, cols] = sigma * (1.0 + pre * (1.0 - sigma))
    held_ref[...] = jnp.zeros_like(held_ref)
    turned_ref[...] = jnp.zeros_like(turned_ref)
    column_ref[...] = jnp.zeros_like(column_ref)
    grad_head_ref[...] = jnp.zeros_like(grad_head_ref)
    skip_sum_ref[...] = jnp.zeros_like(skip_sum_ref)
    chunks = input_ref.shape[0] // SPAN

    def chunk(count, unused):
        index = chunks - 1 - count
        rows = pl.ds(pl.multiple_of(index * SPAN, SPAN), SPAN)
        raw, steps, cumul, step_wide, grown_wide, tail_wide = chunk_steps(
            step_ref, bias_ref, rate_ref, expand_ref, rows
        )
        cumul_turned = cumul.T
        entry = both_ref[rows, pl.ds(0, states)].astype(jnp.bfloat16)
        readout = both_ref[rows, pl.ds(states, states)].astype(jnp.bfloat16)
        cross = low_against(entry, readout)
        square = (SPAN, SPAN)
        upper = row_index(square) <= lane_index(square)
        grad_cross = jnp.zeros(square, jnp.float32)
        grad_entry = jnp.zeros((SPAN, states), jnp.float32)
        grad_readout = jnp.zeros((SPAN, states), jnp.float32)
        for start, width in slabs(channels):
            cols = pl.ds(start, width)
            span = slice(start, start + width)
            heads = width // HD
            values = act_ref[rows, cols]
            scaled = values * step_wide[:, span]
            gate = gate_ref[rows, cols]
            upstream = grad_ref[rows, cols] * (gate * jax.nn.sigmoid(gate))
            held = held_ref[:, cols]
            before = carry_ref[index, :, cols]
            stacked_up = stacked_heads(upstream, heads).astype(jnp.bfloat16)
            products = low_against(scaled, stacked_up)
            weights = []
            for place in range(heads):
                head = start // HD + place
                spread = cumul_turned[head : head + 1, :] - cumul[:, head : head + 1]
                decay = jnp.exp(jnp.where(upper, spread, -jnp.inf))
                product = products[:, place * SPAN : (place + 1) * SPAN] * decay
                grad_cross = grad_cross + product
                flow = product * cross
                turned_ref[head : head + 1, :] = jnp.sum(flow, axis=0, keepdims=True)
                column_ref[:, head : head + 1] = jnp.sum(flow, axis=1, keepdims=True)
                weights.append((decay * cross).astype(jnp.bfloat16))
            weights = jnp.concatenate(weights, axis=1) if heads > 1 else weights[0]
            grown_up = upstream * grown_wide[:, span]
            tailed = scaled * tail_wide[:, span]
            from_held = low_dot(entry, held)
            grad_scaled = low_dot(weights, stacked_up) + tail_wide[:, span] * from_held
            wide_ref[0, :, cols] = grown_up * low_dot(readout, before)
            wide_ref[1, :, cols] = tailed * from_held
            wide_ref[2, :, cols] = values * grad_scaled
            grad_readout = grad_readout + low_against(grown_up, before)
            grad_entry = grad_entry + low_against(tailed, held)
            last = grown_wide[SPAN - 1 : SPAN, span]
            scale_sum_ref[:, cols] = jnp.sum(held * before, axis=0, keepdims=True) * last
            skip_sum_ref[:, cols] += jnp.sum(upstream * values, axis=0, keepdims=True)
            held_ref[:, cols] = held * last + low_inner(readout, grown_up)
            act_ref[rows, cols] = step_wide[:, span] * grad_scaled + skip_ref[:, cols] * upstream
        sums = exact_dot(
            jnp.concatenate([wide_ref[0], wide_ref[1], wide_ref[2]], axis=0), collect_ref[...]
        )
        scale_sum = exact_dot(jnp.broadcast_to(scale_sum_ref[...], (8, channels)), collect_ref[...])
        flows = turned_ref[...].T - column_ref[...] + sums[:SPAN]
        onward = (row_index(square) <= lane_index(square)).astype(jnp.float32)
        strict = (row_index(square) > lane_index(square)).astype(jnp.float32)
        grad_log = (
            exact_dot(onward, flows)
            + exact_dot(strict, sums[SPAN : 2 * SPAN])
            + scale_sum[:1]
        )
        grad_steps = grad_log * rate_ref[...] + sums[2 * SPAN :]
        grad_raw = grad_steps * jax.nn.sigmoid(raw)
        grad_step_ref[rows, :] = grad_raw.astype(jnp.bfloat16)
        grad_head_ref[0, 0:1, :] += jnp.sum(grad_raw, axis=0, keepdims=True)
        grad_head_ref[0, 1:2, :] += (
            jnp.sum(grad_log * steps, axis=0, keepdims=True) * rate_ref[...]
        )
        both_ref[rows, pl.ds(0, states)] = grad_entry + low_dot(grad_cross, readout)
        both_ref[rows, pl.ds(states, states)] = grad_readout + low_inner(grad_cross, entry)
        return unused

    lax.fori_loop(0, chunks, chunk, 0)
    grad_head_ref[0, 2:3, :] = exact_dot(
        jnp.broadcast_to(skip_sum_ref[...], (8, channels)), collect_ref[...]
    )[:1]

    def convolve_back(raw_ref, grads_ref, slopes_ref, kernel_ref, out_ref, sums_ref, width_all):
        for start, width in slabs(width_all):
            cols = pl.ds(start, width)
            grad = grads_ref[:, cols] * slopes_ref[:, cols]
            raw = raw_ref[:, cols]
            total = kernel_ref[taps - 1 : taps, cols] * grad
            sums_ref[0, taps - 1 : taps, cols] = jnp.sum(grad * raw, axis=0, keepdims=True)
            for tap in range(taps - 1):
                shifted = sooner(grad, taps - 1 - tap)
                total = total + kernel_ref[tap : tap + 1, cols] * shifted
                sums_ref[0, tap : tap + 1, cols] = jnp.sum(shifted * raw, axis=0, keepdims=True)
            sums_ref[0, taps : taps + 1, cols] = jnp.sum(grad, axis=0, keepdims=True)
            out_ref[:, cols] = total.astype(jnp.bfloat16)

    convolve_back(
        input_ref,
        act_ref,
        slope_ref,
        input_kernel_ref,
        grad_input_ref,
        grad_input_conv_ref,
        channels,
    )
    convolve_back(
        state_ref,
        both_ref,
        both_slope_ref,
        state_kernel_ref,
        grad_state_ref,
        grad_state_conv_ref,
        2 * states,
    )


def by_sequence(length, width):
    return pl.BlockSpec((length, width), lambda seq: (seq, 0))


def fixed(*shape):
    return pl.BlockSpec(shape, lambda seq: (0,) * len(shape))


def head_spread(heads):
    marks = np.zeros((LANES, heads * HD), np.float32)
    for head in range(heads):
        marks[head, head * HD : (head + 1) * HD] = 1.0
    return marks


def pad_lanes(part):
    return jnp.pad(part, ((0, 0), (0, LANES - part.shape[1])))


def ssd_small(input_kernel, input_shift, state_kernel, state_shift, step_bias, decay_log, skip_gain):
    rates = -jnp.exp(decay_log)
    return (
        input_kernel,
        input_shift[None, :],
        state_kernel,
        state_shift[None, :],
        pad_lanes(step_bias[None, :]),
        pad_lanes(rates[None, :]),
        jnp.repeat(skip_gain, HD)[None, :],
    )


def ssd_forward(inputs, states_raw, gate, step, small, heads, length):
    group, channels = inputs.shape
    seqs = group // length
    both = states_raw.shape[1]
    states = both // 2
    chunks = length // SPAN
    taps = small[0].shape[0]
    return pl.pallas_call(
        ssd_forward_kernel,
        grid=(seqs,),
        in_specs=[
            by_sequence(length, channels),
            by_sequence(length, both),
            by_sequence(length, channels),
            by_sequence(length, LANES),
            fixed(taps, channels),
            fixed(1, channels),
            fixed(taps, both),
            fixed(1, both),
            fixed(1, LANES),
            fixed(1, LANES),
            fixed(1, channels),
            fixed(LANES, channels),
        ],
        out_specs=[
            by_sequence(length, channels),
            by_sequence(length, channels),
            pl.BlockSpec((chunks, states, channels), lambda seq: (seq, 0, 0)),
        ],
        out_shape=[
            jax.ShapeDtypeStruct((group, channels), jnp.bfloat16),
            jax.ShapeDtypeStruct((group, channels), jnp.float32),
            jax.ShapeDtypeStruct((seqs * chunks, states, channels), jnp.float32),
        ],
        scratch_shapes=[
            pltpu.VMEM((length, channels), jnp.float32),
            pltpu.VMEM((length, both), jnp.float32),
            pltpu.VMEM((states, channels), jnp.float32),
        ],
        compiler_params=pltpu.CompilerParams(vmem_limit_bytes=VMEM_LIMIT),
        cost_estimate=pl.CostEstimate(
            flops=8 * group * channels * SPAN,
            bytes_accessed=20 * group * channels,
            transcendentals=group * heads * SPAN,
        ),
        name="ssd_forward",
    )(inputs, states_raw, gate, step, *small, jnp.asarray(head_spread(heads)))


def ssd_backward(inputs, states_raw, gate, step, grad, carry, small, heads, length):
    group, channels = inputs.shape
    seqs = group // length
    both = states_raw.shape[1]
    states = both // 2
    chunks = length // SPAN
    taps = small[0].shape[0]
    return pl.pallas_call(
        ssd_backward_kernel,
        grid=(seqs,),
        in_specs=[
            by_sequence(length, channels),
            by_sequence(length, both),
            by_sequence(length, channels),
            by_sequence(length, LANES),
            by_sequence(length, channels),
            pl.BlockSpec((chunks, states, channels), lambda seq: (seq, 0, 0)),
            fixed(taps, channels),
            fixed(1, channels),
            fixed(taps, both),
            fixed(1, both),
            fixed(1, LANES),
            fixed(1, LANES),
            fixed(1, channels),
            fixed(LANES, channels),
            fixed(channels, LANES),
        ],
        out_specs=[
            by_sequence(length, channels),
            by_sequence(length, both),
            by_sequence(length, LANES),
            pl.BlockSpec((1, 8, channels), lambda seq: (seq, 0, 0)),
            pl.BlockSpec((1, 8, both), lambda seq: (seq, 0, 0)),
            pl.BlockSpec((1, 8, LANES), lambda seq: (seq, 0, 0)),
        ],
        out_shape=[
            jax.ShapeDtypeStruct((group, channels), jnp.bfloat16),
            jax.ShapeDtypeStruct((group, both), jnp.bfloat16),
            jax.ShapeDtypeStruct((group, LANES), jnp.bfloat16),
            jax.ShapeDtypeStruct((seqs, 8, channels), jnp.float32),
            jax.ShapeDtypeStruct((seqs, 8, both), jnp.float32),
            jax.ShapeDtypeStruct((seqs, 8, LANES), jnp.float32),
        ],
        scratch_shapes=[
            pltpu.VMEM((length, channels), jnp.float32),
            pltpu.VMEM((length, channels), jnp.float32),
            pltpu.VMEM((length, both), jnp.float32),
            pltpu.VMEM((length, both), jnp.float32),
            pltpu.VMEM((states, channels), jnp.float32),
            pltpu.VMEM((3, SPAN, channels), jnp.float32),
            pltpu.VMEM((LANES, SPAN), jnp.float32),
            pltpu.VMEM((SPAN, LANES), jnp.float32),
            pltpu.VMEM((1, channels), jnp.float32),
            pltpu.VMEM((1, channels), jnp.float32),
        ],
        compiler_params=pltpu.CompilerParams(vmem_limit_bytes=VMEM_LIMIT),
        cost_estimate=pl.CostEstimate(
            flops=20 * group * channels * SPAN,
            bytes_accessed=20 * group * channels,
            transcendentals=group * heads * SPAN,
        ),
        name="ssd_backward",
    )(
        inputs,
        states_raw,
        gate,
        step,
        grad,
        carry,
        *small,
        jnp.asarray(head_spread(heads)),
        jnp.asarray(head_spread(heads).T.copy()),
    )


def rope_wide(length):
    half = HD // 2
    freqs = np.float32(ROPE_BASE) ** (-np.arange(half, dtype=np.float32) * np.float32(2.0 / HD))
    angles = np.arange(length, dtype=np.float32)[:, None] * freqs[None, :].astype(np.float32)
    cosine, sine = np.cos(angles), np.sin(angles)
    count = LANES // HD
    return (
        np.concatenate([cosine, cosine] * count, axis=1).astype(np.float32),
        np.concatenate([-sine, sine] * count, axis=1).astype(np.float32),
    )


def turn(part, cosine, sine):
    half = HD // 2
    first = lane_index(part.shape) % HD < half
    swapped = jnp.where(first, pltpu.roll(part, LANES - half, 1), pltpu.roll(part, half, 1))
    return part * cosine + swapped * sine


def attend_forward_kernel(
    query_ref, pair_ref, cosine_ref, sine_ref, context_ref, query_out_ref, pair_out_ref, total_ref
):
    length = query_ref.shape[0]
    cosine, sine = cosine_ref[...], sine_ref[...]
    pair = pair_ref[...]
    left = lane_index(pair.shape) < HD
    pair = jnp.where(left, turn(pair, cosine, sine), pair)
    pair_out_ref[...] = pair.astype(jnp.bfloat16)
    moved = pltpu.roll(pair, HD, 1)
    keys = jnp.where(left, pair, moved).astype(jnp.bfloat16)
    values = jnp.where(left, moved, pair).astype(jnp.bfloat16)
    scale = HD ** (-0.5)
    for slab in range(query_ref.shape[1] // LANES):
        cols = pl.ds(slab * LANES, LANES)
        query_out_ref[:, cols] = turn(query_ref[:, cols], cosine, sine).astype(jnp.bfloat16)
        for tile in range(length // SPAN):
            rows = slice(tile * SPAN, (tile + 1) * SPAN)
            count = (tile + 1) * SPAN
            query = query_out_ref[rows, cols]
            lane = lane_index(query.shape)
            square = (SPAN, count)
            causal = row_index(square) + tile * SPAN >= lane_index(square)
            results = []
            for place in range(LANES // HD):
                mine = (lane >= place * HD) & (lane < place * HD + HD)
                scores = low_against(jnp.where(mine, query, 0), keys[:count]) * scale
                scores = jnp.where(causal, scores, -jnp.inf)
                peak = jnp.max(scores, axis=-1, keepdims=True)
                grown = jnp.exp(scores - peak)
                total = jnp.sum(grown, axis=-1, keepdims=True)
                probs = grown * (1.0 / total)
                results.append(low_dot(probs, values[:count]))
                head = slab * (LANES // HD) + place
                total_ref[rows, head : head + 1] = jnp.log(total) + peak
            context_ref[rows, cols] = jnp.where(lane < HD, results[0], results[1]).astype(
                jnp.bfloat16
            )


def attend_backward_kernel(
    query_ref,
    pair_ref,
    total_ref,
    grad_ref,
    cosine_ref,
    sine_ref,
    grad_query_ref,
    grad_pair_ref,
    key_sum_ref,
    value_sum_ref,
):
    length = query_ref.shape[0]
    cosine, sine = cosine_ref[...], -sine_ref[...]
    pair = pair_ref[...].astype(jnp.float32)
    left = lane_index(pair.shape) < HD
    moved = pltpu.roll(pair, HD, 1)
    keys = jnp.where(left, pair, moved).astype(jnp.bfloat16)
    values = jnp.where(left, moved, pair).astype(jnp.bfloat16)
    scale = HD ** (-0.5)
    key_sum_ref[...] = jnp.zeros_like(key_sum_ref)
    value_sum_ref[...] = jnp.zeros_like(value_sum_ref)
    for slab in range(query_ref.shape[1] // LANES):
        cols = pl.ds(slab * LANES, LANES)
        for tile in range(length // SPAN):
            rows = slice(tile * SPAN, (tile + 1) * SPAN)
            count = (tile + 1) * SPAN
            query = query_ref[rows, cols]
            upstream = grad_ref[rows, cols]
            lane = lane_index(query.shape)
            square = (SPAN, count)
            causal = row_index(square) + tile * SPAN >= lane_index(square)
            results = []
            for place in range(LANES // HD):
                mine = (lane >= place * HD) & (lane < place * HD + HD)
                head = slab * (LANES // HD) + place
                own_query = jnp.where(mine, query, 0)
                own_up = jnp.where(mine, upstream, 0)
                scores = low_against(own_query, keys[:count]) * scale
                scores = jnp.where(causal, scores, -jnp.inf)
                probs = jnp.exp(scores - total_ref[rows, head : head + 1])
                grad_probs = low_against(own_up, values[:count])
                mean = jnp.sum(probs * grad_probs, axis=-1, keepdims=True)
                grad_scores = (probs * (grad_probs - mean)).astype(jnp.bfloat16)
                results.append(low_dot(grad_scores, keys[:count]))
                key_sum_ref[0:count, :] += low_inner(grad_scores, own_query)
                value_sum_ref[0:count, :] += low_inner(probs, own_up)
            grad_query = jnp.where(lane < HD, results[0], results[1]) * scale
            grad_query_ref[rows, cols] = turn(
                grad_query, cosine[rows, :], sine[rows, :]
            ).astype(jnp.bfloat16)
    grad_key = key_sum_ref[...]
    grad_key = turn((grad_key + pltpu.roll(grad_key, HD, 1)) * scale, cosine, sine)
    grad_value = value_sum_ref[...]
    grad_value = grad_value + pltpu.roll(grad_value, HD, 1)
    grad_pair_ref[...] = jnp.where(left, grad_key, grad_value).astype(jnp.bfloat16)


def attend_forward(query, pair, length):
    group, width = query.shape
    heads = width // HD
    cosine, sine = rope_wide(length)
    return pl.pallas_call(
        attend_forward_kernel,
        grid=(group // length,),
        in_specs=[
            by_sequence(length, width),
            by_sequence(length, LANES),
            fixed(length, LANES),
            fixed(length, LANES),
        ],
        out_specs=[
            by_sequence(length, width),
            by_sequence(length, width),
            by_sequence(length, LANES),
            by_sequence(length, LANES),
        ],
        out_shape=[
            jax.ShapeDtypeStruct((group, width), jnp.bfloat16),
            jax.ShapeDtypeStruct((group, width), jnp.bfloat16),
            jax.ShapeDtypeStruct((group, LANES), jnp.bfloat16),
            jax.ShapeDtypeStruct((group, LANES), jnp.float32),
        ],
        compiler_params=pltpu.CompilerParams(vmem_limit_bytes=VMEM_LIMIT),
        cost_estimate=pl.CostEstimate(
            flops=4 * group * width * length,
            bytes_accessed=12 * group * width,
            transcendentals=group * heads * length // 2,
        ),
        name="attend_forward",
    )(query, pair, jnp.asarray(cosine), jnp.asarray(sine))


def attend_backward(query, pair, total, grad, length):
    group, width = query.shape
    heads = width // HD
    cosine, sine = rope_wide(length)
    return pl.pallas_call(
        attend_backward_kernel,
        grid=(group // length,),
        in_specs=[
            by_sequence(length, width),
            by_sequence(length, LANES),
            by_sequence(length, LANES),
            by_sequence(length, width),
            fixed(length, LANES),
            fixed(length, LANES),
        ],
        out_specs=[by_sequence(length, width), by_sequence(length, LANES)],
        out_shape=[
            jax.ShapeDtypeStruct((group, width), jnp.bfloat16),
            jax.ShapeDtypeStruct((group, LANES), jnp.bfloat16),
        ],
        scratch_shapes=[
            pltpu.VMEM((length, LANES), jnp.float32),
            pltpu.VMEM((length, LANES), jnp.float32),
        ],
        compiler_params=pltpu.CompilerParams(vmem_limit_bytes=VMEM_LIMIT),
        cost_estimate=pl.CostEstimate(
            flops=10 * group * width * length,
            bytes_accessed=12 * group * width,
            transcendentals=group * heads * length // 2,
        ),
        name="attend_backward",
    )(query, pair, total, grad, jnp.asarray(cosine), jnp.asarray(sine))


def bit_pairs(size, bit):
    return [(index, index ^ (1 << bit)) for index in range(size)]


def split_sides(part, bit):
    side = (lax.axis_index("dp") >> bit) & 1
    halves = part.reshape(2, part.shape[0] // 2, part.shape[1])
    keep = lax.dynamic_index_in_dim(halves, side, 0, False)
    give = lax.dynamic_index_in_dim(halves, 1 - side, 0, False)
    return keep, give


def add_half(keep, give, bit, size):
    got = lax.ppermute(give, "dp", bit_pairs(size, bit))
    return (keep.astype(jnp.float32) + got.astype(jnp.float32)).astype(jnp.bfloat16)


def join_half(part, bit, size):
    side = (lax.axis_index("dp") >> bit) & 1
    got = lax.ppermute(part, "dp", bit_pairs(size, bit))
    return jnp.where(
        side == 0, jnp.concatenate([part, got], axis=0), jnp.concatenate([got, part], axis=0)
    )


def after(part, *deps):
    return lax.optimization_barrier((part,) + deps)[0]


def behind(part, dep):
    zero = jnp.minimum(jnp.abs(dep[:1, :1].astype(jnp.float32)), 0.0)
    return part + zero.astype(part.dtype)


class Sum:
    def __init__(self, part, size, swapped):
        self.size = size
        self.direct = bool(size & (size - 1) or part.shape[0] % size)
        self.order = [] if self.direct else bit_order(size, swapped)
        self.part = part
        self.step = 0
        self.give = part
        self.prepare()

    def prepare(self):
        if self.step < len(self.order):
            self.keep, self.give = split_sides(self.part, self.order[self.step])
        else:
            self.give = self.part

    def advance(self):
        if self.step < len(self.order):
            self.part = add_half(self.keep, self.give, self.order[self.step], self.size)
            self.step += 1
            self.prepare()
        return self.give

    def finish(self, middle=None):
        while self.step < len(self.order):
            self.advance()
        if self.direct:
            self.part = lax.psum(self.part, "dp")
        if middle is not None:
            self.part = middle(self.part)
        for bit in reversed(self.order):
            self.part = join_half(self.part, bit, self.size)
        return self.part


def bit_order(size, swapped):
    order = list(range(size.bit_length() - 1))
    if swapped and len(order) > 2:
        order[1], order[2] = order[2], order[1]
    return order


def other(part):
    return lax.ppermute(part, "tensor", [(0, 1), (1, 0)])


def all_rows(part, shards):
    if shards != 2:
        return lax.all_gather(part, "tensor", axis=0, tiled=True)
    got = other(part)
    return jnp.where(
        lax.axis_index("tensor") == 0,
        jnp.concatenate([part, got], axis=0),
        jnp.concatenate([got, part], axis=0),
    )


def sum_all(part, shards):
    if shards != 2:
        return lax.psum(part, "tensor").astype(jnp.float32)
    return part.astype(jnp.float32) + other(part).astype(jnp.float32)


def sum_own(part, shards):
    if shards != 2:
        return lax.psum_scatter(part, "tensor", scatter_dimension=0, tiled=True).astype(jnp.float32)
    me = lax.axis_index("tensor")
    halves = part.reshape(2, part.shape[0] // 2, part.shape[1])
    keep = lax.dynamic_index_in_dim(halves, me, 0, False)
    got = other(lax.dynamic_index_in_dim(halves, 1 - me, 0, False))
    return keep.astype(jnp.float32) + got.astype(jnp.float32)


def own_rows(part, rows):
    return lax.dynamic_slice_in_dim(part, lax.axis_index("tensor") * rows, rows, 0)


def column_pack(vectors, rows):
    flat = jnp.concatenate([item.reshape(-1) for item in vectors])
    width = -(-flat.shape[0] // rows)
    return jnp.pad(flat, (0, width * rows - flat.shape[0])).reshape(width, rows).T


def column_unpack(packed, shapes):
    flat = packed.T.reshape(-1)
    out, start = [], 0
    for shape in shapes:
        count = 1
        for size in shape:
            count *= size
        out.append(flat[start : start + count].reshape(shape))
        start += count
    return out


def body(
    dp_size,
    shards,
    layer_input,
    input_gain,
    middle_gain,
    mamba_gate,
    mamba_input,
    step_weight,
    state_weight,
    input_kernel,
    input_shift,
    state_kernel,
    state_shift,
    step_bias,
    decay_log,
    skip_gain,
    mamba_output,
    query_weight,
    keyvalue_weight,
    context_weight,
    gate_weight,
    up_weight,
    down_weight,
    cotangent,
):
    own = layer_input.shape[0]
    rows_low = all_rows(layer_input, shards)
    cotan_low = all_rows(cotangent, shards)
    rows = rows_low.astype(jnp.float32)
    gain_first = input_gain.astype(jnp.float32)
    gain_second = middle_gain.astype(jnp.float32)
    factor_first = lax.rsqrt(jnp.mean(rows * rows, axis=-1, keepdims=True) + EPSILON)
    normal_first = rows * factor_first
    whole = (normal_first * gain_first).astype(jnp.bfloat16)
    group = whole.shape[0]
    length = min(SEQ_LEN, group)
    seqs = group // length
    heads_here = query_weight.shape[1] // HD
    kv_head = lax.axis_index("tensor") * heads_here // (HQ // KVH)
    key_cols = lax.dynamic_slice_in_dim(keyvalue_weight, kv_head * HD, HD, 1)
    value_cols = lax.dynamic_slice_in_dim(keyvalue_weight, (KVH + kv_head) * HD, HD, 1)
    pair_weight = jnp.concatenate([key_cols, value_cols], axis=1)
    query_cols = query_weight.shape[1]
    query_pad = -query_cols % LANES
    query_wide = jnp.pad(query_weight, ((0, 0), (0, query_pad)))
    step_wide = pad_lanes(step_weight)
    heads = step_weight.shape[1]
    input_raw = forward_dot(whole, mamba_input)
    state_raw = forward_dot(whole, state_weight)
    step_raw = forward_dot(whole, step_wide)
    gate_raw = forward_dot(whole, mamba_gate)
    query_raw = forward_dot(whole, query_wide)
    pair_raw = forward_dot(whole, pair_weight)
    small = ssd_small(
        input_kernel.astype(jnp.float32),
        input_shift.astype(jnp.float32),
        state_kernel.astype(jnp.float32),
        state_shift.astype(jnp.float32),
        step_bias.astype(jnp.float32),
        decay_log.astype(jnp.float32),
        skip_gain.astype(jnp.float32),
    )
    gated_low, ssm_out, carries = ssd_forward(
        input_raw, state_raw, gate_raw, step_raw, small, heads, length
    )
    context_wide, queries, pairs, totals = attend_forward(
        after(query_raw, cotan_low), pair_raw, length
    )
    context_rows = context_wide[:, :query_cols]
    mixed_part = forward_dot(gated_low, mamba_output) + forward_dot(context_rows, context_weight)
    resid = rows + sum_all(mixed_part.astype(jnp.bfloat16), shards)
    factor_second = lax.rsqrt(jnp.mean(resid * resid, axis=-1, keepdims=True) + EPSILON)
    normal_second = resid * factor_second
    whole_mid = (normal_second * gain_second).astype(jnp.bfloat16)
    gate = forward_dot(whole_mid, gate_weight)
    upper = forward_dot(whole_mid, up_weight)
    sigmoid_gate = jax.nn.sigmoid(gate)
    silu_gate = gate * sigmoid_gate
    hidden = (silu_gate * upper).astype(jnp.bfloat16)
    grad_hidden = against(cotan_low, down_weight)
    slope = sigmoid_gate * (1.0 + gate * (1.0 - sigmoid_gate))
    grad_gate_low = (grad_hidden * upper * slope).astype(jnp.bfloat16)
    grad_upper_low = (grad_hidden * silu_gate).astype(jnp.bfloat16)
    back_part = (against(grad_gate_low, gate_weight) + against(grad_upper_low, up_weight)).astype(
        jnp.bfloat16
    )
    back_mid = sum_all(back_part, shards)
    hidden_late = after(hidden, back_part)
    mid_late = after(whole_mid, back_part)
    grad_down = inner_rows(hidden_late, cotan_low).astype(jnp.bfloat16)
    grad_gate = inner_rows(mid_late, grad_gate_low).astype(jnp.bfloat16)
    grad_up = inner_rows(mid_late, grad_upper_low).astype(jnp.bfloat16)
    grad_gate, grad_up, grad_down = lax.psum((grad_gate, grad_up, grad_down), "dp")
    feed_part = behind(forward_dot(hidden_late, down_weight), back_mid).astype(jnp.bfloat16)
    feed = sum_own(feed_part, shards)
    layer_output = (own_rows(resid, own) + feed).astype(jnp.bfloat16)
    grad_middle = jnp.sum(back_part.astype(jnp.float32) * normal_second, axis=0)
    grad_resid = cotan_low.astype(jnp.float32) + norm_back(
        back_mid, gain_second, normal_second, factor_second
    )
    mixer_all = grad_resid.astype(jnp.bfloat16)
    mixer_sum = Sum(
        inner_rows(jnp.concatenate([gated_low, context_rows], axis=1), mixer_all).astype(
            jnp.bfloat16
        ),
        dp_size,
        False,
    )
    ssm_rows = gated_low.shape[1]
    grad_gated = against(mixer_all, mamba_output)
    sigmoid_raw = jax.nn.sigmoid(gate_raw)
    grad_gate_raw = (
        grad_gated * ssm_out * (sigmoid_raw * (1.0 + gate_raw * (1.0 - sigmoid_raw)))
    ).astype(jnp.bfloat16)
    grad_context = against(mixer_all, context_weight).astype(jnp.bfloat16)
    grad_query_raw, grad_pair_raw = attend_backward(
        queries,
        pairs,
        totals,
        after(jnp.pad(grad_context, ((0, 0), (0, query_pad))), mixer_sum.give),
        length,
    )
    grad_query_raw = grad_query_raw[:, :query_cols]
    early_cols = jnp.concatenate([grad_gate_raw, grad_query_raw], axis=1)
    early_sum = Sum(inner_rows(whole, early_cols).astype(jnp.bfloat16), dp_size, True)
    grad_gated = after(grad_gated, early_sum.give, mixer_sum.advance())
    grad_input_raw, grad_state_raw, grad_step_raw, input_sums, state_sums, head_sums = ssd_backward(
        input_raw, state_raw, gate_raw, step_raw, grad_gated, carries, small, heads, length
    )
    input_sums = jnp.sum(input_sums, axis=0)
    state_sums = jnp.sum(state_sums, axis=0)
    head_sums = jnp.sum(head_sums, axis=0)[:, :heads]
    taps = input_kernel.shape[0]
    early_sum.advance()
    mixer_sum.advance()
    grad_input_raw = after(grad_input_raw, early_sum.give, mixer_sum.give)
    late_cols = jnp.concatenate(
        [grad_input_raw, grad_state_raw, grad_pair_raw, grad_step_raw], axis=1
    )
    total = against(early_cols, jnp.concatenate([mamba_gate, query_weight], axis=1))
    total = total + against(
        late_cols, jnp.concatenate([mamba_input, state_weight, pair_weight, step_wide], axis=1)
    )
    total_low = total.astype(jnp.bfloat16)
    grad_first = jnp.sum(total_low.astype(jnp.float32) * normal_first, axis=0)
    width = whole.shape[1]
    gate_cols = grad_gate_raw.shape[1]
    input_cols = grad_input_raw.shape[1]
    state_cols = grad_state_raw.shape[1]
    step_cols = heads
    pair_cols = grad_pair_raw.shape[1]

    own_vectors = (input_sums[:taps], input_sums[taps], head_sums[0], head_sums[1], head_sums[2])
    shared_vectors = (grad_first, grad_middle, state_sums[:taps], state_sums[taps])
    own_pack = column_pack(own_vectors, width).astype(jnp.bfloat16)
    shared_pack = column_pack(shared_vectors, width).astype(jnp.bfloat16)
    own_width = own_pack.shape[1]
    shared_width = shared_pack.shape[1]

    split_pairs = shards == KVH
    late = inner_rows(whole, late_cols).astype(jnp.bfloat16)
    marks = (input_cols, input_cols + state_cols, input_cols + state_cols + pair_cols)
    late_pair = late[:, marks[1] : marks[2]]
    if not split_pairs:
        spread = jnp.zeros((width, 2 * KVH * HD), jnp.bfloat16)
        spread = lax.dynamic_update_slice_in_dim(spread, late_pair[:, :HD], kv_head * HD, 1)
        late_pair = lax.dynamic_update_slice_in_dim(
            spread, late_pair[:, HD:], (KVH + kv_head) * HD, 1
        )
    tail = jnp.concatenate(
        [late[:, input_cols : marks[1]], late_pair, shared_pack, late[:, marks[2] : marks[2] + step_cols], own_pack],
        axis=1,
    )
    sent = state_cols + late_pair.shape[1] + shared_width

    def over_tensor(part):
        shared, rest = part[:, :sent], part[:, sent:]
        if not split_pairs:
            return jnp.concatenate([lax.psum(shared, "tensor"), rest], axis=1)
        got = other(shared)
        first = lax.axis_index("tensor") == 0
        low = jnp.where(first, shared, got)[:, state_cols : state_cols + pair_cols]
        high = jnp.where(first, got, shared)[:, state_cols : state_cols + pair_cols]
        both = (shared.astype(jnp.float32) + got.astype(jnp.float32)).astype(jnp.bfloat16)
        return jnp.concatenate(
            [
                both[:, :state_cols],
                low[:, :HD],
                high[:, :HD],
                low[:, HD:],
                high[:, HD:],
                both[:, state_cols + pair_cols :],
                rest,
            ],
            axis=1,
        )

    tail_sum = Sum(tail, dp_size, True)
    input_sum = Sum(late[:, :input_cols], dp_size, False)
    tail = tail_sum.finish(over_tensor)
    grad_mamba_input = input_sum.finish()
    grad_mixer_out = mixer_sum.finish()
    grad_mamba_out = grad_mixer_out[:ssm_rows]
    grad_context_w = grad_mixer_out[ssm_rows:]
    early = early_sum.finish()
    back_in = sum_own(total_low, shards)
    normal_own = own_rows(normal_first, own)
    factor_own = own_rows(factor_first, own)
    input_grad = own_rows(grad_resid, own) + norm_back(back_in, gain_first, normal_own, factor_own)
    start = state_cols + keyvalue_weight.shape[1]
    grad_first, grad_middle, grad_st_kernel, grad_st_shift = column_unpack(
        tail[:, start : start + shared_width], [item.shape for item in shared_vectors]
    )
    start = start + shared_width
    grad_step = tail[:, start : start + step_cols]
    grad_in_kernel, grad_in_shift, grad_bias, grad_decay, grad_skip = column_unpack(
        tail[:, start + step_cols :], [item.shape for item in own_vectors]
    )
    results = (
        grad_first,
        grad_middle,
        early[:, :gate_cols],
        grad_mamba_input,
        grad_step,
        tail[:, :state_cols],
        grad_in_kernel,
        grad_in_shift,
        grad_st_kernel,
        grad_st_shift,
        grad_bias,
        grad_decay,
        grad_skip,
        grad_mamba_out,
        early[:, gate_cols:],
        tail[:, state_cols : state_cols + keyvalue_weight.shape[1]],
        grad_context_w,
        grad_gate,
        grad_up,
        grad_down,
    )
    return (layer_output, input_grad) + tuple(item.astype(jnp.float32) for item in results)


def solution(mesh):
    in_specs = (
        P(("dp", "tensor"), None),
        P(),
        P(),
        P(None, "tensor"),
        P(None, "tensor"),
        P(None, "tensor"),
        P(),
        P(None, "tensor"),
        P("tensor"),
        P(),
        P(),
        P("tensor"),
        P("tensor"),
        P("tensor"),
        P("tensor", None),
        P(None, "tensor"),
        P(),
        P("tensor", None),
        P(None, "tensor"),
        P(None, "tensor"),
        P("tensor", None),
        P(("dp", "tensor"), None),
    )
    out_specs = (
        P(("dp", "tensor"), None),
        P(("dp", "tensor"), None),
        P(),
        P(),
        P(None, "tensor"),
        P(None, "tensor"),
        P(None, "tensor"),
        P(),
        P(None, "tensor"),
        P("tensor"),
        P(),
        P(),
        P("tensor"),
        P("tensor"),
        P("tensor"),
        P("tensor", None),
        P(None, "tensor"),
        P(),
        P("tensor", None),
        P(None, "tensor"),
        P(None, "tensor"),
        P("tensor", None),
    )
    run = partial(body, mesh.shape["dp"], mesh.shape["tensor"])
    return jax.shard_map(run, mesh=mesh, in_specs=in_specs, out_specs=out_specs, check_vma=False)
```

```python
from functools import partial

import jax
import jax.numpy as jnp
import numpy as np
from jax import lax
from jax.experimental import pallas as pl
from jax.experimental.pallas import tpu as pltpu
from jax.sharding import PartitionSpec as P

HD = 64
HQ = 8
KVH = 2
SPAN = 128
SEQ_LEN = 1024


EPSILON = 1e-05
ROPE_BASE = 10000.0
PRECISE = lax.Precision.HIGHEST


def forward_dot(left, right):
    return jnp.dot(left, right, preferred_element_type=jnp.float32)


def inner_rows(left, right):
    return lax.dot_general(
        left, right, (((0,), (0,)), ((), ())), preferred_element_type=jnp.float32
    )


def against(left, right):
    return lax.dot_general(
        left, right, (((1,), (1,)), ((), ())), preferred_element_type=jnp.float32
    )


def norm_back(upstream, gain, normal, factor):
    scaled = upstream * gain
    return factor * (scaled - normal * jnp.mean(scaled * normal, axis=-1, keepdims=True))


LANES = 128
VMEM_LIMIT = 44 * 1024 * 1024


def exact_dot(left, right):
    return jnp.dot(left, right, precision=PRECISE, preferred_element_type=jnp.float32)


def low_dot(left, right):
    return jnp.dot(
        left.astype(jnp.bfloat16), right.astype(jnp.bfloat16), preferred_element_type=jnp.float32
    )


def low_against(left, right):
    return lax.dot_general(
        left.astype(jnp.bfloat16),
        right.astype(jnp.bfloat16),
        (((1,), (1,)), ((), ())),
        preferred_element_type=jnp.float32,
    )


def low_inner(left, right):
    return lax.dot_general(
        left.astype(jnp.bfloat16),
        right.astype(jnp.bfloat16),
        (((0,), (0,)), ((), ())),
        preferred_element_type=jnp.float32,
    )


def row_index(shape):
    return lax.broadcasted_iota(jnp.int32, shape, 0)


def lane_index(shape):
    return lax.broadcasted_iota(jnp.int32, shape, 1)


def later(part, count):
    if count == 0:
        return part
    return jnp.where(row_index(part.shape) >= count, pltpu.roll(part, count, 0), 0.0)


def sooner(part, count):
    if count == 0:
        return part
    rows = part.shape[0]
    return jnp.where(row_index(part.shape) < rows - count, pltpu.roll(part, rows - count, 0), 0.0)


def slabs(width):
    return [(start, min(LANES, width - start)) for start in range(0, width, LANES)]


def soft_plus(value):
    return jnp.maximum(value, 0.0) + jnp.log1p(jnp.exp(-jnp.abs(value)))


def stacked_heads(part, heads):
    if heads == 1:
        return part
    lane = lane_index(part.shape)
    return jnp.concatenate(
        [jnp.where((lane >= head * HD) & (lane < head * HD + HD), part, 0.0) for head in range(heads)],
        axis=0,
    )


def convolve(raw, kernel_ref, shift_ref, cols):
    taps = kernel_ref.shape[0]
    out = shift_ref[:, cols] + kernel_ref[taps - 1 : taps, cols] * raw
    for tap in range(taps - 1):
        out = out + kernel_ref[tap : tap + 1, cols] * later(raw, taps - 1 - tap)
    return out


def chunk_steps(step_ref, bias_ref, rate_ref, expand_ref, rows):
    raw = step_ref[rows, :] + bias_ref[...]
    steps = soft_plus(raw)
    logdec = steps * rate_ref[...]
    square = (SPAN, SPAN)
    lower = (row_index(square) >= lane_index(square)).astype(jnp.float32)
    cumul = exact_dot(lower, logdec)
    grown = jnp.exp(cumul)
    tail = jnp.exp(cumul[SPAN - 1 : SPAN, :] - cumul)
    wide = exact_dot(jnp.concatenate([steps, grown, tail], axis=0), expand_ref[...])
    return raw, steps, cumul, wide[:SPAN], wide[SPAN : 2 * SPAN], wide[2 * SPAN :]


def ssd_forward_kernel(
    input_ref,
    state_ref,
    gate_ref,
    step_ref,
    input_kernel_ref,
    input_shift_ref,
    state_kernel_ref,
    state_shift_ref,
    bias_ref,
    rate_ref,
    skip_ref,
    expand_ref,
    gated_ref,
    out_ref,
    carry_ref,
    act_ref,
    both_ref,
    held_ref,
):
    channels = input_ref.shape[1]
    states = state_ref.shape[1] // 2
    for start, width in slabs(channels):
        cols = pl.ds(start, width)
        pre = convolve(input_ref[:, cols], input_kernel_ref, input_shift_ref, cols)
        act_ref[:, cols] = pre * jax.nn.sigmoid(pre)
    for start, width in slabs(2 * states):
        cols = pl.ds(start, width)
        pre = convolve(state_ref[:, cols], state_kernel_ref, state_shift_ref, cols)
        both_ref[:, cols] = pre * jax.nn.sigmoid(pre)
    held_ref[...] = jnp.zeros_like(held_ref)

    def chunk(index, unused):
        rows = pl.ds(pl.multiple_of(index * SPAN, SPAN), SPAN)
        raw, steps, cumul, step_wide, grown_wide, tail_wide = chunk_steps(
            step_ref, bias_ref, rate_ref, expand_ref, rows
        )
        cumul_turned = cumul.T
        entry = both_ref[rows, pl.ds(0, states)].astype(jnp.bfloat16)
        readout = both_ref[rows, pl.ds(states, states)].astype(jnp.bfloat16)
        cross = low_against(readout, entry)
        square = (SPAN, SPAN)
        lower = row_index(square) >= lane_index(square)
        for start, width in slabs(channels):
            cols = pl.ds(start, width)
            span = slice(start, start + width)
            heads = width // HD
            values = act_ref[rows, cols]
            scaled = values * step_wide[:, span]
            held = held_ref[:, cols]
            carry_ref[index, :, cols] = held
            weights = []
            for head in range(start // HD, start // HD + heads):
                spread = cumul[:, head : head + 1] - cumul_turned[head : head + 1, :]
                decay = jnp.exp(jnp.where(lower, spread, -jnp.inf))
                weights.append((decay * cross).astype(jnp.bfloat16))
            weights = jnp.concatenate(weights, axis=1) if heads > 1 else weights[0]
            result = low_dot(weights, stacked_heads(scaled, heads))
            result = result + low_dot(readout, held) * grown_wide[:, span]
            held_ref[:, cols] = held * grown_wide[SPAN - 1 : SPAN, span] + low_inner(
                entry, scaled * tail_wide[:, span]
            )
            result = result + skip_ref[:, cols] * values
            out_ref[rows, cols] = result
            gate = gate_ref[rows, cols]
            gated_ref[rows, cols] = (result * (gate * jax.nn.sigmoid(gate))).astype(jnp.bfloat16)
        return unused

    lax.fori_loop(0, input_ref.shape[0] // SPAN, chunk, 0)


def ssd_backward_kernel(
    input_ref,
    state_ref,
    gate_ref,
    step_ref,
    grad_ref,
    carry_ref,
    input_kernel_ref,
    input_shift_ref,
    state_kernel_ref,
    state_shift_ref,
    bias_ref,
    rate_ref,
    skip_ref,
    expand_ref,
    collect_ref,
    grad_input_ref,
    grad_state_ref,
    grad_step_ref,
    grad_input_conv_ref,
    grad_state_conv_ref,
    grad_head_ref,
    act_ref,
    slope_ref,
    both_ref,
    both_slope_ref,
    held_ref,
    wide_ref,
    turned_ref,
    column_ref,
    skip_sum_ref,
    scale_sum_ref,
):
    channels = input_ref.shape[1]
    states = state_ref.shape[1] // 2
    taps = input_kernel_ref.shape[0]
    for start, width in slabs(channels):
        cols = pl.ds(start, width)
        pre = convolve(input_ref[:, cols], input_kernel_ref, input_shift_ref, cols)
        sigma = jax.nn.sigmoid(pre)
        act_ref[:, cols] = pre * sigma
        slope_ref[:, cols] = sigma * (1.0 + pre * (1.0 - sigma))
    for start, width in slabs(2 * states):
        cols = pl.ds(start, width)
        pre = convolve(state_ref[:, cols], state_kernel_ref, state_shift_ref, cols)
        sigma = jax.nn.sigmoid(pre)
        both_ref[:, cols] = pre * sigma
        both_slope_ref[:, cols] = sigma * (1.0 + pre * (1.0 - sigma))
    held_ref[...] = jnp.zeros_like(held_ref)
    turned_ref[...] = jnp.zeros_like(turned_ref)
    column_ref[...] = jnp.zeros_like(column_ref)
    grad_head_ref[...] = jnp.zeros_like(grad_head_ref)
    skip_sum_ref[...] = jnp.zeros_like(skip_sum_ref)
    chunks = input_ref.shape[0] // SPAN

    def chunk(count, unused):
        index = chunks - 1 - count
        rows = pl.ds(pl.multiple_of(index * SPAN, SPAN), SPAN)
        raw, steps, cumul, step_wide, grown_wide, tail_wide = chunk_steps(
            step_ref, bias_ref, rate_ref, expand_ref, rows
        )
        cumul_turned = cumul.T
        entry = both_ref[rows, pl.ds(0, states)].astype(jnp.bfloat16)
        readout = both_ref[rows, pl.ds(states, states)].astype(jnp.bfloat16)
        cross = low_against(entry, readout)
        square = (SPAN, SPAN)
        upper = row_index(square) <= lane_index(square)
        grad_cross = jnp.zeros(square, jnp.float32)
        grad_entry = jnp.zeros((SPAN, states), jnp.float32)
        grad_readout = jnp.zeros((SPAN, states), jnp.float32)
        for start, width in slabs(channels):
            cols = pl.ds(start, width)
            span = slice(start, start + width)
            heads = width // HD
            values = act_ref[rows, cols]
            scaled = values * step_wide[:, span]
            gate = gate_ref[rows, cols]
            upstream = grad_ref[rows, cols] * (gate * jax.nn.sigmoid(gate))
            held = held_ref[:, cols]
            before = carry_ref[index, :, cols]
            stacked_up = stacked_heads(upstream, heads).astype(jnp.bfloat16)
            products = low_against(scaled, stacked_up)
            weights = []
            for place in range(heads):
                head = start // HD + place
                spread = cumul_turned[head : head + 1, :] - cumul[:, head : head + 1]
                decay = jnp.exp(jnp.where(upper, spread, -jnp.inf))
                product = products[:, place * SPAN : (place + 1) * SPAN] * decay
                grad_cross = grad_cross + product
                flow = product * cross
                turned_ref[head : head + 1, :] = jnp.sum(flow, axis=0, keepdims=True)
                column_ref[:, head : head + 1] = jnp.sum(flow, axis=1, keepdims=True)
                weights.append((decay * cross).astype(jnp.bfloat16))
            weights = jnp.concatenate(weights, axis=1) if heads > 1 else weights[0]
            grown_up = upstream * grown_wide[:, span]
            tailed = scaled * tail_wide[:, span]
            from_held = low_dot(entry, held)
            grad_scaled = low_dot(weights, stacked_up) + tail_wide[:, span] * from_held
            wide_ref[0, :, cols] = grown_up * low_dot(readout, before)
            wide_ref[1, :, cols] = tailed * from_held
            wide_ref[2, :, cols] = values * grad_scaled
            grad_readout = grad_readout + low_against(grown_up, before)
            grad_entry = grad_entry + low_against(tailed, held)
            last = grown_wide[SPAN - 1 : SPAN, span]
            scale_sum_ref[:, cols] = jnp.sum(held * before, axis=0, keepdims=True) * last
            skip_sum_ref[:, cols] += jnp.sum(upstream * values, axis=0, keepdims=True)
            held_ref[:, cols] = held * last + low_inner(readout, grown_up)
            act_ref[rows, cols] = step_wide[:, span] * grad_scaled + skip_ref[:, cols] * upstream
        sums = exact_dot(
            jnp.concatenate([wide_ref[0], wide_ref[1], wide_ref[2]], axis=0), collect_ref[...]
        )
        scale_sum = exact_dot(jnp.broadcast_to(scale_sum_ref[...], (8, channels)), collect_ref[...])
        flows = turned_ref[...].T - column_ref[...] + sums[:SPAN]
        onward = (row_index(square) <= lane_index(square)).astype(jnp.float32)
        strict = (row_index(square) > lane_index(square)).astype(jnp.float32)
        grad_log = (
            exact_dot(onward, flows)
            + exact_dot(strict, sums[SPAN : 2 * SPAN])
            + scale_sum[:1]
        )
        grad_steps = grad_log * rate_ref[...] + sums[2 * SPAN :]
        grad_raw = grad_steps * jax.nn.sigmoid(raw)
        grad_step_ref[rows, :] = grad_raw.astype(jnp.bfloat16)
        grad_head_ref[0, 0:1, :] += jnp.sum(grad_raw, axis=0, keepdims=True)
        grad_head_ref[0, 1:2, :] += (
            jnp.sum(grad_log * steps, axis=0, keepdims=True) * rate_ref[...]
        )
        both_ref[rows, pl.ds(0, states)] = grad_entry + low_dot(grad_cross, readout)
        both_ref[rows, pl.ds(states, states)] = grad_readout + low_inner(grad_cross, entry)
        return unused

    lax.fori_loop(0, chunks, chunk, 0)
    grad_head_ref[0, 2:3, :] = exact_dot(
        jnp.broadcast_to(skip_sum_ref[...], (8, channels)), collect_ref[...]
    )[:1]

    def convolve_back(raw_ref, grads_ref, slopes_ref, kernel_ref, out_ref, sums_ref, width_all):
        for start, width in slabs(width_all):
            cols = pl.ds(start, width)
            grad = grads_ref[:, cols] * slopes_ref[:, cols]
            raw = raw_ref[:, cols]
            total = kernel_ref[taps - 1 : taps, cols] * grad
            sums_ref[0, taps - 1 : taps, cols] = jnp.sum(grad * raw, axis=0, keepdims=True)
            for tap in range(taps - 1):
                shifted = sooner(grad, taps - 1 - tap)
                total = total + kernel_ref[tap : tap + 1, cols] * shifted
                sums_ref[0, tap : tap + 1, cols] = jnp.sum(shifted * raw, axis=0, keepdims=True)
            sums_ref[0, taps : taps + 1, cols] = jnp.sum(grad, axis=0, keepdims=True)
            out_ref[:, cols] = total.astype(jnp.bfloat16)

    convolve_back(
        input_ref,
        act_ref,
        slope_ref,
        input_kernel_ref,
        grad_input_ref,
        grad_input_conv_ref,
        channels,
    )
    convolve_back(
        state_ref,
        both_ref,
        both_slope_ref,
        state_kernel_ref,
        grad_state_ref,
        grad_state_conv_ref,
        2 * states,
    )


def by_sequence(length, width):
    return pl.BlockSpec((length, width), lambda seq: (seq, 0))


def fixed(*shape):
    return pl.BlockSpec(shape, lambda seq: (0,) * len(shape))


def head_spread(heads):
    marks = np.zeros((LANES, heads * HD), np.float32)
    for head in range(heads):
        marks[head, head * HD : (head + 1) * HD] = 1.0
    return marks


def pad_lanes(part):
    return jnp.pad(part, ((0, 0), (0, LANES - part.shape[1])))


def ssd_small(input_kernel, input_shift, state_kernel, state_shift, step_bias, decay_log, skip_gain):
    rates = -jnp.exp(decay_log)
    return (
        input_kernel,
        input_shift[None, :],
        state_kernel,
        state_shift[None, :],
        pad_lanes(step_bias[None, :]),
        pad_lanes(rates[None, :]),
        jnp.repeat(skip_gain, HD)[None, :],
    )


def ssd_forward(inputs, states_raw, gate, step, small, heads, length):
    group, channels = inputs.shape
    seqs = group // length
    both = states_raw.shape[1]
    states = both // 2
    chunks = length // SPAN
    taps = small[0].shape[0]
    return pl.pallas_call(
        ssd_forward_kernel,
        grid=(seqs,),
        in_specs=[
            by_sequence(length, channels),
            by_sequence(length, both),
            by_sequence(length, channels),
            by_sequence(length, LANES),
            fixed(taps, channels),
            fixed(1, channels),
            fixed(taps, both),
            fixed(1, both),
            fixed(1, LANES),
            fixed(1, LANES),
            fixed(1, channels),
            fixed(LANES, channels),
        ],
        out_specs=[
            by_sequence(length, channels),
            by_sequence(length, channels),
            pl.BlockSpec((chunks, states, channels), lambda seq: (seq, 0, 0)),
        ],
        out_shape=[
            jax.ShapeDtypeStruct((group, channels), jnp.bfloat16),
            jax.ShapeDtypeStruct((group, channels), jnp.float32),
            jax.ShapeDtypeStruct((seqs * chunks, states, channels), jnp.float32),
        ],
        scratch_shapes=[
            pltpu.VMEM((length, channels), jnp.float32),
            pltpu.VMEM((length, both), jnp.float32),
            pltpu.VMEM((states, channels), jnp.float32),
        ],
        compiler_params=pltpu.CompilerParams(vmem_limit_bytes=VMEM_LIMIT),
        cost_estimate=pl.CostEstimate(
            flops=8 * group * channels * SPAN,
            bytes_accessed=20 * group * channels,
            transcendentals=group * heads * SPAN,
        ),
        name="ssd_forward",
    )(inputs, states_raw, gate, step, *small, jnp.asarray(head_spread(heads)))


def ssd_backward(inputs, states_raw, gate, step, grad, carry, small, heads, length):
    group, channels = inputs.shape
    seqs = group // length
    both = states_raw.shape[1]
    states = both // 2
    chunks = length // SPAN
    taps = small[0].shape[0]
    return pl.pallas_call(
        ssd_backward_kernel,
        grid=(seqs,),
        in_specs=[
            by_sequence(length, channels),
            by_sequence(length, both),
            by_sequence(length, channels),
            by_sequence(length, LANES),
            by_sequence(length, channels),
            pl.BlockSpec((chunks, states, channels), lambda seq: (seq, 0, 0)),
            fixed(taps, channels),
            fixed(1, channels),
            fixed(taps, both),
            fixed(1, both),
            fixed(1, LANES),
            fixed(1, LANES),
            fixed(1, channels),
            fixed(LANES, channels),
            fixed(channels, LANES),
        ],
        out_specs=[
            by_sequence(length, channels),
            by_sequence(length, both),
            by_sequence(length, LANES),
            pl.BlockSpec((1, 8, channels), lambda seq: (seq, 0, 0)),
            pl.BlockSpec((1, 8, both), lambda seq: (seq, 0, 0)),
            pl.BlockSpec((1, 8, LANES), lambda seq: (seq, 0, 0)),
        ],
        out_shape=[
            jax.ShapeDtypeStruct((group, channels), jnp.bfloat16),
            jax.ShapeDtypeStruct((group, both), jnp.bfloat16),
            jax.ShapeDtypeStruct((group, LANES), jnp.bfloat16),
            jax.ShapeDtypeStruct((seqs, 8, channels), jnp.float32),
            jax.ShapeDtypeStruct((seqs, 8, both), jnp.float32),
            jax.ShapeDtypeStruct((seqs, 8, LANES), jnp.float32),
        ],
        scratch_shapes=[
            pltpu.VMEM((length, channels), jnp.float32),
            pltpu.VMEM((length, channels), jnp.float32),
            pltpu.VMEM((length, both), jnp.float32),
            pltpu.VMEM((length, both), jnp.float32),
            pltpu.VMEM((states, channels), jnp.float32),
            pltpu.VMEM((3, SPAN, channels), jnp.float32),
            pltpu.VMEM((LANES, SPAN), jnp.float32),
            pltpu.VMEM((SPAN, LANES), jnp.float32),
            pltpu.VMEM((1, channels), jnp.float32),
            pltpu.VMEM((1, channels), jnp.float32),
        ],
        compiler_params=pltpu.CompilerParams(vmem_limit_bytes=VMEM_LIMIT),
        cost_estimate=pl.CostEstimate(
            flops=20 * group * channels * SPAN,
            bytes_accessed=20 * group * channels,
            transcendentals=group * heads * SPAN,
        ),
        name="ssd_backward",
    )(
        inputs,
        states_raw,
        gate,
        step,
        grad,
        carry,
        *small,
        jnp.asarray(head_spread(heads)),
        jnp.asarray(head_spread(heads).T.copy()),
    )


def rope_wide(length):
    half = HD // 2
    freqs = np.float32(ROPE_BASE) ** (-np.arange(half, dtype=np.float32) * np.float32(2.0 / HD))
    angles = np.arange(length, dtype=np.float32)[:, None] * freqs[None, :].astype(np.float32)
    cosine, sine = np.cos(angles), np.sin(angles)
    count = LANES // HD
    return (
        np.concatenate([cosine, cosine] * count, axis=1).astype(np.float32),
        np.concatenate([-sine, sine] * count, axis=1).astype(np.float32),
    )


def turn(part, cosine, sine):
    half = HD // 2
    first = lane_index(part.shape) % HD < half
    swapped = jnp.where(first, pltpu.roll(part, LANES - half, 1), pltpu.roll(part, half, 1))
    return part * cosine + swapped * sine


def attend_forward_kernel(
    query_ref, pair_ref, cosine_ref, sine_ref, context_ref, query_out_ref, pair_out_ref, total_ref
):
    length = query_ref.shape[0]
    cosine, sine = cosine_ref[...], sine_ref[...]
    pair = pair_ref[...]
    left = lane_index(pair.shape) < HD
    pair = jnp.where(left, turn(pair, cosine, sine), pair)
    pair_out_ref[...] = pair.astype(jnp.bfloat16)
    moved = pltpu.roll(pair, HD, 1)
    keys = jnp.where(left, pair, moved).astype(jnp.bfloat16)
    values = jnp.where(left, moved, pair).astype(jnp.bfloat16)
    scale = HD ** (-0.5)
    for slab in range(query_ref.shape[1] // LANES):
        cols = pl.ds(slab * LANES, LANES)
        query_out_ref[:, cols] = turn(query_ref[:, cols], cosine, sine).astype(jnp.bfloat16)
        for tile in range(length // SPAN):
            rows = slice(tile * SPAN, (tile + 1) * SPAN)
            count = (tile + 1) * SPAN
            query = query_out_ref[rows, cols]
            lane = lane_index(query.shape)
            square = (SPAN, count)
            causal = row_index(square) + tile * SPAN >= lane_index(square)
            results = []
            for place in range(LANES // HD):
                mine = (lane >= place * HD) & (lane < place * HD + HD)
                scores = low_against(jnp.where(mine, query, 0), keys[:count]) * scale
                scores = jnp.where(causal, scores, -jnp.inf)
                peak = jnp.max(scores, axis=-1, keepdims=True)
                grown = jnp.exp(scores - peak)
                total = jnp.sum(grown, axis=-1, keepdims=True)
                probs = grown * (1.0 / total)
                results.append(low_dot(probs, values[:count]))
                head = slab * (LANES // HD) + place
                total_ref[rows, head : head + 1] = jnp.log(total) + peak
            context_ref[rows, cols] = jnp.where(lane < HD, results[0], results[1]).astype(
                jnp.bfloat16
            )


def attend_backward_kernel(
    query_ref,
    pair_ref,
    total_ref,
    grad_ref,
    cosine_ref,
    sine_ref,
    grad_query_ref,
    grad_pair_ref,
    key_sum_ref,
    value_sum_ref,
):
    length = query_ref.shape[0]
    cosine, sine = cosine_ref[...], -sine_ref[...]
    pair = pair_ref[...].astype(jnp.float32)
    left = lane_index(pair.shape) < HD
    moved = pltpu.roll(pair, HD, 1)
    keys = jnp.where(left, pair, moved).astype(jnp.bfloat16)
    values = jnp.where(left, moved, pair).astype(jnp.bfloat16)
    scale = HD ** (-0.5)
    key_sum_ref[...] = jnp.zeros_like(key_sum_ref)
    value_sum_ref[...] = jnp.zeros_like(value_sum_ref)
    for slab in range(query_ref.shape[1] // LANES):
        cols = pl.ds(slab * LANES, LANES)
        for tile in range(length // SPAN):
            rows = slice(tile * SPAN, (tile + 1) * SPAN)
            count = (tile + 1) * SPAN
            query = query_ref[rows, cols]
            upstream = grad_ref[rows, cols]
            lane = lane_index(query.shape)
            square = (SPAN, count)
            causal = row_index(square) + tile * SPAN >= lane_index(square)
            results = []
            for place in range(LANES // HD):
                mine = (lane >= place * HD) & (lane < place * HD + HD)
                head = slab * (LANES // HD) + place
                own_query = jnp.where(mine, query, 0)
                own_up = jnp.where(mine, upstream, 0)
                scores = low_against(own_query, keys[:count]) * scale
                scores = jnp.where(causal, scores, -jnp.inf)
                probs = jnp.exp(scores - total_ref[rows, head : head + 1])
                grad_probs = low_against(own_up, values[:count])
                mean = jnp.sum(probs * grad_probs, axis=-1, keepdims=True)
                grad_scores = (probs * (grad_probs - mean)).astype(jnp.bfloat16)
                results.append(low_dot(grad_scores, keys[:count]))
                key_sum_ref[0:count, :] += low_inner(grad_scores, own_query)
                value_sum_ref[0:count, :] += low_inner(probs, own_up)
            grad_query = jnp.where(lane < HD, results[0], results[1]) * scale
            grad_query_ref[rows, cols] = turn(
                grad_query, cosine[rows, :], sine[rows, :]
            ).astype(jnp.bfloat16)
    grad_key = key_sum_ref[...]
    grad_key = turn((grad_key + pltpu.roll(grad_key, HD, 1)) * scale, cosine, sine)
    grad_value = value_sum_ref[...]
    grad_value = grad_value + pltpu.roll(grad_value, HD, 1)
    grad_pair_ref[...] = jnp.where(left, grad_key, grad_value).astype(jnp.bfloat16)


def attend_forward(query, pair, length):
    group, width = query.shape
    heads = width // HD
    cosine, sine = rope_wide(length)
    return pl.pallas_call(
        attend_forward_kernel,
        grid=(group // length,),
        in_specs=[
            by_sequence(length, width),
            by_sequence(length, LANES),
            fixed(length, LANES),
            fixed(length, LANES),
        ],
        out_specs=[
            by_sequence(length, width),
            by_sequence(length, width),
            by_sequence(length, LANES),
            by_sequence(length, LANES),
        ],
        out_shape=[
            jax.ShapeDtypeStruct((group, width), jnp.bfloat16),
            jax.ShapeDtypeStruct((group, width), jnp.bfloat16),
            jax.ShapeDtypeStruct((group, LANES), jnp.bfloat16),
            jax.ShapeDtypeStruct((group, LANES), jnp.float32),
        ],
        compiler_params=pltpu.CompilerParams(vmem_limit_bytes=VMEM_LIMIT),
        cost_estimate=pl.CostEstimate(
            flops=4 * group * width * length,
            bytes_accessed=12 * group * width,
            transcendentals=group * heads * length // 2,
        ),
        name="attend_forward",
    )(query, pair, jnp.asarray(cosine), jnp.asarray(sine))


def attend_backward(query, pair, total, grad, length):
    group, width = query.shape
    heads = width // HD
    cosine, sine = rope_wide(length)
    return pl.pallas_call(
        attend_backward_kernel,
        grid=(group // length,),
        in_specs=[
            by_sequence(length, width),
            by_sequence(length, LANES),
            by_sequence(length, LANES),
            by_sequence(length, width),
            fixed(length, LANES),
            fixed(length, LANES),
        ],
        out_specs=[by_sequence(length, width), by_sequence(length, LANES)],
        out_shape=[
            jax.ShapeDtypeStruct((group, width), jnp.bfloat16),
            jax.ShapeDtypeStruct((group, LANES), jnp.bfloat16),
        ],
        scratch_shapes=[
            pltpu.VMEM((length, LANES), jnp.float32),
            pltpu.VMEM((length, LANES), jnp.float32),
        ],
        compiler_params=pltpu.CompilerParams(vmem_limit_bytes=VMEM_LIMIT),
        cost_estimate=pl.CostEstimate(
            flops=10 * group * width * length,
            bytes_accessed=12 * group * width,
            transcendentals=group * heads * length // 2,
        ),
        name="attend_backward",
    )(query, pair, total, grad, jnp.asarray(cosine), jnp.asarray(sine))


def step_groups(size):
    bits = size.bit_length() - 1
    return [1] * min(bits, 2) + [2] * (max(bits - 2, 0) // 2) + [1] * (max(bits - 2, 0) % 2)


def after(part, *deps):
    return lax.optimization_barrier((part,) + deps)[0]


def behind(part, dep):
    zero = jnp.minimum(jnp.abs(dep[:1, :1].astype(jnp.float32)), 0.0)
    return part + zero.astype(part.dtype)


class Sum:
    def __init__(self, part, size, place):
        self.size = size
        self.place = place
        self.direct = bool(size & (size - 1) or part.shape[0] % size)
        self.steps = [] if self.direct else step_groups(size)
        self.shift = 0
        self.part = part
        self.gives = [part]
        if not self.direct:
            self.part = part.reshape(size, part.shape[0] // size, part.shape[1])
            self.prepare()

    def prepare(self):
        if not self.steps:
            self.gives = [self.part]
            return
        ways = 1 << self.steps[0]
        rest = self.part.shape[0] // ways
        view = self.part.reshape((rest, ways) + self.part.shape[1:])
        mine = (lax.axis_index("dp") >> self.shift) & (ways - 1)
        self.keep = lax.dynamic_index_in_dim(view, mine, 1, False)
        self.gives = [
            lax.dynamic_index_in_dim(view, mine ^ way, 1, False) for way in range(1, ways)
        ]

    def advance(self):
        if self.steps:
            total = self.keep.astype(jnp.float32)
            for way, give in enumerate(self.gives, 1):
                pairs = [(index, index ^ (way << self.shift)) for index in range(self.size)]
                total = total + lax.ppermute(give, "dp", pairs).astype(jnp.float32)
            self.part = total.astype(jnp.bfloat16)
            self.shift += self.steps.pop(0)
            self.prepare()
        return self.gives

    def finish(self, middle=None):
        while self.steps:
            self.advance()
        if self.direct:
            part = lax.psum(self.part, "dp")
            return part if middle is None else middle(part)
        part = self.part[0]
        if middle is not None:
            part = middle(part)
        lead = (1,) * (self.place + 1)
        whole = lax.all_gather(part.reshape(lead + part.shape), "dp", axis=self.place, tiled=True)
        return whole.reshape(self.size * part.shape[0], part.shape[1])


def other(part):
    return lax.ppermute(part, "tensor", [(0, 1), (1, 0)])


def all_rows(part, shards):
    if shards != 2:
        return lax.all_gather(part, "tensor", axis=0, tiled=True)
    got = other(part)
    return jnp.where(
        lax.axis_index("tensor") == 0,
        jnp.concatenate([part, got], axis=0),
        jnp.concatenate([got, part], axis=0),
    )


def sum_all(part, shards):
    if shards != 2:
        return lax.psum(part, "tensor").astype(jnp.float32)
    return part.astype(jnp.float32) + other(part).astype(jnp.float32)


def sum_own(part, shards):
    if shards != 2:
        return lax.psum_scatter(part, "tensor", scatter_dimension=0, tiled=True).astype(jnp.float32)
    me = lax.axis_index("tensor")
    halves = part.reshape(2, part.shape[0] // 2, part.shape[1])
    keep = lax.dynamic_index_in_dim(halves, me, 0, False)
    got = other(lax.dynamic_index_in_dim(halves, 1 - me, 0, False))
    return keep.astype(jnp.float32) + got.astype(jnp.float32)


def own_rows(part, rows):
    return lax.dynamic_slice_in_dim(part, lax.axis_index("tensor") * rows, rows, 0)


def column_pack(vectors, rows):
    flat = jnp.concatenate([item.reshape(-1) for item in vectors])
    width = -(-flat.shape[0] // rows)
    return jnp.pad(flat, (0, width * rows - flat.shape[0])).reshape(width, rows).T


def column_unpack(packed, shapes):
    flat = packed.T.reshape(-1)
    out, start = [], 0
    for shape in shapes:
        count = 1
        for size in shape:
            count *= size
        out.append(flat[start : start + count].reshape(shape))
        start += count
    return out


def body(
    dp_size,
    shards,
    layer_input,
    input_gain,
    middle_gain,
    mamba_gate,
    mamba_input,
    step_weight,
    state_weight,
    input_kernel,
    input_shift,
    state_kernel,
    state_shift,
    step_bias,
    decay_log,
    skip_gain,
    mamba_output,
    query_weight,
    keyvalue_weight,
    context_weight,
    gate_weight,
    up_weight,
    down_weight,
    cotangent,
):
    own = layer_input.shape[0]
    rows_low = all_rows(layer_input, shards)
    cotan_low = all_rows(cotangent, shards)
    rows = rows_low.astype(jnp.float32)
    gain_first = input_gain.astype(jnp.float32)
    gain_second = middle_gain.astype(jnp.float32)
    factor_first = lax.rsqrt(jnp.mean(rows * rows, axis=-1, keepdims=True) + EPSILON)
    normal_first = rows * factor_first
    whole = (normal_first * gain_first).astype(jnp.bfloat16)
    group = whole.shape[0]
    length = min(SEQ_LEN, group)
    seqs = group // length
    heads_here = query_weight.shape[1] // HD
    kv_head = lax.axis_index("tensor") * heads_here // (HQ // KVH)
    key_cols = lax.dynamic_slice_in_dim(keyvalue_weight, kv_head * HD, HD, 1)
    value_cols = lax.dynamic_slice_in_dim(keyvalue_weight, (KVH + kv_head) * HD, HD, 1)
    pair_weight = jnp.concatenate([key_cols, value_cols], axis=1)
    query_cols = query_weight.shape[1]
    query_pad = -query_cols % LANES
    query_wide = jnp.pad(query_weight, ((0, 0), (0, query_pad)))
    step_wide = pad_lanes(step_weight)
    heads = step_weight.shape[1]
    input_raw = forward_dot(whole, mamba_input)
    state_raw = forward_dot(whole, state_weight)
    step_raw = forward_dot(whole, step_wide)
    gate_raw = forward_dot(whole, mamba_gate)
    query_raw = forward_dot(whole, query_wide)
    pair_raw = forward_dot(whole, pair_weight)
    small = ssd_small(
        input_kernel.astype(jnp.float32),
        input_shift.astype(jnp.float32),
        state_kernel.astype(jnp.float32),
        state_shift.astype(jnp.float32),
        step_bias.astype(jnp.float32),
        decay_log.astype(jnp.float32),
        skip_gain.astype(jnp.float32),
    )
    gated_low, ssm_out, carries = ssd_forward(
        input_raw, state_raw, gate_raw, step_raw, small, heads, length
    )
    context_wide, queries, pairs, totals = attend_forward(
        after(query_raw, cotan_low), pair_raw, length
    )
    context_rows = context_wide[:, :query_cols]
    mixed_part = forward_dot(gated_low, mamba_output) + forward_dot(context_rows, context_weight)
    resid = rows + sum_all(mixed_part.astype(jnp.bfloat16), shards)
    factor_second = lax.rsqrt(jnp.mean(resid * resid, axis=-1, keepdims=True) + EPSILON)
    normal_second = resid * factor_second
    whole_mid = (normal_second * gain_second).astype(jnp.bfloat16)
    gate = forward_dot(whole_mid, gate_weight)
    upper = forward_dot(whole_mid, up_weight)
    sigmoid_gate = jax.nn.sigmoid(gate)
    silu_gate = gate * sigmoid_gate
    hidden = (silu_gate * upper).astype(jnp.bfloat16)
    grad_hidden = against(cotan_low, down_weight)
    slope = sigmoid_gate * (1.0 + gate * (1.0 - sigmoid_gate))
    grad_gate_low = (grad_hidden * upper * slope).astype(jnp.bfloat16)
    grad_upper_low = (grad_hidden * silu_gate).astype(jnp.bfloat16)
    back_part = (against(grad_gate_low, gate_weight) + against(grad_upper_low, up_weight)).astype(
        jnp.bfloat16
    )
    back_mid = sum_all(back_part, shards)
    hidden_late = after(hidden, back_part)
    mid_late = after(whole_mid, back_part)
    down_sum = Sum(inner_rows(hidden_late, cotan_low).astype(jnp.bfloat16), dp_size, 0)
    hidden_cols = gate_weight.shape[1]
    wide_sum = Sum(
        inner_rows(mid_late, jnp.concatenate([grad_gate_low, grad_upper_low], axis=1)).astype(
            jnp.bfloat16
        ),
        dp_size,
        0,
    )
    down_sum.advance()
    wide_sum.advance()
    back_mid = after(back_mid, *down_sum.gives, *wide_sum.gives)
    feed_part = behind(forward_dot(hidden_late, down_weight), back_mid).astype(jnp.bfloat16)
    feed = sum_own(feed_part, shards)
    layer_output = (own_rows(resid, own) + feed).astype(jnp.bfloat16)
    grad_middle = jnp.sum(back_part.astype(jnp.float32) * normal_second, axis=0)
    grad_resid = cotan_low.astype(jnp.float32) + norm_back(
        back_mid, gain_second, normal_second, factor_second
    )
    mixer_all = grad_resid.astype(jnp.bfloat16)
    mixer_sum = Sum(
        inner_rows(jnp.concatenate([gated_low, context_rows], axis=1), mixer_all).astype(
            jnp.bfloat16
        ),
        dp_size,
        1,
    )
    ssm_rows = gated_low.shape[1]
    grad_gated = against(mixer_all, mamba_output)
    sigmoid_raw = jax.nn.sigmoid(gate_raw)
    grad_gate_raw = (
        grad_gated * ssm_out * (sigmoid_raw * (1.0 + gate_raw * (1.0 - sigmoid_raw)))
    ).astype(jnp.bfloat16)
    grad_context = against(mixer_all, context_weight).astype(jnp.bfloat16)
    grad_query_raw, grad_pair_raw = attend_backward(
        queries,
        pairs,
        totals,
        after(jnp.pad(grad_context, ((0, 0), (0, query_pad))), *mixer_sum.gives, *down_sum.advance()),
        length,
    )
    grad_query_raw = grad_query_raw[:, :query_cols]
    early_cols = jnp.concatenate([grad_gate_raw, grad_query_raw], axis=1)
    early_sum = Sum(inner_rows(whole, early_cols).astype(jnp.bfloat16), dp_size, 2)
    grad_gated = after(
        grad_gated, *early_sum.gives, *mixer_sum.advance(), *wide_sum.advance()
    )
    grad_input_raw, grad_state_raw, grad_step_raw, input_sums, state_sums, head_sums = ssd_backward(
        input_raw, state_raw, gate_raw, step_raw, grad_gated, carries, small, heads, length
    )
    input_sums = jnp.sum(input_sums, axis=0)
    state_sums = jnp.sum(state_sums, axis=0)
    head_sums = jnp.sum(head_sums, axis=0)[:, :heads]
    taps = input_kernel.shape[0]
    early_sum.advance()
    mixer_sum.advance()
    down_sum.advance()
    wide_sum.advance()
    grad_input_raw = after(
        grad_input_raw, *early_sum.gives, *mixer_sum.gives, *down_sum.gives, *wide_sum.gives
    )
    grad_down = down_sum.finish()
    grad_wide = wide_sum.finish()
    grad_gate, grad_up = grad_wide[:, :hidden_cols], grad_wide[:, hidden_cols:]
    late_cols = jnp.concatenate(
        [grad_input_raw, grad_state_raw, grad_pair_raw, grad_step_raw], axis=1
    )
    total = against(early_cols, jnp.concatenate([mamba_gate, query_weight], axis=1))
    total = total + against(
        late_cols, jnp.concatenate([mamba_input, state_weight, pair_weight, step_wide], axis=1)
    )
    total_low = total.astype(jnp.bfloat16)
    grad_first = jnp.sum(total_low.astype(jnp.float32) * normal_first, axis=0)
    width = whole.shape[1]
    gate_cols = grad_gate_raw.shape[1]
    input_cols = grad_input_raw.shape[1]
    state_cols = grad_state_raw.shape[1]
    step_cols = heads
    pair_cols = grad_pair_raw.shape[1]

    own_vectors = (input_sums[:taps], input_sums[taps], head_sums[0], head_sums[1], head_sums[2])
    shared_vectors = (grad_first, grad_middle, state_sums[:taps], state_sums[taps])
    own_pack = column_pack(own_vectors, width)
    shared_pack = column_pack(shared_vectors, width)
    shared_lane = step_cols + own_pack.shape[1]
    last_lane = shared_lane + shared_pack.shape[1]
    packs = jnp.pad(
        jnp.concatenate([own_pack, shared_pack], axis=1),
        ((0, 0), (step_cols, LANES - last_lane)),
    )
    split_pairs = shards == KVH
    late = inner_rows(whole, late_cols)
    marks = (input_cols, input_cols + state_cols, input_cols + state_cols + pair_cols)
    late_pair = late[:, marks[1] : marks[2]]
    if not split_pairs:
        spread = jnp.zeros((width, 2 * KVH * HD), jnp.float32)
        spread = lax.dynamic_update_slice_in_dim(spread, late_pair[:, :HD], kv_head * HD, 1)
        late_pair = lax.dynamic_update_slice_in_dim(
            spread, late_pair[:, HD:], (KVH + kv_head) * HD, 1
        )
        late = jnp.concatenate([late[:, : marks[1]], late_pair, late[:, marks[2] :]], axis=1)
    misc = late.shape[1] - LANES
    late = (late + jnp.pad(packs, ((0, 0), (misc, 0)))).astype(jnp.bfloat16)
    late_sum = Sum(late, dp_size, 3)

    def over_tensor(part):
        own_part = part[:, input_cols:]
        if split_pairs:
            got = other(own_part)
            both = (own_part.astype(jnp.float32) + got.astype(jnp.float32)).astype(jnp.bfloat16)
            first = lax.axis_index("tensor") == 0
            pair_span = slice(state_cols, state_cols + pair_cols)
            low = jnp.where(first, own_part[:, pair_span], got[:, pair_span])
            high = jnp.where(first, got[:, pair_span], own_part[:, pair_span])
            pair = [low[:, :HD], high[:, :HD], low[:, HD:], high[:, HD:]]
        else:
            both = lax.psum(own_part, "tensor")
            pair = [both[:, state_cols:-LANES]]
        lane = lane_index((part.shape[0], LANES))
        extra = jnp.where(
            (lane >= shared_lane) & (lane < last_lane), both[:, -LANES:], own_part[:, -LANES:]
        )
        return jnp.concatenate(
            [part[:, :input_cols], both[:, :state_cols]] + pair + [extra], axis=1
        )

    grad_mixer_out = mixer_sum.finish()
    grad_mamba_out = grad_mixer_out[:ssm_rows]
    grad_context_w = grad_mixer_out[ssm_rows:]
    early = early_sum.finish()
    tail = late_sum.finish(over_tensor)
    grad_mamba_input = tail[:, :input_cols]
    tail = tail[:, input_cols:]
    back_in = sum_own(total_low, shards)
    normal_own = own_rows(normal_first, own)
    factor_own = own_rows(factor_first, own)
    input_grad = own_rows(grad_resid, own) + norm_back(back_in, gain_first, normal_own, factor_own)
    extra = tail[:, state_cols + keyvalue_weight.shape[1] :]
    grad_step = extra[:, :step_cols]
    grad_in_kernel, grad_in_shift, grad_bias, grad_decay, grad_skip = column_unpack(
        extra[:, step_cols:shared_lane], [item.shape for item in own_vectors]
    )
    grad_first, grad_middle, grad_st_kernel, grad_st_shift = column_unpack(
        extra[:, shared_lane:last_lane], [item.shape for item in shared_vectors]
    )
    results = (
        grad_first,
        grad_middle,
        early[:, :gate_cols],
        grad_mamba_input,
        grad_step,
        tail[:, :state_cols],
        grad_in_kernel,
        grad_in_shift,
        grad_st_kernel,
        grad_st_shift,
        grad_bias,
        grad_decay,
        grad_skip,
        grad_mamba_out,
        early[:, gate_cols:],
        tail[:, state_cols : state_cols + keyvalue_weight.shape[1]],
        grad_context_w,
        grad_gate,
        grad_up,
        grad_down,
    )
    return (layer_output, input_grad) + tuple(item.astype(jnp.float32) for item in results)


def solution(mesh):
    in_specs = (
        P(("dp", "tensor"), None),
        P(),
        P(),
        P(None, "tensor"),
        P(None, "tensor"),
        P(None, "tensor"),
        P(),
        P(None, "tensor"),
        P("tensor"),
        P(),
        P(),
        P("tensor"),
        P("tensor"),
        P("tensor"),
        P("tensor", None),
        P(None, "tensor"),
        P(),
        P("tensor", None),
        P(None, "tensor"),
        P(None, "tensor"),
        P("tensor", None),
        P(("dp", "tensor"), None),
    )
    out_specs = (
        P(("dp", "tensor"), None),
        P(("dp", "tensor"), None),
        P(),
        P(),
        P(None, "tensor"),
        P(None, "tensor"),
        P(None, "tensor"),
        P(),
        P(None, "tensor"),
        P("tensor"),
        P(),
        P(),
        P("tensor"),
        P("tensor"),
        P("tensor"),
        P("tensor", None),
        P(None, "tensor"),
        P(),
        P("tensor", None),
        P(None, "tensor"),
        P(None, "tensor"),
        P("tensor", None),
    )
    run = partial(body, mesh.shape["dp"], mesh.shape["tensor"])
    return jax.shard_map(run, mesh=mesh, in_specs=in_specs, out_specs=out_specs, check_vma=False)
```

```python
from functools import partial

import jax
import jax.numpy as jnp
import numpy as np
from jax import lax
from jax.experimental import pallas as pl
from jax.experimental.pallas import tpu as pltpu
from jax.sharding import PartitionSpec as P

HD = 64
HQ = 8
KVH = 2
SPAN = 128
SEQ_LEN = 1024


EPSILON = 1e-05
ROPE_BASE = 10000.0
PRECISE = lax.Precision.HIGHEST


def forward_dot(left, right):
    return jnp.dot(left, right, preferred_element_type=jnp.float32)


def inner_rows(left, right):
    return lax.dot_general(
        left, right, (((0,), (0,)), ((), ())), preferred_element_type=jnp.float32
    )


def against(left, right):
    return lax.dot_general(
        left, right, (((1,), (1,)), ((), ())), preferred_element_type=jnp.float32
    )


def norm_back(upstream, gain, normal, factor):
    scaled = upstream * gain
    return factor * (scaled - normal * jnp.mean(scaled * normal, axis=-1, keepdims=True))


LANES = 128
VMEM_LIMIT = 44 * 1024 * 1024
LIGHT = pl.CostEstimate(flops=1024, bytes_accessed=1024, transcendentals=0)


def exact_dot(left, right):
    return jnp.dot(left, right, precision=PRECISE, preferred_element_type=jnp.float32)


def low_dot(left, right):
    return jnp.dot(
        left.astype(jnp.bfloat16), right.astype(jnp.bfloat16), preferred_element_type=jnp.float32
    )


def low_against(left, right):
    return lax.dot_general(
        left.astype(jnp.bfloat16),
        right.astype(jnp.bfloat16),
        (((1,), (1,)), ((), ())),
        preferred_element_type=jnp.float32,
    )


def low_inner(left, right):
    return lax.dot_general(
        left.astype(jnp.bfloat16),
        right.astype(jnp.bfloat16),
        (((0,), (0,)), ((), ())),
        preferred_element_type=jnp.float32,
    )


def row_index(shape):
    return lax.broadcasted_iota(jnp.int32, shape, 0)


def lane_index(shape):
    return lax.broadcasted_iota(jnp.int32, shape, 1)


def later(part, count):
    if count == 0:
        return part
    return jnp.where(row_index(part.shape) >= count, pltpu.roll(part, count, 0), 0.0)


def sooner(part, count):
    if count == 0:
        return part
    rows = part.shape[0]
    return jnp.where(row_index(part.shape) < rows - count, pltpu.roll(part, rows - count, 0), 0.0)


def slabs(width):
    return [(start, min(LANES, width - start)) for start in range(0, width, LANES)]


def soft_plus(value):
    return jnp.maximum(value, 0.0) + jnp.log1p(jnp.exp(-jnp.abs(value)))


def stacked_heads(part, heads):
    if heads == 1:
        return part
    lane = lane_index(part.shape)
    return jnp.concatenate(
        [jnp.where((lane >= head * HD) & (lane < head * HD + HD), part, 0.0) for head in range(heads)],
        axis=0,
    )


def convolve(raw, kernel_ref, shift_ref, cols):
    taps = kernel_ref.shape[0]
    out = shift_ref[:, cols] + kernel_ref[taps - 1 : taps, cols] * raw
    for tap in range(taps - 1):
        out = out + kernel_ref[tap : tap + 1, cols] * later(raw, taps - 1 - tap)
    return out


def chunk_steps(step_ref, bias_ref, rate_ref, expand_ref, rows):
    raw = step_ref[rows, :] + bias_ref[...]
    steps = soft_plus(raw)
    logdec = steps * rate_ref[...]
    square = (SPAN, SPAN)
    lower = (row_index(square) >= lane_index(square)).astype(jnp.float32)
    cumul = exact_dot(lower, logdec)
    grown = jnp.exp(cumul)
    tail = jnp.exp(cumul[SPAN - 1 : SPAN, :] - cumul)
    wide = exact_dot(jnp.concatenate([steps, grown, tail], axis=0), expand_ref[...])
    return raw, steps, cumul, wide[:SPAN], wide[SPAN : 2 * SPAN], wide[2 * SPAN :]


def ssd_forward_kernel(
    input_ref,
    state_ref,
    gate_ref,
    step_ref,
    input_kernel_ref,
    input_shift_ref,
    state_kernel_ref,
    state_shift_ref,
    bias_ref,
    rate_ref,
    skip_ref,
    expand_ref,
    gated_ref,
    out_ref,
    carry_ref,
    act_ref,
    both_ref,
    held_ref,
):
    channels = input_ref.shape[1]
    states = state_ref.shape[1] // 2
    for start, width in slabs(channels):
        cols = pl.ds(start, width)
        pre = convolve(input_ref[:, cols], input_kernel_ref, input_shift_ref, cols)
        act_ref[:, cols] = pre * jax.nn.sigmoid(pre)
    for start, width in slabs(2 * states):
        cols = pl.ds(start, width)
        pre = convolve(state_ref[:, cols], state_kernel_ref, state_shift_ref, cols)
        both_ref[:, cols] = pre * jax.nn.sigmoid(pre)
    held_ref[...] = jnp.zeros_like(held_ref)

    def chunk(index, unused):
        rows = pl.ds(pl.multiple_of(index * SPAN, SPAN), SPAN)
        raw, steps, cumul, step_wide, grown_wide, tail_wide = chunk_steps(
            step_ref, bias_ref, rate_ref, expand_ref, rows
        )
        cumul_turned = cumul.T
        entry = both_ref[rows, pl.ds(0, states)].astype(jnp.bfloat16)
        readout = both_ref[rows, pl.ds(states, states)].astype(jnp.bfloat16)
        cross = low_against(readout, entry)
        square = (SPAN, SPAN)
        lower = row_index(square) >= lane_index(square)
        for start, width in slabs(channels):
            cols = pl.ds(start, width)
            span = slice(start, start + width)
            heads = width // HD
            values = act_ref[rows, cols]
            scaled = values * step_wide[:, span]
            held = held_ref[:, cols]
            carry_ref[index, :, cols] = held
            weights = []
            for head in range(start // HD, start // HD + heads):
                spread = cumul[:, head : head + 1] - cumul_turned[head : head + 1, :]
                decay = jnp.exp(jnp.where(lower, spread, -jnp.inf))
                weights.append((decay * cross).astype(jnp.bfloat16))
            weights = jnp.concatenate(weights, axis=1) if heads > 1 else weights[0]
            result = low_dot(weights, stacked_heads(scaled, heads))
            result = result + low_dot(readout, held) * grown_wide[:, span]
            held_ref[:, cols] = held * grown_wide[SPAN - 1 : SPAN, span] + low_inner(
                entry, scaled * tail_wide[:, span]
            )
            result = result + skip_ref[:, cols] * values
            out_ref[rows, cols] = result
            gate = gate_ref[rows, cols]
            gated_ref[rows, cols] = (result * (gate * jax.nn.sigmoid(gate))).astype(jnp.bfloat16)
        return unused

    lax.fori_loop(0, input_ref.shape[0] // SPAN, chunk, 0)


def ssd_backward_kernel(
    head_from,
    begun,
    ended,
    input_ref,
    state_ref,
    gate_ref,
    step_ref,
    grad_ref,
    carry_ref,
    input_kernel_ref,
    input_shift_ref,
    state_kernel_ref,
    state_shift_ref,
    bias_ref,
    rate_ref,
    skip_ref,
    expand_ref,
    collect_ref,
    *rest,
):
    begun_ref, rest = (rest[0], rest[1:]) if begun else (None, rest)
    grad_input_ref, grad_step_ref, grad_input_conv_ref, grad_head_ref = rest[:4]
    if ended:
        grad_state_ref, grad_state_conv_ref = rest[4:6]
    else:
        partial_ref = rest[4]
    (
        act_ref,
        slope_ref,
        both_ref,
        both_slope_ref,
        held_ref,
        wide_ref,
        turned_ref,
        column_ref,
        skip_sum_ref,
        scale_sum_ref,
    ) = rest[-10:]
    channels = input_ref.shape[1]
    states = state_ref.shape[1] // 2
    taps = input_kernel_ref.shape[0]
    for start, width in slabs(channels):
        cols = pl.ds(start, width)
        pre = convolve(input_ref[:, cols], input_kernel_ref, input_shift_ref, cols)
        sigma = jax.nn.sigmoid(pre)
        act_ref[:, cols] = pre * sigma
        slope_ref[:, cols] = sigma * (1.0 + pre * (1.0 - sigma))
    for start, width in slabs(2 * states):
        cols = pl.ds(start, width)
        pre = convolve(state_ref[:, cols], state_kernel_ref, state_shift_ref, cols)
        sigma = jax.nn.sigmoid(pre)
        both_ref[:, cols] = pre * sigma
        both_slope_ref[:, cols] = sigma * (1.0 + pre * (1.0 - sigma))
    held_ref[...] = jnp.zeros_like(held_ref)
    turned_ref[...] = jnp.zeros_like(turned_ref)
    column_ref[...] = jnp.zeros_like(column_ref)
    grad_head_ref[...] = jnp.zeros_like(grad_head_ref)
    skip_sum_ref[...] = jnp.zeros_like(skip_sum_ref)
    chunks = input_ref.shape[0] // SPAN

    def chunk(count, unused):
        index = chunks - 1 - count
        rows = pl.ds(pl.multiple_of(index * SPAN, SPAN), SPAN)
        raw, steps, cumul, step_wide, grown_wide, tail_wide = chunk_steps(
            step_ref, bias_ref, rate_ref, expand_ref, rows
        )
        cumul_turned = cumul.T
        entry = both_ref[rows, pl.ds(0, states)].astype(jnp.bfloat16)
        readout = both_ref[rows, pl.ds(states, states)].astype(jnp.bfloat16)
        cross = low_against(entry, readout)
        square = (SPAN, SPAN)
        upper = row_index(square) <= lane_index(square)
        grad_cross = jnp.zeros(square, jnp.float32)
        grad_entry = jnp.zeros((SPAN, states), jnp.float32)
        grad_readout = jnp.zeros((SPAN, states), jnp.float32)
        for start, width in slabs(channels):
            cols = pl.ds(start, width)
            span = slice(start, start + width)
            heads = width // HD
            values = act_ref[rows, cols]
            scaled = values * step_wide[:, span]
            gate = gate_ref[rows, cols]
            upstream = grad_ref[rows, cols] * (gate * jax.nn.sigmoid(gate))
            held = held_ref[:, cols]
            before = carry_ref[index, :, cols]
            stacked_up = stacked_heads(upstream, heads).astype(jnp.bfloat16)
            products = low_against(scaled, stacked_up)
            weights = []
            for place in range(heads):
                head = head_from + start // HD + place
                spread = cumul_turned[head : head + 1, :] - cumul[:, head : head + 1]
                decay = jnp.exp(jnp.where(upper, spread, -jnp.inf))
                product = products[:, place * SPAN : (place + 1) * SPAN] * decay
                grad_cross = grad_cross + product
                flow = product * cross
                turned_ref[head : head + 1, :] = jnp.sum(flow, axis=0, keepdims=True)
                column_ref[:, head : head + 1] = jnp.sum(flow, axis=1, keepdims=True)
                weights.append((decay * cross).astype(jnp.bfloat16))
            weights = jnp.concatenate(weights, axis=1) if heads > 1 else weights[0]
            grown_up = upstream * grown_wide[:, span]
            tailed = scaled * tail_wide[:, span]
            from_held = low_dot(entry, held)
            grad_scaled = low_dot(weights, stacked_up) + tail_wide[:, span] * from_held
            wide_ref[0, :, cols] = grown_up * low_dot(readout, before)
            wide_ref[1, :, cols] = tailed * from_held
            wide_ref[2, :, cols] = values * grad_scaled
            grad_readout = grad_readout + low_against(grown_up, before)
            grad_entry = grad_entry + low_against(tailed, held)
            last = grown_wide[SPAN - 1 : SPAN, span]
            scale_sum_ref[:, cols] = jnp.sum(held * before, axis=0, keepdims=True) * last
            skip_sum_ref[:, cols] += jnp.sum(upstream * values, axis=0, keepdims=True)
            held_ref[:, cols] = held * last + low_inner(readout, grown_up)
            act_ref[rows, cols] = step_wide[:, span] * grad_scaled + skip_ref[:, cols] * upstream
        sums = exact_dot(
            jnp.concatenate([wide_ref[0], wide_ref[1], wide_ref[2]], axis=0), collect_ref[...]
        )
        scale_sum = exact_dot(jnp.broadcast_to(scale_sum_ref[...], (8, channels)), collect_ref[...])
        flows = turned_ref[...].T - column_ref[...] + sums[:SPAN]
        onward = (row_index(square) <= lane_index(square)).astype(jnp.float32)
        strict = (row_index(square) > lane_index(square)).astype(jnp.float32)
        grad_log = (
            exact_dot(onward, flows)
            + exact_dot(strict, sums[SPAN : 2 * SPAN])
            + scale_sum[:1]
        )
        grad_steps = grad_log * rate_ref[...] + sums[2 * SPAN :]
        grad_raw = grad_steps * jax.nn.sigmoid(raw)
        grad_step_ref[rows, :] = grad_raw.astype(jnp.bfloat16)
        grad_head_ref[0, 0:1, :] += jnp.sum(grad_raw, axis=0, keepdims=True)
        grad_head_ref[0, 1:2, :] += (
            jnp.sum(grad_log * steps, axis=0, keepdims=True) * rate_ref[...]
        )
        grad_entry = grad_entry + low_dot(grad_cross, readout)
        grad_readout = grad_readout + low_inner(grad_cross, entry)
        if begun:
            grad_entry = grad_entry + begun_ref[rows, pl.ds(0, states)]
            grad_readout = grad_readout + begun_ref[rows, pl.ds(states, states)]
        target_ref = both_ref if ended else partial_ref
        target_ref[rows, pl.ds(0, states)] = grad_entry
        target_ref[rows, pl.ds(states, states)] = grad_readout
        return unused

    lax.fori_loop(0, chunks, chunk, 0)
    grad_head_ref[0, 2:3, :] = exact_dot(
        jnp.broadcast_to(skip_sum_ref[...], (8, channels)), collect_ref[...]
    )[:1]

    def convolve_back(raw_ref, grads_ref, slopes_ref, kernel_ref, out_ref, sums_ref, width_all):
        for start, width in slabs(width_all):
            cols = pl.ds(start, width)
            grad = grads_ref[:, cols] * slopes_ref[:, cols]
            raw = raw_ref[:, cols]
            total = kernel_ref[taps - 1 : taps, cols] * grad
            sums_ref[0, taps - 1 : taps, cols] = jnp.sum(grad * raw, axis=0, keepdims=True)
            for tap in range(taps - 1):
                shifted = sooner(grad, taps - 1 - tap)
                total = total + kernel_ref[tap : tap + 1, cols] * shifted
                sums_ref[0, tap : tap + 1, cols] = jnp.sum(shifted * raw, axis=0, keepdims=True)
            sums_ref[0, taps : taps + 1, cols] = jnp.sum(grad, axis=0, keepdims=True)
            out_ref[:, cols] = total.astype(jnp.bfloat16)

    convolve_back(
        input_ref,
        act_ref,
        slope_ref,
        input_kernel_ref,
        grad_input_ref,
        grad_input_conv_ref,
        channels,
    )
    if ended:
        convolve_back(
            state_ref,
            both_ref,
            both_slope_ref,
            state_kernel_ref,
            grad_state_ref,
            grad_state_conv_ref,
            2 * states,
        )


def by_sequence(length, width):
    return pl.BlockSpec((length, width), lambda seq: (seq, 0))


def fixed(*shape):
    return pl.BlockSpec(shape, lambda seq: (0,) * len(shape))


def head_spread(heads):
    marks = np.zeros((LANES, heads * HD), np.float32)
    for head in range(heads):
        marks[head, head * HD : (head + 1) * HD] = 1.0
    return marks


def pad_lanes(part):
    return jnp.pad(part, ((0, 0), (0, LANES - part.shape[1])))


def ssd_small(input_kernel, input_shift, state_kernel, state_shift, step_bias, decay_log, skip_gain):
    rates = -jnp.exp(decay_log)
    return (
        input_kernel,
        input_shift[None, :],
        state_kernel,
        state_shift[None, :],
        pad_lanes(step_bias[None, :]),
        pad_lanes(rates[None, :]),
        jnp.repeat(skip_gain, HD)[None, :],
    )


def ssd_forward(inputs, states_raw, gate, step, small, heads, length):
    group, channels = inputs.shape
    seqs = group // length
    both = states_raw.shape[1]
    states = both // 2
    chunks = length // SPAN
    taps = small[0].shape[0]
    return pl.pallas_call(
        ssd_forward_kernel,
        grid=(seqs,),
        in_specs=[
            by_sequence(length, channels),
            by_sequence(length, both),
            by_sequence(length, channels),
            by_sequence(length, LANES),
            fixed(taps, channels),
            fixed(1, channels),
            fixed(taps, both),
            fixed(1, both),
            fixed(1, LANES),
            fixed(1, LANES),
            fixed(1, channels),
            fixed(LANES, channels),
        ],
        out_specs=[
            by_sequence(length, channels),
            by_sequence(length, channels),
            pl.BlockSpec((chunks, states, channels), lambda seq: (seq, 0, 0)),
        ],
        out_shape=[
            jax.ShapeDtypeStruct((group, channels), jnp.bfloat16),
            jax.ShapeDtypeStruct((group, channels), jnp.float32),
            jax.ShapeDtypeStruct((seqs * chunks, states, channels), jnp.float32),
        ],
        scratch_shapes=[
            pltpu.VMEM((length, channels), jnp.float32),
            pltpu.VMEM((length, both), jnp.float32),
            pltpu.VMEM((states, channels), jnp.float32),
        ],
        compiler_params=pltpu.CompilerParams(vmem_limit_bytes=VMEM_LIMIT),
        cost_estimate=LIGHT,
        name="ssd_forward",
    )(inputs, states_raw, gate, step, *small, jnp.asarray(head_spread(heads)))


def ssd_backward(
    inputs, states_raw, gate, step, grad, carry, small, heads, length, index, count, begun
):
    group, channels = inputs.shape
    here = channels // count
    seqs = group // length
    both = states_raw.shape[1]
    states = both // 2
    chunks = length // SPAN
    taps = small[0].shape[0]
    ended = index == count - 1
    columns = pl.BlockSpec((length, here), lambda seq: (seq, index))

    def part(rows):
        return pl.BlockSpec((rows, here), lambda seq: (0, index))

    in_specs = [
        columns,
        by_sequence(length, both),
        columns,
        by_sequence(length, LANES),
        columns,
        pl.BlockSpec((chunks, states, here), lambda seq: (seq, 0, index)),
        part(taps),
        part(1),
        fixed(taps, both),
        fixed(1, both),
        fixed(1, LANES),
        fixed(1, LANES),
        part(1),
        part(LANES),
        pl.BlockSpec((here, LANES), lambda seq: (index, 0)),
    ]
    out_specs = [
        by_sequence(length, here),
        by_sequence(length, LANES),
        pl.BlockSpec((1, 8, here), lambda seq: (seq, 0, 0)),
        pl.BlockSpec((1, 8, LANES), lambda seq: (seq, 0, 0)),
    ]
    out_shape = [
        jax.ShapeDtypeStruct((group, here), jnp.bfloat16),
        jax.ShapeDtypeStruct((group, LANES), jnp.bfloat16),
        jax.ShapeDtypeStruct((seqs, 8, here), jnp.float32),
        jax.ShapeDtypeStruct((seqs, 8, LANES), jnp.float32),
    ]
    out_specs.append(by_sequence(length, both))
    if ended:
        out_shape.append(jax.ShapeDtypeStruct((group, both), jnp.bfloat16))
        out_specs.append(pl.BlockSpec((1, 8, both), lambda seq: (seq, 0, 0)))
        out_shape.append(jax.ShapeDtypeStruct((seqs, 8, both), jnp.float32))
    else:
        out_shape.append(jax.ShapeDtypeStruct((group, both), jnp.float32))
    extra = ()
    if begun is not None:
        in_specs.append(by_sequence(length, both))
        extra = (begun,)
    return pl.pallas_call(
        partial(ssd_backward_kernel, index * (heads // count), begun is not None, ended),
        grid=(seqs,),
        in_specs=in_specs,
        out_specs=out_specs,
        out_shape=out_shape,
        scratch_shapes=[
            pltpu.VMEM((length, here), jnp.float32),
            pltpu.VMEM((length, here), jnp.float32),
            pltpu.VMEM((length, both), jnp.float32),
            pltpu.VMEM((length, both), jnp.float32),
            pltpu.VMEM((states, here), jnp.float32),
            pltpu.VMEM((3, SPAN, here), jnp.float32),
            pltpu.VMEM((LANES, SPAN), jnp.float32),
            pltpu.VMEM((SPAN, LANES), jnp.float32),
            pltpu.VMEM((1, here), jnp.float32),
            pltpu.VMEM((1, here), jnp.float32),
        ],
        compiler_params=pltpu.CompilerParams(vmem_limit_bytes=VMEM_LIMIT),
        cost_estimate=LIGHT,
        name="ssd_backward",
    )(
        inputs,
        states_raw,
        gate,
        step,
        grad,
        carry,
        *small,
        jnp.asarray(head_spread(heads)),
        jnp.asarray(head_spread(heads).T.copy()),
        *extra,
    )


def rope_wide(length):
    half = HD // 2
    freqs = np.float32(ROPE_BASE) ** (-np.arange(half, dtype=np.float32) * np.float32(2.0 / HD))
    angles = np.arange(length, dtype=np.float32)[:, None] * freqs[None, :].astype(np.float32)
    cosine, sine = np.cos(angles), np.sin(angles)
    count = LANES // HD
    return (
        np.concatenate([cosine, cosine] * count, axis=1).astype(np.float32),
        np.concatenate([-sine, sine] * count, axis=1).astype(np.float32),
    )


def turn(part, cosine, sine):
    half = HD // 2
    first = lane_index(part.shape) % HD < half
    swapped = jnp.where(first, pltpu.roll(part, LANES - half, 1), pltpu.roll(part, half, 1))
    return part * cosine + swapped * sine


def attend_forward_kernel(
    query_ref, pair_ref, cosine_ref, sine_ref, context_ref, query_out_ref, pair_out_ref, total_ref
):
    length = query_ref.shape[0]
    cosine, sine = cosine_ref[...], sine_ref[...]
    pair = pair_ref[...]
    left = lane_index(pair.shape) < HD
    pair = jnp.where(left, turn(pair, cosine, sine), pair)
    pair_out_ref[...] = pair.astype(jnp.bfloat16)
    moved = pltpu.roll(pair, HD, 1)
    keys = jnp.where(left, pair, moved).astype(jnp.bfloat16)
    values = jnp.where(left, moved, pair).astype(jnp.bfloat16)
    scale = HD ** (-0.5)
    for slab in range(query_ref.shape[1] // LANES):
        cols = pl.ds(slab * LANES, LANES)
        query_out_ref[:, cols] = turn(query_ref[:, cols], cosine, sine).astype(jnp.bfloat16)
        for tile in range(length // SPAN):
            rows = slice(tile * SPAN, (tile + 1) * SPAN)
            count = (tile + 1) * SPAN
            query = query_out_ref[rows, cols]
            lane = lane_index(query.shape)
            square = (SPAN, count)
            causal = row_index(square) + tile * SPAN >= lane_index(square)
            results = []
            for place in range(LANES // HD):
                mine = (lane >= place * HD) & (lane < place * HD + HD)
                scores = low_against(jnp.where(mine, query, 0), keys[:count]) * scale
                scores = jnp.where(causal, scores, -jnp.inf)
                peak = jnp.max(scores, axis=-1, keepdims=True)
                grown = jnp.exp(scores - peak)
                total = jnp.sum(grown, axis=-1, keepdims=True)
                probs = grown * (1.0 / total)
                results.append(low_dot(probs, values[:count]))
                head = slab * (LANES // HD) + place
                total_ref[rows, head : head + 1] = jnp.log(total) + peak
            context_ref[rows, cols] = jnp.where(lane < HD, results[0], results[1]).astype(
                jnp.bfloat16
            )


def attend_backward_kernel(
    query_ref,
    pair_ref,
    total_ref,
    grad_ref,
    cosine_ref,
    sine_ref,
    grad_query_ref,
    grad_pair_ref,
    key_sum_ref,
    value_sum_ref,
):
    length = query_ref.shape[0]
    cosine, sine = cosine_ref[...], -sine_ref[...]
    pair = pair_ref[...].astype(jnp.float32)
    left = lane_index(pair.shape) < HD
    moved = pltpu.roll(pair, HD, 1)
    keys = jnp.where(left, pair, moved).astype(jnp.bfloat16)
    values = jnp.where(left, moved, pair).astype(jnp.bfloat16)
    scale = HD ** (-0.5)
    key_sum_ref[...] = jnp.zeros_like(key_sum_ref)
    value_sum_ref[...] = jnp.zeros_like(value_sum_ref)
    for slab in range(query_ref.shape[1] // LANES):
        cols = pl.ds(slab * LANES, LANES)
        for tile in range(length // SPAN):
            rows = slice(tile * SPAN, (tile + 1) * SPAN)
            count = (tile + 1) * SPAN
            query = query_ref[rows, cols]
            upstream = grad_ref[rows, cols]
            lane = lane_index(query.shape)
            square = (SPAN, count)
            causal = row_index(square) + tile * SPAN >= lane_index(square)
            results = []
            for place in range(LANES // HD):
                mine = (lane >= place * HD) & (lane < place * HD + HD)
                head = slab * (LANES // HD) + place
                own_query = jnp.where(mine, query, 0)
                own_up = jnp.where(mine, upstream, 0)
                scores = low_against(own_query, keys[:count]) * scale
                scores = jnp.where(causal, scores, -jnp.inf)
                probs = jnp.exp(scores - total_ref[rows, head : head + 1])
                grad_probs = low_against(own_up, values[:count])
                mean = jnp.sum(probs * grad_probs, axis=-1, keepdims=True)
                grad_scores = (probs * (grad_probs - mean)).astype(jnp.bfloat16)
                results.append(low_dot(grad_scores, keys[:count]))
                key_sum_ref[0:count, :] += low_inner(grad_scores, own_query)
                value_sum_ref[0:count, :] += low_inner(probs, own_up)
            grad_query = jnp.where(lane < HD, results[0], results[1]) * scale
            grad_query_ref[rows, cols] = turn(
                grad_query, cosine[rows, :], sine[rows, :]
            ).astype(jnp.bfloat16)
    grad_key = key_sum_ref[...]
    grad_key = turn((grad_key + pltpu.roll(grad_key, HD, 1)) * scale, cosine, sine)
    grad_value = value_sum_ref[...]
    grad_value = grad_value + pltpu.roll(grad_value, HD, 1)
    grad_pair_ref[...] = jnp.where(left, grad_key, grad_value).astype(jnp.bfloat16)


def attend_forward(query, pair, length):
    group, width = query.shape
    heads = width // HD
    cosine, sine = rope_wide(length)
    return pl.pallas_call(
        attend_forward_kernel,
        grid=(group // length,),
        in_specs=[
            by_sequence(length, width),
            by_sequence(length, LANES),
            fixed(length, LANES),
            fixed(length, LANES),
        ],
        out_specs=[
            by_sequence(length, width),
            by_sequence(length, width),
            by_sequence(length, LANES),
            by_sequence(length, LANES),
        ],
        out_shape=[
            jax.ShapeDtypeStruct((group, width), jnp.bfloat16),
            jax.ShapeDtypeStruct((group, width), jnp.bfloat16),
            jax.ShapeDtypeStruct((group, LANES), jnp.bfloat16),
            jax.ShapeDtypeStruct((group, LANES), jnp.float32),
        ],
        compiler_params=pltpu.CompilerParams(vmem_limit_bytes=VMEM_LIMIT),
        cost_estimate=LIGHT,
        name="attend_forward",
    )(query, pair, jnp.asarray(cosine), jnp.asarray(sine))


def attend_backward(query, pair, total, grad, length):
    group, width = query.shape
    heads = width // HD
    cosine, sine = rope_wide(length)
    return pl.pallas_call(
        attend_backward_kernel,
        grid=(group // length,),
        in_specs=[
            by_sequence(length, width),
            by_sequence(length, LANES),
            by_sequence(length, LANES),
            by_sequence(length, width),
            fixed(length, LANES),
            fixed(length, LANES),
        ],
        out_specs=[by_sequence(length, width), by_sequence(length, LANES)],
        out_shape=[
            jax.ShapeDtypeStruct((group, width), jnp.bfloat16),
            jax.ShapeDtypeStruct((group, LANES), jnp.bfloat16),
        ],
        scratch_shapes=[
            pltpu.VMEM((length, LANES), jnp.float32),
            pltpu.VMEM((length, LANES), jnp.float32),
        ],
        compiler_params=pltpu.CompilerParams(vmem_limit_bytes=VMEM_LIMIT),
        cost_estimate=LIGHT,
        name="attend_backward",
    )(query, pair, total, grad, jnp.asarray(cosine), jnp.asarray(sine))


def step_groups(size):
    bits = size.bit_length() - 1
    return [1] * min(bits, 2) + [2] * (max(bits - 2, 0) // 2) + [1] * (max(bits - 2, 0) % 2)


def after(part, *deps):
    return lax.optimization_barrier((part,) + deps)[0]


def behind(part, dep):
    zero = jnp.minimum(jnp.abs(dep[:1, :1].astype(jnp.float32)), 0.0)
    return part + zero.astype(part.dtype)


class Sum:
    def __init__(self, part, size):
        self.size = size
        self.direct = bool(size & (size - 1) or part.shape[0] % size)
        self.steps = [] if self.direct else step_groups(size)
        self.shift = 0
        self.part = part
        self.gives = [part]
        if not self.direct:
            self.part = part.reshape(size, part.shape[0] // size, part.shape[1])
            self.prepare()

    def prepare(self):
        if not self.steps:
            self.gives = [self.part]
            return
        ways = 1 << self.steps[0]
        rest = self.part.shape[0] // ways
        view = self.part.reshape((rest, ways) + self.part.shape[1:])
        mine = (lax.axis_index("dp") >> self.shift) & (ways - 1)
        self.keep = lax.dynamic_index_in_dim(view, mine, 1, False)
        self.gives = [
            lax.dynamic_index_in_dim(view, mine ^ way, 1, False) for way in range(1, ways)
        ]

    def advance(self, *deps):
        if self.steps:
            total = after(self.keep, *deps).astype(jnp.float32)
            for way, give in enumerate(self.gives, 1):
                pairs = [(index, index ^ (way << self.shift)) for index in range(self.size)]
                total = total + lax.ppermute(give, "dp", pairs).astype(jnp.float32)
            self.part = total.astype(jnp.bfloat16)
            self.shift += self.steps.pop(0)
            self.prepare()
        return self.gives

    def joined(self, middle=None):
        groups, shift = step_groups(self.size), self.size.bit_length() - 1
        part = self.reduced()
        if middle is not None:
            part = middle(part)
        if self.direct:
            return part
        rows, width = part.shape
        for group in reversed(groups):
            ways = 1 << group
            shift -= group
            mine = (lax.axis_index("dp") >> shift) & (ways - 1)
            part = part.reshape(-1, 1, rows, width)
            got = [part]
            for way in range(1, ways):
                pairs = [(index, index ^ (way << shift)) for index in range(self.size)]
                got.append(lax.ppermute(part, "dp", pairs))
            for bit in range(group):
                flip = ((mine >> bit) & 1) == 1
                got = [
                    jnp.where(flip, got[way ^ (1 << bit)], got[way]) for way in range(ways)
                ]
            part = jnp.concatenate(got, axis=1)
        return part.reshape(-1, width)

    def reduced(self):
        while self.steps:
            self.advance()
        return lax.psum(self.part, "dp") if self.direct else self.part[0]


def gather_dp(parts, direct, size, place):
    widths = [part.shape[1] for part in parts]
    part = jnp.concatenate(parts, axis=1) if len(parts) > 1 else parts[0]
    if not direct:
        lead = (1,) * (place + 1)
        part = lax.all_gather(part.reshape(lead + part.shape), "dp", axis=place, tiled=True)
        part = part.reshape(size * part.shape[-2], part.shape[-1])
    out, start = [], 0
    for width in widths:
        out.append(part[:, start : start + width])
        start += width
    return out


def other(part):
    return lax.ppermute(part, "tensor", [(0, 1), (1, 0)])


def all_rows(part, shards):
    if shards != 2:
        return lax.all_gather(part, "tensor", axis=0, tiled=True)
    got = other(part)
    return jnp.where(
        lax.axis_index("tensor") == 0,
        jnp.concatenate([part, got], axis=0),
        jnp.concatenate([got, part], axis=0),
    )


def sum_all(part, shards):
    if shards != 2:
        return lax.psum(part, "tensor").astype(jnp.float32)
    return part.astype(jnp.float32) + other(part).astype(jnp.float32)


def sum_own(part, shards):
    if shards != 2:
        return lax.psum_scatter(part, "tensor", scatter_dimension=0, tiled=True).astype(jnp.float32)
    me = lax.axis_index("tensor")
    halves = part.reshape(2, part.shape[0] // 2, part.shape[1])
    keep = lax.dynamic_index_in_dim(halves, me, 0, False)
    got = other(lax.dynamic_index_in_dim(halves, 1 - me, 0, False))
    return keep.astype(jnp.float32) + got.astype(jnp.float32)


def own_rows(part, rows):
    return lax.dynamic_slice_in_dim(part, lax.axis_index("tensor") * rows, rows, 0)


def column_pack(vectors, rows):
    flat = jnp.concatenate([item.reshape(-1) for item in vectors])
    width = -(-flat.shape[0] // rows)
    return jnp.pad(flat, (0, width * rows - flat.shape[0])).reshape(width, rows).T


def column_unpack(packed, shapes):
    flat = packed.T.reshape(-1)
    out, start = [], 0
    for shape in shapes:
        count = 1
        for size in shape:
            count *= size
        out.append(flat[start : start + count].reshape(shape))
        start += count
    return out


def body(
    dp_size,
    shards,
    layer_input,
    input_gain,
    middle_gain,
    mamba_gate,
    mamba_input,
    step_weight,
    state_weight,
    input_kernel,
    input_shift,
    state_kernel,
    state_shift,
    step_bias,
    decay_log,
    skip_gain,
    mamba_output,
    query_weight,
    keyvalue_weight,
    context_weight,
    gate_weight,
    up_weight,
    down_weight,
    cotangent,
):
    own = layer_input.shape[0]
    rows_low = all_rows(layer_input, shards)
    cotan_low = all_rows(cotangent, shards)
    rows = rows_low.astype(jnp.float32)
    gain_first = input_gain.astype(jnp.float32)
    gain_second = middle_gain.astype(jnp.float32)
    factor_first = lax.rsqrt(jnp.mean(rows * rows, axis=-1, keepdims=True) + EPSILON)
    normal_first = rows * factor_first
    whole = (normal_first * gain_first).astype(jnp.bfloat16)
    group = whole.shape[0]
    length = min(SEQ_LEN, group)
    seqs = group // length
    heads_here = query_weight.shape[1] // HD
    kv_head = lax.axis_index("tensor") * heads_here // (HQ // KVH)
    key_cols = lax.dynamic_slice_in_dim(keyvalue_weight, kv_head * HD, HD, 1)
    value_cols = lax.dynamic_slice_in_dim(keyvalue_weight, (KVH + kv_head) * HD, HD, 1)
    pair_weight = jnp.concatenate([key_cols, value_cols], axis=1)
    query_cols = query_weight.shape[1]
    query_pad = -query_cols % LANES
    query_wide = jnp.pad(query_weight, ((0, 0), (0, query_pad)))
    step_wide = pad_lanes(step_weight)
    heads = step_weight.shape[1]
    input_raw = forward_dot(whole, mamba_input)
    state_raw = forward_dot(whole, state_weight)
    step_raw = forward_dot(whole, step_wide)
    gate_raw = forward_dot(whole, mamba_gate)
    query_raw = forward_dot(whole, query_wide)
    pair_raw = forward_dot(whole, pair_weight)
    small = ssd_small(
        input_kernel.astype(jnp.float32),
        input_shift.astype(jnp.float32),
        state_kernel.astype(jnp.float32),
        state_shift.astype(jnp.float32),
        step_bias.astype(jnp.float32),
        decay_log.astype(jnp.float32),
        skip_gain.astype(jnp.float32),
    )
    gated_low, ssm_out, carries = ssd_forward(
        input_raw, state_raw, gate_raw, step_raw, small, heads, length
    )
    context_wide, queries, pairs, totals = attend_forward(
        after(query_raw, cotan_low), pair_raw, length
    )
    context_rows = context_wide[:, :query_cols]
    mixed_part = forward_dot(gated_low, mamba_output) + forward_dot(context_rows, context_weight)
    resid = rows + sum_all(mixed_part.astype(jnp.bfloat16), shards)
    factor_second = lax.rsqrt(jnp.mean(resid * resid, axis=-1, keepdims=True) + EPSILON)
    normal_second = resid * factor_second
    whole_mid = (normal_second * gain_second).astype(jnp.bfloat16)
    gate = forward_dot(whole_mid, gate_weight)
    upper = forward_dot(whole_mid, up_weight)
    sigmoid_gate = jax.nn.sigmoid(gate)
    silu_gate = gate * sigmoid_gate
    hidden = (silu_gate * upper).astype(jnp.bfloat16)
    grad_hidden = against(cotan_low, down_weight)
    slope = sigmoid_gate * (1.0 + gate * (1.0 - sigmoid_gate))
    grad_gate_low = (grad_hidden * upper * slope).astype(jnp.bfloat16)
    grad_upper_low = (grad_hidden * silu_gate).astype(jnp.bfloat16)
    back_part = (against(grad_gate_low, gate_weight) + against(grad_upper_low, up_weight)).astype(
        jnp.bfloat16
    )
    back_mid = sum_all(back_part, shards)
    hidden, grad_gate_low, grad_upper_low = (
        after(hidden, back_part),
        after(grad_gate_low, back_part),
        after(grad_upper_low, back_part),
    )
    down_sum = Sum(inner_rows(hidden, cotan_low).astype(jnp.bfloat16), dp_size)
    hidden_cols = gate_weight.shape[1]
    wide_sum = Sum(
        inner_rows(whole_mid, jnp.concatenate([grad_gate_low, grad_upper_low], axis=1)).astype(
            jnp.bfloat16
        ),
        dp_size,
    )
    down_sum.advance()
    wide_sum.advance()
    back_mid = after(back_mid, *down_sum.gives, *wide_sum.gives)
    feed_part = behind(forward_dot(hidden, down_weight), back_mid).astype(jnp.bfloat16)
    feed = sum_own(feed_part, shards)
    layer_output = (own_rows(resid, own) + feed).astype(jnp.bfloat16)
    grad_middle = jnp.sum(back_part.astype(jnp.float32) * normal_second, axis=0)
    grad_resid = cotan_low.astype(jnp.float32) + norm_back(
        back_mid, gain_second, normal_second, factor_second
    )
    mixer_all = grad_resid.astype(jnp.bfloat16)
    mixer_sum = Sum(
        inner_rows(jnp.concatenate([gated_low, context_rows], axis=1), mixer_all).astype(
            jnp.bfloat16
        ),
        dp_size,
    )
    ssm_rows = gated_low.shape[1]
    grad_gated = against(mixer_all, mamba_output)
    sigmoid_raw = jax.nn.sigmoid(gate_raw)
    grad_gate_raw = (
        grad_gated * ssm_out * (sigmoid_raw * (1.0 + gate_raw * (1.0 - sigmoid_raw)))
    ).astype(jnp.bfloat16)
    grad_context = against(mixer_all, context_weight).astype(jnp.bfloat16)
    grad_query_raw, grad_pair_raw = attend_backward(
        queries,
        pairs,
        totals,
        after(jnp.pad(grad_context, ((0, 0), (0, query_pad))), *mixer_sum.gives),
        length,
    )
    grad_query_raw = grad_query_raw[:, :query_cols]
    early_cols = jnp.concatenate([grad_gate_raw, grad_query_raw], axis=1)
    early_sum = Sum(inner_rows(whole, early_cols).astype(jnp.bfloat16), dp_size)
    grad_gated = after(
        grad_gated,
        *early_sum.gives,
        *mixer_sum.advance(early_sum.gives[0]),
        *down_sum.advance(early_sum.gives[0]),
    )
    parts = 2 if heads % 4 == 0 else 1
    begun = None
    input_pieces, step_pieces, conv_pieces, head_pieces = [], [], [], []
    for index in range(parts):
        piece = ssd_backward(
            input_raw,
            state_raw,
            gate_raw,
            step_raw,
            grad_gated,
            carries,
            small,
            heads,
            length,
            index,
            parts,
            begun,
        )
        begun = piece[4]
        input_pieces.append(piece[0])
        step_pieces.append(piece[1])
        conv_pieces.append(jnp.sum(piece[2], axis=0))
        head_pieces.append(jnp.sum(piece[3], axis=0))
        if index == 0:
            begun = after(
                begun,
                *wide_sum.advance(piece[1]),
                *early_sum.advance(piece[1]),
                *down_sum.advance(piece[1]),
            )
    grad_state_raw, state_sums = piece[4:]
    grad_input_raw = jnp.concatenate(input_pieces, axis=1)
    grad_step_raw = sum(step_pieces[1:], step_pieces[0])
    input_sums = jnp.concatenate(conv_pieces, axis=1)
    state_sums = jnp.sum(state_sums, axis=0)
    head_sums = sum(head_pieces[1:], head_pieces[0])[:, :heads]
    taps = input_kernel.shape[0]
    late_cols = jnp.concatenate(
        [grad_input_raw, grad_state_raw, grad_pair_raw, grad_step_raw], axis=1
    )
    total = against(early_cols, jnp.concatenate([mamba_gate, query_weight], axis=1))
    total = total + against(
        late_cols, jnp.concatenate([mamba_input, state_weight, pair_weight, step_wide], axis=1)
    )
    total_low = total.astype(jnp.bfloat16)
    grad_first = jnp.sum(total_low.astype(jnp.float32) * normal_first, axis=0)
    width = whole.shape[1]
    gate_cols = grad_gate_raw.shape[1]
    input_cols = grad_input_raw.shape[1]
    state_cols = grad_state_raw.shape[1]
    step_cols = heads
    pair_cols = grad_pair_raw.shape[1]

    own_vectors = (input_sums[:taps], input_sums[taps], head_sums[0], head_sums[1], head_sums[2])
    shared_vectors = (grad_first, grad_middle, state_sums[:taps], state_sums[taps])
    own_pack = column_pack(own_vectors, width)
    shared_pack = column_pack(shared_vectors, width)
    shared_lane = step_cols + own_pack.shape[1]
    last_lane = shared_lane + shared_pack.shape[1]
    packs = jnp.pad(
        jnp.concatenate([own_pack, shared_pack], axis=1),
        ((0, 0), (step_cols, LANES - last_lane)),
    )
    split_pairs = shards == KVH
    late = inner_rows(whole, late_cols)
    marks = (input_cols, input_cols + state_cols, input_cols + state_cols + pair_cols)
    late_pair = late[:, marks[1] : marks[2]]
    if not split_pairs:
        spread = jnp.zeros((width, 2 * KVH * HD), jnp.float32)
        spread = lax.dynamic_update_slice_in_dim(spread, late_pair[:, :HD], kv_head * HD, 1)
        late_pair = lax.dynamic_update_slice_in_dim(
            spread, late_pair[:, HD:], (KVH + kv_head) * HD, 1
        )
        late = jnp.concatenate([late[:, : marks[1]], late_pair, late[:, marks[2] :]], axis=1)
    misc = late.shape[1] - LANES
    late = (late + jnp.pad(packs, ((0, 0), (misc, 0)))).astype(jnp.bfloat16)
    late_sum = Sum(late, dp_size)

    def over_tensor(part):
        own_part = part[:, input_cols:]
        if split_pairs:
            got = other(own_part)
            both = (own_part.astype(jnp.float32) + got.astype(jnp.float32)).astype(jnp.bfloat16)
            first = lax.axis_index("tensor") == 0
            pair_span = slice(state_cols, state_cols + pair_cols)
            low = jnp.where(first, own_part[:, pair_span], got[:, pair_span])
            high = jnp.where(first, got[:, pair_span], own_part[:, pair_span])
            pair = [low[:, :HD], high[:, :HD], low[:, HD:], high[:, HD:]]
        else:
            both = lax.psum(own_part, "tensor")
            pair = [both[:, state_cols:-LANES]]
        lane = lane_index((part.shape[0], LANES))
        extra = jnp.where(
            (lane >= shared_lane) & (lane < last_lane), both[:, -LANES:], own_part[:, -LANES:]
        )
        return jnp.concatenate(
            [part[:, :input_cols], both[:, :state_cols]] + pair + [extra], axis=1
        )

    queue = late_sum.gives[0]
    mixer_sum.advance(queue)
    wide_sum.advance(queue)
    early_sum.advance(queue)
    sums = [wide_sum, down_sum, mixer_sum, early_sum]
    blocks = [item.reduced() for item in sums]
    if len({block.shape[0] for block in blocks}) == 1:
        wholes = gather_dp(blocks, wide_sum.direct, dp_size, 0)
    else:
        wholes = [
            gather_dp([block], item.direct, dp_size, 0)[0] for item, block in zip(sums, blocks)
        ]
    grad_wide, grad_down, grad_mixer_out, early = wholes
    grad_gate, grad_up = grad_wide[:, :hidden_cols], grad_wide[:, hidden_cols:]
    tail = late_sum.joined(over_tensor)
    grad_mamba_out = grad_mixer_out[:ssm_rows]
    grad_context_w = grad_mixer_out[ssm_rows:]
    grad_mamba_input = tail[:, :input_cols]
    tail = tail[:, input_cols:]
    back_in = sum_own(total_low, shards)
    normal_own = own_rows(normal_first, own)
    factor_own = own_rows(factor_first, own)
    input_grad = own_rows(grad_resid, own) + norm_back(back_in, gain_first, normal_own, factor_own)
    extra = tail[:, state_cols + keyvalue_weight.shape[1] :]
    grad_step = extra[:, :step_cols]
    grad_in_kernel, grad_in_shift, grad_bias, grad_decay, grad_skip = column_unpack(
        extra[:, step_cols:shared_lane], [item.shape for item in own_vectors]
    )
    grad_first, grad_middle, grad_st_kernel, grad_st_shift = column_unpack(
        extra[:, shared_lane:last_lane], [item.shape for item in shared_vectors]
    )
    results = (
        grad_first,
        grad_middle,
        early[:, :gate_cols],
        grad_mamba_input,
        grad_step,
        tail[:, :state_cols],
        grad_in_kernel,
        grad_in_shift,
        grad_st_kernel,
        grad_st_shift,
        grad_bias,
        grad_decay,
        grad_skip,
        grad_mamba_out,
        early[:, gate_cols:],
        tail[:, state_cols : state_cols + keyvalue_weight.shape[1]],
        grad_context_w,
        grad_gate,
        grad_up,
        grad_down,
    )
    return (layer_output, input_grad) + tuple(item.astype(jnp.float32) for item in results)


def solution(mesh):
    in_specs = (
        P(("dp", "tensor"), None),
        P(),
        P(),
        P(None, "tensor"),
        P(None, "tensor"),
        P(None, "tensor"),
        P(),
        P(None, "tensor"),
        P("tensor"),
        P(),
        P(),
        P("tensor"),
        P("tensor"),
        P("tensor"),
        P("tensor", None),
        P(None, "tensor"),
        P(),
        P("tensor", None),
        P(None, "tensor"),
        P(None, "tensor"),
        P("tensor", None),
        P(("dp", "tensor"), None),
    )
    out_specs = (
        P(("dp", "tensor"), None),
        P(("dp", "tensor"), None),
        P(),
        P(),
        P(None, "tensor"),
        P(None, "tensor"),
        P(None, "tensor"),
        P(),
        P(None, "tensor"),
        P("tensor"),
        P(),
        P(),
        P("tensor"),
        P("tensor"),
        P("tensor"),
        P("tensor", None),
        P(None, "tensor"),
        P(),
        P("tensor", None),
        P(None, "tensor"),
        P(None, "tensor"),
        P("tensor", None),
    )
    run = partial(body, mesh.shape["dp"], mesh.shape["tensor"])
    return jax.shard_map(run, mesh=mesh, in_specs=in_specs, out_specs=out_specs, check_vma=False)
```

```python
from functools import partial

import jax
import jax.numpy as jnp
import numpy as np
from jax import lax
from jax.experimental import pallas as pl
from jax.experimental.pallas import tpu as pltpu
from jax.sharding import PartitionSpec as P

HD = 64
HQ = 8
KVH = 2
SPAN = 128
SEQ_LEN = 1024


EPSILON = 1e-05
ROPE_BASE = 10000.0
PRECISE = lax.Precision.HIGHEST


def forward_dot(left, right):
    return jnp.dot(left, right, preferred_element_type=jnp.float32)


def inner_rows(left, right):
    return lax.dot_general(
        left, right, (((0,), (0,)), ((), ())), preferred_element_type=jnp.float32
    )


def against(left, right):
    return lax.dot_general(
        left, right, (((1,), (1,)), ((), ())), preferred_element_type=jnp.float32
    )


def norm_back(upstream, gain, normal, factor):
    scaled = upstream * gain
    return factor * (scaled - normal * jnp.mean(scaled * normal, axis=-1, keepdims=True))


LANES = 128
VMEM_LIMIT = 44 * 1024 * 1024
LIGHT = pl.CostEstimate(flops=1024, bytes_accessed=1024, transcendentals=0)


def exact_dot(left, right):
    return jnp.dot(left, right, precision=PRECISE, preferred_element_type=jnp.float32)


def low_dot(left, right):
    return jnp.dot(
        left.astype(jnp.bfloat16), right.astype(jnp.bfloat16), preferred_element_type=jnp.float32
    )


def low_against(left, right):
    return lax.dot_general(
        left.astype(jnp.bfloat16),
        right.astype(jnp.bfloat16),
        (((1,), (1,)), ((), ())),
        preferred_element_type=jnp.float32,
    )


def low_inner(left, right):
    return lax.dot_general(
        left.astype(jnp.bfloat16),
        right.astype(jnp.bfloat16),
        (((0,), (0,)), ((), ())),
        preferred_element_type=jnp.float32,
    )


def row_index(shape):
    return lax.broadcasted_iota(jnp.int32, shape, 0)


def lane_index(shape):
    return lax.broadcasted_iota(jnp.int32, shape, 1)


def later(part, count):
    if count == 0:
        return part
    return jnp.where(row_index(part.shape) >= count, pltpu.roll(part, count, 0), 0.0)


def sooner(part, count):
    if count == 0:
        return part
    rows = part.shape[0]
    return jnp.where(row_index(part.shape) < rows - count, pltpu.roll(part, rows - count, 0), 0.0)


def slabs(width):
    return [(start, min(LANES, width - start)) for start in range(0, width, LANES)]


def soft_plus(value):
    return jnp.maximum(value, 0.0) + jnp.log1p(jnp.exp(-jnp.abs(value)))


def stacked_heads(part, heads):
    if heads == 1:
        return part
    lane = lane_index(part.shape)
    return jnp.concatenate(
        [jnp.where((lane >= head * HD) & (lane < head * HD + HD), part, 0.0) for head in range(heads)],
        axis=0,
    )


def convolve(raw, kernel_ref, shift_ref, cols):
    taps = kernel_ref.shape[0]
    out = shift_ref[:, cols] + kernel_ref[taps - 1 : taps, cols] * raw
    for tap in range(taps - 1):
        out = out + kernel_ref[tap : tap + 1, cols] * later(raw, taps - 1 - tap)
    return out


def chunk_steps(step_ref, bias_ref, rate_ref, expand_ref, rows):
    raw = step_ref[rows, :] + bias_ref[...]
    steps = soft_plus(raw)
    logdec = steps * rate_ref[...]
    square = (SPAN, SPAN)
    lower = (row_index(square) >= lane_index(square)).astype(jnp.float32)
    cumul = exact_dot(lower, logdec)
    grown = jnp.exp(cumul)
    tail = jnp.exp(cumul[SPAN - 1 : SPAN, :] - cumul)
    wide = exact_dot(jnp.concatenate([steps, grown, tail], axis=0), expand_ref[...])
    return raw, steps, cumul, wide[:SPAN], wide[SPAN : 2 * SPAN], wide[2 * SPAN :]


def ssd_forward_kernel(
    input_ref,
    state_ref,
    gate_ref,
    step_ref,
    input_kernel_ref,
    input_shift_ref,
    state_kernel_ref,
    state_shift_ref,
    bias_ref,
    rate_ref,
    skip_ref,
    expand_ref,
    gated_ref,
    out_ref,
    carry_ref,
    act_ref,
    both_ref,
    held_ref,
):
    channels = input_ref.shape[1]
    states = state_ref.shape[1] // 2
    for start, width in slabs(channels):
        cols = pl.ds(start, width)
        pre = convolve(input_ref[:, cols], input_kernel_ref, input_shift_ref, cols)
        act_ref[:, cols] = pre * jax.nn.sigmoid(pre)
    for start, width in slabs(2 * states):
        cols = pl.ds(start, width)
        pre = convolve(state_ref[:, cols], state_kernel_ref, state_shift_ref, cols)
        both_ref[:, cols] = pre * jax.nn.sigmoid(pre)
    held_ref[...] = jnp.zeros_like(held_ref)

    def chunk(index, unused):
        rows = pl.ds(pl.multiple_of(index * SPAN, SPAN), SPAN)
        raw, steps, cumul, step_wide, grown_wide, tail_wide = chunk_steps(
            step_ref, bias_ref, rate_ref, expand_ref, rows
        )
        cumul_turned = cumul.T
        entry = both_ref[rows, pl.ds(0, states)].astype(jnp.bfloat16)
        readout = both_ref[rows, pl.ds(states, states)].astype(jnp.bfloat16)
        cross = low_against(readout, entry)
        square = (SPAN, SPAN)
        lower = row_index(square) >= lane_index(square)
        for start, width in slabs(channels):
            cols = pl.ds(start, width)
            span = slice(start, start + width)
            heads = width // HD
            values = act_ref[rows, cols]
            scaled = values * step_wide[:, span]
            held = held_ref[:, cols]
            carry_ref[index, :, cols] = held
            weights = []
            for head in range(start // HD, start // HD + heads):
                spread = cumul[:, head : head + 1] - cumul_turned[head : head + 1, :]
                decay = jnp.exp(jnp.where(lower, spread, -jnp.inf))
                weights.append((decay * cross).astype(jnp.bfloat16))
            weights = jnp.concatenate(weights, axis=1) if heads > 1 else weights[0]
            result = low_dot(weights, stacked_heads(scaled, heads))
            result = result + low_dot(readout, held) * grown_wide[:, span]
            held_ref[:, cols] = held * grown_wide[SPAN - 1 : SPAN, span] + low_inner(
                entry, scaled * tail_wide[:, span]
            )
            result = result + skip_ref[:, cols] * values
            out_ref[rows, cols] = result
            gate = gate_ref[rows, cols]
            gated_ref[rows, cols] = (result * (gate * jax.nn.sigmoid(gate))).astype(jnp.bfloat16)
        return unused

    lax.fori_loop(0, input_ref.shape[0] // SPAN, chunk, 0)


def ssd_backward_kernel(
    head_from,
    begun,
    ended,
    input_ref,
    state_ref,
    gate_ref,
    step_ref,
    grad_ref,
    carry_ref,
    input_kernel_ref,
    input_shift_ref,
    state_kernel_ref,
    state_shift_ref,
    bias_ref,
    rate_ref,
    skip_ref,
    expand_ref,
    collect_ref,
    *rest,
):
    begun_ref, rest = (rest[0], rest[1:]) if begun else (None, rest)
    grad_input_ref, grad_step_ref, grad_input_conv_ref, grad_head_ref = rest[:4]
    if ended:
        grad_state_ref, grad_state_conv_ref = rest[4:6]
    else:
        partial_ref = rest[4]
    (
        act_ref,
        slope_ref,
        both_ref,
        both_slope_ref,
        held_ref,
        wide_ref,
        turned_ref,
        column_ref,
        skip_sum_ref,
        scale_sum_ref,
    ) = rest[-10:]
    channels = input_ref.shape[1]
    states = state_ref.shape[1] // 2
    taps = input_kernel_ref.shape[0]
    for start, width in slabs(channels):
        cols = pl.ds(start, width)
        pre = convolve(input_ref[:, cols], input_kernel_ref, input_shift_ref, cols)
        sigma = jax.nn.sigmoid(pre)
        act_ref[:, cols] = pre * sigma
        slope_ref[:, cols] = sigma * (1.0 + pre * (1.0 - sigma))
    for start, width in slabs(2 * states):
        cols = pl.ds(start, width)
        pre = convolve(state_ref[:, cols], state_kernel_ref, state_shift_ref, cols)
        sigma = jax.nn.sigmoid(pre)
        both_ref[:, cols] = pre * sigma
        both_slope_ref[:, cols] = sigma * (1.0 + pre * (1.0 - sigma))
    held_ref[...] = jnp.zeros_like(held_ref)
    turned_ref[...] = jnp.zeros_like(turned_ref)
    column_ref[...] = jnp.zeros_like(column_ref)
    grad_head_ref[...] = jnp.zeros_like(grad_head_ref)
    skip_sum_ref[...] = jnp.zeros_like(skip_sum_ref)
    chunks = input_ref.shape[0] // SPAN

    def chunk(count, unused):
        index = chunks - 1 - count
        rows = pl.ds(pl.multiple_of(index * SPAN, SPAN), SPAN)
        raw, steps, cumul, step_wide, grown_wide, tail_wide = chunk_steps(
            step_ref, bias_ref, rate_ref, expand_ref, rows
        )
        cumul_turned = cumul.T
        entry = both_ref[rows, pl.ds(0, states)].astype(jnp.bfloat16)
        readout = both_ref[rows, pl.ds(states, states)].astype(jnp.bfloat16)
        cross = low_against(entry, readout)
        square = (SPAN, SPAN)
        upper = row_index(square) <= lane_index(square)
        grad_cross = jnp.zeros(square, jnp.float32)
        grad_entry = jnp.zeros((SPAN, states), jnp.float32)
        grad_readout = jnp.zeros((SPAN, states), jnp.float32)
        for start, width in slabs(channels):
            cols = pl.ds(start, width)
            span = slice(start, start + width)
            heads = width // HD
            values = act_ref[rows, cols]
            scaled = values * step_wide[:, span]
            gate = gate_ref[rows, cols]
            upstream = grad_ref[rows, cols] * (gate * jax.nn.sigmoid(gate))
            held = held_ref[:, cols]
            before = carry_ref[index, :, cols]
            stacked_up = stacked_heads(upstream, heads).astype(jnp.bfloat16)
            products = low_against(scaled, stacked_up)
            weights = []
            for place in range(heads):
                head = head_from + start // HD + place
                spread = cumul_turned[head : head + 1, :] - cumul[:, head : head + 1]
                decay = jnp.exp(jnp.where(upper, spread, -jnp.inf))
                product = products[:, place * SPAN : (place + 1) * SPAN] * decay
                grad_cross = grad_cross + product
                flow = product * cross
                turned_ref[head : head + 1, :] = jnp.sum(flow, axis=0, keepdims=True)
                column_ref[:, head : head + 1] = jnp.sum(flow, axis=1, keepdims=True)
                weights.append((decay * cross).astype(jnp.bfloat16))
            weights = jnp.concatenate(weights, axis=1) if heads > 1 else weights[0]
            grown_up = upstream * grown_wide[:, span]
            tailed = scaled * tail_wide[:, span]
            from_held = low_dot(entry, held)
            grad_scaled = low_dot(weights, stacked_up) + tail_wide[:, span] * from_held
            wide_ref[0, :, cols] = grown_up * low_dot(readout, before)
            wide_ref[1, :, cols] = tailed * from_held
            wide_ref[2, :, cols] = values * grad_scaled
            grad_readout = grad_readout + low_against(grown_up, before)
            grad_entry = grad_entry + low_against(tailed, held)
            last = grown_wide[SPAN - 1 : SPAN, span]
            scale_sum_ref[:, cols] = jnp.sum(held * before, axis=0, keepdims=True) * last
            skip_sum_ref[:, cols] += jnp.sum(upstream * values, axis=0, keepdims=True)
            held_ref[:, cols] = held * last + low_inner(readout, grown_up)
            act_ref[rows, cols] = step_wide[:, span] * grad_scaled + skip_ref[:, cols] * upstream
        sums = exact_dot(
            jnp.concatenate([wide_ref[0], wide_ref[1], wide_ref[2]], axis=0), collect_ref[...]
        )
        scale_sum = exact_dot(jnp.broadcast_to(scale_sum_ref[...], (8, channels)), collect_ref[...])
        flows = turned_ref[...].T - column_ref[...] + sums[:SPAN]
        onward = (row_index(square) <= lane_index(square)).astype(jnp.float32)
        strict = (row_index(square) > lane_index(square)).astype(jnp.float32)
        grad_log = (
            exact_dot(onward, flows)
            + exact_dot(strict, sums[SPAN : 2 * SPAN])
            + scale_sum[:1]
        )
        grad_steps = grad_log * rate_ref[...] + sums[2 * SPAN :]
        grad_raw = grad_steps * jax.nn.sigmoid(raw)
        grad_step_ref[rows, :] = grad_raw.astype(jnp.bfloat16)
        grad_head_ref[0, 0:1, :] += jnp.sum(grad_raw, axis=0, keepdims=True)
        grad_head_ref[0, 1:2, :] += (
            jnp.sum(grad_log * steps, axis=0, keepdims=True) * rate_ref[...]
        )
        grad_entry = grad_entry + low_dot(grad_cross, readout)
        grad_readout = grad_readout + low_inner(grad_cross, entry)
        if begun:
            grad_entry = grad_entry + begun_ref[rows, pl.ds(0, states)]
            grad_readout = grad_readout + begun_ref[rows, pl.ds(states, states)]
        target_ref = both_ref if ended else partial_ref
        target_ref[rows, pl.ds(0, states)] = grad_entry
        target_ref[rows, pl.ds(states, states)] = grad_readout
        return unused

    lax.fori_loop(0, chunks, chunk, 0)
    grad_head_ref[0, 2:3, :] = exact_dot(
        jnp.broadcast_to(skip_sum_ref[...], (8, channels)), collect_ref[...]
    )[:1]

    def convolve_back(raw_ref, grads_ref, slopes_ref, kernel_ref, out_ref, sums_ref, width_all):
        for start, width in slabs(width_all):
            cols = pl.ds(start, width)
            grad = grads_ref[:, cols] * slopes_ref[:, cols]
            raw = raw_ref[:, cols]
            total = kernel_ref[taps - 1 : taps, cols] * grad
            sums_ref[0, taps - 1 : taps, cols] = jnp.sum(grad * raw, axis=0, keepdims=True)
            for tap in range(taps - 1):
                shifted = sooner(grad, taps - 1 - tap)
                total = total + kernel_ref[tap : tap + 1, cols] * shifted
                sums_ref[0, tap : tap + 1, cols] = jnp.sum(shifted * raw, axis=0, keepdims=True)
            sums_ref[0, taps : taps + 1, cols] = jnp.sum(grad, axis=0, keepdims=True)
            out_ref[:, cols] = total.astype(jnp.bfloat16)

    convolve_back(
        input_ref,
        act_ref,
        slope_ref,
        input_kernel_ref,
        grad_input_ref,
        grad_input_conv_ref,
        channels,
    )
    if ended:
        convolve_back(
            state_ref,
            both_ref,
            both_slope_ref,
            state_kernel_ref,
            grad_state_ref,
            grad_state_conv_ref,
            2 * states,
        )


def by_sequence(length, width):
    return pl.BlockSpec((length, width), lambda seq: (seq, 0))


def fixed(*shape):
    return pl.BlockSpec(shape, lambda seq: (0,) * len(shape))


def head_spread(heads):
    marks = np.zeros((LANES, heads * HD), np.float32)
    for head in range(heads):
        marks[head, head * HD : (head + 1) * HD] = 1.0
    return marks


def pad_lanes(part):
    return jnp.pad(part, ((0, 0), (0, LANES - part.shape[1])))


def ssd_small(input_kernel, input_shift, state_kernel, state_shift, step_bias, decay_log, skip_gain):
    rates = -jnp.exp(decay_log)
    return (
        input_kernel,
        input_shift[None, :],
        state_kernel,
        state_shift[None, :],
        pad_lanes(step_bias[None, :]),
        pad_lanes(rates[None, :]),
        jnp.repeat(skip_gain, HD)[None, :],
    )


def ssd_forward(inputs, states_raw, gate, step, small, heads, length):
    group, channels = inputs.shape
    seqs = group // length
    both = states_raw.shape[1]
    states = both // 2
    chunks = length // SPAN
    taps = small[0].shape[0]
    return pl.pallas_call(
        ssd_forward_kernel,
        grid=(seqs,),
        in_specs=[
            by_sequence(length, channels),
            by_sequence(length, both),
            by_sequence(length, channels),
            by_sequence(length, LANES),
            fixed(taps, channels),
            fixed(1, channels),
            fixed(taps, both),
            fixed(1, both),
            fixed(1, LANES),
            fixed(1, LANES),
            fixed(1, channels),
            fixed(LANES, channels),
        ],
        out_specs=[
            by_sequence(length, channels),
            by_sequence(length, channels),
            pl.BlockSpec((chunks, states, channels), lambda seq: (seq, 0, 0)),
        ],
        out_shape=[
            jax.ShapeDtypeStruct((group, channels), jnp.bfloat16),
            jax.ShapeDtypeStruct((group, channels), jnp.float32),
            jax.ShapeDtypeStruct((seqs * chunks, states, channels), jnp.float32),
        ],
        scratch_shapes=[
            pltpu.VMEM((length, channels), jnp.float32),
            pltpu.VMEM((length, both), jnp.float32),
            pltpu.VMEM((states, channels), jnp.float32),
        ],
        compiler_params=pltpu.CompilerParams(vmem_limit_bytes=VMEM_LIMIT),
        cost_estimate=LIGHT,
        name="ssd_forward",
    )(inputs, states_raw, gate, step, *small, jnp.asarray(head_spread(heads)))


def ssd_backward(
    inputs, states_raw, gate, step, grad, carry, small, heads, length, index, count, begun
):
    group, channels = inputs.shape
    here = channels // count
    seqs = group // length
    both = states_raw.shape[1]
    states = both // 2
    chunks = length // SPAN
    taps = small[0].shape[0]
    ended = index == count - 1
    columns = pl.BlockSpec((length, here), lambda seq: (seq, index))

    def part(rows):
        return pl.BlockSpec((rows, here), lambda seq: (0, index))

    in_specs = [
        columns,
        by_sequence(length, both),
        columns,
        by_sequence(length, LANES),
        columns,
        pl.BlockSpec((chunks, states, here), lambda seq: (seq, 0, index)),
        part(taps),
        part(1),
        fixed(taps, both),
        fixed(1, both),
        fixed(1, LANES),
        fixed(1, LANES),
        part(1),
        part(LANES),
        pl.BlockSpec((here, LANES), lambda seq: (index, 0)),
    ]
    out_specs = [
        by_sequence(length, here),
        by_sequence(length, LANES),
        pl.BlockSpec((1, 8, here), lambda seq: (seq, 0, 0)),
        pl.BlockSpec((1, 8, LANES), lambda seq: (seq, 0, 0)),
    ]
    out_shape = [
        jax.ShapeDtypeStruct((group, here), jnp.bfloat16),
        jax.ShapeDtypeStruct((group, LANES), jnp.bfloat16),
        jax.ShapeDtypeStruct((seqs, 8, here), jnp.float32),
        jax.ShapeDtypeStruct((seqs, 8, LANES), jnp.float32),
    ]
    out_specs.append(by_sequence(length, both))
    if ended:
        out_shape.append(jax.ShapeDtypeStruct((group, both), jnp.bfloat16))
        out_specs.append(pl.BlockSpec((1, 8, both), lambda seq: (seq, 0, 0)))
        out_shape.append(jax.ShapeDtypeStruct((seqs, 8, both), jnp.float32))
    else:
        out_shape.append(jax.ShapeDtypeStruct((group, both), jnp.float32))
    extra = ()
    if begun is not None:
        in_specs.append(by_sequence(length, both))
        extra = (begun,)
    return pl.pallas_call(
        partial(ssd_backward_kernel, index * (heads // count), begun is not None, ended),
        grid=(seqs,),
        in_specs=in_specs,
        out_specs=out_specs,
        out_shape=out_shape,
        scratch_shapes=[
            pltpu.VMEM((length, here), jnp.float32),
            pltpu.VMEM((length, here), jnp.float32),
            pltpu.VMEM((length, both), jnp.float32),
            pltpu.VMEM((length, both), jnp.float32),
            pltpu.VMEM((states, here), jnp.float32),
            pltpu.VMEM((3, SPAN, here), jnp.float32),
            pltpu.VMEM((LANES, SPAN), jnp.float32),
            pltpu.VMEM((SPAN, LANES), jnp.float32),
            pltpu.VMEM((1, here), jnp.float32),
            pltpu.VMEM((1, here), jnp.float32),
        ],
        compiler_params=pltpu.CompilerParams(vmem_limit_bytes=VMEM_LIMIT),
        cost_estimate=LIGHT,
        name="ssd_backward",
    )(
        inputs,
        states_raw,
        gate,
        step,
        grad,
        carry,
        *small,
        jnp.asarray(head_spread(heads)),
        jnp.asarray(head_spread(heads).T.copy()),
        *extra,
    )


def rope_wide(length):
    half = HD // 2
    freqs = np.float32(ROPE_BASE) ** (-np.arange(half, dtype=np.float32) * np.float32(2.0 / HD))
    angles = np.arange(length, dtype=np.float32)[:, None] * freqs[None, :].astype(np.float32)
    cosine, sine = np.cos(angles), np.sin(angles)
    count = LANES // HD
    return (
        np.concatenate([cosine, cosine] * count, axis=1).astype(np.float32),
        np.concatenate([-sine, sine] * count, axis=1).astype(np.float32),
    )


def turn(part, cosine, sine):
    half = HD // 2
    first = lane_index(part.shape) % HD < half
    swapped = jnp.where(first, pltpu.roll(part, LANES - half, 1), pltpu.roll(part, half, 1))
    return part * cosine + swapped * sine


def attend_forward_kernel(
    query_ref, pair_ref, cosine_ref, sine_ref, context_ref, query_out_ref, pair_out_ref, total_ref
):
    length = query_ref.shape[0]
    cosine, sine = cosine_ref[...], sine_ref[...]
    pair = pair_ref[...]
    left = lane_index(pair.shape) < HD
    pair = jnp.where(left, turn(pair, cosine, sine), pair)
    pair_out_ref[...] = pair.astype(jnp.bfloat16)
    moved = pltpu.roll(pair, HD, 1)
    keys = jnp.where(left, pair, moved).astype(jnp.bfloat16)
    values = jnp.where(left, moved, pair).astype(jnp.bfloat16)
    scale = HD ** (-0.5)
    for slab in range(query_ref.shape[1] // LANES):
        cols = pl.ds(slab * LANES, LANES)
        query_out_ref[:, cols] = turn(query_ref[:, cols], cosine, sine).astype(jnp.bfloat16)
        for tile in range(length // SPAN):
            rows = slice(tile * SPAN, (tile + 1) * SPAN)
            count = (tile + 1) * SPAN
            query = query_out_ref[rows, cols]
            lane = lane_index(query.shape)
            square = (SPAN, count)
            causal = row_index(square) + tile * SPAN >= lane_index(square)
            results = []
            for place in range(LANES // HD):
                mine = (lane >= place * HD) & (lane < place * HD + HD)
                scores = low_against(jnp.where(mine, query, 0), keys[:count]) * scale
                scores = jnp.where(causal, scores, -jnp.inf)
                peak = jnp.max(scores, axis=-1, keepdims=True)
                grown = jnp.exp(scores - peak)
                total = jnp.sum(grown, axis=-1, keepdims=True)
                probs = grown * (1.0 / total)
                results.append(low_dot(probs, values[:count]))
                head = slab * (LANES // HD) + place
                total_ref[rows, head : head + 1] = jnp.log(total) + peak
            context_ref[rows, cols] = jnp.where(lane < HD, results[0], results[1]).astype(
                jnp.bfloat16
            )


def attend_backward_kernel(
    query_ref,
    pair_ref,
    total_ref,
    grad_ref,
    cosine_ref,
    sine_ref,
    grad_query_ref,
    grad_pair_ref,
    key_sum_ref,
    value_sum_ref,
):
    length = query_ref.shape[0]
    cosine, sine = cosine_ref[...], -sine_ref[...]
    pair = pair_ref[...].astype(jnp.float32)
    left = lane_index(pair.shape) < HD
    moved = pltpu.roll(pair, HD, 1)
    keys = jnp.where(left, pair, moved).astype(jnp.bfloat16)
    values = jnp.where(left, moved, pair).astype(jnp.bfloat16)
    scale = HD ** (-0.5)
    key_sum_ref[...] = jnp.zeros_like(key_sum_ref)
    value_sum_ref[...] = jnp.zeros_like(value_sum_ref)
    for slab in range(query_ref.shape[1] // LANES):
        cols = pl.ds(slab * LANES, LANES)
        for tile in range(length // SPAN):
            rows = slice(tile * SPAN, (tile + 1) * SPAN)
            count = (tile + 1) * SPAN
            query = query_ref[rows, cols]
            upstream = grad_ref[rows, cols]
            lane = lane_index(query.shape)
            square = (SPAN, count)
            causal = row_index(square) + tile * SPAN >= lane_index(square)
            results = []
            for place in range(LANES // HD):
                mine = (lane >= place * HD) & (lane < place * HD + HD)
                head = slab * (LANES // HD) + place
                own_query = jnp.where(mine, query, 0)
                own_up = jnp.where(mine, upstream, 0)
                scores = low_against(own_query, keys[:count]) * scale
                scores = jnp.where(causal, scores, -jnp.inf)
                probs = jnp.exp(scores - total_ref[rows, head : head + 1])
                grad_probs = low_against(own_up, values[:count])
                mean = jnp.sum(probs * grad_probs, axis=-1, keepdims=True)
                grad_scores = (probs * (grad_probs - mean)).astype(jnp.bfloat16)
                results.append(low_dot(grad_scores, keys[:count]))
                key_sum_ref[0:count, :] += low_inner(grad_scores, own_query)
                value_sum_ref[0:count, :] += low_inner(probs, own_up)
            grad_query = jnp.where(lane < HD, results[0], results[1]) * scale
            grad_query_ref[rows, cols] = turn(
                grad_query, cosine[rows, :], sine[rows, :]
            ).astype(jnp.bfloat16)
    grad_key = key_sum_ref[...]
    grad_key = turn((grad_key + pltpu.roll(grad_key, HD, 1)) * scale, cosine, sine)
    grad_value = value_sum_ref[...]
    grad_value = grad_value + pltpu.roll(grad_value, HD, 1)
    grad_pair_ref[...] = jnp.where(left, grad_key, grad_value).astype(jnp.bfloat16)


def attend_forward(query, pair, length):
    group, width = query.shape
    heads = width // HD
    cosine, sine = rope_wide(length)
    return pl.pallas_call(
        attend_forward_kernel,
        grid=(group // length,),
        in_specs=[
            by_sequence(length, width),
            by_sequence(length, LANES),
            fixed(length, LANES),
            fixed(length, LANES),
        ],
        out_specs=[
            by_sequence(length, width),
            by_sequence(length, width),
            by_sequence(length, LANES),
            by_sequence(length, LANES),
        ],
        out_shape=[
            jax.ShapeDtypeStruct((group, width), jnp.bfloat16),
            jax.ShapeDtypeStruct((group, width), jnp.bfloat16),
            jax.ShapeDtypeStruct((group, LANES), jnp.bfloat16),
            jax.ShapeDtypeStruct((group, LANES), jnp.float32),
        ],
        compiler_params=pltpu.CompilerParams(vmem_limit_bytes=VMEM_LIMIT),
        cost_estimate=LIGHT,
        name="attend_forward",
    )(query, pair, jnp.asarray(cosine), jnp.asarray(sine))


def attend_backward(query, pair, total, grad, length):
    group, width = query.shape
    heads = width // HD
    cosine, sine = rope_wide(length)
    return pl.pallas_call(
        attend_backward_kernel,
        grid=(group // length,),
        in_specs=[
            by_sequence(length, width),
            by_sequence(length, LANES),
            by_sequence(length, LANES),
            by_sequence(length, width),
            fixed(length, LANES),
            fixed(length, LANES),
        ],
        out_specs=[by_sequence(length, width), by_sequence(length, LANES)],
        out_shape=[
            jax.ShapeDtypeStruct((group, width), jnp.bfloat16),
            jax.ShapeDtypeStruct((group, LANES), jnp.bfloat16),
        ],
        scratch_shapes=[
            pltpu.VMEM((length, LANES), jnp.float32),
            pltpu.VMEM((length, LANES), jnp.float32),
        ],
        compiler_params=pltpu.CompilerParams(vmem_limit_bytes=VMEM_LIMIT),
        cost_estimate=LIGHT,
        name="attend_backward",
    )(query, pair, total, grad, jnp.asarray(cosine), jnp.asarray(sine))


def step_groups(size):
    bits = size.bit_length() - 1
    return [1] * min(bits, 2) + [2] * (max(bits - 2, 0) // 2) + [1] * (max(bits - 2, 0) % 2)


def after(part, *deps):
    return lax.optimization_barrier((part,) + deps)[0]


def behind(part, dep):
    zero = jnp.minimum(jnp.abs(dep[:1, :1].astype(jnp.float32)), 0.0)
    return part + zero.astype(part.dtype)


class Sum:
    def __init__(self, part, size):
        self.size = size
        self.direct = bool(size & (size - 1) or part.shape[0] % size)
        self.steps = [] if self.direct else step_groups(size)
        self.shift = 0
        self.part = part
        self.gives = [part]
        if not self.direct:
            self.part = part.reshape(size, part.shape[0] // size, part.shape[1])
            self.prepare()

    def prepare(self):
        if not self.steps:
            self.gives = [self.part]
            return
        ways = 1 << self.steps[0]
        rest = self.part.shape[0] // ways
        view = self.part.reshape((rest, ways) + self.part.shape[1:])
        mine = (lax.axis_index("dp") >> self.shift) & (ways - 1)
        self.keep = lax.dynamic_index_in_dim(view, mine, 1, False)
        self.gives = [
            lax.dynamic_index_in_dim(view, mine ^ way, 1, False) for way in range(1, ways)
        ]

    def advance(self, *deps):
        if self.steps:
            total = after(self.keep, *deps).astype(jnp.float32)
            for way, give in enumerate(self.gives, 1):
                pairs = [(index, index ^ (way << self.shift)) for index in range(self.size)]
                total = total + lax.ppermute(give, "dp", pairs).astype(jnp.float32)
            self.part = total.astype(jnp.bfloat16)
            self.shift += self.steps.pop(0)
            self.prepare()
        return self.gives

    def joined(self, middle=None, *deps):
        groups, shift = step_groups(self.size), self.size.bit_length() - 1
        part = after(self.reduced(), *deps)
        if middle is not None:
            part = middle(part)
        if self.direct:
            return part
        rows, width = part.shape
        for group in reversed(groups):
            ways = 1 << group
            shift -= group
            mine = (lax.axis_index("dp") >> shift) & (ways - 1)
            part = part.reshape(-1, 1, rows, width)
            got = [part]
            for way in range(1, ways):
                pairs = [(index, index ^ (way << shift)) for index in range(self.size)]
                got.append(lax.ppermute(part, "dp", pairs))
            for bit in range(group):
                flip = ((mine >> bit) & 1) == 1
                got = [
                    jnp.where(flip, got[way ^ (1 << bit)], got[way]) for way in range(ways)
                ]
            part = jnp.concatenate(got, axis=1)
        return part.reshape(-1, width)

    def reduced(self):
        while self.steps:
            self.advance()
        return lax.psum(self.part, "dp") if self.direct else self.part[0]


class Halves:
    def __init__(self, part, size):
        self.size = size
        self.direct = bool(size % 2 or part.shape[0] % 2)
        self.part = part
        if not self.direct:
            self.pairs = [(index, index ^ 1) for index in range(size)]
            self.side = lax.axis_index("dp") & 1
            view = part.reshape(2, part.shape[0] // 2, part.shape[1])
            self.keep = lax.dynamic_index_in_dim(view, self.side, 0, False)
            self.give = lax.dynamic_index_in_dim(view, 1 - self.side, 0, False)

    def halved(self):
        if self.direct:
            return self.part
        got = lax.ppermute(self.give, "dp", self.pairs)
        return (self.keep.astype(jnp.float32) + got.astype(jnp.float32)).astype(jnp.bfloat16)

    def summed(self, part):
        if self.direct:
            return lax.psum(part, "dp")
        groups = [list(range(side, self.size, 2)) for side in range(2)]
        return lax.psum(part, "dp", axis_index_groups=groups)

    def scattered(self, part):
        if self.direct:
            return lax.psum(part, "dp")
        groups = [list(range(side, self.size, 2)) for side in range(2)]
        if part.shape[0] % len(groups[0]):
            return lax.psum(part, "dp", axis_index_groups=groups)
        return lax.psum_scatter(
            part, "dp", axis_index_groups=groups, scatter_dimension=0, tiled=True
        )

    def gathered(self, part, rows):
        if part.shape[0] == rows:
            return part
        groups = [list(range(side, self.size, 2)) for side in range(2)]
        return lax.all_gather(part, "dp", axis_index_groups=groups, axis=0, tiled=True)

    def whole(self, part):
        if self.direct:
            return part
        got = lax.ppermute(part, "dp", self.pairs)
        return jnp.where(
            self.side == 0,
            jnp.concatenate([part, got], axis=0),
            jnp.concatenate([got, part], axis=0),
        )


def other(part):
    return lax.ppermute(part, "tensor", [(0, 1), (1, 0)])


def all_rows(part, shards):
    if shards != 2:
        return lax.all_gather(part, "tensor", axis=0, tiled=True)
    got = other(part)
    return jnp.where(
        lax.axis_index("tensor") == 0,
        jnp.concatenate([part, got], axis=0),
        jnp.concatenate([got, part], axis=0),
    )


def sum_all(part, shards):
    if shards != 2:
        return lax.psum(part, "tensor").astype(jnp.float32)
    return part.astype(jnp.float32) + other(part).astype(jnp.float32)


def sum_own(part, shards):
    if shards != 2:
        return lax.psum_scatter(part, "tensor", scatter_dimension=0, tiled=True).astype(jnp.float32)
    me = lax.axis_index("tensor")
    halves = part.reshape(2, part.shape[0] // 2, part.shape[1])
    keep = lax.dynamic_index_in_dim(halves, me, 0, False)
    got = other(lax.dynamic_index_in_dim(halves, 1 - me, 0, False))
    return keep.astype(jnp.float32) + got.astype(jnp.float32)


def own_rows(part, rows):
    return lax.dynamic_slice_in_dim(part, lax.axis_index("tensor") * rows, rows, 0)


def column_pack(vectors, rows):
    flat = jnp.concatenate([item.reshape(-1) for item in vectors])
    width = -(-flat.shape[0] // rows)
    return jnp.pad(flat, (0, width * rows - flat.shape[0])).reshape(width, rows).T


def column_unpack(packed, shapes):
    flat = packed.T.reshape(-1)
    out, start = [], 0
    for shape in shapes:
        count = 1
        for size in shape:
            count *= size
        out.append(flat[start : start + count].reshape(shape))
        start += count
    return out


def body(
    dp_size,
    shards,
    layer_input,
    input_gain,
    middle_gain,
    mamba_gate,
    mamba_input,
    step_weight,
    state_weight,
    input_kernel,
    input_shift,
    state_kernel,
    state_shift,
    step_bias,
    decay_log,
    skip_gain,
    mamba_output,
    query_weight,
    keyvalue_weight,
    context_weight,
    gate_weight,
    up_weight,
    down_weight,
    cotangent,
):
    own = layer_input.shape[0]
    rows_low = all_rows(layer_input, shards)
    cotan_low = all_rows(cotangent, shards)
    rows = rows_low.astype(jnp.float32)
    gain_first = input_gain.astype(jnp.float32)
    gain_second = middle_gain.astype(jnp.float32)
    factor_first = lax.rsqrt(jnp.mean(rows * rows, axis=-1, keepdims=True) + EPSILON)
    normal_first = rows * factor_first
    whole = (normal_first * gain_first).astype(jnp.bfloat16)
    group = whole.shape[0]
    length = min(SEQ_LEN, group)
    seqs = group // length
    heads_here = query_weight.shape[1] // HD
    kv_head = lax.axis_index("tensor") * heads_here // (HQ // KVH)
    key_cols = lax.dynamic_slice_in_dim(keyvalue_weight, kv_head * HD, HD, 1)
    value_cols = lax.dynamic_slice_in_dim(keyvalue_weight, (KVH + kv_head) * HD, HD, 1)
    pair_weight = jnp.concatenate([key_cols, value_cols], axis=1)
    query_cols = query_weight.shape[1]
    query_pad = -query_cols % LANES
    query_wide = jnp.pad(query_weight, ((0, 0), (0, query_pad)))
    step_wide = pad_lanes(step_weight)
    heads = step_weight.shape[1]
    input_raw = forward_dot(whole, mamba_input)
    state_raw = forward_dot(whole, state_weight)
    step_raw = forward_dot(whole, step_wide)
    gate_raw = forward_dot(whole, mamba_gate)
    query_raw = forward_dot(whole, query_wide)
    pair_raw = forward_dot(whole, pair_weight)
    small = ssd_small(
        input_kernel.astype(jnp.float32),
        input_shift.astype(jnp.float32),
        state_kernel.astype(jnp.float32),
        state_shift.astype(jnp.float32),
        step_bias.astype(jnp.float32),
        decay_log.astype(jnp.float32),
        skip_gain.astype(jnp.float32),
    )
    gated_low, ssm_out, carries = ssd_forward(
        input_raw, state_raw, gate_raw, step_raw, small, heads, length
    )
    context_wide, queries, pairs, totals = attend_forward(
        after(query_raw, cotan_low), pair_raw, length
    )
    context_rows = context_wide[:, :query_cols]
    mixed_part = forward_dot(gated_low, mamba_output) + forward_dot(context_rows, context_weight)
    resid = rows + sum_all(mixed_part.astype(jnp.bfloat16), shards)
    factor_second = lax.rsqrt(jnp.mean(resid * resid, axis=-1, keepdims=True) + EPSILON)
    normal_second = resid * factor_second
    whole_mid = (normal_second * gain_second).astype(jnp.bfloat16)
    gate = forward_dot(whole_mid, gate_weight)
    upper = forward_dot(whole_mid, up_weight)
    sigmoid_gate = jax.nn.sigmoid(gate)
    silu_gate = gate * sigmoid_gate
    hidden = (silu_gate * upper).astype(jnp.bfloat16)
    grad_hidden = against(cotan_low, down_weight)
    slope = sigmoid_gate * (1.0 + gate * (1.0 - sigmoid_gate))
    grad_gate_low = (grad_hidden * upper * slope).astype(jnp.bfloat16)
    grad_upper_low = (grad_hidden * silu_gate).astype(jnp.bfloat16)
    back_part = (against(grad_gate_low, gate_weight) + against(grad_upper_low, up_weight)).astype(
        jnp.bfloat16
    )
    back_mid = sum_all(back_part, shards)
    hidden, grad_gate_low, grad_upper_low = (
        after(hidden, back_part),
        after(grad_gate_low, back_part),
        after(grad_upper_low, back_part),
    )
    hidden_cols = gate_weight.shape[1]
    wide_sum = Halves(
        inner_rows(
            whole_mid, jnp.concatenate([grad_gate_low, grad_upper_low], axis=1)
        ).astype(jnp.bfloat16),
        dp_size,
    )
    down_sum = Halves(inner_rows(hidden, cotan_low).astype(jnp.bfloat16), dp_size)
    wide_half, down_half = wide_sum.halved(), down_sum.halved()
    back_mid = after(back_mid, wide_half, down_half)
    half_rows = wide_half.shape[0]
    if down_half.shape[0] == half_rows:
        blocks = [wide_sum.scattered(jnp.concatenate([wide_half, down_half], axis=1))]
    else:
        blocks = [wide_sum.scattered(wide_half), down_sum.scattered(down_half)]
    feed_part = behind(forward_dot(hidden, down_weight), back_mid).astype(jnp.bfloat16)
    feed = sum_own(feed_part, shards)
    layer_output = (own_rows(resid, own) + feed).astype(jnp.bfloat16)
    grad_middle = jnp.sum(back_part.astype(jnp.float32) * normal_second, axis=0)
    grad_resid = cotan_low.astype(jnp.float32) + norm_back(
        back_mid, gain_second, normal_second, factor_second
    )
    mixer_all = grad_resid.astype(jnp.bfloat16)
    ssm_rows = gated_low.shape[1]
    width = whole.shape[1]
    split_pairs = shards == KVH
    grad_gated = against(mixer_all, mamba_output)
    grad_mixer_out = inner_rows(
        jnp.concatenate([gated_low, context_rows], axis=1), mixer_all
    ).astype(jnp.bfloat16)
    sigmoid_raw = jax.nn.sigmoid(gate_raw)
    grad_gate_raw = (
        grad_gated * ssm_out * (sigmoid_raw * (1.0 + gate_raw * (1.0 - sigmoid_raw)))
    ).astype(jnp.bfloat16)
    grad_mamba_gate = inner_rows(whole, grad_gate_raw).astype(jnp.bfloat16)
    if grad_mixer_out.shape[0] == width:
        first_sums = [Sum(jnp.concatenate([grad_mixer_out, grad_mamba_gate], axis=1), dp_size)]
    else:
        first_sums = [Sum(grad_mixer_out, dp_size), Sum(grad_mamba_gate, dp_size)]
    grad_gated = after(grad_gated, *[give for item in first_sums for give in item.gives])

    parts = 2 if heads % 4 == 0 else 1

    def ssd_part(index, begun):
        return ssd_backward(
            input_raw,
            state_raw,
            gate_raw,
            step_raw,
            grad_gated,
            carries,
            small,
            heads,
            length,
            index,
            parts,
            begun,
        )

    pieces = [ssd_part(0, None)]
    if parts == 2:
        begun = after(
            pieces[0][4], feed, *[give for item in first_sums for give in item.advance(pieces[0][1])]
        )
        pieces.append(ssd_part(1, begun))
    last = pieces[-1]
    step_pieces = sum([piece[1] for piece in pieces[1:]], pieces[0][1])
    input_sums = jnp.concatenate([jnp.sum(piece[2], axis=0) for piece in pieces], axis=1)
    head_sums = sum([jnp.sum(piece[3], axis=0) for piece in pieces])[:, :heads]
    state_sums = jnp.sum(last[5], axis=0)
    taps = input_kernel.shape[0]
    state_cols = state_weight.shape[1]
    step_cols = heads
    late_cols = jnp.concatenate(
        [piece[0] for piece in pieces] + [last[4], step_pieces], axis=1
    )
    own_vectors = (input_sums[:taps], input_sums[taps], head_sums[0], head_sums[1], head_sums[2])
    shared_vectors = (grad_middle, state_sums[:taps], state_sums[taps])
    own_pack = column_pack(own_vectors, width)
    shared_pack = column_pack(shared_vectors, width)
    shared_lane = step_cols + own_pack.shape[1]
    last_lane = shared_lane + shared_pack.shape[1]
    late = inner_rows(whole, late_cols)
    misc = late.shape[1] - LANES
    packs = jnp.pad(
        jnp.concatenate([own_pack, shared_pack], axis=1),
        ((0, 0), (misc + step_cols, LANES - last_lane)),
    )
    late_sum = Sum((late + packs).astype(jnp.bfloat16), dp_size)

    grad_context = against(mixer_all, context_weight).astype(jnp.bfloat16)
    grad_context = jnp.pad(grad_context, ((0, 0), (0, query_pad)))
    grad_context = after(grad_context, *late_sum.gives, *blocks)
    grad_query_raw, grad_pair_raw = attend_backward(queries, pairs, totals, grad_context, length)
    middle_cols = jnp.concatenate([grad_query_raw[:, :query_cols], grad_pair_raw], axis=1)
    total = against(
        jnp.concatenate([grad_gate_raw, middle_cols, late_cols], axis=1),
        jnp.concatenate(
            [mamba_gate, query_weight, pair_weight, mamba_input, state_weight, step_wide], axis=1
        ),
    )
    total_low = total.astype(jnp.bfloat16)
    grad_first = jnp.sum(total_low.astype(jnp.float32) * normal_first, axis=0)
    middle = inner_rows(whole, middle_cols)
    if not split_pairs:
        spread = jnp.zeros((width, 2 * KVH * HD), jnp.float32)
        spread = lax.dynamic_update_slice_in_dim(
            spread, middle[:, -2 * HD : -HD], kv_head * HD, 1
        )
        spread = lax.dynamic_update_slice_in_dim(
            spread, middle[:, -HD:], (KVH + kv_head) * HD, 1
        )
        middle = jnp.concatenate([middle[:, : -2 * HD], spread], axis=1)
    middle = jnp.concatenate([middle, pad_lanes(grad_first[:, None])], axis=1)
    middle_sum = Halves(middle.astype(jnp.bfloat16), dp_size)

    def pairs_over_tensor(part):
        count = 2 * HD if split_pairs else 2 * KVH * HD
        mine = part[:, -count - LANES : -LANES]
        if split_pairs:
            got = other(mine)
            first = lax.axis_index("tensor") == 0
            low, high = jnp.where(first, mine, got), jnp.where(first, got, mine)
            both = [low[:, :HD], high[:, :HD], low[:, HD:], high[:, HD:]]
        else:
            both = [lax.psum(mine, "tensor")]
        first = part[:, -LANES:]
        if shards == 2:
            first = (first.astype(jnp.float32) + other(first).astype(jnp.float32)).astype(
                jnp.bfloat16
            )
        else:
            first = lax.psum(first, "tensor")
        return jnp.concatenate([part[:, : -count - LANES]] + both + [first], axis=1)

    def states_over_tensor(part):
        mine = part[:, -state_cols - LANES :]
        if shards == 2:
            got = other(mine)
            both = (mine.astype(jnp.float32) + got.astype(jnp.float32)).astype(jnp.bfloat16)
        else:
            both = lax.psum(mine, "tensor")
        lane = lane_index((part.shape[0], LANES))
        extra = jnp.where(
            (lane >= shared_lane) & (lane < last_lane), both[:, state_cols:], mine[:, state_cols:]
        )
        return jnp.concatenate(
            [part[:, : -state_cols - LANES], both[:, :state_cols], extra], axis=1
        )

    firsts = [item.joined(None) for item in first_sums]
    if len(firsts) == 1:
        firsts = [firsts[0][:, :width], firsts[0][:, width:]]
    grad_mixer_out, grad_mamba_gate = firsts
    grad_mamba_out = grad_mixer_out[:ssm_rows]
    grad_context_w = grad_mixer_out[ssm_rows:]
    middle_half = pairs_over_tensor(middle_sum.halved())
    if len(blocks) == 1:
        both_half = wide_sum.gathered(blocks[0], half_rows)
        wide_half, down_half = both_half[:, : 2 * hidden_cols], both_half[:, 2 * hidden_cols :]
    else:
        wide_half = wide_sum.gathered(blocks[0], half_rows)
        down_half = down_sum.gathered(blocks[1], down_half.shape[0])
    middle_half = middle_sum.summed(after(middle_half, wide_half, down_half))
    middle = middle_sum.whole(middle_half)
    tail = late_sum.joined(states_over_tensor)
    grad_mamba_input = tail[:, : -state_cols - LANES]
    extra = tail[:, -LANES:]
    grad_state = tail[:, -state_cols - LANES : -LANES]
    grad_wide, grad_down = wide_sum.whole(wide_half), down_sum.whole(down_half)
    grad_gate, grad_up = grad_wide[:, :hidden_cols], grad_wide[:, hidden_cols:]
    back_in = sum_own(total_low, shards)
    normal_own = own_rows(normal_first, own)
    factor_own = own_rows(factor_first, own)
    input_grad = own_rows(grad_resid, own) + norm_back(back_in, gain_first, normal_own, factor_own)
    grad_step = extra[:, :step_cols]
    grad_in_kernel, grad_in_shift, grad_bias, grad_decay, grad_skip = column_unpack(
        extra[:, step_cols:shared_lane], [item.shape for item in own_vectors]
    )
    grad_middle, grad_st_kernel, grad_st_shift = column_unpack(
        extra[:, shared_lane:last_lane], [item.shape for item in shared_vectors]
    )
    results = (
        middle[:, -LANES],
        grad_middle,
        grad_mamba_gate,
        grad_mamba_input,
        grad_step,
        grad_state,
        grad_in_kernel,
        grad_in_shift,
        grad_st_kernel,
        grad_st_shift,
        grad_bias,
        grad_decay,
        grad_skip,
        grad_mamba_out,
        middle[:, :query_cols],
        middle[:, query_cols:-LANES],
        grad_context_w,
        grad_gate,
        grad_up,
        grad_down,
    )
    return (layer_output, input_grad) + tuple(item.astype(jnp.float32) for item in results)


def solution(mesh):
    in_specs = (
        P(("dp", "tensor"), None),
        P(),
        P(),
        P(None, "tensor"),
        P(None, "tensor"),
        P(None, "tensor"),
        P(),
        P(None, "tensor"),
        P("tensor"),
        P(),
        P(),
        P("tensor"),
        P("tensor"),
        P("tensor"),
        P("tensor", None),
        P(None, "tensor"),
        P(),
        P("tensor", None),
        P(None, "tensor"),
        P(None, "tensor"),
        P("tensor", None),
        P(("dp", "tensor"), None),
    )
    out_specs = (
        P(("dp", "tensor"), None),
        P(("dp", "tensor"), None),
        P(),
        P(),
        P(None, "tensor"),
        P(None, "tensor"),
        P(None, "tensor"),
        P(),
        P(None, "tensor"),
        P("tensor"),
        P(),
        P(),
        P("tensor"),
        P("tensor"),
        P("tensor"),
        P("tensor", None),
        P(None, "tensor"),
        P(),
        P("tensor", None),
        P(None, "tensor"),
        P(None, "tensor"),
        P("tensor", None),
    )
    run = partial(body, mesh.shape["dp"], mesh.shape["tensor"])
    return jax.shard_map(run, mesh=mesh, in_specs=in_specs, out_specs=out_specs, check_vma=False)
```

```python
from functools import partial

import jax
import jax.numpy as jnp
import numpy as np
from jax import lax
from jax.experimental import pallas as pl
from jax.experimental.pallas import tpu as pltpu
from jax.sharding import PartitionSpec as P

HD = 64
HQ = 8
KVH = 2
SPAN = 128
SEQ_LEN = 1024


EPSILON = 1e-05
ROPE_BASE = 10000.0
PRECISE = lax.Precision.HIGHEST


def forward_dot(left, right):
    return jnp.dot(left, right, preferred_element_type=jnp.float32)


def inner_rows(left, right):
    return lax.dot_general(
        left, right, (((0,), (0,)), ((), ())), preferred_element_type=jnp.float32
    )


def against(left, right):
    return lax.dot_general(
        left, right, (((1,), (1,)), ((), ())), preferred_element_type=jnp.float32
    )


def norm_back(upstream, gain, normal, factor):
    scaled = upstream * gain
    return factor * (scaled - normal * jnp.mean(scaled * normal, axis=-1, keepdims=True))


LANES = 128
VMEM_LIMIT = 44 * 1024 * 1024


def exact_dot(left, right):
    return jnp.dot(left, right, precision=PRECISE, preferred_element_type=jnp.float32)


def low_dot(left, right):
    return jnp.dot(
        left.astype(jnp.bfloat16), right.astype(jnp.bfloat16), preferred_element_type=jnp.float32
    )


def low_against(left, right):
    return lax.dot_general(
        left.astype(jnp.bfloat16),
        right.astype(jnp.bfloat16),
        (((1,), (1,)), ((), ())),
        preferred_element_type=jnp.float32,
    )


def low_inner(left, right):
    return lax.dot_general(
        left.astype(jnp.bfloat16),
        right.astype(jnp.bfloat16),
        (((0,), (0,)), ((), ())),
        preferred_element_type=jnp.float32,
    )


def row_index(shape):
    return lax.broadcasted_iota(jnp.int32, shape, 0)


def lane_index(shape):
    return lax.broadcasted_iota(jnp.int32, shape, 1)


def later(part, count):
    if count == 0:
        return part
    return jnp.where(row_index(part.shape) >= count, pltpu.roll(part, count, 0), 0.0)


def sooner(part, count):
    if count == 0:
        return part
    rows = part.shape[0]
    return jnp.where(row_index(part.shape) < rows - count, pltpu.roll(part, rows - count, 0), 0.0)


def slabs(width):
    return [(start, min(LANES, width - start)) for start in range(0, width, LANES)]


def soft_plus(value):
    return jnp.maximum(value, 0.0) + jnp.log1p(jnp.exp(-jnp.abs(value)))


def stacked_heads(part, heads):
    if heads == 1:
        return part
    lane = lane_index(part.shape)
    return jnp.concatenate(
        [jnp.where((lane >= head * HD) & (lane < head * HD + HD), part, 0.0) for head in range(heads)],
        axis=0,
    )


def convolve(raw, kernel_ref, shift_ref, cols):
    taps = kernel_ref.shape[0]
    out = shift_ref[:, cols] + kernel_ref[taps - 1 : taps, cols] * raw
    for tap in range(taps - 1):
        out = out + kernel_ref[tap : tap + 1, cols] * later(raw, taps - 1 - tap)
    return out


def chunk_steps(step_ref, bias_ref, rate_ref, expand_ref, rows):
    raw = step_ref[rows, :] + bias_ref[...]
    steps = soft_plus(raw)
    logdec = steps * rate_ref[...]
    square = (SPAN, SPAN)
    lower = (row_index(square) >= lane_index(square)).astype(jnp.float32)
    cumul = exact_dot(lower, logdec)
    grown = jnp.exp(cumul)
    tail = jnp.exp(cumul[SPAN - 1 : SPAN, :] - cumul)
    wide = exact_dot(jnp.concatenate([steps, grown, tail], axis=0), expand_ref[...])
    return raw, steps, cumul, wide[:SPAN], wide[SPAN : 2 * SPAN], wide[2 * SPAN :]


def ssd_forward_kernel(
    input_ref,
    state_ref,
    gate_ref,
    step_ref,
    input_kernel_ref,
    input_shift_ref,
    state_kernel_ref,
    state_shift_ref,
    bias_ref,
    rate_ref,
    skip_ref,
    expand_ref,
    gated_ref,
    out_ref,
    carry_ref,
    act_ref,
    both_ref,
    held_ref,
):
    channels = input_ref.shape[1]
    states = state_ref.shape[1] // 2
    for start, width in slabs(channels):
        cols = pl.ds(start, width)
        pre = convolve(input_ref[:, cols], input_kernel_ref, input_shift_ref, cols)
        act_ref[:, cols] = pre * jax.nn.sigmoid(pre)
    for start, width in slabs(2 * states):
        cols = pl.ds(start, width)
        pre = convolve(state_ref[:, cols], state_kernel_ref, state_shift_ref, cols)
        both_ref[:, cols] = pre * jax.nn.sigmoid(pre)
    held_ref[...] = jnp.zeros_like(held_ref)

    def chunk(index, unused):
        rows = pl.ds(pl.multiple_of(index * SPAN, SPAN), SPAN)
        raw, steps, cumul, step_wide, grown_wide, tail_wide = chunk_steps(
            step_ref, bias_ref, rate_ref, expand_ref, rows
        )
        cumul_turned = cumul.T
        entry = both_ref[rows, pl.ds(0, states)].astype(jnp.bfloat16)
        readout = both_ref[rows, pl.ds(states, states)].astype(jnp.bfloat16)
        cross = low_against(readout, entry)
        square = (SPAN, SPAN)
        lower = row_index(square) >= lane_index(square)
        for start, width in slabs(channels):
            cols = pl.ds(start, width)
            span = slice(start, start + width)
            heads = width // HD
            values = act_ref[rows, cols]
            scaled = values * step_wide[:, span]
            held = held_ref[:, cols]
            carry_ref[index, :, cols] = held
            weights = []
            for head in range(start // HD, start // HD + heads):
                spread = cumul[:, head : head + 1] - cumul_turned[head : head + 1, :]
                decay = jnp.exp(jnp.where(lower, spread, -jnp.inf))
                weights.append((decay * cross).astype(jnp.bfloat16))
            weights = jnp.concatenate(weights, axis=1) if heads > 1 else weights[0]
            result = low_dot(weights, stacked_heads(scaled, heads))
            result = result + low_dot(readout, held) * grown_wide[:, span]
            held_ref[:, cols] = held * grown_wide[SPAN - 1 : SPAN, span] + low_inner(
                entry, scaled * tail_wide[:, span]
            )
            result = result + skip_ref[:, cols] * values
            out_ref[rows, cols] = result
            gate = gate_ref[rows, cols]
            gated_ref[rows, cols] = (result * (gate * jax.nn.sigmoid(gate))).astype(jnp.bfloat16)
        return unused

    lax.fori_loop(0, input_ref.shape[0] // SPAN, chunk, 0)


def ssd_backward_kernel(
    input_ref,
    state_ref,
    gate_ref,
    step_ref,
    grad_ref,
    carry_ref,
    input_kernel_ref,
    input_shift_ref,
    state_kernel_ref,
    state_shift_ref,
    bias_ref,
    rate_ref,
    skip_ref,
    expand_ref,
    collect_ref,
    grad_input_ref,
    grad_state_ref,
    grad_step_ref,
    grad_input_conv_ref,
    grad_state_conv_ref,
    grad_head_ref,
    act_ref,
    slope_ref,
    both_ref,
    both_slope_ref,
    held_ref,
    wide_ref,
    turned_ref,
    column_ref,
    skip_sum_ref,
    scale_sum_ref,
):
    channels = input_ref.shape[1]
    states = state_ref.shape[1] // 2
    taps = input_kernel_ref.shape[0]
    for start, width in slabs(channels):
        cols = pl.ds(start, width)
        pre = convolve(input_ref[:, cols], input_kernel_ref, input_shift_ref, cols)
        sigma = jax.nn.sigmoid(pre)
        act_ref[:, cols] = pre * sigma
        slope_ref[:, cols] = sigma * (1.0 + pre * (1.0 - sigma))
    for start, width in slabs(2 * states):
        cols = pl.ds(start, width)
        pre = convolve(state_ref[:, cols], state_kernel_ref, state_shift_ref, cols)
        sigma = jax.nn.sigmoid(pre)
        both_ref[:, cols] = pre * sigma
        both_slope_ref[:, cols] = sigma * (1.0 + pre * (1.0 - sigma))
    held_ref[...] = jnp.zeros_like(held_ref)
    turned_ref[...] = jnp.zeros_like(turned_ref)
    column_ref[...] = jnp.zeros_like(column_ref)
    grad_head_ref[...] = jnp.zeros_like(grad_head_ref)
    skip_sum_ref[...] = jnp.zeros_like(skip_sum_ref)
    chunks = input_ref.shape[0] // SPAN

    def chunk(count, unused):
        index = chunks - 1 - count
        rows = pl.ds(pl.multiple_of(index * SPAN, SPAN), SPAN)
        raw, steps, cumul, step_wide, grown_wide, tail_wide = chunk_steps(
            step_ref, bias_ref, rate_ref, expand_ref, rows
        )
        cumul_turned = cumul.T
        entry = both_ref[rows, pl.ds(0, states)].astype(jnp.bfloat16)
        readout = both_ref[rows, pl.ds(states, states)].astype(jnp.bfloat16)
        cross = low_against(entry, readout)
        square = (SPAN, SPAN)
        upper = row_index(square) <= lane_index(square)
        grad_cross = jnp.zeros(square, jnp.float32)
        grad_entry = jnp.zeros((SPAN, states), jnp.float32)
        grad_readout = jnp.zeros((SPAN, states), jnp.float32)
        for start, width in slabs(channels):
            cols = pl.ds(start, width)
            span = slice(start, start + width)
            heads = width // HD
            values = act_ref[rows, cols]
            scaled = values * step_wide[:, span]
            gate = gate_ref[rows, cols]
            upstream = grad_ref[rows, cols] * (gate * jax.nn.sigmoid(gate))
            held = held_ref[:, cols]
            before = carry_ref[index, :, cols]
            stacked_up = stacked_heads(upstream, heads).astype(jnp.bfloat16)
            products = low_against(scaled, stacked_up)
            weights = []
            for place in range(heads):
                head = start // HD + place
                spread = cumul_turned[head : head + 1, :] - cumul[:, head : head + 1]
                decay = jnp.exp(jnp.where(upper, spread, -jnp.inf))
                product = products[:, place * SPAN : (place + 1) * SPAN] * decay
                grad_cross = grad_cross + product
                flow = product * cross
                turned_ref[head : head + 1, :] = jnp.sum(flow, axis=0, keepdims=True)
                column_ref[:, head : head + 1] = jnp.sum(flow, axis=1, keepdims=True)
                weights.append((decay * cross).astype(jnp.bfloat16))
            weights = jnp.concatenate(weights, axis=1) if heads > 1 else weights[0]
            grown_up = upstream * grown_wide[:, span]
            tailed = scaled * tail_wide[:, span]
            from_held = low_dot(entry, held)
            grad_scaled = low_dot(weights, stacked_up) + tail_wide[:, span] * from_held
            wide_ref[0, :, cols] = grown_up * low_dot(readout, before)
            wide_ref[1, :, cols] = tailed * from_held
            wide_ref[2, :, cols] = values * grad_scaled
            grad_readout = grad_readout + low_against(grown_up, before)
            grad_entry = grad_entry + low_against(tailed, held)
            last = grown_wide[SPAN - 1 : SPAN, span]
            scale_sum_ref[:, cols] = jnp.sum(held * before, axis=0, keepdims=True) * last
            skip_sum_ref[:, cols] += jnp.sum(upstream * values, axis=0, keepdims=True)
            held_ref[:, cols] = held * last + low_inner(readout, grown_up)
            act_ref[rows, cols] = step_wide[:, span] * grad_scaled + skip_ref[:, cols] * upstream
        sums = exact_dot(
            jnp.concatenate([wide_ref[0], wide_ref[1], wide_ref[2]], axis=0), collect_ref[...]
        )
        scale_sum = exact_dot(jnp.broadcast_to(scale_sum_ref[...], (8, channels)), collect_ref[...])
        flows = turned_ref[...].T - column_ref[...] + sums[:SPAN]
        onward = (row_index(square) <= lane_index(square)).astype(jnp.float32)
        strict = (row_index(square) > lane_index(square)).astype(jnp.float32)
        grad_log = (
            exact_dot(onward, flows)
            + exact_dot(strict, sums[SPAN : 2 * SPAN])
            + scale_sum[:1]
        )
        grad_steps = grad_log * rate_ref[...] + sums[2 * SPAN :]
        grad_raw = grad_steps * jax.nn.sigmoid(raw)
        grad_step_ref[rows, :] = grad_raw.astype(jnp.bfloat16)
        grad_head_ref[0, 0:1, :] += jnp.sum(grad_raw, axis=0, keepdims=True)
        grad_head_ref[0, 1:2, :] += (
            jnp.sum(grad_log * steps, axis=0, keepdims=True) * rate_ref[...]
        )
        both_ref[rows, pl.ds(0, states)] = grad_entry + low_dot(grad_cross, readout)
        both_ref[rows, pl.ds(states, states)] = grad_readout + low_inner(grad_cross, entry)
        return unused

    lax.fori_loop(0, chunks, chunk, 0)
    grad_head_ref[0, 2:3, :] = exact_dot(
        jnp.broadcast_to(skip_sum_ref[...], (8, channels)), collect_ref[...]
    )[:1]

    def convolve_back(raw_ref, grads_ref, slopes_ref, kernel_ref, out_ref, sums_ref, width_all):
        for start, width in slabs(width_all):
            cols = pl.ds(start, width)
            grad = grads_ref[:, cols] * slopes_ref[:, cols]
            raw = raw_ref[:, cols]
            total = kernel_ref[taps - 1 : taps, cols] * grad
            sums_ref[0, taps - 1 : taps, cols] = jnp.sum(grad * raw, axis=0, keepdims=True)
            for tap in range(taps - 1):
                shifted = sooner(grad, taps - 1 - tap)
                total = total + kernel_ref[tap : tap + 1, cols] * shifted
                sums_ref[0, tap : tap + 1, cols] = jnp.sum(shifted * raw, axis=0, keepdims=True)
            sums_ref[0, taps : taps + 1, cols] = jnp.sum(grad, axis=0, keepdims=True)
            out_ref[:, cols] = total.astype(jnp.bfloat16)

    convolve_back(
        input_ref,
        act_ref,
        slope_ref,
        input_kernel_ref,
        grad_input_ref,
        grad_input_conv_ref,
        channels,
    )
    convolve_back(
        state_ref,
        both_ref,
        both_slope_ref,
        state_kernel_ref,
        grad_state_ref,
        grad_state_conv_ref,
        2 * states,
    )


def by_sequence(length, width):
    return pl.BlockSpec((length, width), lambda seq: (seq, 0))


def fixed(*shape):
    return pl.BlockSpec(shape, lambda seq: (0,) * len(shape))


def head_spread(heads):
    marks = np.zeros((LANES, heads * HD), np.float32)
    for head in range(heads):
        marks[head, head * HD : (head + 1) * HD] = 1.0
    return marks


def pad_lanes(part):
    return jnp.pad(part, ((0, 0), (0, LANES - part.shape[1])))


def ssd_small(input_kernel, input_shift, state_kernel, state_shift, step_bias, decay_log, skip_gain):
    rates = -jnp.exp(decay_log)
    return (
        input_kernel,
        input_shift[None, :],
        state_kernel,
        state_shift[None, :],
        pad_lanes(step_bias[None, :]),
        pad_lanes(rates[None, :]),
        jnp.repeat(skip_gain, HD)[None, :],
    )


def ssd_forward(inputs, states_raw, gate, step, small, heads, length):
    group, channels = inputs.shape
    seqs = group // length
    both = states_raw.shape[1]
    states = both // 2
    chunks = length // SPAN
    taps = small[0].shape[0]
    return pl.pallas_call(
        ssd_forward_kernel,
        grid=(seqs,),
        in_specs=[
            by_sequence(length, channels),
            by_sequence(length, both),
            by_sequence(length, channels),
            by_sequence(length, LANES),
            fixed(taps, channels),
            fixed(1, channels),
            fixed(taps, both),
            fixed(1, both),
            fixed(1, LANES),
            fixed(1, LANES),
            fixed(1, channels),
            fixed(LANES, channels),
        ],
        out_specs=[
            by_sequence(length, channels),
            by_sequence(length, channels),
            pl.BlockSpec((chunks, states, channels), lambda seq: (seq, 0, 0)),
        ],
        out_shape=[
            jax.ShapeDtypeStruct((group, channels), jnp.bfloat16),
            jax.ShapeDtypeStruct((group, channels), jnp.float32),
            jax.ShapeDtypeStruct((seqs * chunks, states, channels), jnp.float32),
        ],
        scratch_shapes=[
            pltpu.VMEM((length, channels), jnp.float32),
            pltpu.VMEM((length, both), jnp.float32),
            pltpu.VMEM((states, channels), jnp.float32),
        ],
        compiler_params=pltpu.CompilerParams(vmem_limit_bytes=VMEM_LIMIT),
        cost_estimate=pl.CostEstimate(
            flops=8 * group * channels * SPAN,
            bytes_accessed=20 * group * channels,
            transcendentals=group * heads * SPAN,
        ),
        name="ssd_forward",
    )(inputs, states_raw, gate, step, *small, jnp.asarray(head_spread(heads)))


def ssd_backward(inputs, states_raw, gate, step, grad, carry, small, heads, length):
    group, channels = inputs.shape
    seqs = group // length
    both = states_raw.shape[1]
    states = both // 2
    chunks = length // SPAN
    taps = small[0].shape[0]
    return pl.pallas_call(
        ssd_backward_kernel,
        grid=(seqs,),
        in_specs=[
            by_sequence(length, channels),
            by_sequence(length, both),
            by_sequence(length, channels),
            by_sequence(length, LANES),
            by_sequence(length, channels),
            pl.BlockSpec((chunks, states, channels), lambda seq: (seq, 0, 0)),
            fixed(taps, channels),
            fixed(1, channels),
            fixed(taps, both),
            fixed(1, both),
            fixed(1, LANES),
            fixed(1, LANES),
            fixed(1, channels),
            fixed(LANES, channels),
            fixed(channels, LANES),
        ],
        out_specs=[
            by_sequence(length, channels),
            by_sequence(length, both),
            by_sequence(length, LANES),
            pl.BlockSpec((1, 8, channels), lambda seq: (seq, 0, 0)),
            pl.BlockSpec((1, 8, both), lambda seq: (seq, 0, 0)),
            pl.BlockSpec((1, 8, LANES), lambda seq: (seq, 0, 0)),
        ],
        out_shape=[
            jax.ShapeDtypeStruct((group, channels), jnp.bfloat16),
            jax.ShapeDtypeStruct((group, both), jnp.bfloat16),
            jax.ShapeDtypeStruct((group, LANES), jnp.bfloat16),
            jax.ShapeDtypeStruct((seqs, 8, channels), jnp.float32),
            jax.ShapeDtypeStruct((seqs, 8, both), jnp.float32),
            jax.ShapeDtypeStruct((seqs, 8, LANES), jnp.float32),
        ],
        scratch_shapes=[
            pltpu.VMEM((length, channels), jnp.float32),
            pltpu.VMEM((length, channels), jnp.float32),
            pltpu.VMEM((length, both), jnp.float32),
            pltpu.VMEM((length, both), jnp.float32),
            pltpu.VMEM((states, channels), jnp.float32),
            pltpu.VMEM((3, SPAN, channels), jnp.float32),
            pltpu.VMEM((LANES, SPAN), jnp.float32),
            pltpu.VMEM((SPAN, LANES), jnp.float32),
            pltpu.VMEM((1, channels), jnp.float32),
            pltpu.VMEM((1, channels), jnp.float32),
        ],
        compiler_params=pltpu.CompilerParams(vmem_limit_bytes=VMEM_LIMIT),
        cost_estimate=pl.CostEstimate(
            flops=20 * group * channels * SPAN,
            bytes_accessed=20 * group * channels,
            transcendentals=group * heads * SPAN,
        ),
        name="ssd_backward",
    )(
        inputs,
        states_raw,
        gate,
        step,
        grad,
        carry,
        *small,
        jnp.asarray(head_spread(heads)),
        jnp.asarray(head_spread(heads).T.copy()),
    )


def rope_wide(length):
    half = HD // 2
    freqs = np.float32(ROPE_BASE) ** (-np.arange(half, dtype=np.float32) * np.float32(2.0 / HD))
    angles = np.arange(length, dtype=np.float32)[:, None] * freqs[None, :].astype(np.float32)
    cosine, sine = np.cos(angles), np.sin(angles)
    count = LANES // HD
    return (
        np.concatenate([cosine, cosine] * count, axis=1).astype(np.float32),
        np.concatenate([-sine, sine] * count, axis=1).astype(np.float32),
    )


def turn(part, cosine, sine):
    half = HD // 2
    first = lane_index(part.shape) % HD < half
    swapped = jnp.where(first, pltpu.roll(part, LANES - half, 1), pltpu.roll(part, half, 1))
    return part * cosine + swapped * sine


def attend_forward_kernel(
    query_ref, pair_ref, cosine_ref, sine_ref, context_ref, query_out_ref, pair_out_ref, total_ref
):
    length = query_ref.shape[0]
    cosine, sine = cosine_ref[...], sine_ref[...]
    pair = pair_ref[...]
    left = lane_index(pair.shape) < HD
    pair = jnp.where(left, turn(pair, cosine, sine), pair)
    pair_out_ref[...] = pair.astype(jnp.bfloat16)
    moved = pltpu.roll(pair, HD, 1)
    keys = jnp.where(left, pair, moved).astype(jnp.bfloat16)
    values = jnp.where(left, moved, pair).astype(jnp.bfloat16)
    scale = HD ** (-0.5)
    for slab in range(query_ref.shape[1] // LANES):
        cols = pl.ds(slab * LANES, LANES)
        query_out_ref[:, cols] = turn(query_ref[:, cols], cosine, sine).astype(jnp.bfloat16)
        for tile in range(length // SPAN):
            rows = slice(tile * SPAN, (tile + 1) * SPAN)
            count = (tile + 1) * SPAN
            query = query_out_ref[rows, cols]
            lane = lane_index(query.shape)
            square = (SPAN, count)
            causal = row_index(square) + tile * SPAN >= lane_index(square)
            results = []
            for place in range(LANES // HD):
                mine = (lane >= place * HD) & (lane < place * HD + HD)
                scores = low_against(jnp.where(mine, query, 0), keys[:count]) * scale
                scores = jnp.where(causal, scores, -jnp.inf)
                peak = jnp.max(scores, axis=-1, keepdims=True)
                grown = jnp.exp(scores - peak)
                total = jnp.sum(grown, axis=-1, keepdims=True)
                probs = grown * (1.0 / total)
                results.append(low_dot(probs, values[:count]))
                head = slab * (LANES // HD) + place
                total_ref[rows, head : head + 1] = jnp.log(total) + peak
            context_ref[rows, cols] = jnp.where(lane < HD, results[0], results[1]).astype(
                jnp.bfloat16
            )


def attend_backward_kernel(
    query_ref,
    pair_ref,
    total_ref,
    grad_ref,
    cosine_ref,
    sine_ref,
    grad_query_ref,
    grad_pair_ref,
    key_sum_ref,
    value_sum_ref,
):
    length = query_ref.shape[0]
    cosine, sine = cosine_ref[...], -sine_ref[...]
    pair = pair_ref[...].astype(jnp.float32)
    left = lane_index(pair.shape) < HD
    moved = pltpu.roll(pair, HD, 1)
    keys = jnp.where(left, pair, moved).astype(jnp.bfloat16)
    values = jnp.where(left, moved, pair).astype(jnp.bfloat16)
    scale = HD ** (-0.5)
    key_sum_ref[...] = jnp.zeros_like(key_sum_ref)
    value_sum_ref[...] = jnp.zeros_like(value_sum_ref)
    for slab in range(query_ref.shape[1] // LANES):
        cols = pl.ds(slab * LANES, LANES)
        for tile in range(length // SPAN):
            rows = slice(tile * SPAN, (tile + 1) * SPAN)
            count = (tile + 1) * SPAN
            query = query_ref[rows, cols]
            upstream = grad_ref[rows, cols]
            lane = lane_index(query.shape)
            square = (SPAN, count)
            causal = row_index(square) + tile * SPAN >= lane_index(square)
            results = []
            for place in range(LANES // HD):
                mine = (lane >= place * HD) & (lane < place * HD + HD)
                head = slab * (LANES // HD) + place
                own_query = jnp.where(mine, query, 0)
                own_up = jnp.where(mine, upstream, 0)
                scores = low_against(own_query, keys[:count]) * scale
                scores = jnp.where(causal, scores, -jnp.inf)
                probs = jnp.exp(scores - total_ref[rows, head : head + 1])
                grad_probs = low_against(own_up, values[:count])
                mean = jnp.sum(probs * grad_probs, axis=-1, keepdims=True)
                grad_scores = (probs * (grad_probs - mean)).astype(jnp.bfloat16)
                results.append(low_dot(grad_scores, keys[:count]))
                key_sum_ref[0:count, :] += low_inner(grad_scores, own_query)
                value_sum_ref[0:count, :] += low_inner(probs, own_up)
            grad_query = jnp.where(lane < HD, results[0], results[1]) * scale
            grad_query_ref[rows, cols] = turn(
                grad_query, cosine[rows, :], sine[rows, :]
            ).astype(jnp.bfloat16)
    grad_key = key_sum_ref[...]
    grad_key = turn((grad_key + pltpu.roll(grad_key, HD, 1)) * scale, cosine, sine)
    grad_value = value_sum_ref[...]
    grad_value = grad_value + pltpu.roll(grad_value, HD, 1)
    grad_pair_ref[...] = jnp.where(left, grad_key, grad_value).astype(jnp.bfloat16)


def attend_forward(query, pair, length):
    group, width = query.shape
    heads = width // HD
    cosine, sine = rope_wide(length)
    return pl.pallas_call(
        attend_forward_kernel,
        grid=(group // length,),
        in_specs=[
            by_sequence(length, width),
            by_sequence(length, LANES),
            fixed(length, LANES),
            fixed(length, LANES),
        ],
        out_specs=[
            by_sequence(length, width),
            by_sequence(length, width),
            by_sequence(length, LANES),
            by_sequence(length, LANES),
        ],
        out_shape=[
            jax.ShapeDtypeStruct((group, width), jnp.bfloat16),
            jax.ShapeDtypeStruct((group, width), jnp.bfloat16),
            jax.ShapeDtypeStruct((group, LANES), jnp.bfloat16),
            jax.ShapeDtypeStruct((group, LANES), jnp.float32),
        ],
        compiler_params=pltpu.CompilerParams(vmem_limit_bytes=VMEM_LIMIT),
        cost_estimate=pl.CostEstimate(
            flops=4 * group * width * length,
            bytes_accessed=12 * group * width,
            transcendentals=group * heads * length // 2,
        ),
        name="attend_forward",
    )(query, pair, jnp.asarray(cosine), jnp.asarray(sine))


def attend_backward(query, pair, total, grad, length):
    group, width = query.shape
    heads = width // HD
    cosine, sine = rope_wide(length)
    return pl.pallas_call(
        attend_backward_kernel,
        grid=(group // length,),
        in_specs=[
            by_sequence(length, width),
            by_sequence(length, LANES),
            by_sequence(length, LANES),
            by_sequence(length, width),
            fixed(length, LANES),
            fixed(length, LANES),
        ],
        out_specs=[by_sequence(length, width), by_sequence(length, LANES)],
        out_shape=[
            jax.ShapeDtypeStruct((group, width), jnp.bfloat16),
            jax.ShapeDtypeStruct((group, LANES), jnp.bfloat16),
        ],
        scratch_shapes=[
            pltpu.VMEM((length, LANES), jnp.float32),
            pltpu.VMEM((length, LANES), jnp.float32),
        ],
        compiler_params=pltpu.CompilerParams(vmem_limit_bytes=VMEM_LIMIT),
        cost_estimate=pl.CostEstimate(
            flops=10 * group * width * length,
            bytes_accessed=12 * group * width,
            transcendentals=group * heads * length // 2,
        ),
        name="attend_backward",
    )(query, pair, total, grad, jnp.asarray(cosine), jnp.asarray(sine))


def step_groups(size):
    bits = size.bit_length() - 1
    return [1] * min(bits, 2) + [2] * (max(bits - 2, 0) // 2) + [1] * (max(bits - 2, 0) % 2)


def after(part, *deps):
    return lax.optimization_barrier((part,) + deps)[0]


def behind(part, dep):
    zero = jnp.minimum(jnp.abs(dep[:1, :1].astype(jnp.float32)), 0.0)
    return part + zero.astype(part.dtype)


class Sum:
    def __init__(self, part, size):
        self.size = size
        self.direct = bool(size & (size - 1) or part.shape[0] % size)
        self.steps = [] if self.direct else step_groups(size)
        self.shift = 0
        self.part = part
        self.gives = [part]
        if not self.direct:
            self.part = part.reshape(size, part.shape[0] // size, part.shape[1])
            self.prepare()

    def prepare(self):
        if not self.steps:
            self.gives = [self.part]
            return
        ways = 1 << self.steps[0]
        rest = self.part.shape[0] // ways
        view = self.part.reshape((rest, ways) + self.part.shape[1:])
        mine = (lax.axis_index("dp") >> self.shift) & (ways - 1)
        self.keep = lax.dynamic_index_in_dim(view, mine, 1, False)
        self.gives = [
            lax.dynamic_index_in_dim(view, mine ^ way, 1, False) for way in range(1, ways)
        ]

    def advance(self, *deps):
        if self.steps:
            total = after(self.keep, *deps).astype(jnp.float32)
            for way, give in enumerate(self.gives, 1):
                pairs = [(index, index ^ (way << self.shift)) for index in range(self.size)]
                total = total + lax.ppermute(give, "dp", pairs).astype(jnp.float32)
            self.part = total.astype(jnp.bfloat16)
            self.shift += self.steps.pop(0)
            self.prepare()
        return self.gives

    def joined(self, middle=None, *deps):
        groups, shift = step_groups(self.size), self.size.bit_length() - 1
        part = after(self.reduced(), *deps)
        if middle is not None:
            part = middle(part)
        self.trail = [part]
        if self.direct:
            return part
        rows, width = part.shape
        for group in reversed(groups):
            ways = 1 << group
            shift -= group
            mine = (lax.axis_index("dp") >> shift) & (ways - 1)
            part = part.reshape(-1, 1, rows, width)
            got = [part]
            for way in range(1, ways):
                pairs = [(index, index ^ (way << shift)) for index in range(self.size)]
                got.append(lax.ppermute(part, "dp", pairs))
            for bit in range(group):
                flip = ((mine >> bit) & 1) == 1
                got = [
                    jnp.where(flip, got[way ^ (1 << bit)], got[way]) for way in range(ways)
                ]
            part = jnp.concatenate(got, axis=1)
            self.trail.append(part)
        return part.reshape(-1, width)

    def reduced(self):
        while self.steps:
            self.advance()
        return lax.psum(self.part, "dp") if self.direct else self.part[0]


def other(part):
    return lax.ppermute(part, "tensor", [(0, 1), (1, 0)])


def all_rows(part, shards):
    if shards != 2:
        return lax.all_gather(part, "tensor", axis=0, tiled=True)
    got = other(part)
    return jnp.where(
        lax.axis_index("tensor") == 0,
        jnp.concatenate([part, got], axis=0),
        jnp.concatenate([got, part], axis=0),
    )


def sum_all(part, shards):
    if shards != 2:
        return lax.psum(part, "tensor").astype(jnp.float32)
    return part.astype(jnp.float32) + other(part).astype(jnp.float32)


def sum_own(part, shards):
    if shards != 2:
        return lax.psum_scatter(part, "tensor", scatter_dimension=0, tiled=True).astype(jnp.float32)
    me = lax.axis_index("tensor")
    halves = part.reshape(2, part.shape[0] // 2, part.shape[1])
    keep = lax.dynamic_index_in_dim(halves, me, 0, False)
    got = other(lax.dynamic_index_in_dim(halves, 1 - me, 0, False))
    return keep.astype(jnp.float32) + got.astype(jnp.float32)


def own_rows(part, rows):
    return lax.dynamic_slice_in_dim(part, lax.axis_index("tensor") * rows, rows, 0)


def column_pack(vectors, rows):
    flat = jnp.concatenate([item.reshape(-1) for item in vectors])
    width = -(-flat.shape[0] // rows)
    return jnp.pad(flat, (0, width * rows - flat.shape[0])).reshape(width, rows).T


def column_unpack(packed, shapes):
    flat = packed.T.reshape(-1)
    out, start = [], 0
    for shape in shapes:
        count = 1
        for size in shape:
            count *= size
        out.append(flat[start : start + count].reshape(shape))
        start += count
    return out


def body(
    dp_size,
    shards,
    layer_input,
    input_gain,
    middle_gain,
    mamba_gate,
    mamba_input,
    step_weight,
    state_weight,
    input_kernel,
    input_shift,
    state_kernel,
    state_shift,
    step_bias,
    decay_log,
    skip_gain,
    mamba_output,
    query_weight,
    keyvalue_weight,
    context_weight,
    gate_weight,
    up_weight,
    down_weight,
    cotangent,
):
    own = layer_input.shape[0]
    rows_low = all_rows(layer_input, shards)
    cotan_low = all_rows(cotangent, shards)
    rows = rows_low.astype(jnp.float32)
    gain_first = input_gain.astype(jnp.float32)
    gain_second = middle_gain.astype(jnp.float32)
    factor_first = lax.rsqrt(jnp.mean(rows * rows, axis=-1, keepdims=True) + EPSILON)
    normal_first = rows * factor_first
    whole = (normal_first * gain_first).astype(jnp.bfloat16)
    group = whole.shape[0]
    length = min(SEQ_LEN, group)
    seqs = group // length
    heads_here = query_weight.shape[1] // HD
    kv_head = lax.axis_index("tensor") * heads_here // (HQ // KVH)
    key_cols = lax.dynamic_slice_in_dim(keyvalue_weight, kv_head * HD, HD, 1)
    value_cols = lax.dynamic_slice_in_dim(keyvalue_weight, (KVH + kv_head) * HD, HD, 1)
    pair_weight = jnp.concatenate([key_cols, value_cols], axis=1)
    query_cols = query_weight.shape[1]
    query_pad = -query_cols % LANES
    query_wide = jnp.pad(query_weight, ((0, 0), (0, query_pad)))
    step_wide = pad_lanes(step_weight)
    heads = step_weight.shape[1]
    input_raw = forward_dot(whole, mamba_input)
    state_raw = forward_dot(whole, state_weight)
    step_raw = forward_dot(whole, step_wide)
    gate_raw = forward_dot(whole, mamba_gate)
    query_raw = forward_dot(whole, query_wide)
    pair_raw = forward_dot(whole, pair_weight)
    small = ssd_small(
        input_kernel.astype(jnp.float32),
        input_shift.astype(jnp.float32),
        state_kernel.astype(jnp.float32),
        state_shift.astype(jnp.float32),
        step_bias.astype(jnp.float32),
        decay_log.astype(jnp.float32),
        skip_gain.astype(jnp.float32),
    )
    gated_low, ssm_out, carries = ssd_forward(
        input_raw, state_raw, gate_raw, step_raw, small, heads, length
    )
    context_wide, queries, pairs, totals = attend_forward(
        after(query_raw, cotan_low), pair_raw, length
    )
    context_rows = context_wide[:, :query_cols]
    mixed_part = forward_dot(gated_low, mamba_output) + forward_dot(context_rows, context_weight)
    resid = rows + sum_all(mixed_part.astype(jnp.bfloat16), shards)
    factor_second = lax.rsqrt(jnp.mean(resid * resid, axis=-1, keepdims=True) + EPSILON)
    normal_second = resid * factor_second
    whole_mid = (normal_second * gain_second).astype(jnp.bfloat16)
    gate = forward_dot(whole_mid, gate_weight)
    upper = forward_dot(whole_mid, up_weight)
    sigmoid_gate = jax.nn.sigmoid(gate)
    silu_gate = gate * sigmoid_gate
    hidden = (silu_gate * upper).astype(jnp.bfloat16)
    grad_hidden = against(cotan_low, down_weight)
    slope = sigmoid_gate * (1.0 + gate * (1.0 - sigmoid_gate))
    grad_gate_low = (grad_hidden * upper * slope).astype(jnp.bfloat16)
    grad_upper_low = (grad_hidden * silu_gate).astype(jnp.bfloat16)
    back_part = (against(grad_gate_low, gate_weight) + against(grad_upper_low, up_weight)).astype(
        jnp.bfloat16
    )
    back_mid = sum_all(back_part, shards)
    hidden_late = after(hidden, back_part)
    mid_late = after(whole_mid, back_part)
    grad_down = inner_rows(hidden_late, cotan_low).astype(jnp.bfloat16)
    grad_gate = inner_rows(mid_late, grad_gate_low).astype(jnp.bfloat16)
    grad_up = inner_rows(mid_late, grad_upper_low).astype(jnp.bfloat16)
    grad_gate, grad_up, grad_down = lax.psum((grad_gate, grad_up, grad_down), "dp")
    feed_part = behind(forward_dot(hidden_late, down_weight), back_mid).astype(jnp.bfloat16)
    feed = sum_own(feed_part, shards)
    layer_output = (own_rows(resid, own) + feed).astype(jnp.bfloat16)
    grad_middle = jnp.sum(back_part.astype(jnp.float32) * normal_second, axis=0)
    grad_resid = cotan_low.astype(jnp.float32) + norm_back(
        back_mid, gain_second, normal_second, factor_second
    )
    mixer_all = grad_resid.astype(jnp.bfloat16)
    ssm_rows = gated_low.shape[1]
    width = whole.shape[1]
    split_pairs = shards == KVH
    grad_gated = against(mixer_all, mamba_output)
    mixer_sum = Sum(
        inner_rows(jnp.concatenate([gated_low, context_rows], axis=1), mixer_all).astype(
            jnp.bfloat16
        ),
        dp_size,
    )
    grad_input_raw, grad_state_raw, grad_step_raw, input_sums, state_sums, head_sums = ssd_backward(
        input_raw,
        state_raw,
        gate_raw,
        step_raw,
        after(grad_gated, *mixer_sum.gives),
        carries,
        small,
        heads,
        length,
    )
    input_sums = jnp.sum(input_sums, axis=0)
    state_sums = jnp.sum(state_sums, axis=0)
    head_sums = jnp.sum(head_sums, axis=0)[:, :heads]
    taps = input_kernel.shape[0]
    state_cols = state_weight.shape[1]
    step_cols = heads
    late_cols = jnp.concatenate([grad_input_raw, grad_state_raw], axis=1)
    late_sum = Sum(inner_rows(whole, late_cols).astype(jnp.bfloat16), dp_size)

    sigmoid_raw = jax.nn.sigmoid(gate_raw)
    grad_gate_raw = (
        grad_gated * ssm_out * (sigmoid_raw * (1.0 + gate_raw * (1.0 - sigmoid_raw)))
    ).astype(jnp.bfloat16)
    grad_context = against(mixer_all, context_weight).astype(jnp.bfloat16)
    grad_context = jnp.pad(grad_context, ((0, 0), (0, query_pad)))
    grad_query_raw, grad_pair_raw = attend_backward(
        queries, pairs, totals, after(grad_context, *late_sum.gives, *mixer_sum.advance()), length
    )
    early_cols = jnp.concatenate(
        [grad_gate_raw, grad_query_raw[:, :query_cols], grad_pair_raw, grad_step_raw], axis=1
    )
    total = against(late_cols, jnp.concatenate([mamba_input, state_weight], axis=1))
    total = total + against(
        early_cols, jnp.concatenate([mamba_gate, query_weight, pair_weight, step_wide], axis=1)
    )
    total_low = total.astype(jnp.bfloat16)
    grad_first = jnp.sum(total_low.astype(jnp.float32) * normal_first, axis=0)
    own_vectors = (input_sums[:taps], input_sums[taps], head_sums[0], head_sums[1], head_sums[2])
    shared_vectors = (grad_first, grad_middle, state_sums[:taps], state_sums[taps])
    own_pack = column_pack(own_vectors, width)
    shared_pack = column_pack(shared_vectors, width)
    shared_lane = step_cols + own_pack.shape[1]
    last_lane = shared_lane + shared_pack.shape[1]
    early = inner_rows(whole, early_cols)
    if not split_pairs:
        spread = jnp.zeros((width, 2 * KVH * HD), jnp.float32)
        spread = lax.dynamic_update_slice_in_dim(
            spread, early[:, -2 * HD - LANES : -HD - LANES], kv_head * HD, 1
        )
        spread = lax.dynamic_update_slice_in_dim(
            spread, early[:, -HD - LANES : -LANES], (KVH + kv_head) * HD, 1
        )
        early = jnp.concatenate(
            [early[:, : -2 * HD - LANES], spread, early[:, -LANES:]], axis=1
        )
    packs = jnp.pad(
        jnp.concatenate([own_pack, shared_pack], axis=1),
        ((0, 0), (early.shape[1] - LANES + step_cols, LANES - last_lane)),
    )
    early_sum = Sum((early + packs).astype(jnp.bfloat16), dp_size)

    def early_over_tensor(part):
        count = (2 * HD if split_pairs else 2 * KVH * HD) + LANES
        mine = part[:, -count:]
        if split_pairs:
            got = other(mine)
            both = (mine.astype(jnp.float32) + got.astype(jnp.float32)).astype(jnp.bfloat16)
            first = lax.axis_index("tensor") == 0
            low, high = jnp.where(first, mine, got), jnp.where(first, got, mine)
            pair = [low[:, :HD], high[:, :HD], low[:, HD : 2 * HD], high[:, HD : 2 * HD]]
        else:
            both = lax.psum(mine, "tensor")
            pair = [both[:, :-LANES]]
        lane = lane_index((part.shape[0], LANES))
        extra = jnp.where(
            (lane >= shared_lane) & (lane < last_lane), both[:, -LANES:], mine[:, -LANES:]
        )
        return jnp.concatenate([part[:, :-count]] + pair + [extra], axis=1)

    def late_over_tensor(part):
        mine = part[:, -state_cols:]
        if shards == 2:
            both = mine.astype(jnp.float32) + other(mine).astype(jnp.float32)
        else:
            both = lax.psum(mine, "tensor")
        return jnp.concatenate([part[:, :-state_cols], both.astype(jnp.bfloat16)], axis=1)

    early_sum.advance()
    tail = late_sum.joined(late_over_tensor, *early_sum.gives)
    grad_mixer_out = mixer_sum.joined(None, *early_sum.gives)
    early = early_sum.joined(early_over_tensor)
    grad_gate, grad_up, grad_down = [
        after(item, early_sum.trail[min(1, len(early_sum.trail) - 1)])
        for item in (grad_gate, grad_up, grad_down)
    ]
    grad_mamba_out = grad_mixer_out[:ssm_rows]
    grad_context_w = grad_mixer_out[ssm_rows:]
    grad_mamba_input, grad_state = tail[:, :-state_cols], tail[:, -state_cols:]
    gate_cols = gate_raw.shape[1]
    extra = early[:, -LANES:]
    back_in = sum_own(total_low, shards)
    normal_own = own_rows(normal_first, own)
    factor_own = own_rows(factor_first, own)
    input_grad = own_rows(grad_resid, own) + norm_back(back_in, gain_first, normal_own, factor_own)
    grad_step = extra[:, :step_cols]
    grad_in_kernel, grad_in_shift, grad_bias, grad_decay, grad_skip = column_unpack(
        extra[:, step_cols:shared_lane], [item.shape for item in own_vectors]
    )
    grad_first, grad_middle, grad_st_kernel, grad_st_shift = column_unpack(
        extra[:, shared_lane:last_lane], [item.shape for item in shared_vectors]
    )
    results = (
        grad_first,
        grad_middle,
        early[:, :gate_cols],
        grad_mamba_input,
        grad_step,
        grad_state,
        grad_in_kernel,
        grad_in_shift,
        grad_st_kernel,
        grad_st_shift,
        grad_bias,
        grad_decay,
        grad_skip,
        grad_mamba_out,
        early[:, gate_cols : gate_cols + query_cols],
        early[:, gate_cols + query_cols : -LANES],
        grad_context_w,
        grad_gate,
        grad_up,
        grad_down,
    )
    return (layer_output, input_grad) + tuple(item.astype(jnp.float32) for item in results)


def solution(mesh):
    in_specs = (
        P(("dp", "tensor"), None),
        P(),
        P(),
        P(None, "tensor"),
        P(None, "tensor"),
        P(None, "tensor"),
        P(),
        P(None, "tensor"),
        P("tensor"),
        P(),
        P(),
        P("tensor"),
        P("tensor"),
        P("tensor"),
        P("tensor", None),
        P(None, "tensor"),
        P(),
        P("tensor", None),
        P(None, "tensor"),
        P(None, "tensor"),
        P("tensor", None),
        P(("dp", "tensor"), None),
    )
    out_specs = (
        P(("dp", "tensor"), None),
        P(("dp", "tensor"), None),
        P(),
        P(),
        P(None, "tensor"),
        P(None, "tensor"),
        P(None, "tensor"),
        P(),
        P(None, "tensor"),
        P("tensor"),
        P(),
        P(),
        P("tensor"),
        P("tensor"),
        P("tensor"),
        P("tensor", None),
        P(None, "tensor"),
        P(),
        P("tensor", None),
        P(None, "tensor"),
        P(None, "tensor"),
        P("tensor", None),
    )
    run = partial(body, mesh.shape["dp"], mesh.shape["tensor"])
    return jax.shard_map(run, mesh=mesh, in_specs=in_specs, out_specs=out_specs, check_vma=False)
```

```python
from functools import partial

import jax
import jax.numpy as jnp
import numpy as np
from jax import lax
from jax.experimental import pallas as pl
from jax.experimental.pallas import tpu as pltpu
from jax.sharding import PartitionSpec as P

HD = 64
HQ = 8
KVH = 2
SPAN = 128
SEQ_LEN = 1024


EPSILON = 1e-05
ROPE_BASE = 10000.0
PRECISE = lax.Precision.HIGHEST


def forward_dot(left, right):
    return jnp.dot(left, right, preferred_element_type=jnp.float32)


def inner_rows(left, right):
    return lax.dot_general(
        left, right, (((0,), (0,)), ((), ())), preferred_element_type=jnp.float32
    )


def against(left, right):
    return lax.dot_general(
        left, right, (((1,), (1,)), ((), ())), preferred_element_type=jnp.float32
    )


def norm_back(upstream, gain, normal, factor):
    scaled = upstream * gain
    return factor * (scaled - normal * jnp.mean(scaled * normal, axis=-1, keepdims=True))


LANES = 128
VMEM_LIMIT = 44 * 1024 * 1024


def exact_dot(left, right):
    return jnp.dot(left, right, precision=PRECISE, preferred_element_type=jnp.float32)


def low_dot(left, right):
    return jnp.dot(
        left.astype(jnp.bfloat16), right.astype(jnp.bfloat16), preferred_element_type=jnp.float32
    )


def low_against(left, right):
    return lax.dot_general(
        left.astype(jnp.bfloat16),
        right.astype(jnp.bfloat16),
        (((1,), (1,)), ((), ())),
        preferred_element_type=jnp.float32,
    )


def low_inner(left, right):
    return lax.dot_general(
        left.astype(jnp.bfloat16),
        right.astype(jnp.bfloat16),
        (((0,), (0,)), ((), ())),
        preferred_element_type=jnp.float32,
    )


def row_index(shape):
    return lax.broadcasted_iota(jnp.int32, shape, 0)


def lane_index(shape):
    return lax.broadcasted_iota(jnp.int32, shape, 1)


def later(part, count):
    if count == 0:
        return part
    return jnp.where(row_index(part.shape) >= count, pltpu.roll(part, count, 0), 0.0)


def sooner(part, count):
    if count == 0:
        return part
    rows = part.shape[0]
    return jnp.where(row_index(part.shape) < rows - count, pltpu.roll(part, rows - count, 0), 0.0)


def slabs(width):
    return [(start, min(LANES, width - start)) for start in range(0, width, LANES)]


def soft_plus(value):
    return jnp.maximum(value, 0.0) + jnp.log1p(jnp.exp(-jnp.abs(value)))


def stacked_heads(part, heads):
    if heads == 1:
        return part
    lane = lane_index(part.shape)
    return jnp.concatenate(
        [jnp.where((lane >= head * HD) & (lane < head * HD + HD), part, 0.0) for head in range(heads)],
        axis=0,
    )


def convolve(raw, kernel_ref, shift_ref, cols):
    taps = kernel_ref.shape[0]
    out = shift_ref[:, cols] + kernel_ref[taps - 1 : taps, cols] * raw
    for tap in range(taps - 1):
        out = out + kernel_ref[tap : tap + 1, cols] * later(raw, taps - 1 - tap)
    return out


def chunk_steps(step_ref, bias_ref, rate_ref, expand_ref, rows):
    raw = step_ref[rows, :] + bias_ref[...]
    steps = soft_plus(raw)
    logdec = steps * rate_ref[...]
    square = (SPAN, SPAN)
    lower = (row_index(square) >= lane_index(square)).astype(jnp.float32)
    cumul = exact_dot(lower, logdec)
    grown = jnp.exp(cumul)
    tail = jnp.exp(cumul[SPAN - 1 : SPAN, :] - cumul)
    wide = exact_dot(jnp.concatenate([steps, grown, tail], axis=0), expand_ref[...])
    return raw, steps, cumul, wide[:SPAN], wide[SPAN : 2 * SPAN], wide[2 * SPAN :]


def ssd_forward_kernel(
    input_ref,
    state_ref,
    gate_ref,
    step_ref,
    input_kernel_ref,
    input_shift_ref,
    state_kernel_ref,
    state_shift_ref,
    bias_ref,
    rate_ref,
    skip_ref,
    expand_ref,
    gated_ref,
    out_ref,
    carry_ref,
    act_ref,
    both_ref,
    held_ref,
):
    channels = input_ref.shape[1]
    states = state_ref.shape[1] // 2
    for start, width in slabs(channels):
        cols = pl.ds(start, width)
        pre = convolve(input_ref[:, cols], input_kernel_ref, input_shift_ref, cols)
        act_ref[:, cols] = pre * jax.nn.sigmoid(pre)
    for start, width in slabs(2 * states):
        cols = pl.ds(start, width)
        pre = convolve(state_ref[:, cols], state_kernel_ref, state_shift_ref, cols)
        both_ref[:, cols] = pre * jax.nn.sigmoid(pre)
    held_ref[...] = jnp.zeros_like(held_ref)

    def chunk(index, unused):
        rows = pl.ds(pl.multiple_of(index * SPAN, SPAN), SPAN)
        raw, steps, cumul, step_wide, grown_wide, tail_wide = chunk_steps(
            step_ref, bias_ref, rate_ref, expand_ref, rows
        )
        cumul_turned = cumul.T
        entry = both_ref[rows, pl.ds(0, states)].astype(jnp.bfloat16)
        readout = both_ref[rows, pl.ds(states, states)].astype(jnp.bfloat16)
        cross = low_against(readout, entry)
        square = (SPAN, SPAN)
        lower = row_index(square) >= lane_index(square)
        for start, width in slabs(channels):
            cols = pl.ds(start, width)
            span = slice(start, start + width)
            heads = width // HD
            values = act_ref[rows, cols]
            scaled = values * step_wide[:, span]
            held = held_ref[:, cols]
            carry_ref[index, :, cols] = held
            weights = []
            for head in range(start // HD, start // HD + heads):
                spread = cumul[:, head : head + 1] - cumul_turned[head : head + 1, :]
                decay = jnp.exp(jnp.where(lower, spread, -jnp.inf))
                weights.append((decay * cross).astype(jnp.bfloat16))
            weights = jnp.concatenate(weights, axis=1) if heads > 1 else weights[0]
            result = low_dot(weights, stacked_heads(scaled, heads))
            result = result + low_dot(readout, held) * grown_wide[:, span]
            held_ref[:, cols] = held * grown_wide[SPAN - 1 : SPAN, span] + low_inner(
                entry, scaled * tail_wide[:, span]
            )
            result = result + skip_ref[:, cols] * values
            out_ref[rows, cols] = result
            gate = gate_ref[rows, cols]
            gated_ref[rows, cols] = (result * (gate * jax.nn.sigmoid(gate))).astype(jnp.bfloat16)
        return unused

    lax.fori_loop(0, input_ref.shape[0] // SPAN, chunk, 0)


def ssd_backward_kernel(
    input_ref,
    state_ref,
    gate_ref,
    step_ref,
    grad_ref,
    carry_ref,
    input_kernel_ref,
    input_shift_ref,
    state_kernel_ref,
    state_shift_ref,
    bias_ref,
    rate_ref,
    skip_ref,
    expand_ref,
    collect_ref,
    grad_input_ref,
    grad_state_ref,
    grad_step_ref,
    grad_input_conv_ref,
    grad_state_conv_ref,
    grad_head_ref,
    act_ref,
    slope_ref,
    both_ref,
    both_slope_ref,
    held_ref,
    wide_ref,
    turned_ref,
    column_ref,
    skip_sum_ref,
    scale_sum_ref,
):
    channels = input_ref.shape[1]
    states = state_ref.shape[1] // 2
    taps = input_kernel_ref.shape[0]
    for start, width in slabs(channels):
        cols = pl.ds(start, width)
        pre = convolve(input_ref[:, cols], input_kernel_ref, input_shift_ref, cols)
        sigma = jax.nn.sigmoid(pre)
        act_ref[:, cols] = pre * sigma
        slope_ref[:, cols] = sigma * (1.0 + pre * (1.0 - sigma))
    for start, width in slabs(2 * states):
        cols = pl.ds(start, width)
        pre = convolve(state_ref[:, cols], state_kernel_ref, state_shift_ref, cols)
        sigma = jax.nn.sigmoid(pre)
        both_ref[:, cols] = pre * sigma
        both_slope_ref[:, cols] = sigma * (1.0 + pre * (1.0 - sigma))
    held_ref[...] = jnp.zeros_like(held_ref)
    turned_ref[...] = jnp.zeros_like(turned_ref)
    column_ref[...] = jnp.zeros_like(column_ref)
    grad_head_ref[...] = jnp.zeros_like(grad_head_ref)
    skip_sum_ref[...] = jnp.zeros_like(skip_sum_ref)
    chunks = input_ref.shape[0] // SPAN

    def chunk(count, unused):
        index = chunks - 1 - count
        rows = pl.ds(pl.multiple_of(index * SPAN, SPAN), SPAN)
        raw, steps, cumul, step_wide, grown_wide, tail_wide = chunk_steps(
            step_ref, bias_ref, rate_ref, expand_ref, rows
        )
        cumul_turned = cumul.T
        entry = both_ref[rows, pl.ds(0, states)].astype(jnp.bfloat16)
        readout = both_ref[rows, pl.ds(states, states)].astype(jnp.bfloat16)
        cross = low_against(entry, readout)
        square = (SPAN, SPAN)
        upper = row_index(square) <= lane_index(square)
        grad_cross = jnp.zeros(square, jnp.float32)
        grad_entry = jnp.zeros((SPAN, states), jnp.float32)
        grad_readout = jnp.zeros((SPAN, states), jnp.float32)
        for start, width in slabs(channels):
            cols = pl.ds(start, width)
            span = slice(start, start + width)
            heads = width // HD
            values = act_ref[rows, cols]
            scaled = values * step_wide[:, span]
            gate = gate_ref[rows, cols]
            upstream = grad_ref[rows, cols] * (gate * jax.nn.sigmoid(gate))
            held = held_ref[:, cols]
            before = carry_ref[index, :, cols]
            stacked_up = stacked_heads(upstream, heads).astype(jnp.bfloat16)
            products = low_against(scaled, stacked_up)
            weights = []
            for place in range(heads):
                head = start // HD + place
                spread = cumul_turned[head : head + 1, :] - cumul[:, head : head + 1]
                decay = jnp.exp(jnp.where(upper, spread, -jnp.inf))
                product = products[:, place * SPAN : (place + 1) * SPAN] * decay
                grad_cross = grad_cross + product
                flow = product * cross
                turned_ref[head : head + 1, :] = jnp.sum(flow, axis=0, keepdims=True)
                column_ref[:, head : head + 1] = jnp.sum(flow, axis=1, keepdims=True)
                weights.append((decay * cross).astype(jnp.bfloat16))
            weights = jnp.concatenate(weights, axis=1) if heads > 1 else weights[0]
            grown_up = upstream * grown_wide[:, span]
            tailed = scaled * tail_wide[:, span]
            from_held = low_dot(entry, held)
            grad_scaled = low_dot(weights, stacked_up) + tail_wide[:, span] * from_held
            wide_ref[0, :, cols] = grown_up * low_dot(readout, before)
            wide_ref[1, :, cols] = tailed * from_held
            wide_ref[2, :, cols] = values * grad_scaled
            grad_readout = grad_readout + low_against(grown_up, before)
            grad_entry = grad_entry + low_against(tailed, held)
            last = grown_wide[SPAN - 1 : SPAN, span]
            scale_sum_ref[:, cols] = jnp.sum(held * before, axis=0, keepdims=True) * last
            skip_sum_ref[:, cols] += jnp.sum(upstream * values, axis=0, keepdims=True)
            held_ref[:, cols] = held * last + low_inner(readout, grown_up)
            act_ref[rows, cols] = step_wide[:, span] * grad_scaled + skip_ref[:, cols] * upstream
        sums = exact_dot(
            jnp.concatenate([wide_ref[0], wide_ref[1], wide_ref[2]], axis=0), collect_ref[...]
        )
        scale_sum = exact_dot(jnp.broadcast_to(scale_sum_ref[...], (8, channels)), collect_ref[...])
        flows = turned_ref[...].T - column_ref[...] + sums[:SPAN]
        onward = (row_index(square) <= lane_index(square)).astype(jnp.float32)
        strict = (row_index(square) > lane_index(square)).astype(jnp.float32)
        grad_log = (
            exact_dot(onward, flows)
            + exact_dot(strict, sums[SPAN : 2 * SPAN])
            + scale_sum[:1]
        )
        grad_steps = grad_log * rate_ref[...] + sums[2 * SPAN :]
        grad_raw = grad_steps * jax.nn.sigmoid(raw)
        grad_step_ref[rows, :] = grad_raw.astype(jnp.bfloat16)
        grad_head_ref[0, 0:1, :] += jnp.sum(grad_raw, axis=0, keepdims=True)
        grad_head_ref[0, 1:2, :] += (
            jnp.sum(grad_log * steps, axis=0, keepdims=True) * rate_ref[...]
        )
        both_ref[rows, pl.ds(0, states)] = grad_entry + low_dot(grad_cross, readout)
        both_ref[rows, pl.ds(states, states)] = grad_readout + low_inner(grad_cross, entry)
        return unused

    lax.fori_loop(0, chunks, chunk, 0)
    grad_head_ref[0, 2:3, :] = exact_dot(
        jnp.broadcast_to(skip_sum_ref[...], (8, channels)), collect_ref[...]
    )[:1]

    def convolve_back(raw_ref, grads_ref, slopes_ref, kernel_ref, out_ref, sums_ref, width_all):
        for start, width in slabs(width_all):
            cols = pl.ds(start, width)
            grad = grads_ref[:, cols] * slopes_ref[:, cols]
            raw = raw_ref[:, cols]
            total = kernel_ref[taps - 1 : taps, cols] * grad
            sums_ref[0, taps - 1 : taps, cols] = jnp.sum(grad * raw, axis=0, keepdims=True)
            for tap in range(taps - 1):
                shifted = sooner(grad, taps - 1 - tap)
                total = total + kernel_ref[tap : tap + 1, cols] * shifted
                sums_ref[0, tap : tap + 1, cols] = jnp.sum(shifted * raw, axis=0, keepdims=True)
            sums_ref[0, taps : taps + 1, cols] = jnp.sum(grad, axis=0, keepdims=True)
            out_ref[:, cols] = total.astype(jnp.bfloat16)

    convolve_back(
        input_ref,
        act_ref,
        slope_ref,
        input_kernel_ref,
        grad_input_ref,
        grad_input_conv_ref,
        channels,
    )
    convolve_back(
        state_ref,
        both_ref,
        both_slope_ref,
        state_kernel_ref,
        grad_state_ref,
        grad_state_conv_ref,
        2 * states,
    )


def by_sequence(length, width):
    return pl.BlockSpec((length, width), lambda seq: (seq, 0))


def fixed(*shape):
    return pl.BlockSpec(shape, lambda seq: (0,) * len(shape))


def head_spread(heads):
    marks = np.zeros((LANES, heads * HD), np.float32)
    for head in range(heads):
        marks[head, head * HD : (head + 1) * HD] = 1.0
    return marks


def pad_lanes(part):
    return jnp.pad(part, ((0, 0), (0, LANES - part.shape[1])))


def ssd_small(input_kernel, input_shift, state_kernel, state_shift, step_bias, decay_log, skip_gain):
    rates = -jnp.exp(decay_log)
    return (
        input_kernel,
        input_shift[None, :],
        state_kernel,
        state_shift[None, :],
        pad_lanes(step_bias[None, :]),
        pad_lanes(rates[None, :]),
        jnp.repeat(skip_gain, HD)[None, :],
    )


def ssd_forward(inputs, states_raw, gate, step, small, heads, length):
    group, channels = inputs.shape
    seqs = group // length
    both = states_raw.shape[1]
    states = both // 2
    chunks = length // SPAN
    taps = small[0].shape[0]
    return pl.pallas_call(
        ssd_forward_kernel,
        grid=(seqs,),
        in_specs=[
            by_sequence(length, channels),
            by_sequence(length, both),
            by_sequence(length, channels),
            by_sequence(length, LANES),
            fixed(taps, channels),
            fixed(1, channels),
            fixed(taps, both),
            fixed(1, both),
            fixed(1, LANES),
            fixed(1, LANES),
            fixed(1, channels),
            fixed(LANES, channels),
        ],
        out_specs=[
            by_sequence(length, channels),
            by_sequence(length, channels),
            pl.BlockSpec((chunks, states, channels), lambda seq: (seq, 0, 0)),
        ],
        out_shape=[
            jax.ShapeDtypeStruct((group, channels), jnp.bfloat16),
            jax.ShapeDtypeStruct((group, channels), jnp.float32),
            jax.ShapeDtypeStruct((seqs * chunks, states, channels), jnp.float32),
        ],
        scratch_shapes=[
            pltpu.VMEM((length, channels), jnp.float32),
            pltpu.VMEM((length, both), jnp.float32),
            pltpu.VMEM((states, channels), jnp.float32),
        ],
        compiler_params=pltpu.CompilerParams(vmem_limit_bytes=VMEM_LIMIT),
        cost_estimate=pl.CostEstimate(
            flops=8 * group * channels * SPAN,
            bytes_accessed=20 * group * channels,
            transcendentals=group * heads * SPAN,
        ),
        name="ssd_forward",
    )(inputs, states_raw, gate, step, *small, jnp.asarray(head_spread(heads)))


def ssd_backward(inputs, states_raw, gate, step, grad, carry, small, heads, length):
    group, channels = inputs.shape
    seqs = group // length
    both = states_raw.shape[1]
    states = both // 2
    chunks = length // SPAN
    taps = small[0].shape[0]
    return pl.pallas_call(
        ssd_backward_kernel,
        grid=(seqs,),
        in_specs=[
            by_sequence(length, channels),
            by_sequence(length, both),
            by_sequence(length, channels),
            by_sequence(length, LANES),
            by_sequence(length, channels),
            pl.BlockSpec((chunks, states, channels), lambda seq: (seq, 0, 0)),
            fixed(taps, channels),
            fixed(1, channels),
            fixed(taps, both),
            fixed(1, both),
            fixed(1, LANES),
            fixed(1, LANES),
            fixed(1, channels),
            fixed(LANES, channels),
            fixed(channels, LANES),
        ],
        out_specs=[
            by_sequence(length, channels),
            by_sequence(length, both),
            by_sequence(length, LANES),
            pl.BlockSpec((1, 8, channels), lambda seq: (seq, 0, 0)),
            pl.BlockSpec((1, 8, both), lambda seq: (seq, 0, 0)),
            pl.BlockSpec((1, 8, LANES), lambda seq: (seq, 0, 0)),
        ],
        out_shape=[
            jax.ShapeDtypeStruct((group, channels), jnp.bfloat16),
            jax.ShapeDtypeStruct((group, both), jnp.bfloat16),
            jax.ShapeDtypeStruct((group, LANES), jnp.bfloat16),
            jax.ShapeDtypeStruct((seqs, 8, channels), jnp.float32),
            jax.ShapeDtypeStruct((seqs, 8, both), jnp.float32),
            jax.ShapeDtypeStruct((seqs, 8, LANES), jnp.float32),
        ],
        scratch_shapes=[
            pltpu.VMEM((length, channels), jnp.float32),
            pltpu.VMEM((length, channels), jnp.float32),
            pltpu.VMEM((length, both), jnp.float32),
            pltpu.VMEM((length, both), jnp.float32),
            pltpu.VMEM((states, channels), jnp.float32),
            pltpu.VMEM((3, SPAN, channels), jnp.float32),
            pltpu.VMEM((LANES, SPAN), jnp.float32),
            pltpu.VMEM((SPAN, LANES), jnp.float32),
            pltpu.VMEM((1, channels), jnp.float32),
            pltpu.VMEM((1, channels), jnp.float32),
        ],
        compiler_params=pltpu.CompilerParams(vmem_limit_bytes=VMEM_LIMIT),
        cost_estimate=pl.CostEstimate(
            flops=20 * group * channels * SPAN,
            bytes_accessed=20 * group * channels,
            transcendentals=group * heads * SPAN,
        ),
        name="ssd_backward",
    )(
        inputs,
        states_raw,
        gate,
        step,
        grad,
        carry,
        *small,
        jnp.asarray(head_spread(heads)),
        jnp.asarray(head_spread(heads).T.copy()),
    )


def rope_wide(length):
    half = HD // 2
    freqs = np.float32(ROPE_BASE) ** (-np.arange(half, dtype=np.float32) * np.float32(2.0 / HD))
    angles = np.arange(length, dtype=np.float32)[:, None] * freqs[None, :].astype(np.float32)
    cosine, sine = np.cos(angles), np.sin(angles)
    count = LANES // HD
    return (
        np.concatenate([cosine, cosine] * count, axis=1).astype(np.float32),
        np.concatenate([-sine, sine] * count, axis=1).astype(np.float32),
    )


def turn(part, cosine, sine):
    half = HD // 2
    first = lane_index(part.shape) % HD < half
    swapped = jnp.where(first, pltpu.roll(part, LANES - half, 1), pltpu.roll(part, half, 1))
    return part * cosine + swapped * sine


def attend_forward_kernel(
    query_ref, pair_ref, cosine_ref, sine_ref, context_ref, query_out_ref, pair_out_ref, total_ref
):
    length = query_ref.shape[0]
    cosine, sine = cosine_ref[...], sine_ref[...]
    pair = pair_ref[...]
    left = lane_index(pair.shape) < HD
    pair = jnp.where(left, turn(pair, cosine, sine), pair)
    pair_out_ref[...] = pair.astype(jnp.bfloat16)
    moved = pltpu.roll(pair, HD, 1)
    keys = jnp.where(left, pair, moved).astype(jnp.bfloat16)
    values = jnp.where(left, moved, pair).astype(jnp.bfloat16)
    scale = HD ** (-0.5)
    for slab in range(query_ref.shape[1] // LANES):
        cols = pl.ds(slab * LANES, LANES)
        query_out_ref[:, cols] = turn(query_ref[:, cols], cosine, sine).astype(jnp.bfloat16)
        for tile in range(length // SPAN):
            rows = slice(tile * SPAN, (tile + 1) * SPAN)
            count = (tile + 1) * SPAN
            query = query_out_ref[rows, cols]
            lane = lane_index(query.shape)
            square = (SPAN, count)
            causal = row_index(square) + tile * SPAN >= lane_index(square)
            results = []
            for place in range(LANES // HD):
                mine = (lane >= place * HD) & (lane < place * HD + HD)
                scores = low_against(jnp.where(mine, query, 0), keys[:count]) * scale
                scores = jnp.where(causal, scores, -jnp.inf)
                peak = jnp.max(scores, axis=-1, keepdims=True)
                grown = jnp.exp(scores - peak)
                total = jnp.sum(grown, axis=-1, keepdims=True)
                probs = grown * (1.0 / total)
                results.append(low_dot(probs, values[:count]))
                head = slab * (LANES // HD) + place
                total_ref[rows, head : head + 1] = jnp.log(total) + peak
            context_ref[rows, cols] = jnp.where(lane < HD, results[0], results[1]).astype(
                jnp.bfloat16
            )


def attend_backward_kernel(
    query_ref,
    pair_ref,
    total_ref,
    grad_ref,
    cosine_ref,
    sine_ref,
    grad_query_ref,
    grad_pair_ref,
    key_sum_ref,
    value_sum_ref,
):
    length = query_ref.shape[0]
    cosine, sine = cosine_ref[...], -sine_ref[...]
    pair = pair_ref[...].astype(jnp.float32)
    left = lane_index(pair.shape) < HD
    moved = pltpu.roll(pair, HD, 1)
    keys = jnp.where(left, pair, moved).astype(jnp.bfloat16)
    values = jnp.where(left, moved, pair).astype(jnp.bfloat16)
    scale = HD ** (-0.5)
    key_sum_ref[...] = jnp.zeros_like(key_sum_ref)
    value_sum_ref[...] = jnp.zeros_like(value_sum_ref)
    for slab in range(query_ref.shape[1] // LANES):
        cols = pl.ds(slab * LANES, LANES)
        for tile in range(length // SPAN):
            rows = slice(tile * SPAN, (tile + 1) * SPAN)
            count = (tile + 1) * SPAN
            query = query_ref[rows, cols]
            upstream = grad_ref[rows, cols]
            lane = lane_index(query.shape)
            square = (SPAN, count)
            causal = row_index(square) + tile * SPAN >= lane_index(square)
            results = []
            for place in range(LANES // HD):
                mine = (lane >= place * HD) & (lane < place * HD + HD)
                head = slab * (LANES // HD) + place
                own_query = jnp.where(mine, query, 0)
                own_up = jnp.where(mine, upstream, 0)
                scores = low_against(own_query, keys[:count]) * scale
                scores = jnp.where(causal, scores, -jnp.inf)
                probs = jnp.exp(scores - total_ref[rows, head : head + 1])
                grad_probs = low_against(own_up, values[:count])
                mean = jnp.sum(probs * grad_probs, axis=-1, keepdims=True)
                grad_scores = (probs * (grad_probs - mean)).astype(jnp.bfloat16)
                results.append(low_dot(grad_scores, keys[:count]))
                key_sum_ref[0:count, :] += low_inner(grad_scores, own_query)
                value_sum_ref[0:count, :] += low_inner(probs, own_up)
            grad_query = jnp.where(lane < HD, results[0], results[1]) * scale
            grad_query_ref[rows, cols] = turn(
                grad_query, cosine[rows, :], sine[rows, :]
            ).astype(jnp.bfloat16)
    grad_key = key_sum_ref[...]
    grad_key = turn((grad_key + pltpu.roll(grad_key, HD, 1)) * scale, cosine, sine)
    grad_value = value_sum_ref[...]
    grad_value = grad_value + pltpu.roll(grad_value, HD, 1)
    grad_pair_ref[...] = jnp.where(left, grad_key, grad_value).astype(jnp.bfloat16)


def attend_forward(query, pair, length):
    group, width = query.shape
    heads = width // HD
    cosine, sine = rope_wide(length)
    return pl.pallas_call(
        attend_forward_kernel,
        grid=(group // length,),
        in_specs=[
            by_sequence(length, width),
            by_sequence(length, LANES),
            fixed(length, LANES),
            fixed(length, LANES),
        ],
        out_specs=[
            by_sequence(length, width),
            by_sequence(length, width),
            by_sequence(length, LANES),
            by_sequence(length, LANES),
        ],
        out_shape=[
            jax.ShapeDtypeStruct((group, width), jnp.bfloat16),
            jax.ShapeDtypeStruct((group, width), jnp.bfloat16),
            jax.ShapeDtypeStruct((group, LANES), jnp.bfloat16),
            jax.ShapeDtypeStruct((group, LANES), jnp.float32),
        ],
        compiler_params=pltpu.CompilerParams(vmem_limit_bytes=VMEM_LIMIT),
        cost_estimate=pl.CostEstimate(
            flops=4 * group * width * length,
            bytes_accessed=12 * group * width,
            transcendentals=group * heads * length // 2,
        ),
        name="attend_forward",
    )(query, pair, jnp.asarray(cosine), jnp.asarray(sine))


def attend_backward(query, pair, total, grad, length):
    group, width = query.shape
    heads = width // HD
    cosine, sine = rope_wide(length)
    return pl.pallas_call(
        attend_backward_kernel,
        grid=(group // length,),
        in_specs=[
            by_sequence(length, width),
            by_sequence(length, LANES),
            by_sequence(length, LANES),
            by_sequence(length, width),
            fixed(length, LANES),
            fixed(length, LANES),
        ],
        out_specs=[by_sequence(length, width), by_sequence(length, LANES)],
        out_shape=[
            jax.ShapeDtypeStruct((group, width), jnp.bfloat16),
            jax.ShapeDtypeStruct((group, LANES), jnp.bfloat16),
        ],
        scratch_shapes=[
            pltpu.VMEM((length, LANES), jnp.float32),
            pltpu.VMEM((length, LANES), jnp.float32),
        ],
        compiler_params=pltpu.CompilerParams(vmem_limit_bytes=VMEM_LIMIT),
        cost_estimate=pl.CostEstimate(
            flops=10 * group * width * length,
            bytes_accessed=12 * group * width,
            transcendentals=group * heads * length // 2,
        ),
        name="attend_backward",
    )(query, pair, total, grad, jnp.asarray(cosine), jnp.asarray(sine))


def step_groups(size):
    bits = size.bit_length() - 1
    return [1] * min(bits, 2) + [2] * (max(bits - 2, 0) // 2) + [1] * (max(bits - 2, 0) % 2)


def after(part, *deps):
    return lax.optimization_barrier((part,) + deps)[0]


def behind(part, dep):
    zero = jnp.minimum(jnp.abs(dep[:1, :1].astype(jnp.float32)), 0.0)
    return part + zero.astype(part.dtype)


class Sum:
    def __init__(self, part, size):
        self.size = size
        self.direct = bool(size & (size - 1) or part.shape[0] % size)
        self.steps = [] if self.direct else step_groups(size)
        self.shift = 0
        self.part = part
        self.gives = [part]
        if not self.direct:
            self.part = part.reshape(size, part.shape[0] // size, part.shape[1])
            self.prepare()

    def prepare(self):
        if not self.steps:
            self.gives = [self.part]
            return
        ways = 1 << self.steps[0]
        rest = self.part.shape[0] // ways
        view = self.part.reshape((rest, ways) + self.part.shape[1:])
        mine = (lax.axis_index("dp") >> self.shift) & (ways - 1)
        self.keep = lax.dynamic_index_in_dim(view, mine, 1, False)
        self.gives = [
            lax.dynamic_index_in_dim(view, mine ^ way, 1, False) for way in range(1, ways)
        ]

    def advance(self, *deps):
        if self.steps:
            total = after(self.keep, *deps).astype(jnp.float32)
            for way, give in enumerate(self.gives, 1):
                pairs = [(index, index ^ (way << self.shift)) for index in range(self.size)]
                total = total + lax.ppermute(give, "dp", pairs).astype(jnp.float32)
            self.part = total.astype(jnp.bfloat16)
            self.shift += self.steps.pop(0)
            self.prepare()
        return self.gives

    def joined(self, middle=None, *deps):
        groups, shift = step_groups(self.size), self.size.bit_length() - 1
        part = after(self.reduced(), *deps)
        if middle is not None:
            part = middle(part)
        self.trail = [part]
        if self.direct:
            return part
        rows, width = part.shape
        for group in reversed(groups):
            ways = 1 << group
            shift -= group
            mine = (lax.axis_index("dp") >> shift) & (ways - 1)
            part = part.reshape(-1, 1, rows, width)
            got = [part]
            for way in range(1, ways):
                pairs = [(index, index ^ (way << shift)) for index in range(self.size)]
                got.append(lax.ppermute(part, "dp", pairs))
            for bit in range(group):
                flip = ((mine >> bit) & 1) == 1
                got = [
                    jnp.where(flip, got[way ^ (1 << bit)], got[way]) for way in range(ways)
                ]
            part = jnp.concatenate(got, axis=1)
            self.trail.append(part)
        return part.reshape(-1, width)

    def reduced(self):
        while self.steps:
            self.advance()
        return lax.psum(self.part, "dp") if self.direct else self.part[0]


def other(part):
    return lax.ppermute(part, "tensor", [(0, 1), (1, 0)])


def all_rows(part, shards):
    if shards != 2:
        return lax.all_gather(part, "tensor", axis=0, tiled=True)
    got = other(part)
    return jnp.where(
        lax.axis_index("tensor") == 0,
        jnp.concatenate([part, got], axis=0),
        jnp.concatenate([got, part], axis=0),
    )


def sum_all(part, shards, *deps):
    if shards != 2:
        return lax.psum(part, "tensor").astype(jnp.float32)
    return after(part, *deps).astype(jnp.float32) + other(part).astype(jnp.float32)


def sum_own(part, shards):
    if shards != 2:
        return lax.psum_scatter(part, "tensor", scatter_dimension=0, tiled=True).astype(jnp.float32)
    me = lax.axis_index("tensor")
    halves = part.reshape(2, part.shape[0] // 2, part.shape[1])
    keep = lax.dynamic_index_in_dim(halves, me, 0, False)
    got = other(lax.dynamic_index_in_dim(halves, 1 - me, 0, False))
    return keep.astype(jnp.float32) + got.astype(jnp.float32)


def own_rows(part, rows):
    return lax.dynamic_slice_in_dim(part, lax.axis_index("tensor") * rows, rows, 0)


def column_pack(vectors, rows):
    flat = jnp.concatenate([item.reshape(-1) for item in vectors])
    width = -(-flat.shape[0] // rows)
    return jnp.pad(flat, (0, width * rows - flat.shape[0])).reshape(width, rows).T


def column_unpack(packed, shapes):
    flat = packed.T.reshape(-1)
    out, start = [], 0
    for shape in shapes:
        count = 1
        for size in shape:
            count *= size
        out.append(flat[start : start + count].reshape(shape))
        start += count
    return out


def body(
    dp_size,
    shards,
    layer_input,
    input_gain,
    middle_gain,
    mamba_gate,
    mamba_input,
    step_weight,
    state_weight,
    input_kernel,
    input_shift,
    state_kernel,
    state_shift,
    step_bias,
    decay_log,
    skip_gain,
    mamba_output,
    query_weight,
    keyvalue_weight,
    context_weight,
    gate_weight,
    up_weight,
    down_weight,
    cotangent,
):
    own = layer_input.shape[0]
    rows_low = all_rows(layer_input, shards)
    cotan_low = all_rows(cotangent, shards)
    rows = rows_low.astype(jnp.float32)
    gain_first = input_gain.astype(jnp.float32)
    gain_second = middle_gain.astype(jnp.float32)
    factor_first = lax.rsqrt(jnp.mean(rows * rows, axis=-1, keepdims=True) + EPSILON)
    normal_first = rows * factor_first
    whole = (normal_first * gain_first).astype(jnp.bfloat16)
    group = whole.shape[0]
    length = min(SEQ_LEN, group)
    seqs = group // length
    heads_here = query_weight.shape[1] // HD
    kv_head = lax.axis_index("tensor") * heads_here // (HQ // KVH)
    key_cols = lax.dynamic_slice_in_dim(keyvalue_weight, kv_head * HD, HD, 1)
    value_cols = lax.dynamic_slice_in_dim(keyvalue_weight, (KVH + kv_head) * HD, HD, 1)
    pair_weight = jnp.concatenate([key_cols, value_cols], axis=1)
    query_cols = query_weight.shape[1]
    query_pad = -query_cols % LANES
    query_wide = jnp.pad(query_weight, ((0, 0), (0, query_pad)))
    step_wide = pad_lanes(step_weight)
    heads = step_weight.shape[1]
    input_raw = forward_dot(whole, mamba_input)
    state_raw = forward_dot(whole, state_weight)
    step_raw = forward_dot(whole, step_wide)
    gate_raw = forward_dot(whole, mamba_gate)
    query_raw = forward_dot(whole, query_wide)
    pair_raw = forward_dot(whole, pair_weight)
    small = ssd_small(
        input_kernel.astype(jnp.float32),
        input_shift.astype(jnp.float32),
        state_kernel.astype(jnp.float32),
        state_shift.astype(jnp.float32),
        step_bias.astype(jnp.float32),
        decay_log.astype(jnp.float32),
        skip_gain.astype(jnp.float32),
    )
    gated_low, ssm_out, carries = ssd_forward(
        input_raw, state_raw, gate_raw, step_raw, small, heads, length
    )
    context_wide, queries, pairs, totals = attend_forward(
        query_raw, pair_raw, length
    )
    context_rows = context_wide[:, :query_cols]
    count = 2 if shards == 2 else 1
    spans = [slice(index * group // count, (index + 1) * group // count) for index in range(count)]
    context_rows = after(context_rows, cotan_low)
    resids, normals, factors, mids = [], [], [], []
    hiddens, gate_lows, upper_lows, back_parts, back_mids = [], [], [], [], []
    mixed_parts = [
        (
            forward_dot(gated_low[span], mamba_output)
            + forward_dot(context_rows[span], context_weight)
        ).astype(jnp.bfloat16)
        for span in spans
    ]
    for span, mixed_part in zip(spans, mixed_parts):
        resid = rows[span] + sum_all(mixed_part, shards, *back_parts)
        factor = lax.rsqrt(jnp.mean(resid * resid, axis=-1, keepdims=True) + EPSILON)
        normal = resid * factor
        mid = (normal * gain_second).astype(jnp.bfloat16)
        gate = forward_dot(mid, gate_weight)
        upper = forward_dot(mid, up_weight)
        sigmoid_gate = jax.nn.sigmoid(gate)
        silu_gate = gate * sigmoid_gate
        grad_hidden = against(cotan_low[span], down_weight)
        slope = sigmoid_gate * (1.0 + gate * (1.0 - sigmoid_gate))
        gate_low = (grad_hidden * upper * slope).astype(jnp.bfloat16)
        upper_low = (grad_hidden * silu_gate).astype(jnp.bfloat16)
        back_part = (against(gate_low, gate_weight) + against(upper_low, up_weight)).astype(
            jnp.bfloat16
        )
        resids.append(resid)
        normals.append(normal)
        factors.append(factor)
        mids.append(mid)
        hiddens.append((silu_gate * upper).astype(jnp.bfloat16))
        gate_lows.append(gate_low)
        upper_lows.append(upper_low)
        back_parts.append(back_part)
    back_mids = [sum_all(back_part, shards, *back_parts) for back_part in back_parts]
    whole_mid = jnp.concatenate(mids, axis=0)
    hidden = jnp.concatenate(hiddens, axis=0)
    grad_down = inner_rows(hidden, cotan_low).astype(jnp.bfloat16)
    grad_gate = inner_rows(whole_mid, jnp.concatenate(gate_lows, axis=0)).astype(jnp.bfloat16)
    grad_up = inner_rows(whole_mid, jnp.concatenate(upper_lows, axis=0)).astype(jnp.bfloat16)
    grad_gate, grad_up, grad_down = lax.psum((grad_gate, grad_up, grad_down), "dp")
    feed_part = behind(forward_dot(hidden, down_weight), back_mids[-1]).astype(jnp.bfloat16)
    grad_middle = sum(
        jnp.sum(back_part.astype(jnp.float32) * normal, axis=0)
        for back_part, normal in zip(back_parts, normals)
    )
    grad_resids = [
        cotan_low[span].astype(jnp.float32) + norm_back(back_mid, gain_second, normal, factor)
        for span, back_mid, normal, factor in zip(spans, back_mids, normals, factors)
    ]

    def own_piece(pieces):
        if len(pieces) == 1:
            return own_rows(pieces[0], own)
        return jnp.where(lax.axis_index("tensor") == 0, pieces[0], pieces[1])

    mixer_all = jnp.concatenate([piece.astype(jnp.bfloat16) for piece in grad_resids], axis=0)
    ssm_rows = gated_low.shape[1]
    width = whole.shape[1]
    split_pairs = shards == KVH
    grad_gated = against(mixer_all, mamba_output)
    mixer_sum = Sum(
        inner_rows(jnp.concatenate([gated_low, context_rows], axis=1), mixer_all).astype(
            jnp.bfloat16
        ),
        dp_size,
    )
    grad_input_raw, grad_state_raw, grad_step_raw, input_sums, state_sums, head_sums = ssd_backward(
        input_raw,
        state_raw,
        gate_raw,
        step_raw,
        after(grad_gated, *mixer_sum.gives),
        carries,
        small,
        heads,
        length,
    )
    input_sums = jnp.sum(input_sums, axis=0)
    state_sums = jnp.sum(state_sums, axis=0)
    head_sums = jnp.sum(head_sums, axis=0)[:, :heads]
    taps = input_kernel.shape[0]
    state_cols = state_weight.shape[1]
    step_cols = heads
    late_cols = jnp.concatenate([grad_input_raw, grad_state_raw], axis=1)
    late_sum = Sum(inner_rows(whole, late_cols).astype(jnp.bfloat16), dp_size)

    sigmoid_raw = jax.nn.sigmoid(gate_raw)
    grad_gate_raw = (
        grad_gated * ssm_out * (sigmoid_raw * (1.0 + gate_raw * (1.0 - sigmoid_raw)))
    ).astype(jnp.bfloat16)
    grad_context = against(mixer_all, context_weight).astype(jnp.bfloat16)
    grad_context = jnp.pad(grad_context, ((0, 0), (0, query_pad)))
    grad_query_raw, grad_pair_raw = attend_backward(
        queries, pairs, totals, after(grad_context, *late_sum.gives, *mixer_sum.advance()), length
    )
    early_cols = jnp.concatenate(
        [grad_gate_raw, grad_query_raw[:, :query_cols], grad_pair_raw, grad_step_raw], axis=1
    )
    total = against(late_cols, jnp.concatenate([mamba_input, state_weight], axis=1))
    total = total + against(
        early_cols, jnp.concatenate([mamba_gate, query_weight, pair_weight, step_wide], axis=1)
    )
    total_low = total.astype(jnp.bfloat16)
    grad_first = jnp.sum(total_low.astype(jnp.float32) * normal_first, axis=0)
    own_vectors = (input_sums[:taps], input_sums[taps], head_sums[0], head_sums[1], head_sums[2])
    shared_vectors = (grad_first, grad_middle, state_sums[:taps], state_sums[taps])
    own_pack = column_pack(own_vectors, width)
    shared_pack = column_pack(shared_vectors, width)
    shared_lane = step_cols + own_pack.shape[1]
    last_lane = shared_lane + shared_pack.shape[1]
    early = inner_rows(whole, early_cols)
    if not split_pairs:
        spread = jnp.zeros((width, 2 * KVH * HD), jnp.float32)
        spread = lax.dynamic_update_slice_in_dim(
            spread, early[:, -2 * HD - LANES : -HD - LANES], kv_head * HD, 1
        )
        spread = lax.dynamic_update_slice_in_dim(
            spread, early[:, -HD - LANES : -LANES], (KVH + kv_head) * HD, 1
        )
        early = jnp.concatenate(
            [early[:, : -2 * HD - LANES], spread, early[:, -LANES:]], axis=1
        )
    packs = jnp.pad(
        jnp.concatenate([own_pack, shared_pack], axis=1),
        ((0, 0), (early.shape[1] - LANES + step_cols, LANES - last_lane)),
    )
    early_sum = Sum((early + packs).astype(jnp.bfloat16), dp_size)

    def early_over_tensor(part):
        count = (2 * HD if split_pairs else 2 * KVH * HD) + LANES
        mine = part[:, -count:]
        if split_pairs:
            got = other(mine)
            both = (mine.astype(jnp.float32) + got.astype(jnp.float32)).astype(jnp.bfloat16)
            first = lax.axis_index("tensor") == 0
            low, high = jnp.where(first, mine, got), jnp.where(first, got, mine)
            pair = [low[:, :HD], high[:, :HD], low[:, HD : 2 * HD], high[:, HD : 2 * HD]]
        else:
            both = lax.psum(mine, "tensor")
            pair = [both[:, :-LANES]]
        lane = lane_index((part.shape[0], LANES))
        extra = jnp.where(
            (lane >= shared_lane) & (lane < last_lane), both[:, -LANES:], mine[:, -LANES:]
        )
        return jnp.concatenate([part[:, :-count]] + pair + [extra], axis=1)

    def late_over_tensor(part):
        mine = part[:, -state_cols:]
        if shards == 2:
            both = mine.astype(jnp.float32) + other(mine).astype(jnp.float32)
        else:
            both = lax.psum(mine, "tensor")
        return jnp.concatenate([part[:, :-state_cols], both.astype(jnp.bfloat16)], axis=1)

    early_sum.advance()
    tail = late_sum.joined(late_over_tensor, *early_sum.gives)
    grad_mixer_out = mixer_sum.joined(None, *early_sum.gives)
    early = early_sum.joined(early_over_tensor)
    grad_gate, grad_up, grad_down = [
        after(item, early_sum.trail[min(1, len(early_sum.trail) - 1)])
        for item in (grad_gate, grad_up, grad_down)
    ]
    grad_mamba_out = grad_mixer_out[:ssm_rows]
    grad_context_w = grad_mixer_out[ssm_rows:]
    grad_mamba_input, grad_state = tail[:, :-state_cols], tail[:, -state_cols:]
    gate_cols = gate_raw.shape[1]
    extra = early[:, -LANES:]
    feed = sum_own(feed_part, shards)
    layer_output = (after(own_piece(resids), late_sum.trail[0]) + feed).astype(jnp.bfloat16)
    back_in = sum_own(total_low, shards)
    normal_own = own_rows(normal_first, own)
    factor_own = own_rows(factor_first, own)
    input_grad = after(own_piece(grad_resids), late_sum.trail[0]) + norm_back(back_in, gain_first, normal_own, factor_own)
    grad_step = extra[:, :step_cols]
    grad_in_kernel, grad_in_shift, grad_bias, grad_decay, grad_skip = column_unpack(
        extra[:, step_cols:shared_lane], [item.shape for item in own_vectors]
    )
    grad_first, grad_middle, grad_st_kernel, grad_st_shift = column_unpack(
        extra[:, shared_lane:last_lane], [item.shape for item in shared_vectors]
    )
    results = (
        grad_first,
        grad_middle,
        early[:, :gate_cols],
        grad_mamba_input,
        grad_step,
        grad_state,
        grad_in_kernel,
        grad_in_shift,
        grad_st_kernel,
        grad_st_shift,
        grad_bias,
        grad_decay,
        grad_skip,
        grad_mamba_out,
        early[:, gate_cols : gate_cols + query_cols],
        early[:, gate_cols + query_cols : -LANES],
        grad_context_w,
        grad_gate,
        grad_up,
        grad_down,
    )
    return (layer_output, input_grad) + tuple(item.astype(jnp.float32) for item in results)


def solution(mesh):
    in_specs = (
        P(("dp", "tensor"), None),
        P(),
        P(),
        P(None, "tensor"),
        P(None, "tensor"),
        P(None, "tensor"),
        P(),
        P(None, "tensor"),
        P("tensor"),
        P(),
        P(),
        P("tensor"),
        P("tensor"),
        P("tensor"),
        P("tensor", None),
        P(None, "tensor"),
        P(),
        P("tensor", None),
        P(None, "tensor"),
        P(None, "tensor"),
        P("tensor", None),
        P(("dp", "tensor"), None),
    )
    out_specs = (
        P(("dp", "tensor"), None),
        P(("dp", "tensor"), None),
        P(),
        P(),
        P(None, "tensor"),
        P(None, "tensor"),
        P(None, "tensor"),
        P(),
        P(None, "tensor"),
        P("tensor"),
        P(),
        P(),
        P("tensor"),
        P("tensor"),
        P("tensor"),
        P("tensor", None),
        P(None, "tensor"),
        P(),
        P("tensor", None),
        P(None, "tensor"),
        P(None, "tensor"),
        P("tensor", None),
    )
    run = partial(body, mesh.shape["dp"], mesh.shape["tensor"])
    return jax.shard_map(run, mesh=mesh, in_specs=in_specs, out_specs=out_specs, check_vma=False)
```

```python
from functools import partial

import jax
import jax.numpy as jnp
import numpy as np
from jax import lax
from jax.experimental import pallas as pl
from jax.experimental.pallas import tpu as pltpu
from jax.sharding import PartitionSpec as P

HD = 64
HQ = 8
KVH = 2
SPAN = 128
SEQ_LEN = 1024


EPSILON = 1e-05
ROPE_BASE = 10000.0
PRECISE = lax.Precision.HIGHEST


def forward_dot(left, right):
    return jnp.dot(left, right, preferred_element_type=jnp.float32)


def inner_rows(left, right):
    return lax.dot_general(
        left, right, (((0,), (0,)), ((), ())), preferred_element_type=jnp.float32
    )


def against(left, right):
    return lax.dot_general(
        left, right, (((1,), (1,)), ((), ())), preferred_element_type=jnp.float32
    )


def norm_back(upstream, gain, normal, factor):
    scaled = upstream * gain
    return factor * (scaled - normal * jnp.mean(scaled * normal, axis=-1, keepdims=True))


LANES = 128
VMEM_LIMIT = 44 * 1024 * 1024


def exact_dot(left, right):
    return jnp.dot(left, right, precision=PRECISE, preferred_element_type=jnp.float32)


def low_dot(left, right):
    return jnp.dot(
        left.astype(jnp.bfloat16), right.astype(jnp.bfloat16), preferred_element_type=jnp.float32
    )


def low_against(left, right):
    return lax.dot_general(
        left.astype(jnp.bfloat16),
        right.astype(jnp.bfloat16),
        (((1,), (1,)), ((), ())),
        preferred_element_type=jnp.float32,
    )


def low_inner(left, right):
    return lax.dot_general(
        left.astype(jnp.bfloat16),
        right.astype(jnp.bfloat16),
        (((0,), (0,)), ((), ())),
        preferred_element_type=jnp.float32,
    )


def row_index(shape):
    return lax.broadcasted_iota(jnp.int32, shape, 0)


def lane_index(shape):
    return lax.broadcasted_iota(jnp.int32, shape, 1)


def later(part, count):
    if count == 0:
        return part
    return jnp.where(row_index(part.shape) >= count, pltpu.roll(part, count, 0), 0.0)


def sooner(part, count):
    if count == 0:
        return part
    rows = part.shape[0]
    return jnp.where(row_index(part.shape) < rows - count, pltpu.roll(part, rows - count, 0), 0.0)


def slabs(width):
    return [(start, min(LANES, width - start)) for start in range(0, width, LANES)]


def soft_plus(value):
    return jnp.maximum(value, 0.0) + jnp.log1p(jnp.exp(-jnp.abs(value)))


def stacked_heads(part, heads):
    if heads == 1:
        return part
    lane = lane_index(part.shape)
    return jnp.concatenate(
        [jnp.where((lane >= head * HD) & (lane < head * HD + HD), part, 0.0) for head in range(heads)],
        axis=0,
    )


def convolve(raw, kernel_ref, shift_ref, cols):
    taps = kernel_ref.shape[0]
    out = shift_ref[:, cols] + kernel_ref[taps - 1 : taps, cols] * raw
    for tap in range(taps - 1):
        out = out + kernel_ref[tap : tap + 1, cols] * later(raw, taps - 1 - tap)
    return out


def chunk_steps(step_ref, bias_ref, rate_ref, expand_ref, rows):
    raw = step_ref[rows, :] + bias_ref[...]
    steps = soft_plus(raw)
    logdec = steps * rate_ref[...]
    square = (SPAN, SPAN)
    lower = (row_index(square) >= lane_index(square)).astype(jnp.float32)
    cumul = exact_dot(lower, logdec)
    grown = jnp.exp(cumul)
    tail = jnp.exp(cumul[SPAN - 1 : SPAN, :] - cumul)
    wide = exact_dot(jnp.concatenate([steps, grown, tail], axis=0), expand_ref[...])
    return raw, steps, cumul, wide[:SPAN], wide[SPAN : 2 * SPAN], wide[2 * SPAN :]


def ssd_forward_kernel(
    input_ref,
    state_ref,
    gate_ref,
    step_ref,
    input_kernel_ref,
    input_shift_ref,
    state_kernel_ref,
    state_shift_ref,
    bias_ref,
    rate_ref,
    skip_ref,
    expand_ref,
    gated_ref,
    out_ref,
    carry_ref,
    act_ref,
    both_ref,
    held_ref,
):
    channels = input_ref.shape[1]
    states = state_ref.shape[1] // 2
    for start, width in slabs(channels):
        cols = pl.ds(start, width)
        pre = convolve(input_ref[:, cols], input_kernel_ref, input_shift_ref, cols)
        act_ref[:, cols] = pre * jax.nn.sigmoid(pre)
    for start, width in slabs(2 * states):
        cols = pl.ds(start, width)
        pre = convolve(state_ref[:, cols], state_kernel_ref, state_shift_ref, cols)
        both_ref[:, cols] = pre * jax.nn.sigmoid(pre)
    held_ref[...] = jnp.zeros_like(held_ref)

    def chunk(index, unused):
        rows = pl.ds(pl.multiple_of(index * SPAN, SPAN), SPAN)
        raw, steps, cumul, step_wide, grown_wide, tail_wide = chunk_steps(
            step_ref, bias_ref, rate_ref, expand_ref, rows
        )
        cumul_turned = cumul.T
        entry = both_ref[rows, pl.ds(0, states)].astype(jnp.bfloat16)
        readout = both_ref[rows, pl.ds(states, states)].astype(jnp.bfloat16)
        cross = low_against(readout, entry)
        square = (SPAN, SPAN)
        lower = row_index(square) >= lane_index(square)
        for start, width in slabs(channels):
            cols = pl.ds(start, width)
            span = slice(start, start + width)
            heads = width // HD
            values = act_ref[rows, cols]
            scaled = values * step_wide[:, span]
            held = held_ref[:, cols]
            carry_ref[index, :, cols] = held
            weights = []
            for head in range(start // HD, start // HD + heads):
                spread = cumul[:, head : head + 1] - cumul_turned[head : head + 1, :]
                decay = jnp.exp(jnp.where(lower, spread, -jnp.inf))
                weights.append((decay * cross).astype(jnp.bfloat16))
            weights = jnp.concatenate(weights, axis=1) if heads > 1 else weights[0]
            result = low_dot(weights, stacked_heads(scaled, heads))
            result = result + low_dot(readout, held) * grown_wide[:, span]
            held_ref[:, cols] = held * grown_wide[SPAN - 1 : SPAN, span] + low_inner(
                entry, scaled * tail_wide[:, span]
            )
            result = result + skip_ref[:, cols] * values
            out_ref[rows, cols] = result
            gate = gate_ref[rows, cols]
            gated_ref[rows, cols] = (result * (gate * jax.nn.sigmoid(gate))).astype(jnp.bfloat16)
        return unused

    lax.fori_loop(0, input_ref.shape[0] // SPAN, chunk, 0)


def ssd_backward_kernel(
    input_ref,
    state_ref,
    gate_ref,
    step_ref,
    grad_ref,
    carry_ref,
    input_kernel_ref,
    input_shift_ref,
    state_kernel_ref,
    state_shift_ref,
    bias_ref,
    rate_ref,
    skip_ref,
    expand_ref,
    collect_ref,
    grad_input_ref,
    grad_state_ref,
    grad_step_ref,
    grad_input_conv_ref,
    grad_state_conv_ref,
    grad_head_ref,
    act_ref,
    slope_ref,
    both_ref,
    both_slope_ref,
    held_ref,
    wide_ref,
    turned_ref,
    column_ref,
    skip_sum_ref,
    scale_sum_ref,
):
    channels = input_ref.shape[1]
    states = state_ref.shape[1] // 2
    taps = input_kernel_ref.shape[0]
    for start, width in slabs(channels):
        cols = pl.ds(start, width)
        pre = convolve(input_ref[:, cols], input_kernel_ref, input_shift_ref, cols)
        sigma = jax.nn.sigmoid(pre)
        act_ref[:, cols] = pre * sigma
        slope_ref[:, cols] = sigma * (1.0 + pre * (1.0 - sigma))
    for start, width in slabs(2 * states):
        cols = pl.ds(start, width)
        pre = convolve(state_ref[:, cols], state_kernel_ref, state_shift_ref, cols)
        sigma = jax.nn.sigmoid(pre)
        both_ref[:, cols] = pre * sigma
        both_slope_ref[:, cols] = sigma * (1.0 + pre * (1.0 - sigma))
    held_ref[...] = jnp.zeros_like(held_ref)
    turned_ref[...] = jnp.zeros_like(turned_ref)
    column_ref[...] = jnp.zeros_like(column_ref)
    grad_head_ref[...] = jnp.zeros_like(grad_head_ref)
    skip_sum_ref[...] = jnp.zeros_like(skip_sum_ref)
    chunks = input_ref.shape[0] // SPAN

    def chunk(count, unused):
        index = chunks - 1 - count
        rows = pl.ds(pl.multiple_of(index * SPAN, SPAN), SPAN)
        raw, steps, cumul, step_wide, grown_wide, tail_wide = chunk_steps(
            step_ref, bias_ref, rate_ref, expand_ref, rows
        )
        cumul_turned = cumul.T
        entry = both_ref[rows, pl.ds(0, states)].astype(jnp.bfloat16)
        readout = both_ref[rows, pl.ds(states, states)].astype(jnp.bfloat16)
        cross = low_against(entry, readout)
        square = (SPAN, SPAN)
        upper = row_index(square) <= lane_index(square)
        grad_cross = jnp.zeros(square, jnp.float32)
        grad_entry = jnp.zeros((SPAN, states), jnp.float32)
        grad_readout = jnp.zeros((SPAN, states), jnp.float32)
        for start, width in slabs(channels):
            cols = pl.ds(start, width)
            span = slice(start, start + width)
            heads = width // HD
            values = act_ref[rows, cols]
            scaled = values * step_wide[:, span]
            gate = gate_ref[rows, cols]
            upstream = grad_ref[rows, cols] * (gate * jax.nn.sigmoid(gate))
            held = held_ref[:, cols]
            before = carry_ref[index, :, cols]
            stacked_up = stacked_heads(upstream, heads).astype(jnp.bfloat16)
            products = low_against(scaled, stacked_up)
            weights = []
            for place in range(heads):
                head = start // HD + place
                spread = cumul_turned[head : head + 1, :] - cumul[:, head : head + 1]
                decay = jnp.exp(jnp.where(upper, spread, -jnp.inf))
                product = products[:, place * SPAN : (place + 1) * SPAN] * decay
                grad_cross = grad_cross + product
                flow = product * cross
                turned_ref[head : head + 1, :] = jnp.sum(flow, axis=0, keepdims=True)
                column_ref[:, head : head + 1] = jnp.sum(flow, axis=1, keepdims=True)
                weights.append((decay * cross).astype(jnp.bfloat16))
            weights = jnp.concatenate(weights, axis=1) if heads > 1 else weights[0]
            grown_up = upstream * grown_wide[:, span]
            tailed = scaled * tail_wide[:, span]
            from_held = low_dot(entry, held)
            grad_scaled = low_dot(weights, stacked_up) + tail_wide[:, span] * from_held
            wide_ref[0, :, cols] = grown_up * low_dot(readout, before)
            wide_ref[1, :, cols] = tailed * from_held
            wide_ref[2, :, cols] = values * grad_scaled
            grad_readout = grad_readout + low_against(grown_up, before)
            grad_entry = grad_entry + low_against(tailed, held)
            last = grown_wide[SPAN - 1 : SPAN, span]
            scale_sum_ref[:, cols] = jnp.sum(held * before, axis=0, keepdims=True) * last
            skip_sum_ref[:, cols] += jnp.sum(upstream * values, axis=0, keepdims=True)
            held_ref[:, cols] = held * last + low_inner(readout, grown_up)
            act_ref[rows, cols] = step_wide[:, span] * grad_scaled + skip_ref[:, cols] * upstream
        sums = exact_dot(
            jnp.concatenate([wide_ref[0], wide_ref[1], wide_ref[2]], axis=0), collect_ref[...]
        )
        scale_sum = exact_dot(jnp.broadcast_to(scale_sum_ref[...], (8, channels)), collect_ref[...])
        flows = turned_ref[...].T - column_ref[...] + sums[:SPAN]
        onward = (row_index(square) <= lane_index(square)).astype(jnp.float32)
        strict = (row_index(square) > lane_index(square)).astype(jnp.float32)
        grad_log = (
            exact_dot(onward, flows)
            + exact_dot(strict, sums[SPAN : 2 * SPAN])
            + scale_sum[:1]
        )
        grad_steps = grad_log * rate_ref[...] + sums[2 * SPAN :]
        grad_raw = grad_steps * jax.nn.sigmoid(raw)
        grad_step_ref[rows, :] = grad_raw.astype(jnp.bfloat16)
        grad_head_ref[0, 0:1, :] += jnp.sum(grad_raw, axis=0, keepdims=True)
        grad_head_ref[0, 1:2, :] += (
            jnp.sum(grad_log * steps, axis=0, keepdims=True) * rate_ref[...]
        )
        both_ref[rows, pl.ds(0, states)] = grad_entry + low_dot(grad_cross, readout)
        both_ref[rows, pl.ds(states, states)] = grad_readout + low_inner(grad_cross, entry)
        return unused

    lax.fori_loop(0, chunks, chunk, 0)
    grad_head_ref[0, 2:3, :] = exact_dot(
        jnp.broadcast_to(skip_sum_ref[...], (8, channels)), collect_ref[...]
    )[:1]

    def convolve_back(raw_ref, grads_ref, slopes_ref, kernel_ref, out_ref, sums_ref, width_all):
        for start, width in slabs(width_all):
            cols = pl.ds(start, width)
            grad = grads_ref[:, cols] * slopes_ref[:, cols]
            raw = raw_ref[:, cols]
            total = kernel_ref[taps - 1 : taps, cols] * grad
            sums_ref[0, taps - 1 : taps, cols] = jnp.sum(grad * raw, axis=0, keepdims=True)
            for tap in range(taps - 1):
                shifted = sooner(grad, taps - 1 - tap)
                total = total + kernel_ref[tap : tap + 1, cols] * shifted
                sums_ref[0, tap : tap + 1, cols] = jnp.sum(shifted * raw, axis=0, keepdims=True)
            sums_ref[0, taps : taps + 1, cols] = jnp.sum(grad, axis=0, keepdims=True)
            out_ref[:, cols] = total.astype(jnp.bfloat16)

    convolve_back(
        input_ref,
        act_ref,
        slope_ref,
        input_kernel_ref,
        grad_input_ref,
        grad_input_conv_ref,
        channels,
    )
    convolve_back(
        state_ref,
        both_ref,
        both_slope_ref,
        state_kernel_ref,
        grad_state_ref,
        grad_state_conv_ref,
        2 * states,
    )


def by_sequence(length, width):
    return pl.BlockSpec((length, width), lambda seq: (seq, 0))


def fixed(*shape):
    return pl.BlockSpec(shape, lambda seq: (0,) * len(shape))


def head_spread(heads):
    marks = np.zeros((LANES, heads * HD), np.float32)
    for head in range(heads):
        marks[head, head * HD : (head + 1) * HD] = 1.0
    return marks


def pad_lanes(part):
    return jnp.pad(part, ((0, 0), (0, LANES - part.shape[1])))


def ssd_small(input_kernel, input_shift, state_kernel, state_shift, step_bias, decay_log, skip_gain):
    rates = -jnp.exp(decay_log)
    return (
        input_kernel,
        input_shift[None, :],
        state_kernel,
        state_shift[None, :],
        pad_lanes(step_bias[None, :]),
        pad_lanes(rates[None, :]),
        jnp.repeat(skip_gain, HD)[None, :],
    )


def ssd_forward(inputs, states_raw, gate, step, small, heads, length):
    group, channels = inputs.shape
    seqs = group // length
    both = states_raw.shape[1]
    states = both // 2
    chunks = length // SPAN
    taps = small[0].shape[0]
    return pl.pallas_call(
        ssd_forward_kernel,
        grid=(seqs,),
        in_specs=[
            by_sequence(length, channels),
            by_sequence(length, both),
            by_sequence(length, channels),
            by_sequence(length, LANES),
            fixed(taps, channels),
            fixed(1, channels),
            fixed(taps, both),
            fixed(1, both),
            fixed(1, LANES),
            fixed(1, LANES),
            fixed(1, channels),
            fixed(LANES, channels),
        ],
        out_specs=[
            by_sequence(length, channels),
            by_sequence(length, channels),
            pl.BlockSpec((chunks, states, channels), lambda seq: (seq, 0, 0)),
        ],
        out_shape=[
            jax.ShapeDtypeStruct((group, channels), jnp.bfloat16),
            jax.ShapeDtypeStruct((group, channels), jnp.float32),
            jax.ShapeDtypeStruct((seqs * chunks, states, channels), jnp.float32),
        ],
        scratch_shapes=[
            pltpu.VMEM((length, channels), jnp.float32),
            pltpu.VMEM((length, both), jnp.float32),
            pltpu.VMEM((states, channels), jnp.float32),
        ],
        compiler_params=pltpu.CompilerParams(vmem_limit_bytes=VMEM_LIMIT),
        cost_estimate=pl.CostEstimate(
            flops=8 * group * channels * SPAN,
            bytes_accessed=20 * group * channels,
            transcendentals=group * heads * SPAN,
        ),
        name="ssd_forward",
    )(inputs, states_raw, gate, step, *small, jnp.asarray(head_spread(heads)))


def ssd_backward(inputs, states_raw, gate, step, grad, carry, small, heads, length):
    group, channels = inputs.shape
    seqs = group // length
    both = states_raw.shape[1]
    states = both // 2
    chunks = length // SPAN
    taps = small[0].shape[0]
    return pl.pallas_call(
        ssd_backward_kernel,
        grid=(seqs,),
        in_specs=[
            by_sequence(length, channels),
            by_sequence(length, both),
            by_sequence(length, channels),
            by_sequence(length, LANES),
            by_sequence(length, channels),
            pl.BlockSpec((chunks, states, channels), lambda seq: (seq, 0, 0)),
            fixed(taps, channels),
            fixed(1, channels),
            fixed(taps, both),
            fixed(1, both),
            fixed(1, LANES),
            fixed(1, LANES),
            fixed(1, channels),
            fixed(LANES, channels),
            fixed(channels, LANES),
        ],
        out_specs=[
            by_sequence(length, channels),
            by_sequence(length, both),
            by_sequence(length, LANES),
            pl.BlockSpec((1, 8, channels), lambda seq: (seq, 0, 0)),
            pl.BlockSpec((1, 8, both), lambda seq: (seq, 0, 0)),
            pl.BlockSpec((1, 8, LANES), lambda seq: (seq, 0, 0)),
        ],
        out_shape=[
            jax.ShapeDtypeStruct((group, channels), jnp.bfloat16),
            jax.ShapeDtypeStruct((group, both), jnp.bfloat16),
            jax.ShapeDtypeStruct((group, LANES), jnp.bfloat16),
            jax.ShapeDtypeStruct((seqs, 8, channels), jnp.float32),
            jax.ShapeDtypeStruct((seqs, 8, both), jnp.float32),
            jax.ShapeDtypeStruct((seqs, 8, LANES), jnp.float32),
        ],
        scratch_shapes=[
            pltpu.VMEM((length, channels), jnp.float32),
            pltpu.VMEM((length, channels), jnp.float32),
            pltpu.VMEM((length, both), jnp.float32),
            pltpu.VMEM((length, both), jnp.float32),
            pltpu.VMEM((states, channels), jnp.float32),
            pltpu.VMEM((3, SPAN, channels), jnp.float32),
            pltpu.VMEM((LANES, SPAN), jnp.float32),
            pltpu.VMEM((SPAN, LANES), jnp.float32),
            pltpu.VMEM((1, channels), jnp.float32),
            pltpu.VMEM((1, channels), jnp.float32),
        ],
        compiler_params=pltpu.CompilerParams(vmem_limit_bytes=VMEM_LIMIT),
        cost_estimate=pl.CostEstimate(
            flops=20 * group * channels * SPAN,
            bytes_accessed=20 * group * channels,
            transcendentals=group * heads * SPAN,
        ),
        name="ssd_backward",
    )(
        inputs,
        states_raw,
        gate,
        step,
        grad,
        carry,
        *small,
        jnp.asarray(head_spread(heads)),
        jnp.asarray(head_spread(heads).T.copy()),
    )


def rope_wide(length):
    half = HD // 2
    freqs = np.float32(ROPE_BASE) ** (-np.arange(half, dtype=np.float32) * np.float32(2.0 / HD))
    angles = np.arange(length, dtype=np.float32)[:, None] * freqs[None, :].astype(np.float32)
    cosine, sine = np.cos(angles), np.sin(angles)
    count = LANES // HD
    return (
        np.concatenate([cosine, cosine] * count, axis=1).astype(np.float32),
        np.concatenate([-sine, sine] * count, axis=1).astype(np.float32),
    )


def turn(part, cosine, sine):
    half = HD // 2
    first = lane_index(part.shape) % HD < half
    swapped = jnp.where(first, pltpu.roll(part, LANES - half, 1), pltpu.roll(part, half, 1))
    return part * cosine + swapped * sine


def attend_forward_kernel(
    query_ref, pair_ref, cosine_ref, sine_ref, context_ref, query_out_ref, pair_out_ref, total_ref
):
    length = query_ref.shape[0]
    cosine, sine = cosine_ref[...], sine_ref[...]
    pair = pair_ref[...]
    left = lane_index(pair.shape) < HD
    pair = jnp.where(left, turn(pair, cosine, sine), pair)
    pair_out_ref[...] = pair.astype(jnp.bfloat16)
    moved = pltpu.roll(pair, HD, 1)
    keys = jnp.where(left, pair, moved).astype(jnp.bfloat16)
    values = jnp.where(left, moved, pair).astype(jnp.bfloat16)
    scale = HD ** (-0.5)
    for slab in range(query_ref.shape[1] // LANES):
        cols = pl.ds(slab * LANES, LANES)
        query_out_ref[:, cols] = turn(query_ref[:, cols], cosine, sine).astype(jnp.bfloat16)
        for tile in range(length // SPAN):
            rows = slice(tile * SPAN, (tile + 1) * SPAN)
            count = (tile + 1) * SPAN
            query = query_out_ref[rows, cols]
            lane = lane_index(query.shape)
            square = (SPAN, count)
            causal = row_index(square) + tile * SPAN >= lane_index(square)
            results = []
            for place in range(LANES // HD):
                mine = (lane >= place * HD) & (lane < place * HD + HD)
                scores = low_against(jnp.where(mine, query, 0), keys[:count]) * scale
                scores = jnp.where(causal, scores, -jnp.inf)
                peak = jnp.max(scores, axis=-1, keepdims=True)
                grown = jnp.exp(scores - peak)
                total = jnp.sum(grown, axis=-1, keepdims=True)
                probs = grown * (1.0 / total)
                results.append(low_dot(probs, values[:count]))
                head = slab * (LANES // HD) + place
                total_ref[rows, head : head + 1] = jnp.log(total) + peak
            context_ref[rows, cols] = jnp.where(lane < HD, results[0], results[1]).astype(
                jnp.bfloat16
            )


def attend_backward_kernel(
    query_ref,
    pair_ref,
    total_ref,
    grad_ref,
    cosine_ref,
    sine_ref,
    grad_query_ref,
    grad_pair_ref,
    key_sum_ref,
    value_sum_ref,
):
    length = query_ref.shape[0]
    cosine, sine = cosine_ref[...], -sine_ref[...]
    pair = pair_ref[...].astype(jnp.float32)
    left = lane_index(pair.shape) < HD
    moved = pltpu.roll(pair, HD, 1)
    keys = jnp.where(left, pair, moved).astype(jnp.bfloat16)
    values = jnp.where(left, moved, pair).astype(jnp.bfloat16)
    scale = HD ** (-0.5)
    key_sum_ref[...] = jnp.zeros_like(key_sum_ref)
    value_sum_ref[...] = jnp.zeros_like(value_sum_ref)
    for slab in range(query_ref.shape[1] // LANES):
        cols = pl.ds(slab * LANES, LANES)
        for tile in range(length // SPAN):
            rows = slice(tile * SPAN, (tile + 1) * SPAN)
            count = (tile + 1) * SPAN
            query = query_ref[rows, cols]
            upstream = grad_ref[rows, cols]
            lane = lane_index(query.shape)
            square = (SPAN, count)
            causal = row_index(square) + tile * SPAN >= lane_index(square)
            results = []
            for place in range(LANES // HD):
                mine = (lane >= place * HD) & (lane < place * HD + HD)
                head = slab * (LANES // HD) + place
                own_query = jnp.where(mine, query, 0)
                own_up = jnp.where(mine, upstream, 0)
                scores = low_against(own_query, keys[:count]) * scale
                scores = jnp.where(causal, scores, -jnp.inf)
                probs = jnp.exp(scores - total_ref[rows, head : head + 1])
                grad_probs = low_against(own_up, values[:count])
                mean = jnp.sum(probs * grad_probs, axis=-1, keepdims=True)
                grad_scores = (probs * (grad_probs - mean)).astype(jnp.bfloat16)
                results.append(low_dot(grad_scores, keys[:count]))
                key_sum_ref[0:count, :] += low_inner(grad_scores, own_query)
                value_sum_ref[0:count, :] += low_inner(probs, own_up)
            grad_query = jnp.where(lane < HD, results[0], results[1]) * scale
            grad_query_ref[rows, cols] = turn(
                grad_query, cosine[rows, :], sine[rows, :]
            ).astype(jnp.bfloat16)
    grad_key = key_sum_ref[...]
    grad_key = turn((grad_key + pltpu.roll(grad_key, HD, 1)) * scale, cosine, sine)
    grad_value = value_sum_ref[...]
    grad_value = grad_value + pltpu.roll(grad_value, HD, 1)
    grad_pair_ref[...] = jnp.where(left, grad_key, grad_value).astype(jnp.bfloat16)


def attend_forward(query, pair, length):
    group, width = query.shape
    heads = width // HD
    cosine, sine = rope_wide(length)
    return pl.pallas_call(
        attend_forward_kernel,
        grid=(group // length,),
        in_specs=[
            by_sequence(length, width),
            by_sequence(length, LANES),
            fixed(length, LANES),
            fixed(length, LANES),
        ],
        out_specs=[
            by_sequence(length, width),
            by_sequence(length, width),
            by_sequence(length, LANES),
            by_sequence(length, LANES),
        ],
        out_shape=[
            jax.ShapeDtypeStruct((group, width), jnp.bfloat16),
            jax.ShapeDtypeStruct((group, width), jnp.bfloat16),
            jax.ShapeDtypeStruct((group, LANES), jnp.bfloat16),
            jax.ShapeDtypeStruct((group, LANES), jnp.float32),
        ],
        compiler_params=pltpu.CompilerParams(vmem_limit_bytes=VMEM_LIMIT),
        cost_estimate=pl.CostEstimate(
            flops=4 * group * width * length,
            bytes_accessed=12 * group * width,
            transcendentals=group * heads * length // 2,
        ),
        name="attend_forward",
    )(query, pair, jnp.asarray(cosine), jnp.asarray(sine))


def attend_backward(query, pair, total, grad, length):
    group, width = query.shape
    heads = width // HD
    cosine, sine = rope_wide(length)
    return pl.pallas_call(
        attend_backward_kernel,
        grid=(group // length,),
        in_specs=[
            by_sequence(length, width),
            by_sequence(length, LANES),
            by_sequence(length, LANES),
            by_sequence(length, width),
            fixed(length, LANES),
            fixed(length, LANES),
        ],
        out_specs=[by_sequence(length, width), by_sequence(length, LANES)],
        out_shape=[
            jax.ShapeDtypeStruct((group, width), jnp.bfloat16),
            jax.ShapeDtypeStruct((group, LANES), jnp.bfloat16),
        ],
        scratch_shapes=[
            pltpu.VMEM((length, LANES), jnp.float32),
            pltpu.VMEM((length, LANES), jnp.float32),
        ],
        compiler_params=pltpu.CompilerParams(vmem_limit_bytes=VMEM_LIMIT),
        cost_estimate=pl.CostEstimate(
            flops=10 * group * width * length,
            bytes_accessed=12 * group * width,
            transcendentals=group * heads * length // 2,
        ),
        name="attend_backward",
    )(query, pair, total, grad, jnp.asarray(cosine), jnp.asarray(sine))


def step_groups(size):
    bits = size.bit_length() - 1
    return [1] * min(bits, 2) + [2] * (max(bits - 2, 0) // 2) + [1] * (max(bits - 2, 0) % 2)


def after(part, *deps):
    return lax.optimization_barrier((part,) + deps)[0]


def behind(part, dep):
    zero = jnp.minimum(jnp.abs(dep[:1, :1].astype(jnp.float32)), 0.0)
    return part + zero.astype(part.dtype)


class Sum:
    def __init__(self, part, size):
        self.size = size
        self.direct = bool(size & (size - 1) or part.shape[0] % size)
        self.steps = [] if self.direct else step_groups(size)
        self.shift = 0
        self.part = part
        self.gives = [part]
        if not self.direct:
            self.part = part.reshape(size, part.shape[0] // size, part.shape[1])
            self.prepare()

    def prepare(self):
        if not self.steps:
            self.gives = [self.part]
            return
        ways = 1 << self.steps[0]
        rest = self.part.shape[0] // ways
        view = self.part.reshape((rest, ways) + self.part.shape[1:])
        mine = (lax.axis_index("dp") >> self.shift) & (ways - 1)
        self.keep = lax.dynamic_index_in_dim(view, mine, 1, False)
        self.gives = [
            lax.dynamic_index_in_dim(view, mine ^ way, 1, False) for way in range(1, ways)
        ]

    def advance(self, *deps):
        if self.steps:
            total = after(self.keep, *deps).astype(jnp.float32)
            for way, give in enumerate(self.gives, 1):
                pairs = [(index, index ^ (way << self.shift)) for index in range(self.size)]
                total = total + lax.ppermute(give, "dp", pairs).astype(jnp.float32)
            self.part = total.astype(jnp.bfloat16)
            self.shift += self.steps.pop(0)
            self.prepare()
        return self.gives

    def joined(self, middle=None, *deps):
        groups, shift = step_groups(self.size), self.size.bit_length() - 1
        part = after(self.reduced(), *deps)
        if middle is not None:
            part = middle(part)
        self.trail = [part]
        if self.direct:
            return part
        rows, width = part.shape
        for group in reversed(groups):
            ways = 1 << group
            shift -= group
            mine = (lax.axis_index("dp") >> shift) & (ways - 1)
            part = part.reshape(-1, 1, rows, width)
            got = [part]
            for way in range(1, ways):
                pairs = [(index, index ^ (way << shift)) for index in range(self.size)]
                got.append(lax.ppermute(part, "dp", pairs))
            for bit in range(group):
                flip = ((mine >> bit) & 1) == 1
                got = [
                    jnp.where(flip, got[way ^ (1 << bit)], got[way]) for way in range(ways)
                ]
            part = jnp.concatenate(got, axis=1)
            self.trail.append(part)
        return part.reshape(-1, width)

    def reduced(self):
        while self.steps:
            self.advance()
        return lax.psum(self.part, "dp") if self.direct else self.part[0]


def other(part):
    return lax.ppermute(part, "tensor", [(0, 1), (1, 0)])


def all_rows(part, shards):
    if shards != 2:
        return lax.all_gather(part, "tensor", axis=0, tiled=True)
    got = other(part)
    return jnp.where(
        lax.axis_index("tensor") == 0,
        jnp.concatenate([part, got], axis=0),
        jnp.concatenate([got, part], axis=0),
    )


def sum_all(part, shards, *deps):
    if shards != 2:
        return lax.psum(part, "tensor").astype(jnp.float32)
    return after(part, *deps).astype(jnp.float32) + other(part).astype(jnp.float32)


def sum_own(part, shards):
    if shards != 2:
        return lax.psum_scatter(part, "tensor", scatter_dimension=0, tiled=True).astype(jnp.float32)
    me = lax.axis_index("tensor")
    halves = part.reshape(2, part.shape[0] // 2, part.shape[1])
    keep = lax.dynamic_index_in_dim(halves, me, 0, False)
    got = other(lax.dynamic_index_in_dim(halves, 1 - me, 0, False))
    return keep.astype(jnp.float32) + got.astype(jnp.float32)


def own_rows(part, rows):
    return lax.dynamic_slice_in_dim(part, lax.axis_index("tensor") * rows, rows, 0)


def column_pack(vectors, rows):
    flat = jnp.concatenate([item.reshape(-1) for item in vectors])
    width = -(-flat.shape[0] // rows)
    return jnp.pad(flat, (0, width * rows - flat.shape[0])).reshape(width, rows).T


def column_unpack(packed, shapes):
    flat = packed.T.reshape(-1)
    out, start = [], 0
    for shape in shapes:
        count = 1
        for size in shape:
            count *= size
        out.append(flat[start : start + count].reshape(shape))
        start += count
    return out


def body(
    dp_size,
    shards,
    layer_input,
    input_gain,
    middle_gain,
    mamba_gate,
    mamba_input,
    step_weight,
    state_weight,
    input_kernel,
    input_shift,
    state_kernel,
    state_shift,
    step_bias,
    decay_log,
    skip_gain,
    mamba_output,
    query_weight,
    keyvalue_weight,
    context_weight,
    gate_weight,
    up_weight,
    down_weight,
    cotangent,
):
    own = layer_input.shape[0]
    rows_low = all_rows(layer_input, shards)
    cotan_low = all_rows(cotangent, shards)
    rows = rows_low.astype(jnp.float32)
    gain_first = input_gain.astype(jnp.float32)
    gain_second = middle_gain.astype(jnp.float32)
    factor_first = lax.rsqrt(jnp.mean(rows * rows, axis=-1, keepdims=True) + EPSILON)
    normal_first = rows * factor_first
    whole = (normal_first * gain_first).astype(jnp.bfloat16)
    group = whole.shape[0]
    length = min(SEQ_LEN, group)
    seqs = group // length
    heads_here = query_weight.shape[1] // HD
    kv_head = lax.axis_index("tensor") * heads_here // (HQ // KVH)
    key_cols = lax.dynamic_slice_in_dim(keyvalue_weight, kv_head * HD, HD, 1)
    value_cols = lax.dynamic_slice_in_dim(keyvalue_weight, (KVH + kv_head) * HD, HD, 1)
    pair_weight = jnp.concatenate([key_cols, value_cols], axis=1)
    query_cols = query_weight.shape[1]
    query_pad = -query_cols % LANES
    query_wide = jnp.pad(query_weight, ((0, 0), (0, query_pad)))
    step_wide = pad_lanes(step_weight)
    heads = step_weight.shape[1]
    input_raw = forward_dot(whole, mamba_input)
    state_raw = forward_dot(whole, state_weight)
    step_raw = forward_dot(whole, step_wide)
    gate_raw = forward_dot(whole, mamba_gate)
    query_raw = forward_dot(whole, query_wide)
    pair_raw = forward_dot(whole, pair_weight)
    small = ssd_small(
        input_kernel.astype(jnp.float32),
        input_shift.astype(jnp.float32),
        state_kernel.astype(jnp.float32),
        state_shift.astype(jnp.float32),
        step_bias.astype(jnp.float32),
        decay_log.astype(jnp.float32),
        skip_gain.astype(jnp.float32),
    )
    gated_low, ssm_out, carries = ssd_forward(
        input_raw, state_raw, gate_raw, step_raw, small, heads, length
    )
    context_wide, queries, pairs, totals = attend_forward(
        query_raw, pair_raw, length
    )
    context_rows = context_wide[:, :query_cols]
    count = 2 if shards == 2 else 1
    spans = [slice(index * group // count, (index + 1) * group // count) for index in range(count)]
    context_rows = after(context_rows, cotan_low)
    resids, normals, factors, mids = [], [], [], []
    hiddens, gate_lows, upper_lows, back_parts, back_mids = [], [], [], [], []
    mixed_parts = [
        (
            forward_dot(gated_low[span], mamba_output)
            + forward_dot(context_rows[span], context_weight)
        ).astype(jnp.bfloat16)
        for span in spans
    ]
    for span, mixed_part in zip(spans, mixed_parts):
        resid = rows[span] + sum_all(mixed_part, shards, *back_parts)
        factor = lax.rsqrt(jnp.mean(resid * resid, axis=-1, keepdims=True) + EPSILON)
        normal = resid * factor
        mid = (normal * gain_second).astype(jnp.bfloat16)
        gate = forward_dot(mid, gate_weight)
        upper = forward_dot(mid, up_weight)
        sigmoid_gate = jax.nn.sigmoid(gate)
        silu_gate = gate * sigmoid_gate
        grad_hidden = against(cotan_low[span], down_weight)
        slope = sigmoid_gate * (1.0 + gate * (1.0 - sigmoid_gate))
        gate_low = (grad_hidden * upper * slope).astype(jnp.bfloat16)
        upper_low = (grad_hidden * silu_gate).astype(jnp.bfloat16)
        back_part = (against(gate_low, gate_weight) + against(upper_low, up_weight)).astype(
            jnp.bfloat16
        )
        resids.append(resid)
        normals.append(normal)
        factors.append(factor)
        mids.append(mid)
        hiddens.append((silu_gate * upper).astype(jnp.bfloat16))
        gate_lows.append(gate_low)
        upper_lows.append(upper_low)
        back_parts.append(back_part)
    back_mids = [sum_all(back_part, shards, *back_parts) for back_part in back_parts]
    whole_mid = jnp.concatenate(mids, axis=0)
    hidden = jnp.concatenate(hiddens, axis=0)
    grad_down = inner_rows(hidden, cotan_low).astype(jnp.bfloat16)
    grad_gate = inner_rows(whole_mid, jnp.concatenate(gate_lows, axis=0)).astype(jnp.bfloat16)
    grad_up = inner_rows(whole_mid, jnp.concatenate(upper_lows, axis=0)).astype(jnp.bfloat16)
    grad_gate, grad_up, grad_down = lax.psum((grad_gate, grad_up, grad_down), "dp")
    grad_middle = sum(
        jnp.sum(back_part.astype(jnp.float32) * normal, axis=0)
        for back_part, normal in zip(back_parts, normals)
    )
    grad_resids = [
        cotan_low[span].astype(jnp.float32) + norm_back(back_mid, gain_second, normal, factor)
        for span, back_mid, normal, factor in zip(spans, back_mids, normals, factors)
    ]

    def own_piece(pieces):
        if len(pieces) == 1:
            return own_rows(pieces[0], own)
        return jnp.where(lax.axis_index("tensor") == 0, pieces[0], pieces[1])

    mixer_all = jnp.concatenate([piece.astype(jnp.bfloat16) for piece in grad_resids], axis=0)
    ssm_rows = gated_low.shape[1]
    width = whole.shape[1]
    split_pairs = shards == KVH
    grad_gated = against(mixer_all, mamba_output)
    mixer_sum = Sum(
        inner_rows(jnp.concatenate([gated_low, context_rows], axis=1), mixer_all).astype(
            jnp.bfloat16
        ),
        dp_size,
    )
    grad_input_raw, grad_state_raw, grad_step_raw, input_sums, state_sums, head_sums = ssd_backward(
        input_raw,
        state_raw,
        gate_raw,
        step_raw,
        grad_gated,
        carries,
        small,
        heads,
        length,
    )
    input_sums = jnp.sum(input_sums, axis=0)
    state_sums = jnp.sum(state_sums, axis=0)
    head_sums = jnp.sum(head_sums, axis=0)[:, :heads]
    taps = input_kernel.shape[0]
    state_cols = state_weight.shape[1]
    step_cols = heads
    late_cols = jnp.concatenate([grad_input_raw, grad_state_raw], axis=1)
    late_sum = Sum(inner_rows(whole, late_cols).astype(jnp.bfloat16), dp_size)

    sigmoid_raw = jax.nn.sigmoid(gate_raw)
    grad_gate_raw = (
        grad_gated * ssm_out * (sigmoid_raw * (1.0 + gate_raw * (1.0 - sigmoid_raw)))
    ).astype(jnp.bfloat16)
    grad_context = against(mixer_all, context_weight).astype(jnp.bfloat16)
    grad_context = jnp.pad(grad_context, ((0, 0), (0, query_pad)))
    grad_query_raw, grad_pair_raw = attend_backward(
        queries, pairs, totals, after(grad_context, *late_sum.gives, *mixer_sum.advance()), length
    )
    early_cols = jnp.concatenate(
        [grad_gate_raw, grad_query_raw[:, :query_cols], grad_pair_raw, grad_step_raw], axis=1
    )
    total = against(late_cols, jnp.concatenate([mamba_input, state_weight], axis=1))
    total = total + against(
        early_cols, jnp.concatenate(
            [mamba_gate, query_weight, pair_weight, after(step_wide, mixed_parts[-1])], axis=1
        )
    )
    total_low = total.astype(jnp.bfloat16)
    grad_first = jnp.sum(total_low.astype(jnp.float32) * normal_first, axis=0)
    own_vectors = (input_sums[:taps], input_sums[taps], head_sums[0], head_sums[1], head_sums[2])
    shared_vectors = (grad_first, grad_middle, state_sums[:taps], state_sums[taps])
    own_pack = column_pack(own_vectors, width)
    shared_pack = column_pack(shared_vectors, width)
    shared_lane = step_cols + own_pack.shape[1]
    last_lane = shared_lane + shared_pack.shape[1]
    early = inner_rows(whole, early_cols)
    if not split_pairs:
        spread = jnp.zeros((width, 2 * KVH * HD), jnp.float32)
        spread = lax.dynamic_update_slice_in_dim(
            spread, early[:, -2 * HD - LANES : -HD - LANES], kv_head * HD, 1
        )
        spread = lax.dynamic_update_slice_in_dim(
            spread, early[:, -HD - LANES : -LANES], (KVH + kv_head) * HD, 1
        )
        early = jnp.concatenate(
            [early[:, : -2 * HD - LANES], spread, early[:, -LANES:]], axis=1
        )
    packs = jnp.pad(
        jnp.concatenate([own_pack, shared_pack], axis=1),
        ((0, 0), (early.shape[1] - LANES + step_cols, LANES - last_lane)),
    )
    early_sum = Sum((early + packs).astype(jnp.bfloat16), dp_size)

    def early_over_tensor(part):
        count = (2 * HD if split_pairs else 2 * KVH * HD) + LANES
        mine = part[:, -count:]
        if split_pairs:
            got = other(mine)
            both = (mine.astype(jnp.float32) + got.astype(jnp.float32)).astype(jnp.bfloat16)
            first = lax.axis_index("tensor") == 0
            low, high = jnp.where(first, mine, got), jnp.where(first, got, mine)
            pair = [low[:, :HD], high[:, :HD], low[:, HD : 2 * HD], high[:, HD : 2 * HD]]
        else:
            both = lax.psum(mine, "tensor")
            pair = [both[:, :-LANES]]
        lane = lane_index((part.shape[0], LANES))
        extra = jnp.where(
            (lane >= shared_lane) & (lane < last_lane), both[:, -LANES:], mine[:, -LANES:]
        )
        return jnp.concatenate([part[:, :-count]] + pair + [extra], axis=1)

    def late_over_tensor(part):
        mine = part[:, -state_cols:]
        if shards == 2:
            both = mine.astype(jnp.float32) + other(mine).astype(jnp.float32)
        else:
            both = lax.psum(mine, "tensor")
        return jnp.concatenate([part[:, :-state_cols], both.astype(jnp.bfloat16)], axis=1)

    early_sum.advance()
    mixer_sum.advance()
    mixer_sum.advance(*early_sum.gives)
    tail = late_sum.joined(late_over_tensor, *early_sum.gives)
    grad_mixer_out = mixer_sum.joined(None, *early_sum.gives)
    early = early_sum.joined(early_over_tensor)
    grad_gate, grad_up, grad_down = [
        after(item, early_sum.trail[min(1, len(early_sum.trail) - 1)])
        for item in (grad_gate, grad_up, grad_down)
    ]
    grad_mamba_out = grad_mixer_out[:ssm_rows]
    grad_context_w = grad_mixer_out[ssm_rows:]
    grad_mamba_input, grad_state = tail[:, :-state_cols], tail[:, -state_cols:]
    gate_cols = gate_raw.shape[1]
    extra = early[:, -LANES:]
    feed_part = behind(forward_dot(hidden, down_weight), total).astype(jnp.bfloat16)
    feed = sum_own(feed_part, shards)
    layer_output = (after(own_piece(resids), late_sum.trail[0]) + feed).astype(jnp.bfloat16)
    back_in = sum_own(total_low, shards)
    normal_own = own_rows(normal_first, own)
    factor_own = own_rows(factor_first, own)
    input_grad = after(own_piece(grad_resids), late_sum.trail[0]) + norm_back(back_in, gain_first, normal_own, factor_own)
    grad_step = extra[:, :step_cols]
    grad_in_kernel, grad_in_shift, grad_bias, grad_decay, grad_skip = column_unpack(
        extra[:, step_cols:shared_lane], [item.shape for item in own_vectors]
    )
    grad_first, grad_middle, grad_st_kernel, grad_st_shift = column_unpack(
        extra[:, shared_lane:last_lane], [item.shape for item in shared_vectors]
    )
    results = (
        grad_first,
        grad_middle,
        early[:, :gate_cols],
        grad_mamba_input,
        grad_step,
        grad_state,
        grad_in_kernel,
        grad_in_shift,
        grad_st_kernel,
        grad_st_shift,
        grad_bias,
        grad_decay,
        grad_skip,
        grad_mamba_out,
        early[:, gate_cols : gate_cols + query_cols],
        early[:, gate_cols + query_cols : -LANES],
        grad_context_w,
        grad_gate,
        grad_up,
        grad_down,
    )
    return (layer_output, input_grad) + tuple(item.astype(jnp.float32) for item in results)


def solution(mesh):
    in_specs = (
        P(("dp", "tensor"), None),
        P(),
        P(),
        P(None, "tensor"),
        P(None, "tensor"),
        P(None, "tensor"),
        P(),
        P(None, "tensor"),
        P("tensor"),
        P(),
        P(),
        P("tensor"),
        P("tensor"),
        P("tensor"),
        P("tensor", None),
        P(None, "tensor"),
        P(),
        P("tensor", None),
        P(None, "tensor"),
        P(None, "tensor"),
        P("tensor", None),
        P(("dp", "tensor"), None),
    )
    out_specs = (
        P(("dp", "tensor"), None),
        P(("dp", "tensor"), None),
        P(),
        P(),
        P(None, "tensor"),
        P(None, "tensor"),
        P(None, "tensor"),
        P(),
        P(None, "tensor"),
        P("tensor"),
        P(),
        P(),
        P("tensor"),
        P("tensor"),
        P("tensor"),
        P("tensor", None),
        P(None, "tensor"),
        P(),
        P("tensor", None),
        P(None, "tensor"),
        P(None, "tensor"),
        P("tensor", None),
    )
    run = partial(body, mesh.shape["dp"], mesh.shape["tensor"])
    return jax.shard_map(run, mesh=mesh, in_specs=in_specs, out_specs=out_specs, check_vma=False)
```

```python
from functools import partial

import jax
import jax.numpy as jnp
import numpy as np
from jax import lax
from jax.experimental import pallas as pl
from jax.experimental.pallas import tpu as pltpu
from jax.sharding import PartitionSpec as P

HD = 64
HQ = 8
KVH = 2
SPAN = 128
SEQ_LEN = 1024


EPSILON = 1e-05
ROPE_BASE = 10000.0
PRECISE = lax.Precision.HIGHEST


def forward_dot(left, right):
    return jnp.dot(left, right, preferred_element_type=jnp.float32)


def inner_rows(left, right):
    return lax.dot_general(
        left, right, (((0,), (0,)), ((), ())), preferred_element_type=jnp.float32
    )


def against(left, right):
    return lax.dot_general(
        left, right, (((1,), (1,)), ((), ())), preferred_element_type=jnp.float32
    )


def norm_back(upstream, gain, normal, factor):
    scaled = upstream * gain
    return factor * (scaled - normal * jnp.mean(scaled * normal, axis=-1, keepdims=True))


LANES = 128
VMEM_LIMIT = 44 * 1024 * 1024


def exact_dot(left, right):
    return jnp.dot(left, right, precision=PRECISE, preferred_element_type=jnp.float32)


def low_dot(left, right):
    return jnp.dot(
        left.astype(jnp.bfloat16), right.astype(jnp.bfloat16), preferred_element_type=jnp.float32
    )


def low_against(left, right):
    return lax.dot_general(
        left.astype(jnp.bfloat16),
        right.astype(jnp.bfloat16),
        (((1,), (1,)), ((), ())),
        preferred_element_type=jnp.float32,
    )


def low_inner(left, right):
    return lax.dot_general(
        left.astype(jnp.bfloat16),
        right.astype(jnp.bfloat16),
        (((0,), (0,)), ((), ())),
        preferred_element_type=jnp.float32,
    )


def row_index(shape):
    return lax.broadcasted_iota(jnp.int32, shape, 0)


def lane_index(shape):
    return lax.broadcasted_iota(jnp.int32, shape, 1)


def later(part, count):
    if count == 0:
        return part
    return jnp.where(row_index(part.shape) >= count, pltpu.roll(part, count, 0), 0.0)


def sooner(part, count):
    if count == 0:
        return part
    rows = part.shape[0]
    return jnp.where(row_index(part.shape) < rows - count, pltpu.roll(part, rows - count, 0), 0.0)


def slabs(width):
    return [(start, min(LANES, width - start)) for start in range(0, width, LANES)]


def soft_plus(value):
    return jnp.maximum(value, 0.0) + jnp.log1p(jnp.exp(-jnp.abs(value)))


def stacked_heads(part, heads):
    if heads == 1:
        return part
    lane = lane_index(part.shape)
    return jnp.concatenate(
        [jnp.where((lane >= head * HD) & (lane < head * HD + HD), part, 0.0) for head in range(heads)],
        axis=0,
    )


def convolve(raw, kernel_ref, shift_ref, cols):
    taps = kernel_ref.shape[0]
    out = shift_ref[:, cols] + kernel_ref[taps - 1 : taps, cols] * raw
    for tap in range(taps - 1):
        out = out + kernel_ref[tap : tap + 1, cols] * later(raw, taps - 1 - tap)
    return out


def chunk_steps(step_ref, bias_ref, rate_ref, expand_ref, rows):
    raw = step_ref[rows, :] + bias_ref[...]
    steps = soft_plus(raw)
    logdec = steps * rate_ref[...]
    square = (SPAN, SPAN)
    lower = (row_index(square) >= lane_index(square)).astype(jnp.float32)
    cumul = exact_dot(lower, logdec)
    grown = jnp.exp(cumul)
    tail = jnp.exp(cumul[SPAN - 1 : SPAN, :] - cumul)
    wide = exact_dot(jnp.concatenate([steps, grown, tail], axis=0), expand_ref[...])
    return raw, steps, cumul, wide[:SPAN], wide[SPAN : 2 * SPAN], wide[2 * SPAN :]


def ssd_forward_kernel(
    input_ref,
    state_ref,
    gate_ref,
    step_ref,
    input_kernel_ref,
    input_shift_ref,
    state_kernel_ref,
    state_shift_ref,
    bias_ref,
    rate_ref,
    skip_ref,
    expand_ref,
    gated_ref,
    out_ref,
    carry_ref,
    act_ref,
    both_ref,
    held_ref,
):
    channels = input_ref.shape[1]
    states = state_ref.shape[1] // 2
    for start, width in slabs(channels):
        cols = pl.ds(start, width)
        pre = convolve(input_ref[:, cols], input_kernel_ref, input_shift_ref, cols)
        act_ref[:, cols] = pre * jax.nn.sigmoid(pre)
    for start, width in slabs(2 * states):
        cols = pl.ds(start, width)
        pre = convolve(state_ref[:, cols], state_kernel_ref, state_shift_ref, cols)
        both_ref[:, cols] = pre * jax.nn.sigmoid(pre)
    held_ref[...] = jnp.zeros_like(held_ref)

    def chunk(index, unused):
        rows = pl.ds(pl.multiple_of(index * SPAN, SPAN), SPAN)
        raw, steps, cumul, step_wide, grown_wide, tail_wide = chunk_steps(
            step_ref, bias_ref, rate_ref, expand_ref, rows
        )
        cumul_turned = cumul.T
        entry = both_ref[rows, pl.ds(0, states)].astype(jnp.bfloat16)
        readout = both_ref[rows, pl.ds(states, states)].astype(jnp.bfloat16)
        cross = low_against(readout, entry)
        square = (SPAN, SPAN)
        lower = row_index(square) >= lane_index(square)
        for start, width in slabs(channels):
            cols = pl.ds(start, width)
            span = slice(start, start + width)
            heads = width // HD
            values = act_ref[rows, cols]
            scaled = values * step_wide[:, span]
            held = held_ref[:, cols]
            carry_ref[index, :, cols] = held
            weights = []
            for head in range(start // HD, start // HD + heads):
                spread = cumul[:, head : head + 1] - cumul_turned[head : head + 1, :]
                decay = jnp.exp(jnp.where(lower, spread, -jnp.inf))
                weights.append((decay * cross).astype(jnp.bfloat16))
            weights = jnp.concatenate(weights, axis=1) if heads > 1 else weights[0]
            result = low_dot(weights, stacked_heads(scaled, heads))
            result = result + low_dot(readout, held) * grown_wide[:, span]
            held_ref[:, cols] = held * grown_wide[SPAN - 1 : SPAN, span] + low_inner(
                entry, scaled * tail_wide[:, span]
            )
            result = result + skip_ref[:, cols] * values
            out_ref[rows, cols] = result
            gate = gate_ref[rows, cols]
            gated_ref[rows, cols] = (result * (gate * jax.nn.sigmoid(gate))).astype(jnp.bfloat16)
        return unused

    lax.fori_loop(0, input_ref.shape[0] // SPAN, chunk, 0)


def ssd_backward_kernel(
    input_ref,
    state_ref,
    gate_ref,
    step_ref,
    grad_ref,
    carry_ref,
    input_kernel_ref,
    input_shift_ref,
    state_kernel_ref,
    state_shift_ref,
    bias_ref,
    rate_ref,
    skip_ref,
    expand_ref,
    collect_ref,
    grad_input_ref,
    grad_state_ref,
    grad_step_ref,
    grad_input_conv_ref,
    grad_state_conv_ref,
    grad_head_ref,
    act_ref,
    slope_ref,
    both_ref,
    both_slope_ref,
    held_ref,
    wide_ref,
    turned_ref,
    column_ref,
    skip_sum_ref,
    scale_sum_ref,
):
    channels = input_ref.shape[1]
    states = state_ref.shape[1] // 2
    taps = input_kernel_ref.shape[0]
    for start, width in slabs(channels):
        cols = pl.ds(start, width)
        pre = convolve(input_ref[:, cols], input_kernel_ref, input_shift_ref, cols)
        sigma = jax.nn.sigmoid(pre)
        act_ref[:, cols] = pre * sigma
        slope_ref[:, cols] = sigma * (1.0 + pre * (1.0 - sigma))
    for start, width in slabs(2 * states):
        cols = pl.ds(start, width)
        pre = convolve(state_ref[:, cols], state_kernel_ref, state_shift_ref, cols)
        sigma = jax.nn.sigmoid(pre)
        both_ref[:, cols] = pre * sigma
        both_slope_ref[:, cols] = sigma * (1.0 + pre * (1.0 - sigma))
    held_ref[...] = jnp.zeros_like(held_ref)
    turned_ref[...] = jnp.zeros_like(turned_ref)
    column_ref[...] = jnp.zeros_like(column_ref)
    grad_head_ref[...] = jnp.zeros_like(grad_head_ref)
    skip_sum_ref[...] = jnp.zeros_like(skip_sum_ref)
    chunks = input_ref.shape[0] // SPAN

    def chunk(count, unused):
        index = chunks - 1 - count
        rows = pl.ds(pl.multiple_of(index * SPAN, SPAN), SPAN)
        raw, steps, cumul, step_wide, grown_wide, tail_wide = chunk_steps(
            step_ref, bias_ref, rate_ref, expand_ref, rows
        )
        cumul_turned = cumul.T
        entry = both_ref[rows, pl.ds(0, states)].astype(jnp.bfloat16)
        readout = both_ref[rows, pl.ds(states, states)].astype(jnp.bfloat16)
        cross = low_against(entry, readout)
        square = (SPAN, SPAN)
        upper = row_index(square) <= lane_index(square)
        grad_cross = jnp.zeros(square, jnp.float32)
        grad_entry = jnp.zeros((SPAN, states), jnp.float32)
        grad_readout = jnp.zeros((SPAN, states), jnp.float32)
        for start, width in slabs(channels):
            cols = pl.ds(start, width)
            span = slice(start, start + width)
            heads = width // HD
            values = act_ref[rows, cols]
            scaled = values * step_wide[:, span]
            gate = gate_ref[rows, cols]
            upstream = grad_ref[rows, cols] * (gate * jax.nn.sigmoid(gate))
            held = held_ref[:, cols]
            before = carry_ref[index, :, cols]
            stacked_up = stacked_heads(upstream, heads).astype(jnp.bfloat16)
            products = low_against(scaled, stacked_up)
            weights = []
            for place in range(heads):
                head = start // HD + place
                spread = cumul_turned[head : head + 1, :] - cumul[:, head : head + 1]
                decay = jnp.exp(jnp.where(upper, spread, -jnp.inf))
                product = products[:, place * SPAN : (place + 1) * SPAN] * decay
                grad_cross = grad_cross + product
                flow = product * cross
                turned_ref[head : head + 1, :] = jnp.sum(flow, axis=0, keepdims=True)
                column_ref[:, head : head + 1] = jnp.sum(flow, axis=1, keepdims=True)
                weights.append((decay * cross).astype(jnp.bfloat16))
            weights = jnp.concatenate(weights, axis=1) if heads > 1 else weights[0]
            grown_up = upstream * grown_wide[:, span]
            tailed = scaled * tail_wide[:, span]
            from_held = low_dot(entry, held)
            grad_scaled = low_dot(weights, stacked_up) + tail_wide[:, span] * from_held
            wide_ref[0, :, cols] = grown_up * low_dot(readout, before)
            wide_ref[1, :, cols] = tailed * from_held
            wide_ref[2, :, cols] = values * grad_scaled
            grad_readout = grad_readout + low_against(grown_up, before)
            grad_entry = grad_entry + low_against(tailed, held)
            last = grown_wide[SPAN - 1 : SPAN, span]
            scale_sum_ref[:, cols] = jnp.sum(held * before, axis=0, keepdims=True) * last
            skip_sum_ref[:, cols] += jnp.sum(upstream * values, axis=0, keepdims=True)
            held_ref[:, cols] = held * last + low_inner(readout, grown_up)
            act_ref[rows, cols] = step_wide[:, span] * grad_scaled + skip_ref[:, cols] * upstream
        sums = exact_dot(
            jnp.concatenate([wide_ref[0], wide_ref[1], wide_ref[2]], axis=0), collect_ref[...]
        )
        scale_sum = exact_dot(jnp.broadcast_to(scale_sum_ref[...], (8, channels)), collect_ref[...])
        flows = turned_ref[...].T - column_ref[...] + sums[:SPAN]
        onward = (row_index(square) <= lane_index(square)).astype(jnp.float32)
        strict = (row_index(square) > lane_index(square)).astype(jnp.float32)
        grad_log = (
            exact_dot(onward, flows)
            + exact_dot(strict, sums[SPAN : 2 * SPAN])
            + scale_sum[:1]
        )
        grad_steps = grad_log * rate_ref[...] + sums[2 * SPAN :]
        grad_raw = grad_steps * jax.nn.sigmoid(raw)
        grad_step_ref[rows, :] = grad_raw.astype(jnp.bfloat16)
        grad_head_ref[0, 0:1, :] += jnp.sum(grad_raw, axis=0, keepdims=True)
        grad_head_ref[0, 1:2, :] += (
            jnp.sum(grad_log * steps, axis=0, keepdims=True) * rate_ref[...]
        )
        both_ref[rows, pl.ds(0, states)] = grad_entry + low_dot(grad_cross, readout)
        both_ref[rows, pl.ds(states, states)] = grad_readout + low_inner(grad_cross, entry)
        return unused

    lax.fori_loop(0, chunks, chunk, 0)
    grad_head_ref[0, 2:3, :] = exact_dot(
        jnp.broadcast_to(skip_sum_ref[...], (8, channels)), collect_ref[...]
    )[:1]

    def convolve_back(raw_ref, grads_ref, slopes_ref, kernel_ref, out_ref, sums_ref, width_all):
        for start, width in slabs(width_all):
            cols = pl.ds(start, width)
            grad = grads_ref[:, cols] * slopes_ref[:, cols]
            raw = raw_ref[:, cols]
            total = kernel_ref[taps - 1 : taps, cols] * grad
            sums_ref[0, taps - 1 : taps, cols] = jnp.sum(grad * raw, axis=0, keepdims=True)
            for tap in range(taps - 1):
                shifted = sooner(grad, taps - 1 - tap)
                total = total + kernel_ref[tap : tap + 1, cols] * shifted
                sums_ref[0, tap : tap + 1, cols] = jnp.sum(shifted * raw, axis=0, keepdims=True)
            sums_ref[0, taps : taps + 1, cols] = jnp.sum(grad, axis=0, keepdims=True)
            out_ref[:, cols] = total.astype(jnp.bfloat16)

    convolve_back(
        input_ref,
        act_ref,
        slope_ref,
        input_kernel_ref,
        grad_input_ref,
        grad_input_conv_ref,
        channels,
    )
    convolve_back(
        state_ref,
        both_ref,
        both_slope_ref,
        state_kernel_ref,
        grad_state_ref,
        grad_state_conv_ref,
        2 * states,
    )


def by_sequence(length, width):
    return pl.BlockSpec((length, width), lambda seq: (seq, 0))


def fixed(*shape):
    return pl.BlockSpec(shape, lambda seq: (0,) * len(shape))


def head_spread(heads):
    marks = np.zeros((LANES, heads * HD), np.float32)
    for head in range(heads):
        marks[head, head * HD : (head + 1) * HD] = 1.0
    return marks


def pad_lanes(part):
    return jnp.pad(part, ((0, 0), (0, LANES - part.shape[1])))


def ssd_small(input_kernel, input_shift, state_kernel, state_shift, step_bias, decay_log, skip_gain):
    rates = -jnp.exp(decay_log)
    return (
        input_kernel,
        input_shift[None, :],
        state_kernel,
        state_shift[None, :],
        pad_lanes(step_bias[None, :]),
        pad_lanes(rates[None, :]),
        jnp.repeat(skip_gain, HD)[None, :],
    )


def ssd_forward(inputs, states_raw, gate, step, small, heads, length):
    group, channels = inputs.shape
    seqs = group // length
    both = states_raw.shape[1]
    states = both // 2
    chunks = length // SPAN
    taps = small[0].shape[0]
    return pl.pallas_call(
        ssd_forward_kernel,
        grid=(seqs,),
        in_specs=[
            by_sequence(length, channels),
            by_sequence(length, both),
            by_sequence(length, channels),
            by_sequence(length, LANES),
            fixed(taps, channels),
            fixed(1, channels),
            fixed(taps, both),
            fixed(1, both),
            fixed(1, LANES),
            fixed(1, LANES),
            fixed(1, channels),
            fixed(LANES, channels),
        ],
        out_specs=[
            by_sequence(length, channels),
            by_sequence(length, channels),
            pl.BlockSpec((chunks, states, channels), lambda seq: (seq, 0, 0)),
        ],
        out_shape=[
            jax.ShapeDtypeStruct((group, channels), jnp.bfloat16),
            jax.ShapeDtypeStruct((group, channels), jnp.float32),
            jax.ShapeDtypeStruct((seqs * chunks, states, channels), jnp.float32),
        ],
        scratch_shapes=[
            pltpu.VMEM((length, channels), jnp.float32),
            pltpu.VMEM((length, both), jnp.float32),
            pltpu.VMEM((states, channels), jnp.float32),
        ],
        compiler_params=pltpu.CompilerParams(vmem_limit_bytes=VMEM_LIMIT),
        cost_estimate=pl.CostEstimate(
            flops=8 * group * channels * SPAN,
            bytes_accessed=20 * group * channels,
            transcendentals=group * heads * SPAN,
        ),
        name="ssd_forward",
    )(inputs, states_raw, gate, step, *small, jnp.asarray(head_spread(heads)))


def ssd_backward(inputs, states_raw, gate, step, grad, carry, small, heads, length):
    group, channels = inputs.shape
    seqs = group // length
    both = states_raw.shape[1]
    states = both // 2
    chunks = length // SPAN
    taps = small[0].shape[0]
    return pl.pallas_call(
        ssd_backward_kernel,
        grid=(seqs,),
        in_specs=[
            by_sequence(length, channels),
            by_sequence(length, both),
            by_sequence(length, channels),
            by_sequence(length, LANES),
            by_sequence(length, channels),
            pl.BlockSpec((chunks, states, channels), lambda seq: (seq, 0, 0)),
            fixed(taps, channels),
            fixed(1, channels),
            fixed(taps, both),
            fixed(1, both),
            fixed(1, LANES),
            fixed(1, LANES),
            fixed(1, channels),
            fixed(LANES, channels),
            fixed(channels, LANES),
        ],
        out_specs=[
            by_sequence(length, channels),
            by_sequence(length, both),
            by_sequence(length, LANES),
            pl.BlockSpec((1, 8, channels), lambda seq: (seq, 0, 0)),
            pl.BlockSpec((1, 8, both), lambda seq: (seq, 0, 0)),
            pl.BlockSpec((1, 8, LANES), lambda seq: (seq, 0, 0)),
        ],
        out_shape=[
            jax.ShapeDtypeStruct((group, channels), jnp.bfloat16),
            jax.ShapeDtypeStruct((group, both), jnp.bfloat16),
            jax.ShapeDtypeStruct((group, LANES), jnp.bfloat16),
            jax.ShapeDtypeStruct((seqs, 8, channels), jnp.float32),
            jax.ShapeDtypeStruct((seqs, 8, both), jnp.float32),
            jax.ShapeDtypeStruct((seqs, 8, LANES), jnp.float32),
        ],
        scratch_shapes=[
            pltpu.VMEM((length, channels), jnp.float32),
            pltpu.VMEM((length, channels), jnp.float32),
            pltpu.VMEM((length, both), jnp.float32),
            pltpu.VMEM((length, both), jnp.float32),
            pltpu.VMEM((states, channels), jnp.float32),
            pltpu.VMEM((3, SPAN, channels), jnp.float32),
            pltpu.VMEM((LANES, SPAN), jnp.float32),
            pltpu.VMEM((SPAN, LANES), jnp.float32),
            pltpu.VMEM((1, channels), jnp.float32),
            pltpu.VMEM((1, channels), jnp.float32),
        ],
        compiler_params=pltpu.CompilerParams(vmem_limit_bytes=VMEM_LIMIT),
        cost_estimate=pl.CostEstimate(
            flops=20 * group * channels * SPAN,
            bytes_accessed=20 * group * channels,
            transcendentals=group * heads * SPAN,
        ),
        name="ssd_backward",
    )(
        inputs,
        states_raw,
        gate,
        step,
        grad,
        carry,
        *small,
        jnp.asarray(head_spread(heads)),
        jnp.asarray(head_spread(heads).T.copy()),
    )


def rope_wide(length):
    half = HD // 2
    freqs = np.float32(ROPE_BASE) ** (-np.arange(half, dtype=np.float32) * np.float32(2.0 / HD))
    angles = np.arange(length, dtype=np.float32)[:, None] * freqs[None, :].astype(np.float32)
    cosine, sine = np.cos(angles), np.sin(angles)
    count = LANES // HD
    return (
        np.concatenate([cosine, cosine] * count, axis=1).astype(np.float32),
        np.concatenate([-sine, sine] * count, axis=1).astype(np.float32),
    )


def turn(part, cosine, sine):
    half = HD // 2
    first = lane_index(part.shape) % HD < half
    swapped = jnp.where(first, pltpu.roll(part, LANES - half, 1), pltpu.roll(part, half, 1))
    return part * cosine + swapped * sine


def attend_forward_kernel(
    query_ref, pair_ref, cosine_ref, sine_ref, context_ref, query_out_ref, pair_out_ref, total_ref
):
    length = query_ref.shape[0]
    cosine, sine = cosine_ref[...], sine_ref[...]
    pair = pair_ref[...]
    left = lane_index(pair.shape) < HD
    pair = jnp.where(left, turn(pair, cosine, sine), pair)
    pair_out_ref[...] = pair.astype(jnp.bfloat16)
    moved = pltpu.roll(pair, HD, 1)
    keys = jnp.where(left, pair, moved).astype(jnp.bfloat16)
    values = jnp.where(left, moved, pair).astype(jnp.bfloat16)
    scale = HD ** (-0.5)
    for slab in range(query_ref.shape[1] // LANES):
        cols = pl.ds(slab * LANES, LANES)
        query_out_ref[:, cols] = turn(query_ref[:, cols], cosine, sine).astype(jnp.bfloat16)
        for tile in range(length // SPAN):
            rows = slice(tile * SPAN, (tile + 1) * SPAN)
            count = (tile + 1) * SPAN
            query = query_out_ref[rows, cols]
            lane = lane_index(query.shape)
            square = (SPAN, count)
            causal = row_index(square) + tile * SPAN >= lane_index(square)
            results = []
            for place in range(LANES // HD):
                mine = (lane >= place * HD) & (lane < place * HD + HD)
                scores = low_against(jnp.where(mine, query, 0), keys[:count]) * scale
                scores = jnp.where(causal, scores, -jnp.inf)
                peak = jnp.max(scores, axis=-1, keepdims=True)
                grown = jnp.exp(scores - peak)
                total = jnp.sum(grown, axis=-1, keepdims=True)
                probs = grown * (1.0 / total)
                results.append(low_dot(probs, values[:count]))
                head = slab * (LANES // HD) + place
                total_ref[rows, head : head + 1] = jnp.log(total) + peak
            context_ref[rows, cols] = jnp.where(lane < HD, results[0], results[1]).astype(
                jnp.bfloat16
            )


def attend_backward_kernel(
    query_ref,
    pair_ref,
    total_ref,
    grad_ref,
    cosine_ref,
    sine_ref,
    grad_query_ref,
    grad_pair_ref,
    key_sum_ref,
    value_sum_ref,
):
    length = query_ref.shape[0]
    cosine, sine = cosine_ref[...], -sine_ref[...]
    pair = pair_ref[...].astype(jnp.float32)
    left = lane_index(pair.shape) < HD
    moved = pltpu.roll(pair, HD, 1)
    keys = jnp.where(left, pair, moved).astype(jnp.bfloat16)
    values = jnp.where(left, moved, pair).astype(jnp.bfloat16)
    scale = HD ** (-0.5)
    key_sum_ref[...] = jnp.zeros_like(key_sum_ref)
    value_sum_ref[...] = jnp.zeros_like(value_sum_ref)
    for slab in range(query_ref.shape[1] // LANES):
        cols = pl.ds(slab * LANES, LANES)
        for tile in range(length // SPAN):
            rows = slice(tile * SPAN, (tile + 1) * SPAN)
            count = (tile + 1) * SPAN
            query = query_ref[rows, cols]
            upstream = grad_ref[rows, cols]
            lane = lane_index(query.shape)
            square = (SPAN, count)
            causal = row_index(square) + tile * SPAN >= lane_index(square)
            results = []
            for place in range(LANES // HD):
                mine = (lane >= place * HD) & (lane < place * HD + HD)
                head = slab * (LANES // HD) + place
                own_query = jnp.where(mine, query, 0)
                own_up = jnp.where(mine, upstream, 0)
                scores = low_against(own_query, keys[:count]) * scale
                scores = jnp.where(causal, scores, -jnp.inf)
                probs = jnp.exp(scores - total_ref[rows, head : head + 1])
                grad_probs = low_against(own_up, values[:count])
                mean = jnp.sum(probs * grad_probs, axis=-1, keepdims=True)
                grad_scores = (probs * (grad_probs - mean)).astype(jnp.bfloat16)
                results.append(low_dot(grad_scores, keys[:count]))
                key_sum_ref[0:count, :] += low_inner(grad_scores, own_query)
                value_sum_ref[0:count, :] += low_inner(probs, own_up)
            grad_query = jnp.where(lane < HD, results[0], results[1]) * scale
            grad_query_ref[rows, cols] = turn(
                grad_query, cosine[rows, :], sine[rows, :]
            ).astype(jnp.bfloat16)
    grad_key = key_sum_ref[...]
    grad_key = turn((grad_key + pltpu.roll(grad_key, HD, 1)) * scale, cosine, sine)
    grad_value = value_sum_ref[...]
    grad_value = grad_value + pltpu.roll(grad_value, HD, 1)
    grad_pair_ref[...] = jnp.where(left, grad_key, grad_value).astype(jnp.bfloat16)


def attend_forward(query, pair, length):
    group, width = query.shape
    heads = width // HD
    cosine, sine = rope_wide(length)
    return pl.pallas_call(
        attend_forward_kernel,
        grid=(group // length,),
        in_specs=[
            by_sequence(length, width),
            by_sequence(length, LANES),
            fixed(length, LANES),
            fixed(length, LANES),
        ],
        out_specs=[
            by_sequence(length, width),
            by_sequence(length, width),
            by_sequence(length, LANES),
            by_sequence(length, LANES),
        ],
        out_shape=[
            jax.ShapeDtypeStruct((group, width), jnp.bfloat16),
            jax.ShapeDtypeStruct((group, width), jnp.bfloat16),
            jax.ShapeDtypeStruct((group, LANES), jnp.bfloat16),
            jax.ShapeDtypeStruct((group, LANES), jnp.float32),
        ],
        compiler_params=pltpu.CompilerParams(vmem_limit_bytes=VMEM_LIMIT),
        cost_estimate=pl.CostEstimate(
            flops=4 * group * width * length,
            bytes_accessed=12 * group * width,
            transcendentals=group * heads * length // 2,
        ),
        name="attend_forward",
    )(query, pair, jnp.asarray(cosine), jnp.asarray(sine))


def attend_backward(query, pair, total, grad, length):
    group, width = query.shape
    heads = width // HD
    cosine, sine = rope_wide(length)
    return pl.pallas_call(
        attend_backward_kernel,
        grid=(group // length,),
        in_specs=[
            by_sequence(length, width),
            by_sequence(length, LANES),
            by_sequence(length, LANES),
            by_sequence(length, width),
            fixed(length, LANES),
            fixed(length, LANES),
        ],
        out_specs=[by_sequence(length, width), by_sequence(length, LANES)],
        out_shape=[
            jax.ShapeDtypeStruct((group, width), jnp.bfloat16),
            jax.ShapeDtypeStruct((group, LANES), jnp.bfloat16),
        ],
        scratch_shapes=[
            pltpu.VMEM((length, LANES), jnp.float32),
            pltpu.VMEM((length, LANES), jnp.float32),
        ],
        compiler_params=pltpu.CompilerParams(vmem_limit_bytes=VMEM_LIMIT),
        cost_estimate=pl.CostEstimate(
            flops=10 * group * width * length,
            bytes_accessed=12 * group * width,
            transcendentals=group * heads * length // 2,
        ),
        name="attend_backward",
    )(query, pair, total, grad, jnp.asarray(cosine), jnp.asarray(sine))


def step_groups(size):
    return [1] * (size.bit_length() - 1)


def after(part, *deps):
    return lax.optimization_barrier((part,) + deps)[0]


def behind(part, dep):
    zero = jnp.minimum(jnp.abs(dep[:1, :1].astype(jnp.float32)), 0.0)
    return part + zero.astype(part.dtype)


class Sum:
    def __init__(self, part, size):
        self.size = size
        self.direct = bool(size & (size - 1) or part.shape[0] % size)
        self.steps = [] if self.direct else step_groups(size)
        self.shift = 0
        self.part = part
        self.gives = [part]
        if not self.direct:
            self.part = part.reshape(size, part.shape[0] // size, part.shape[1])
            self.prepare()

    def prepare(self):
        if not self.steps:
            self.gives = [self.part]
            return
        ways = 1 << self.steps[0]
        rest = self.part.shape[0] // ways
        view = self.part.reshape((rest, ways) + self.part.shape[1:])
        mine = (lax.axis_index("dp") >> self.shift) & (ways - 1)
        self.keep = lax.dynamic_index_in_dim(view, mine, 1, False)
        self.gives = [
            lax.dynamic_index_in_dim(view, mine ^ way, 1, False) for way in range(1, ways)
        ]

    def advance(self, *deps):
        if self.steps:
            total = after(self.keep, *deps).astype(jnp.float32)
            for way, give in enumerate(self.gives, 1):
                pairs = [(index, index ^ (way << self.shift)) for index in range(self.size)]
                total = total + lax.ppermute(give, "dp", pairs).astype(jnp.float32)
            self.part = total.astype(jnp.bfloat16)
            self.shift += self.steps.pop(0)
            self.prepare()
        return self.gives

    def joined(self, middle=None, *deps):
        groups, shift = step_groups(self.size), self.size.bit_length() - 1
        part = after(self.reduced(), *deps)
        if middle is not None:
            part = middle(part)
        self.trail = [part]
        if self.direct:
            return part
        rows, width = part.shape
        for group in reversed(groups):
            ways = 1 << group
            shift -= group
            mine = (lax.axis_index("dp") >> shift) & (ways - 1)
            part = part.reshape(-1, 1, rows, width)
            got = [part]
            for way in range(1, ways):
                pairs = [(index, index ^ (way << shift)) for index in range(self.size)]
                got.append(lax.ppermute(part, "dp", pairs))
            for bit in range(group):
                flip = ((mine >> bit) & 1) == 1
                got = [
                    jnp.where(flip, got[way ^ (1 << bit)], got[way]) for way in range(ways)
                ]
            part = jnp.concatenate(got, axis=1)
            self.trail.append(part)
        return part.reshape(-1, width)

    def reduced(self):
        while self.steps:
            self.advance()
        return lax.psum(self.part, "dp") if self.direct else self.part[0]


def other(part):
    return lax.ppermute(part, "tensor", [(0, 1), (1, 0)])


def all_rows(part, shards):
    if shards != 2:
        return lax.all_gather(part, "tensor", axis=0, tiled=True)
    got = other(part)
    return jnp.where(
        lax.axis_index("tensor") == 0,
        jnp.concatenate([part, got], axis=0),
        jnp.concatenate([got, part], axis=0),
    )


def sum_all(part, shards, *deps):
    if shards != 2:
        return lax.psum(part, "tensor").astype(jnp.float32)
    return after(part, *deps).astype(jnp.float32) + other(part).astype(jnp.float32)


def sum_own(part, shards):
    if shards != 2:
        return lax.psum_scatter(part, "tensor", scatter_dimension=0, tiled=True).astype(jnp.float32)
    me = lax.axis_index("tensor")
    halves = part.reshape(2, part.shape[0] // 2, part.shape[1])
    keep = lax.dynamic_index_in_dim(halves, me, 0, False)
    got = other(lax.dynamic_index_in_dim(halves, 1 - me, 0, False))
    return keep.astype(jnp.float32) + got.astype(jnp.float32)


def own_rows(part, rows):
    return lax.dynamic_slice_in_dim(part, lax.axis_index("tensor") * rows, rows, 0)


def column_pack(vectors, rows):
    flat = jnp.concatenate([item.reshape(-1) for item in vectors])
    width = -(-flat.shape[0] // rows)
    return jnp.pad(flat, (0, width * rows - flat.shape[0])).reshape(width, rows).T


def column_unpack(packed, shapes):
    flat = packed.T.reshape(-1)
    out, start = [], 0
    for shape in shapes:
        count = 1
        for size in shape:
            count *= size
        out.append(flat[start : start + count].reshape(shape))
        start += count
    return out


def body(
    dp_size,
    shards,
    layer_input,
    input_gain,
    middle_gain,
    mamba_gate,
    mamba_input,
    step_weight,
    state_weight,
    input_kernel,
    input_shift,
    state_kernel,
    state_shift,
    step_bias,
    decay_log,
    skip_gain,
    mamba_output,
    query_weight,
    keyvalue_weight,
    context_weight,
    gate_weight,
    up_weight,
    down_weight,
    cotangent,
):
    own = layer_input.shape[0]
    rows_low = all_rows(layer_input, shards)
    cotan_low = all_rows(cotangent, shards)
    rows = rows_low.astype(jnp.float32)
    gain_first = input_gain.astype(jnp.float32)
    gain_second = middle_gain.astype(jnp.float32)
    factor_first = lax.rsqrt(jnp.mean(rows * rows, axis=-1, keepdims=True) + EPSILON)
    normal_first = rows * factor_first
    whole = (normal_first * gain_first).astype(jnp.bfloat16)
    group = whole.shape[0]
    length = min(SEQ_LEN, group)
    seqs = group // length
    heads_here = query_weight.shape[1] // HD
    kv_head = lax.axis_index("tensor") * heads_here // (HQ // KVH)
    key_cols = lax.dynamic_slice_in_dim(keyvalue_weight, kv_head * HD, HD, 1)
    value_cols = lax.dynamic_slice_in_dim(keyvalue_weight, (KVH + kv_head) * HD, HD, 1)
    pair_weight = jnp.concatenate([key_cols, value_cols], axis=1)
    query_cols = query_weight.shape[1]
    query_pad = -query_cols % LANES
    query_wide = jnp.pad(query_weight, ((0, 0), (0, query_pad)))
    step_wide = pad_lanes(step_weight)
    heads = step_weight.shape[1]
    input_raw = forward_dot(whole, mamba_input)
    state_raw = forward_dot(whole, state_weight)
    step_raw = forward_dot(whole, step_wide)
    gate_raw = forward_dot(whole, mamba_gate)
    query_raw = forward_dot(whole, query_wide)
    pair_raw = forward_dot(whole, pair_weight)
    small = ssd_small(
        input_kernel.astype(jnp.float32),
        input_shift.astype(jnp.float32),
        state_kernel.astype(jnp.float32),
        state_shift.astype(jnp.float32),
        step_bias.astype(jnp.float32),
        decay_log.astype(jnp.float32),
        skip_gain.astype(jnp.float32),
    )
    gated_low, ssm_out, carries = ssd_forward(
        input_raw, state_raw, gate_raw, step_raw, small, heads, length
    )
    context_wide, queries, pairs, totals = attend_forward(
        query_raw, pair_raw, length
    )
    context_rows = context_wide[:, :query_cols]
    count = 2 if shards == 2 else 1
    spans = [slice(index * group // count, (index + 1) * group // count) for index in range(count)]
    context_rows = after(context_rows, cotan_low)
    resids, normals, factors, mids = [], [], [], []
    hiddens, gate_lows, upper_lows, back_parts, back_mids = [], [], [], [], []
    mixed_parts = [
        (
            forward_dot(gated_low[span], mamba_output)
            + forward_dot(context_rows[span], context_weight)
        ).astype(jnp.bfloat16)
        for span in spans
    ]
    for span, mixed_part in zip(spans, mixed_parts):
        resid = rows[span] + sum_all(mixed_part, shards, *back_parts)
        factor = lax.rsqrt(jnp.mean(resid * resid, axis=-1, keepdims=True) + EPSILON)
        normal = resid * factor
        mid = (normal * gain_second).astype(jnp.bfloat16)
        gate = forward_dot(mid, gate_weight)
        upper = forward_dot(mid, up_weight)
        sigmoid_gate = jax.nn.sigmoid(gate)
        silu_gate = gate * sigmoid_gate
        grad_hidden = against(cotan_low[span], down_weight)
        slope = sigmoid_gate * (1.0 + gate * (1.0 - sigmoid_gate))
        gate_low = (grad_hidden * upper * slope).astype(jnp.bfloat16)
        upper_low = (grad_hidden * silu_gate).astype(jnp.bfloat16)
        back_part = (against(gate_low, gate_weight) + against(upper_low, up_weight)).astype(
            jnp.bfloat16
        )
        resids.append(resid)
        normals.append(normal)
        factors.append(factor)
        mids.append(mid)
        hiddens.append((silu_gate * upper).astype(jnp.bfloat16))
        gate_lows.append(gate_low)
        upper_lows.append(upper_low)
        back_parts.append(back_part)
    back_mids = [sum_all(back_part, shards, *back_parts) for back_part in back_parts]
    whole_mid = jnp.concatenate(mids, axis=0)
    hidden = jnp.concatenate(hiddens, axis=0)
    grad_down = inner_rows(hidden, cotan_low).astype(jnp.bfloat16)
    grad_gate = inner_rows(whole_mid, jnp.concatenate(gate_lows, axis=0)).astype(jnp.bfloat16)
    grad_up = inner_rows(whole_mid, jnp.concatenate(upper_lows, axis=0)).astype(jnp.bfloat16)
    grad_gate, grad_up, grad_down = lax.psum((grad_gate, grad_up, grad_down), "dp")
    grad_middle = sum(
        jnp.sum(back_part.astype(jnp.float32) * normal, axis=0)
        for back_part, normal in zip(back_parts, normals)
    )
    grad_resids = [
        cotan_low[span].astype(jnp.float32) + norm_back(back_mid, gain_second, normal, factor)
        for span, back_mid, normal, factor in zip(spans, back_mids, normals, factors)
    ]

    def own_piece(pieces):
        if len(pieces) == 1:
            return own_rows(pieces[0], own)
        return jnp.where(lax.axis_index("tensor") == 0, pieces[0], pieces[1])

    mixer_all = jnp.concatenate([piece.astype(jnp.bfloat16) for piece in grad_resids], axis=0)
    ssm_rows = gated_low.shape[1]
    width = whole.shape[1]
    split_pairs = shards == KVH
    grad_gated = against(mixer_all, mamba_output)
    mixer_sum = Sum(
        inner_rows(jnp.concatenate([gated_low, context_rows], axis=1), mixer_all).astype(
            jnp.bfloat16
        ),
        dp_size,
    )
    grad_input_raw, grad_state_raw, grad_step_raw, input_sums, state_sums, head_sums = ssd_backward(
        input_raw,
        state_raw,
        gate_raw,
        step_raw,
        grad_gated,
        carries,
        small,
        heads,
        length,
    )
    input_sums = jnp.sum(input_sums, axis=0)
    state_sums = jnp.sum(state_sums, axis=0)
    head_sums = jnp.sum(head_sums, axis=0)[:, :heads]
    taps = input_kernel.shape[0]
    state_cols = state_weight.shape[1]
    step_cols = heads
    late_cols = jnp.concatenate([grad_input_raw, grad_state_raw], axis=1)
    late_sum = Sum(inner_rows(whole, late_cols).astype(jnp.bfloat16), dp_size)

    sigmoid_raw = jax.nn.sigmoid(gate_raw)
    grad_gate_raw = (
        grad_gated * ssm_out * (sigmoid_raw * (1.0 + gate_raw * (1.0 - sigmoid_raw)))
    ).astype(jnp.bfloat16)
    grad_context = against(mixer_all, context_weight).astype(jnp.bfloat16)
    grad_context = jnp.pad(grad_context, ((0, 0), (0, query_pad)))
    grad_query_raw, grad_pair_raw = attend_backward(
        queries, pairs, totals, after(grad_context, *late_sum.gives, *mixer_sum.advance()), length
    )
    early_cols = jnp.concatenate(
        [grad_gate_raw, grad_query_raw[:, :query_cols], grad_pair_raw, grad_step_raw], axis=1
    )
    total = against(late_cols, jnp.concatenate([mamba_input, state_weight], axis=1))
    total = total + against(
        early_cols, jnp.concatenate(
            [mamba_gate, query_weight, pair_weight, after(step_wide, mixed_parts[-1])], axis=1
        )
    )
    total_low = total.astype(jnp.bfloat16)
    grad_first = jnp.sum(total_low.astype(jnp.float32) * normal_first, axis=0)
    own_vectors = (input_sums[:taps], input_sums[taps], head_sums[0], head_sums[1], head_sums[2])
    shared_vectors = (grad_first, grad_middle, state_sums[:taps], state_sums[taps])
    own_pack = column_pack(own_vectors, width)
    shared_pack = column_pack(shared_vectors, width)
    shared_lane = step_cols + own_pack.shape[1]
    last_lane = shared_lane + shared_pack.shape[1]
    early = inner_rows(whole, early_cols)
    if not split_pairs:
        spread = jnp.zeros((width, 2 * KVH * HD), jnp.float32)
        spread = lax.dynamic_update_slice_in_dim(
            spread, early[:, -2 * HD - LANES : -HD - LANES], kv_head * HD, 1
        )
        spread = lax.dynamic_update_slice_in_dim(
            spread, early[:, -HD - LANES : -LANES], (KVH + kv_head) * HD, 1
        )
        early = jnp.concatenate(
            [early[:, : -2 * HD - LANES], spread, early[:, -LANES:]], axis=1
        )
    packs = jnp.pad(
        jnp.concatenate([own_pack, shared_pack], axis=1),
        ((0, 0), (early.shape[1] - LANES + step_cols, LANES - last_lane)),
    )
    early_sum = Sum((early + packs).astype(jnp.bfloat16), dp_size)

    def early_over_tensor(part):
        count = (2 * HD if split_pairs else 2 * KVH * HD) + LANES
        mine = part[:, -count:]
        if split_pairs:
            got = other(mine)
            both = (mine.astype(jnp.float32) + got.astype(jnp.float32)).astype(jnp.bfloat16)
            first = lax.axis_index("tensor") == 0
            low, high = jnp.where(first, mine, got), jnp.where(first, got, mine)
            pair = [low[:, :HD], high[:, :HD], low[:, HD : 2 * HD], high[:, HD : 2 * HD]]
        else:
            both = lax.psum(mine, "tensor")
            pair = [both[:, :-LANES]]
        lane = lane_index((part.shape[0], LANES))
        extra = jnp.where(
            (lane >= shared_lane) & (lane < last_lane), both[:, -LANES:], mine[:, -LANES:]
        )
        return jnp.concatenate([part[:, :-count]] + pair + [extra], axis=1)

    def late_over_tensor(part):
        mine = part[:, -state_cols:]
        if shards == 2:
            both = mine.astype(jnp.float32) + other(mine).astype(jnp.float32)
        else:
            both = lax.psum(mine, "tensor")
        return jnp.concatenate([part[:, :-state_cols], both.astype(jnp.bfloat16)], axis=1)

    early_sum.advance()
    mixer_sum.advance()
    mixer_sum.advance(*early_sum.gives)
    tail = late_sum.joined(late_over_tensor, *early_sum.gives)
    grad_mixer_out = mixer_sum.joined(None, *early_sum.gives)
    early = early_sum.joined(early_over_tensor)
    grad_gate, grad_up, grad_down = [
        after(item, early_sum.trail[min(1, len(early_sum.trail) - 1)])
        for item in (grad_gate, grad_up, grad_down)
    ]
    grad_mamba_out = grad_mixer_out[:ssm_rows]
    grad_context_w = grad_mixer_out[ssm_rows:]
    grad_mamba_input, grad_state = tail[:, :-state_cols], tail[:, -state_cols:]
    gate_cols = gate_raw.shape[1]
    extra = early[:, -LANES:]
    feed_part = behind(forward_dot(hidden, down_weight), total).astype(jnp.bfloat16)
    feed = sum_own(feed_part, shards)
    layer_output = (after(own_piece(resids), late_sum.trail[0]) + feed).astype(jnp.bfloat16)
    back_in = sum_own(total_low, shards)
    normal_own = own_rows(normal_first, own)
    factor_own = own_rows(factor_first, own)
    input_grad = after(own_piece(grad_resids), late_sum.trail[0]) + norm_back(back_in, gain_first, normal_own, factor_own)
    grad_step = extra[:, :step_cols]
    grad_in_kernel, grad_in_shift, grad_bias, grad_decay, grad_skip = column_unpack(
        extra[:, step_cols:shared_lane], [item.shape for item in own_vectors]
    )
    grad_first, grad_middle, grad_st_kernel, grad_st_shift = column_unpack(
        extra[:, shared_lane:last_lane], [item.shape for item in shared_vectors]
    )
    results = (
        grad_first,
        grad_middle,
        early[:, :gate_cols],
        grad_mamba_input,
        grad_step,
        grad_state,
        grad_in_kernel,
        grad_in_shift,
        grad_st_kernel,
        grad_st_shift,
        grad_bias,
        grad_decay,
        grad_skip,
        grad_mamba_out,
        early[:, gate_cols : gate_cols + query_cols],
        early[:, gate_cols + query_cols : -LANES],
        grad_context_w,
        grad_gate,
        grad_up,
        grad_down,
    )
    return (layer_output, input_grad) + tuple(item.astype(jnp.float32) for item in results)


def solution(mesh):
    in_specs = (
        P(("dp", "tensor"), None),
        P(),
        P(),
        P(None, "tensor"),
        P(None, "tensor"),
        P(None, "tensor"),
        P(),
        P(None, "tensor"),
        P("tensor"),
        P(),
        P(),
        P("tensor"),
        P("tensor"),
        P("tensor"),
        P("tensor", None),
        P(None, "tensor"),
        P(),
        P("tensor", None),
        P(None, "tensor"),
        P(None, "tensor"),
        P("tensor", None),
        P(("dp", "tensor"), None),
    )
    out_specs = (
        P(("dp", "tensor"), None),
        P(("dp", "tensor"), None),
        P(),
        P(),
        P(None, "tensor"),
        P(None, "tensor"),
        P(None, "tensor"),
        P(),
        P(None, "tensor"),
        P("tensor"),
        P(),
        P(),
        P("tensor"),
        P("tensor"),
        P("tensor"),
        P("tensor", None),
        P(None, "tensor"),
        P(),
        P("tensor", None),
        P(None, "tensor"),
        P(None, "tensor"),
        P("tensor", None),
    )
    run = partial(body, mesh.shape["dp"], mesh.shape["tensor"])
    return jax.shard_map(run, mesh=mesh, in_specs=in_specs, out_specs=out_specs, check_vma=False)
```
